32 devices in a mesh: seq: 32 (over z, y, x, core).
Axes of the slice: x: 2, y: 2, z: 4, core: 2. Of those that a mesh axis runs over, the one named last changes fastest.
Arguments:
- tokens: bfloat16 [8192, 2048], P('seq'), may hold values from -6 to 6
- starts: int32 [8192], P('seq'), may hold values from 0 to 1, as said below
- cotangent: bfloat16 [8192, 2048], P('seq'), may hold values from -6 to 6
- norm_gain: bfloat16 [2048], P('seq'), may hold values from 0.5 to 1.5
- gate_branch: bfloat16 [2048, 2560], P('seq'), may hold values from -0.125 to 0.125
- input_branch: bfloat16 [2048, 2560], P('seq'), may hold values from -0.125 to 0.125
- conv_weight: bfloat16 [4, 2560], P(None, 'seq'), may hold values from -3 to 3
- conv_bias: bfloat16 [2560], P('seq'), may hold values from -3 to 3
- decay_gate: bfloat16 [2560, 160], P('seq'), may hold values from -0.5 to 0.5
- decay_bias: bfloat16 [2560], P('seq'), may hold values from -3 to 3
- input_gate: bfloat16 [2560, 160], P('seq'), may hold values from -0.5 to 0.5
- input_bias: bfloat16 [2560], P('seq'), may hold values from -3 to 3
- decay_param: bfloat16 [2560], P('seq'), may hold values from -14 to -2.5, as said below
- out_proj: bfloat16 [2560, 2048], P('seq'), may hold values from -0.5 to 0.5
- mlp_gain: bfloat16 [2048], P('seq'), may hold values from 0.5 to 1.5
- mlp_gate: bfloat16 [2048, 6144], P('seq'), may hold values from -0.125 to 0.125
- mlp_up: bfloat16 [2048, 6144], P('seq'), may hold values from -0.125 to 0.125
- mlp_down: bfloat16 [6144, 2048], P('seq'), may hold values from -0.15625 to 0.15625
Outputs:
- block_out: bfloat16 [8192, 2048], P('seq')
- grad_tokens: float32 [8192, 2048], P('seq')
- grad_norm_gain: float32 [2048], P('seq')
- grad_gate_branch: float32 [2048, 2560], P('seq')
- grad_input_branch: float32 [2048, 2560], P('seq')
- grad_conv_weight: float32 [4, 2560], P(None, 'seq')
- grad_conv_bias: float32 [2560], P('seq')
- grad_decay_gate: float32 [2560, 160], P('seq')
- grad_decay_bias: float32 [2560], P('seq')
- grad_input_gate: float32 [2560, 160], P('seq')
- grad_input_bias: float32 [2560], P('seq')
- grad_decay_param: float32 [2560], P('seq')
- grad_out_proj: float32 [2560, 2048], P('seq')
- grad_mlp_gain: float32 [2048], P('seq')
- grad_mlp_gate: float32 [2048, 6144], P('seq')
- grad_mlp_up: float32 [2048, 6144], P('seq')
- grad_mlp_down: float32 [6144, 2048], P('seq')
The draws below stay inside these ranges and needn't reach their ends.
Inputs may be any that keep to these rules, and one draw needn't show every extreme that they name: starts marks five sequences: position 0 is a start, two more starts lie in the first 256 positions and two in the last 256, so one sequence covers every position from 256 to 7935. `decay_param`: softplus of it is a channel's decay rate per step.
All inputs are finite; a program needn't handle non-finite values.
Results may differ from the reference program's by a relative error of at most 0.0071.
The reference program's roundings to bfloat16 on the way count: a program that leaves them out, or rounds other values in their place, can miss the bound.
Values may be sent and summed in bfloat16 or wider, within the bound.
A program may use at most 576 MiB of HBM per device.

```python
import jax
import jax.numpy as jnp
from jax import lax

D = 2048
R = 2560
H = 16
FF = 6144
CW = 4
TOK_DEV = 256
TOKENS = 8192


def draw_starts(key, part):
    key = jax.random.fold_in(key, 7)
    subkeys = jax.random.split(key, 4)
    first_start = jax.random.randint(subkeys[0], (), 1, TOK_DEV // 2)
    second_start = jax.random.randint(subkeys[1], (), TOK_DEV // 2, TOK_DEV)
    third_start = TOKENS - TOK_DEV + jax.random.randint(subkeys[2], (), 1, TOK_DEV // 2)
    fourth_start = TOKENS - TOK_DEV + jax.random.randint(subkeys[3], (), TOK_DEV // 2, TOK_DEV)
    position = jnp.arange(TOKENS)
    marked = (position == 0) | (position == first_start) | (position == second_start) | (position == third_start) | (position == fourth_start)
    return marked.astype(jnp.int32)


def draw_decay_param(key, part):
    key = jax.random.fold_in(key, 13)
    subkeys = jax.random.split(key, 3)
    share = 0.5
    slow_pick = jax.random.uniform(subkeys[0], (R,), jnp.float32) < share
    slow_rate = jnp.exp(jax.random.uniform(subkeys[1], (R,), jnp.float32, jnp.log(0.1 / TOKENS), jnp.log(0.5 / TOKENS)))
    fast_rate = jnp.exp(jax.random.uniform(subkeys[2], (R,), jnp.float32, jnp.log(0.5 / TOKENS), jnp.log(0.05)))
    chosen = jnp.where(slow_pick, slow_rate, fast_rate)
    return jnp.log(jnp.expm1(chosen)).astype(jnp.bfloat16)


def levels(own_key, shape, shards, least, top_value):
    level = 1.0
    for dim, parts in shards:
        heights = jax.random.uniform(jax.random.fold_in(jax.random.fold_in(own_key, 6), dim), (parts,), jnp.float32, least / len(shards), top_value / len(shards))
        level = level * jnp.repeat(jnp.exp(heights), shape[dim] // parts).reshape((-1,) + (1,) * (len(shape) - 1 - dim))
    return level


def noise(rng, dims, spread, reach, cuts=(), held_as=jnp.bfloat16):
    loudness = levels(rng, dims, cuts, -0.22, 0.18) if cuts else 1.0
    entries = jax.random.normal(rng, dims, jnp.float32) * spread * loudness
    return jnp.minimum(jnp.maximum(entries, -reach), reach).astype(held_as)


def setup_inputs(seed: int = 0) -> dict:
    splits = jax.random.split(jax.random.key(seed), 19)
    return {
        "tokens": noise(splits[0], (TOKENS, D), 1.0, 6.0, ((0, 32),)),
        "starts": draw_starts(jax.random.fold_in(splits[18], 71), 0),
        "cotangent": noise(splits[2], (TOKENS, D), 1.0, 6.0, ((0, 32),)),
        "norm_gain": jnp.clip(1.0 + 0.1 * jax.random.normal(splits[3], (D,), jnp.float32), 0.5, 1.5).astype(jnp.bfloat16),
        "gate_branch": noise(splits[4], (D, R), D ** -0.5, 0.125, ((0, 32),)),
        "input_branch": noise(splits[5], (D, R), D ** -0.5, 0.125, ((0, 32),)),
        "conv_weight": noise(splits[6], (CW, R), CW ** -0.5, 3.0, ((1, 32),)),
        "conv_bias": noise(splits[7], (R,), 0.5, 3.0, ((0, 32),)),
        "decay_gate": noise(splits[8], (R, R // H), (R // H) ** -0.5, 0.5, ((0, 32),)),
        "decay_bias": noise(splits[9], (R,), 0.5, 3.0, ((0, 32),)),
        "input_gate": noise(splits[10], (R, R // H), (R // H) ** -0.5, 0.5, ((0, 32),)),
        "input_bias": noise(splits[11], (R,), 0.5, 3.0, ((0, 32),)),
        "decay_param": draw_decay_param(jax.random.fold_in(splits[18], 71), 0),
        "out_proj": noise(splits[13], (R, D), (R // 16) ** -0.5, 0.5, ((0, 32),)),
        "mlp_gain": jnp.clip(1.0 + 0.1 * jax.random.normal(splits[14], (D,), jnp.float32), 0.5, 1.5).astype(jnp.bfloat16),
        "mlp_gate": noise(splits[15], (D, FF), D ** -0.5, 0.125, ((0, 32),)),
        "mlp_up": noise(splits[16], (D, FF), D ** -0.5, 0.125, ((0, 32),)),
        "mlp_down": noise(splits[17], (FF, D), (FF // 4) ** -0.5, 0.15625, ((0, 32),)),
    }


epsilon = 1e-06
rate_scale = 8.0

@jax.custom_vjp
def low(v):
    return lax.optimization_barrier(v.astype(jnp.bfloat16)).astype(jnp.float32)

@jax.custom_vjp
def low_back(v):
    return v

def low_keep(v):
    return (low(v), None)

def low_pass(kept, grad):
    return (grad,)

def back_keep(v):
    return (v, None)

def back_low(kept, grad):
    return (low(grad),)
low.defvjp(low_keep, low_pass)
low_back.defvjp(back_keep, back_low)

def product(left_side, right_side):
    return jnp.dot(left_side, right_side, precision=lax.Precision.HIGHEST)

def heads_product(values, weight):
    row_count = values.shape[0]
    shaped = values.reshape(row_count, H, R // H)
    blocks = weight.reshape(H, R // H, R // H)
    return jnp.einsum('thi,hij->thj', shaped, blocks, precision=lax.Precision.HIGHEST).reshape(row_count, R)

def rms_norm(values, scales):
    return values * lax.rsqrt(lax.optimization_barrier(jnp.mean(values * values, axis=-1, keepdims=True)) + epsilon) * scales

def gelu_tanh(values):
    return jax.nn.gelu(values, approximate=True)

def lru_terms(decay_pre, input_pre, conv_out, decay_param, flag_rows):
    log_decay = -rate_scale * jax.nn.sigmoid(decay_pre) * jax.nn.softplus(decay_param)
    keep_rows = 1.0 - flag_rows[:, None]
    coefficient = jnp.exp(log_decay) * keep_rows
    scale_in = flag_rows[:, None] + keep_rows * jnp.sqrt(-jnp.expm1(2.0 * log_decay))
    drive_term = scale_in * jax.nn.sigmoid(input_pre) * conv_out
    return (coefficient, drive_term)

def lru_step(lru_state, element):
    lru_state = element[0] * lru_state + element[1]
    return (lru_state, lru_state)

def block_step(params, carried, inputs):
    norm_gain, gate_branch, input_branch, conv_weight, conv_bias, decay_gate, decay_bias, input_gate, input_bias, decay_param, out_proj, mlp_gain, mlp_gate, mlp_up, mlp_down = params
    conv_tail, seg_tail, lru_state, seg_last = carried
    tokens, starts = inputs
    row_count = tokens.shape[0]
    segment = seg_last + jnp.cumsum(starts).astype(jnp.int32)
    normed = low(rms_norm(tokens, norm_gain))
    gate_pre = low_back(product(normed, gate_branch))
    gate_act = gelu_tanh(gate_pre)
    conv_input = low(low_back(product(normed, input_branch)))
    padded = jnp.concatenate([conv_tail, conv_input], axis=0)
    seg_padded = jnp.concatenate([seg_tail, segment], axis=0)
    conv_out = conv_bias + jnp.zeros((row_count, R), jnp.float32)
    for offset in range(CW):
        lead = CW - 1 - offset
        window = padded[lead:lead + row_count]
        same_doc = (seg_padded[lead:lead + row_count] == segment)[:, None]
        conv_out = conv_out + conv_weight[offset] * jnp.where(same_doc, window, 0.0)
    conv_low = low(conv_out)
    decay_pre = low_back(heads_product(conv_low, decay_gate)) + decay_bias
    input_pre = low_back(heads_product(conv_low, input_gate)) + input_bias
    coefficient, drive_term = lru_terms(decay_pre, input_pre, conv_out, decay_param, starts.astype(jnp.float32))
    final_state, states = lax.scan(lru_step, lru_state, (coefficient, drive_term))
    mixed_rows = low(states * gate_act)
    middle = tokens + low_back(product(mixed_rows, out_proj))
    normed_two = low(rms_norm(middle, mlp_gain))
    gate_mlp = low_back(product(normed_two, mlp_gate))
    up_mlp = low_back(product(normed_two, mlp_up))
    hidden = low(gelu_tanh(gate_mlp) * up_mlp)
    result = middle + low_back(product(hidden, mlp_down))
    carried = (padded[row_count:], seg_padded[row_count:], final_state, segment[-1])
    return (carried, result)

def forward(tokens, starts, params):
    block_rows = TOK_DEV * 8
    block_count = TOKENS // block_rows
    initial = (jnp.zeros((CW - 1, R), jnp.float32), jnp.zeros((CW - 1,), jnp.int32), jnp.zeros((R,), jnp.float32), jnp.zeros((), jnp.int32))
    checked_step = jax.checkpoint(block_step)

    def scan_step(carried, inputs):
        return checked_step(params, carried, inputs)
    final_carry, results = lax.scan(scan_step, initial, (tokens.reshape(block_count, block_rows, D), starts.reshape(block_count, block_rows)))
    return results.reshape(TOKENS, D)

def reference(tokens, starts, cotangent, norm_gain, gate_branch, input_branch, conv_weight, conv_bias, decay_gate, decay_bias, input_gate, input_bias, decay_param, out_proj, mlp_gain, mlp_gate, mlp_up, mlp_down):
    params = tuple((weight.astype(jnp.float32) for weight in (norm_gain, gate_branch, input_branch, conv_weight, conv_bias, decay_gate, decay_bias, input_gate, input_bias, decay_param, out_proj, mlp_gain, mlp_gate, mlp_up, mlp_down)))

    def wrapped(values, *weights):
        return forward(values, starts, weights)
    result, pullback = jax.vjp(wrapped, tokens.astype(jnp.float32), *params)
    gradients = pullback(cotangent.astype(jnp.float32))
    return (result.astype(jnp.bfloat16), gradients[0], gradients[1], gradients[2], gradients[3], gradients[4], gradients[5], gradients[6], gradients[7], gradients[8], gradients[9], gradients[10], gradients[11], gradients[12], gradients[13], gradients[14], gradients[15])
```

```python
import functools

import jax
import jax.numpy as jnp
from jax import lax
from jax.experimental import pallas as pl
from jax.experimental.pallas import tpu as pltpu
from jax.sharding import PartitionSpec as P

H = 16
CW = 4


epsilon = 1e-06
rate_scale = 8.0


def passed_along(block, axis, distance):
    devices = range(lax.axis_size(axis))
    route = [(i - distance, i) for i in devices if i - distance in devices]
    return lax.ppermute(block, axis, route)


def prefix(value, axis, combine, identity, reverse):
    peers, place = (lax.axis_size(axis), lax.axis_index(axis))
    everything = jax.tree.map(lambda part: lax.all_gather(part, axis), value)
    start = jax.tree.map(
        lambda part, zero: jnp.broadcast_to(jnp.asarray(zero, part.dtype), part.shape),
        value,
        identity,
    )

    def hop(k, before):
        at = peers - 1 - k if reverse else k
        reached = at > place if reverse else at < place
        new = combine(before, jax.tree.map(lambda part: part[at], everything))
        return jax.tree.map(lambda a, b: jnp.where(reached, a, b), new, before)

    return lax.fori_loop(0, peers, hop, start)


def gelu_tanh(values):
    return jax.nn.gelu(values, approximate=True)


def rms_norm(values, scales):
    return values * lax.rsqrt(jnp.mean(values * values, axis=-1, keepdims=True) + epsilon) * scales


def combine(earlier_part, later_part):
    return (earlier_part[0] * later_part[0], later_part[0] * earlier_part[1] + later_part[1])


def heads_product(values, weight):
    row_count, lru_width = values.shape
    shaped = values.reshape(row_count, H, lru_width // H)
    blocks = weight.reshape(H, lru_width // H, lru_width // H)
    return jnp.einsum("thi,hij->thj", shaped, blocks, preferred_element_type=jnp.float32).reshape(
        row_count, lru_width
    )


def heads_back(grads_low, weight):
    row_count, lru_width = grads_low.shape
    shaped = grads_low.reshape(row_count, H, lru_width // H)
    blocks = weight.reshape(H, lru_width // H, lru_width // H)
    return jnp.einsum("thj,hij->thi", shaped, blocks, preferred_element_type=jnp.float32).reshape(
        row_count, lru_width
    )


def heads_grad(values, grads_low):
    row_count, lru_width = values.shape
    left_side = values.reshape(row_count, H, lru_width // H)
    right_side = grads_low.reshape(row_count, H, lru_width // H)
    return jnp.einsum(
        "thi,thj->hij", left_side, right_side, preferred_element_type=jnp.float32
    ).reshape(lru_width, lru_width // H)


def lru_terms(decay_pre, input_pre, conv_out, decay_param, flag_rows):
    log_decay = -rate_scale * jax.nn.sigmoid(decay_pre) * jax.nn.softplus(decay_param)
    keep_rows = 1.0 - flag_rows[:, None]
    coefficient = jnp.exp(log_decay) * keep_rows
    scale_in = flag_rows[:, None] + keep_rows * jnp.sqrt(-jnp.expm1(2.0 * log_decay))
    drive_term = scale_in * jax.nn.sigmoid(input_pre) * conv_out
    return (coefficient, drive_term)


def build_masks(flag_rows):
    row_count = flag_rows.shape[0]
    running = jnp.ones((row_count,), jnp.float32)
    masks = [running]
    for offset in range(1, CW):
        earlier_flags = jnp.concatenate(
            [jnp.zeros((offset - 1,), jnp.float32), flag_rows[: row_count - (offset - 1)]]
        )
        running = running * (1.0 - earlier_flags)
        masks.append(running)
    return masks


def send_mask(flag_rows):
    tail_keep = 1.0 - flag_rows[flag_rows.shape[0] - (CW - 1) :]
    after_rows = jnp.cumprod(tail_keep[::-1])[::-1]
    return jnp.concatenate([after_rows[1:], jnp.ones((1,), jnp.float32)])


def conv_local(padded, weight, bias, masks):
    row_count = masks[0].shape[0]
    conv_total = bias + jnp.zeros((row_count, padded.shape[1]), jnp.float32)
    for offset in range(CW):
        lead = CW - 1 - offset
        conv_total = conv_total + weight[offset] * (
            padded[lead : lead + row_count] * masks[offset][:, None]
        )
    return conv_total


def mlp_act(gate_values, up_values):
    return gelu_tanh(gate_values) * up_values


def token_split_body(
    tokens,
    starts,
    cotangent,
    norm_gain,
    gate_branch,
    input_branch,
    conv_weight,
    conv_bias,
    decay_gate,
    decay_bias,
    input_gate,
    input_bias,
    decay_param,
    out_proj,
    mlp_gain,
    mlp_gate,
    mlp_up,
    mlp_down,
):
    (
        whole_norm_gain,
        whole_gate_branch,
        whole_input_branch,
        whole_conv_weight,
        whole_conv_bias,
        whole_decay_gate,
        whole_decay_bias,
        whole_input_gate,
        whole_input_bias,
        whole_decay_param,
        whole_out_proj,
    ) = (
        lax.all_gather(norm_gain, "seq", axis=0, tiled=True),
        lax.all_gather(gate_branch, "seq", axis=0, tiled=True),
        lax.all_gather(input_branch, "seq", axis=0, tiled=True),
        lax.all_gather(conv_weight, "seq", axis=1, tiled=True),
        lax.all_gather(conv_bias, "seq", axis=0, tiled=True),
        lax.all_gather(decay_gate, "seq", axis=0, tiled=True),
        lax.all_gather(decay_bias, "seq", axis=0, tiled=True),
        lax.all_gather(input_gate, "seq", axis=0, tiled=True),
        lax.all_gather(input_bias, "seq", axis=0, tiled=True),
        lax.all_gather(decay_param, "seq", axis=0, tiled=True),
        lax.all_gather(out_proj, "seq", axis=0, tiled=True),
    )
    flag_rows = starts.astype(jnp.float32)
    row_count = tokens.shape[0]
    values = tokens.astype(jnp.float32)
    normed = rms_norm(values, whole_norm_gain.astype(jnp.float32)).astype(jnp.bfloat16)
    gate_pre = jnp.dot(normed, whole_gate_branch, preferred_element_type=jnp.float32)
    gate_act = gelu_tanh(gate_pre)
    conv_input = jnp.dot(normed, whole_input_branch, preferred_element_type=jnp.float32).astype(
        jnp.bfloat16
    )
    lru_width = conv_input.shape[1]
    alive_rows = send_mask(flag_rows)
    masks = build_masks(flag_rows)
    outgoing = conv_input[row_count - (CW - 1) :] * alive_rows[:, None].astype(jnp.bfloat16)
    incoming = passed_along(outgoing, "seq", 1)
    padded = jnp.concatenate([incoming, conv_input], axis=0).astype(jnp.float32)
    conv_out = conv_local(
        padded, whole_conv_weight.astype(jnp.float32), whole_conv_bias.astype(jnp.float32), masks
    )
    conv_low = conv_out.astype(jnp.bfloat16)
    decay_pre = heads_product(conv_low, whole_decay_gate) + whole_decay_bias.astype(jnp.float32)
    input_pre = heads_product(conv_low, whole_input_gate) + whole_input_bias.astype(jnp.float32)
    param_full = whole_decay_param.astype(jnp.float32)
    coefficient, drive_term = lru_terms(decay_pre, input_pre, conv_out, param_full, flag_rows)
    cumulative, local_state = lax.associative_scan(combine, (coefficient, drive_term), axis=0)
    entering = prefix(
        (cumulative[-1], local_state[-1]),
        "seq",
        combine,
        (jnp.ones_like(cumulative[-1]), jnp.zeros_like(local_state[-1])),
        False,
    )
    incoming_state = entering[1]
    states = local_state + cumulative * incoming_state[None, :]
    mixed_rows = (states * gate_act).astype(jnp.bfloat16)
    middle = values + jnp.dot(mixed_rows, whole_out_proj, preferred_element_type=jnp.float32)
    whole_mlp_gain, whole_mlp_gate, whole_mlp_up, whole_mlp_down = (
        lax.all_gather(mlp_gain, "seq", axis=0, tiled=True),
        lax.all_gather(mlp_gate, "seq", axis=0, tiled=True),
        lax.all_gather(mlp_up, "seq", axis=0, tiled=True),
        lax.all_gather(mlp_down, "seq", axis=0, tiled=True),
    )
    gain_two = whole_mlp_gain.astype(jnp.float32)
    normed_two = rms_norm(middle, gain_two).astype(jnp.bfloat16)
    gate_mlp = jnp.dot(normed_two, whole_mlp_gate, preferred_element_type=jnp.float32)
    up_mlp = jnp.dot(normed_two, whole_mlp_up, preferred_element_type=jnp.float32)
    hidden = mlp_act(gate_mlp, up_mlp).astype(jnp.bfloat16)
    result = middle + jnp.dot(hidden, whole_mlp_down, preferred_element_type=jnp.float32)
    block_out = result.astype(jnp.bfloat16)
    back_mlp_gain, back_mlp_gate, back_mlp_up, back_mlp_down = (
        lax.all_gather(mlp_gain, "seq", axis=0, tiled=True),
        lax.all_gather(mlp_gate, "seq", axis=0, tiled=True),
        lax.all_gather(mlp_up, "seq", axis=0, tiled=True),
        lax.all_gather(mlp_down, "seq", axis=0, tiled=True),
    )
    grad_mlp_down = jnp.einsum("tf,td->fd", hidden, cotangent, preferred_element_type=jnp.float32)
    grad_hidden = jnp.einsum(
        "td,fd->tf", cotangent, back_mlp_down, preferred_element_type=jnp.float32
    )
    unused_act, pull_act = jax.vjp(mlp_act, gate_mlp, up_mlp)
    grad_gate_full, grad_up_full = pull_act(grad_hidden)
    grad_gate_low = grad_gate_full.astype(jnp.bfloat16)
    grad_up_low = grad_up_full.astype(jnp.bfloat16)
    grad_mlp_gate = jnp.einsum(
        "td,tf->df", normed_two, grad_gate_low, preferred_element_type=jnp.float32
    )
    grad_mlp_up = jnp.einsum(
        "td,tf->df", normed_two, grad_up_low, preferred_element_type=jnp.float32
    )
    grad_normed_two = jnp.einsum(
        "tf,df->td", grad_gate_low, back_mlp_gate, preferred_element_type=jnp.float32
    ) + jnp.einsum("tf,df->td", grad_up_low, back_mlp_up, preferred_element_type=jnp.float32)
    unused_norm, pull_norm = jax.vjp(rms_norm, middle, back_mlp_gain.astype(jnp.float32))
    grad_middle_norm, grad_mlp_gain = pull_norm(grad_normed_two)
    mlp_sums = (
        lax.psum_scatter(grad_mlp_gain, "seq", scatter_dimension=0, tiled=True),
        lax.psum_scatter(grad_mlp_gate, "seq", scatter_dimension=0, tiled=True),
        lax.psum_scatter(grad_mlp_up, "seq", scatter_dimension=0, tiled=True),
        lax.psum_scatter(grad_mlp_down, "seq", scatter_dimension=0, tiled=True),
    )
    grad_middle = cotangent.astype(jnp.float32) + grad_middle_norm
    grad_branch = grad_middle.astype(jnp.bfloat16)
    (
        back_norm_gain,
        back_gate_branch,
        back_input_branch,
        back_conv_weight,
        back_conv_bias,
        back_decay_gate,
        back_decay_bias,
        back_input_gate,
        back_input_bias,
        back_decay_param,
        back_out_proj,
    ) = (
        lax.all_gather(norm_gain, "seq", axis=0, tiled=True),
        lax.all_gather(gate_branch, "seq", axis=0, tiled=True),
        lax.all_gather(input_branch, "seq", axis=0, tiled=True),
        lax.all_gather(conv_weight, "seq", axis=1, tiled=True),
        lax.all_gather(conv_bias, "seq", axis=0, tiled=True),
        lax.all_gather(decay_gate, "seq", axis=0, tiled=True),
        lax.all_gather(decay_bias, "seq", axis=0, tiled=True),
        lax.all_gather(input_gate, "seq", axis=0, tiled=True),
        lax.all_gather(input_bias, "seq", axis=0, tiled=True),
        lax.all_gather(decay_param, "seq", axis=0, tiled=True),
        lax.all_gather(out_proj, "seq", axis=0, tiled=True),
    )
    grad_out_proj = jnp.einsum(
        "tr,td->rd", mixed_rows, grad_branch, preferred_element_type=jnp.float32
    )
    grad_mixed = jnp.einsum(
        "td,rd->tr", grad_branch, back_out_proj, preferred_element_type=jnp.float32
    )
    grad_states = grad_mixed * gate_act
    unused_gelu, pull_gelu = jax.vjp(gelu_tanh, gate_pre)
    grad_gate_pre = pull_gelu(grad_mixed * states)[0].astype(jnp.bfloat16)
    shifted_coef = jnp.concatenate([coefficient[1:], jnp.ones((1, lru_width), jnp.float32)], axis=0)
    back_cumulative, back_local = lax.associative_scan(
        combine, (shifted_coef[::-1], grad_states[::-1]), axis=0
    )
    back_cumulative = back_cumulative[::-1]
    back_local = back_local[::-1]
    leaving = prefix(
        (coefficient[0] * back_cumulative[0], coefficient[0] * back_local[0]),
        "seq",
        combine,
        (jnp.ones_like(back_local[0]), jnp.zeros_like(back_local[0])),
        True,
    )
    incoming_adjoint = leaving[1]
    adjoint = back_local + back_cumulative * incoming_adjoint[None, :]
    previous = jnp.concatenate([incoming_state[None, :], states[:-1]], axis=0)

    def terms_only(decay_values, input_values, conv_values, param_values):
        return lru_terms(decay_values, input_values, conv_values, param_values, flag_rows)

    unused_terms, pull_terms = jax.vjp(
        terms_only, decay_pre, input_pre, conv_out, back_decay_param.astype(jnp.float32)
    )
    grad_decay_full, grad_input_full, grad_conv_direct, grad_decay_param = pull_terms(
        (adjoint * previous, adjoint)
    )
    grad_decay_bias = jnp.sum(grad_decay_full, axis=0)
    grad_input_bias = jnp.sum(grad_input_full, axis=0)
    grad_decay_low = grad_decay_full.astype(jnp.bfloat16)
    grad_input_low = grad_input_full.astype(jnp.bfloat16)
    grad_decay_gate = heads_grad(conv_low, grad_decay_low)
    grad_input_gate = heads_grad(conv_low, grad_input_low)
    grad_conv_out = (
        grad_conv_direct
        + heads_back(grad_decay_low, back_decay_gate)
        + heads_back(grad_input_low, back_input_gate)
    )

    def conv_only(padded_values, weight_values, bias_values):
        return conv_local(padded_values, weight_values, bias_values, masks)

    unused_conv, pull_conv = jax.vjp(
        conv_only, padded, back_conv_weight.astype(jnp.float32), back_conv_bias.astype(jnp.float32)
    )
    grad_padded, grad_conv_weight, grad_conv_bias = pull_conv(grad_conv_out)
    returned_rows = passed_along(grad_padded[: CW - 1], "seq", -1)
    addition = jnp.concatenate(
        [
            jnp.zeros((row_count - (CW - 1), lru_width), jnp.float32),
            returned_rows * alive_rows[:, None],
        ],
        axis=0,
    )
    grad_conv_input = (grad_padded[CW - 1 :] + addition).astype(jnp.bfloat16)
    grad_input_branch = jnp.einsum(
        "td,tr->dr", normed, grad_conv_input, preferred_element_type=jnp.float32
    )
    grad_gate_branch = jnp.einsum(
        "td,tr->dr", normed, grad_gate_pre, preferred_element_type=jnp.float32
    )
    grad_normed = jnp.einsum(
        "tr,dr->td", grad_conv_input, back_input_branch, preferred_element_type=jnp.float32
    ) + jnp.einsum("tr,dr->td", grad_gate_pre, back_gate_branch, preferred_element_type=jnp.float32)
    unused_first, pull_first = jax.vjp(rms_norm, values, back_norm_gain.astype(jnp.float32))
    grad_values_norm, grad_norm_gain = pull_first(grad_normed)
    grad_tokens = grad_middle + grad_values_norm
    rec_sums = (
        lax.psum_scatter(grad_norm_gain, "seq", scatter_dimension=0, tiled=True),
        lax.psum_scatter(grad_gate_branch, "seq", scatter_dimension=0, tiled=True),
        lax.psum_scatter(grad_input_branch, "seq", scatter_dimension=0, tiled=True),
        lax.psum_scatter(grad_conv_weight, "seq", scatter_dimension=1, tiled=True),
        lax.psum_scatter(grad_conv_bias, "seq", scatter_dimension=0, tiled=True),
        lax.psum_scatter(grad_decay_gate, "seq", scatter_dimension=0, tiled=True),
        lax.psum_scatter(grad_decay_bias, "seq", scatter_dimension=0, tiled=True),
        lax.psum_scatter(grad_input_gate, "seq", scatter_dimension=0, tiled=True),
        lax.psum_scatter(grad_input_bias, "seq", scatter_dimension=0, tiled=True),
        lax.psum_scatter(grad_decay_param, "seq", scatter_dimension=0, tiled=True),
        lax.psum_scatter(grad_out_proj, "seq", scatter_dimension=0, tiled=True),
    )
    return (
        block_out,
        grad_tokens,
        rec_sums[0],
        rec_sums[1],
        rec_sums[2],
        rec_sums[3],
        rec_sums[4],
        rec_sums[5],
        rec_sums[6],
        rec_sums[7],
        rec_sums[8],
        rec_sums[9],
        rec_sums[10],
        mlp_sums[0],
        mlp_sums[1],
        mlp_sums[2],
        mlp_sums[3],
    )


CHIPS = 4
MESH = pl.DeviceIdType.MESH


def place():
    me = lax.axis_index("seq")
    core = lax.rem(me, 2)
    x = lax.rem(lax.div(me, 2), 2)
    y = lax.rem(lax.div(me, 4), 2)
    return me, lax.div(me, 8), 2 * y + x, core, x, y


def column_groups(n):
    return [[8 * z + 2 * p + c for c in range(2) for z in range(n // 8)] for p in range(CHIPS)]


def line_groups(n):
    return [[8 * z + r for z in range(n // 8)] for r in range(8)]


def greet(devices):
    barrier = pltpu.get_barrier_semaphore()
    for device in devices:
        pl.semaphore_signal(barrier, inc=1, device_id=(device,), device_id_type=MESH)
    pl.semaphore_wait(barrier, len(devices))


def remote(source, target, send_sem, recv_sem, device):
    return pltpu.make_async_remote_copy(
        src_ref=source,
        dst_ref=target,
        send_sem=send_sem,
        recv_sem=recv_sem,
        device_id=(device,),
        device_id_type=MESH,
    )


def comm_params(collective_id, vmem_mib=None):
    return pltpu.CompilerParams(
        collective_id=collective_id,
        has_side_effects=True,
        vmem_limit_bytes=None if vmem_mib is None else vmem_mib * 2**20,
    )


ANY = pl.BlockSpec(memory_space=pl.ANY)
VMEM = pl.BlockSpec(memory_space=pltpu.VMEM)


def plane_gather_kernel(x_ref, o_ref, send, recv, local):
    me, z, p, c, x, y = place()
    x_dev, y_dev = me + 2 - 4 * x, me + 4 - 8 * y
    p_x, p_y = p + 1 - 2 * x, p + 2 - 4 * y
    greet((x_dev, y_dev))
    half = x_ref.shape[0] // 2
    to_x = remote(x_ref, o_ref.at[p], send.at[0], recv.at[0], x_dev)
    to_y = remote(x_ref, o_ref.at[p], send.at[1], recv.at[1], y_dev)
    to_x.start()
    to_y.start()
    own = pltpu.make_async_copy(x_ref, o_ref.at[p], local)
    own.start()
    to_x.wait_recv()
    first = o_ref.at[p_x, pl.ds(0, half)]
    on_y = remote(first, first, send.at[2], recv.at[2], y_dev)
    on_y.start()
    to_y.wait_recv()
    second = o_ref.at[p_y, pl.ds(half, half)]
    on_x = remote(second, second, send.at[3], recv.at[3], x_dev)
    on_x.start()
    to_x.wait_send()
    to_y.wait_send()
    on_y.wait()
    on_x.wait()
    own.wait()


def plane_gather(block, collective_id):
    return pl.pallas_call(
        plane_gather_kernel,
        out_shape=jax.ShapeDtypeStruct((CHIPS,) + block.shape, block.dtype),
        in_specs=[ANY],
        out_specs=ANY,
        scratch_shapes=[
            pltpu.SemaphoreType.DMA((4,)),
            pltpu.SemaphoreType.DMA((4,)),
            pltpu.SemaphoreType.DMA,
        ],
        compiler_params=comm_params(collective_id),
        name="plane_gather",
    )(block)


def plane_swap_kernel(count, *refs):
    ins, outs = refs[:count], refs[count : 2 * count]
    send, recv, local = refs[2 * count :]
    me, z, p, c, x, y = place()
    x_dev, y_dev = me + 2 - 4 * x, me + 4 - 8 * y
    d_dev = y_dev + 2 - 4 * x
    p_x, p_y, p_d = p + 1 - 2 * x, p + 2 - 4 * y, 3 - p
    peers = ((x_dev, p_x), (y_dev, p_y), (d_dev, p_d))
    greet([device for device, unused in peers])
    copies = []
    for k in range(count):
        for j, (device, chip) in enumerate(peers):
            copies.append(remote(ins[k].at[chip], outs[k].at[p], send.at[k, j], recv.at[k, j], device))
        copies.append(pltpu.make_async_copy(ins[k].at[p], outs[k].at[p], local.at[k]))
    for copy in copies:
        copy.start()
    for copy in copies:
        copy.wait()


def plane_swap(arrays, collective_id):
    count = len(arrays)
    return pl.pallas_call(
        functools.partial(plane_swap_kernel, count),
        out_shape=[jax.ShapeDtypeStruct(a.shape, a.dtype) for a in arrays],
        in_specs=[ANY] * count,
        out_specs=[ANY] * count,
        scratch_shapes=[
            pltpu.SemaphoreType.DMA((count, 3)),
            pltpu.SemaphoreType.DMA((count, 3)),
            pltpu.SemaphoreType.DMA((count,)),
        ],
        compiler_params=comm_params(collective_id),
        name="plane_swap",
    )(*arrays)


def plane_sum_kernel(part, out, own, from_x, from_y, diag_x, diag_y, on_x, on_y, send, recv, local):
    me, z, p, c, x, y = place()
    x_dev, y_dev = me + 2 - 4 * x, me + 4 - 8 * y
    p_x, p_y, p_d = p + 1 - 2 * x, p + 2 - 4 * y, 3 - p
    greet((x_dev, y_dev))
    rows = part.shape[1]
    half = rows // 2
    low, high = pl.ds(0, half), pl.ds(half, half)
    copies = [
        remote(part.at[p_d, low], diag_x, send.at[0], recv.at[0], x_dev),
        remote(part.at[p_d, high], diag_y, send.at[1], recv.at[1], y_dev),
        remote(part.at[p_x, low], from_x.at[low], send.at[2], recv.at[2], x_dev),
        remote(part.at[p_y, high], from_y.at[high], send.at[3], recv.at[3], y_dev),
    ]
    for copy in copies:
        copy.start()
    locals_ = [
        pltpu.make_async_copy(part.at[p_y, low], on_y, local.at[0]),
        pltpu.make_async_copy(part.at[p_x, high], on_x, local.at[1]),
        pltpu.make_async_copy(part.at[p], own, local.at[2]),
    ]
    for copy in locals_:
        copy.start()

    def add_into(target, addend):
        @pl.loop(0, half // 16)
        def add_rows(i):
            at = pl.ds(pl.multiple_of(i * 16, 16), 16)
            target[at, :] = (
                target[at, :].astype(jnp.float32) + addend[at, :].astype(jnp.float32)
            ).astype(target.dtype)

    locals_[0].wait()
    copies[0].wait_recv()
    add_into(on_y, diag_x)
    to_y = remote(on_y, from_y.at[low], send.at[4], recv.at[4], y_dev)
    to_y.start()
    locals_[1].wait()
    copies[1].wait_recv()
    add_into(on_x, diag_y)
    to_x = remote(on_x, from_x.at[high], send.at[5], recv.at[5], x_dev)
    to_x.start()
    locals_[2].wait()
    copies[2].wait_recv()
    copies[3].wait_recv()
    to_y.wait()
    to_x.wait()
    for copy in copies:
        copy.wait_send()

    @pl.loop(0, rows // 16)
    def sum_rows(i):
        at = pl.ds(pl.multiple_of(i * 16, 16), 16)
        out[at, :] = (
            own[at, :].astype(jnp.float32)
            + from_x[at, :].astype(jnp.float32)
            + from_y[at, :].astype(jnp.float32)
        )


def plane_sum(parts, collective_id):
    unused, rows, columns = parts.shape
    whole, part = (rows, columns), (rows // 2, columns)
    return pl.pallas_call(
        plane_sum_kernel,
        out_shape=jax.ShapeDtypeStruct(whole, jnp.float32),
        in_specs=[ANY],
        out_specs=VMEM,
        scratch_shapes=[
            pltpu.VMEM(whole, parts.dtype),
            pltpu.VMEM(whole, parts.dtype),
            pltpu.VMEM(whole, parts.dtype),
            pltpu.VMEM(part, parts.dtype),
            pltpu.VMEM(part, parts.dtype),
            pltpu.VMEM(part, parts.dtype),
            pltpu.VMEM(part, parts.dtype),
            pltpu.SemaphoreType.DMA((6,)),
            pltpu.SemaphoreType.DMA((6,)),
            pltpu.SemaphoreType.DMA((3,)),
        ],
        compiler_params=comm_params(collective_id, 32),
        name="plane_sum",
    )(parts)


def small_gather_kernel(planes, x_ref, o_ref, send, recv):
    me, z, p, c, x, y = place()
    r = lax.rem(me, 8)
    base = me - r
    near = [base + lax.rem(r + d, 8) for d in range(1, 8)]
    far = [8 * lax.rem(z + d, planes) + r for d in range(1, planes)]
    greet(near + far)
    o_ref[z, r] = x_ref[...]
    copies = [
        remote(x_ref, o_ref.at[z, r], send.at[d], recv.at[d], device) for d, device in enumerate(near)
    ]
    for copy in copies:
        copy.start()
    for copy in copies:
        copy.wait()
    copies = [
        remote(o_ref.at[z], o_ref.at[z], send.at[7 + d], recv.at[7 + d], device)
        for d, device in enumerate(far)
    ]
    for copy in copies:
        copy.start()
    for copy in copies:
        copy.wait()


def small_gather(block, collective_id):
    planes = lax.axis_size("seq") // 8
    return pl.pallas_call(
        functools.partial(small_gather_kernel, planes),
        out_shape=jax.ShapeDtypeStruct((planes, 8) + block.shape, block.dtype),
        in_specs=[VMEM],
        out_specs=VMEM,
        scratch_shapes=[
            pltpu.SemaphoreType.DMA((6 + planes,)),
            pltpu.SemaphoreType.DMA((6 + planes,)),
        ],
        compiler_params=comm_params(collective_id),
        name="small_gather",
    )(block)


def small_sum_kernel(planes, x_ref, o_ref, lines, line, near_parts, send, recv):
    me, z, p, c, x, y = place()
    r = lax.rem(me, 8)
    base = me - r
    near = [(lax.rem(r + d, 8), base + lax.rem(r + d, 8)) for d in range(1, 8)]
    far = [(lax.rem(z + d, planes), 8 * lax.rem(z + d, planes) + r) for d in range(1, planes)]
    greet([device for unused, device in near + far])
    copies = [
        remote(x_ref.at[there], lines.at[d], send.at[d], recv.at[d], device)
        for d, (there, device) in enumerate(far)
    ]
    for copy in copies:
        copy.start()
    for copy in copies:
        copy.wait()
    line[...] = x_ref[z] + sum(lines[d] for d in range(planes - 1))
    copies = [
        remote(
            line.at[there], near_parts.at[d], send.at[planes - 1 + d], recv.at[planes - 1 + d], device
        )
        for d, (there, device) in enumerate(near)
    ]
    for copy in copies:
        copy.start()
    for copy in copies:
        copy.wait()
    o_ref[...] = line[r] + sum(near_parts[d] for d in range(7))


def small_sum(parts, collective_id):
    planes, unused, rows, lanes = parts.shape
    return pl.pallas_call(
        functools.partial(small_sum_kernel, planes),
        out_shape=jax.ShapeDtypeStruct((rows, lanes), jnp.float32),
        in_specs=[VMEM],
        out_specs=VMEM,
        scratch_shapes=[
            pltpu.VMEM((planes - 1, 8, rows, lanes), jnp.float32),
            pltpu.VMEM((8, rows, lanes), jnp.float32),
            pltpu.VMEM((7, rows, lanes), jnp.float32),
            pltpu.SemaphoreType.DMA((6 + planes,)),
            pltpu.SemaphoreType.DMA((6 + planes,)),
        ],
        compiler_params=comm_params(collective_id),
        name="small_sum",
    )(parts)


def carry_kernel(planes, reverse, x_ref, o_ref, everyone, before, send, recv):
    me, z, p, c, x, y = place()
    count = 2 * planes
    q = 2 * z + c
    peers = []
    for d in range(1, count):
        other = lax.rem(q + d, count)
        peers.append(8 * lax.div(other, 2) + 2 * p + lax.rem(other, 2))
    greet(peers)
    everyone[q] = x_ref[...]
    copies = [
        remote(x_ref, everyone.at[q], send.at[d], recv.at[d], device) for d, device in enumerate(peers)
    ]
    for copy in copies:
        copy.start()
    for copy in copies:
        copy.wait()
    carried = jnp.zeros((1, x_ref.shape[1]), jnp.float32)
    order = [(k, j, e) for k in range(planes) for j in range(CHIPS) for e in range(2)]
    for k, j, e in reversed(order) if reverse else order:
        before[8 * k + 2 * j + e : 8 * k + 2 * j + e + 1, :] = carried
        part = everyone.at[2 * k + e]
        carried = part[j : j + 1, :] * carried + part[CHIPS + j : CHIPS + j + 1, :]
    for j in range(CHIPS):
        o_ref[j : j + 1, :] = before[pl.ds(8 * z + 2 * j + c, 1), :]


def carry_in(product, last, reverse, collective_id):
    planes = lax.axis_size("seq") // 8
    channels = product.shape[1]
    return pl.pallas_call(
        functools.partial(carry_kernel, planes, reverse),
        out_shape=jax.ShapeDtypeStruct((CHIPS, channels), jnp.float32),
        in_specs=[VMEM],
        out_specs=VMEM,
        scratch_shapes=[
            pltpu.VMEM((2 * planes, 2 * CHIPS, channels), jnp.float32),
            pltpu.VMEM((8 * planes, channels), jnp.float32),
            pltpu.SemaphoreType.DMA((2 * planes - 1,)),
            pltpu.SemaphoreType.DMA((2 * planes - 1,)),
        ],
        compiler_params=comm_params(collective_id),
        name="carry_in",
    )(jnp.concatenate([product, last], axis=0))


def scan_kernel(reverse, coef_ref, drive_ref, cumulative_ref, local_ref):
    rows, channels = coef_ref.shape[1:]
    row = lax.broadcasted_iota(jnp.int32, (8, channels), 0)

    def shifted(values, step, fill):
        if reverse:
            return jnp.where(row < 8 - step, pltpu.roll(values, 8 - step, 0), fill)
        return jnp.where(row >= step, pltpu.roll(values, step, 0), fill)

    def tile(i, carry):
        i = rows // 8 - 1 - i if reverse else i
        at = pl.ds(pl.multiple_of(i * 8, 8), 8)
        a, b = coef_ref[0, at, :], drive_ref[0, at, :]
        for step in (1, 2, 4):
            b = a * shifted(b, step, 0.0) + b
            a = a * shifted(a, step, 1.0)
        before_a, before_b = carry
        b = a * before_b + b
        a = a * before_a
        cumulative_ref[0, at, :] = a
        local_ref[0, at, :] = b
        last = slice(0, 1) if reverse else slice(7, 8)
        return a[last, :], b[last, :]

    lax.fori_loop(
        0,
        rows // 8,
        tile,
        (jnp.ones((1, channels), jnp.float32), jnp.zeros((1, channels), jnp.float32)),
    )


def block_scan(coefficient, drive, reverse):
    blocks, rows, channels = coefficient.shape
    spec = pl.BlockSpec((1, rows, channels), lambda b: (b, 0, 0))
    return pl.pallas_call(
        functools.partial(scan_kernel, reverse),
        grid=(blocks,),
        out_shape=[jax.ShapeDtypeStruct(coefficient.shape, jnp.float32)] * 2,
        in_specs=[spec, spec],
        out_specs=[spec, spec],
        compiler_params=pltpu.CompilerParams(vmem_limit_bytes=24 * 2**20),
        name="block_scan",
    )(coefficient, drive)


def regrouped(values, axis, n):
    shape = values.shape
    split = shape[:axis] + (n // 2, 2, shape[axis] // n) + shape[axis + 1 :]
    return jnp.moveaxis(values.reshape(split), axis + 1, axis).reshape(shape)


def regrouped_back(values, axis, n):
    shape = values.shape
    split = shape[:axis] + (2, n // 2, shape[axis] // n) + shape[axis + 1 :]
    return jnp.moveaxis(values.reshape(split), axis, axis + 1).reshape(shape)


def by_chip(weight, planes):
    rows, columns = weight.shape
    split = weight.reshape(rows, planes, CHIPS, 2, columns // (planes * 8))
    return split.transpose(2, 0, 3, 1, 4).reshape(CHIPS, rows, columns // CHIPS)


def from_chips(parts, planes):
    unused, rows, columns = parts.shape
    split = parts.reshape(CHIPS, rows, 2, planes, columns // (planes * 2))
    return split.transpose(1, 3, 0, 2, 4).reshape(rows, CHIPS * columns)


def behind(value, *earlier):
    return lax.optimization_barrier((value, *earlier))[0]


def plane_body(
    tokens,
    starts,
    cotangent,
    norm_gain,
    gate_branch,
    input_branch,
    conv_weight,
    conv_bias,
    decay_gate,
    decay_bias,
    input_gate,
    input_bias,
    decay_param,
    out_proj,
    mlp_gain,
    mlp_gate,
    mlp_up,
    mlp_down,
):
    f32, bf16 = jnp.float32, jnp.bfloat16
    n = lax.axis_size("seq")
    planes = n // 8
    me, z, p, c, x, y = place()
    groups = column_groups(n)
    rows, width = tokens.shape
    rows_d, lru_width = gate_branch.shape
    head = decay_gate.shape[1]
    rows_r, rows_f = out_proj.shape[0], mlp_down.shape[0]
    channels = lru_width // CHIPS
    units = mlp_gate.shape[1] // CHIPS
    half_units = units // 2

    def column_gather(block):
        return lax.all_gather(block, "seq", axis=0, tiled=True, axis_index_groups=groups)

    def line_sum(parts):
        return lax.psum_scatter(
            parts, "seq", scatter_dimension=0, tiled=True, axis_index_groups=line_groups(n)
        )

    sibling = [(d, d + 1 - 2 * (d % 2)) for d in range(n)]

    def halves(values, axis):
        half = values.shape[axis] // 2
        return (
            lax.dynamic_slice_in_dim(values, c * half, half, axis),
            lax.dynamic_slice_in_dim(values, (1 - c) * half, half, axis),
        )

    def plane_permuted(block):
        whole = lax.dynamic_update_slice_in_dim(
            jnp.zeros((CHIPS * rows, block.shape[1]), block.dtype), block, p * rows, 0
        )
        p_x, p_y, p_d = p + 1 - 2 * x, p + 2 - 4 * y, 3 - p
        for chip, flip in ((p_x, (1, 0)), (p_y, (0, 1)), (p_d, (1, 1))):
            route = [
                (d, d + flip[0] * (2 - 4 * (d // 2 % 2)) + flip[1] * (4 - 8 * (d // 4 % 2))) for d in range(n)
            ]
            part = lax.ppermute(block, "seq", route)
            whole = lax.dynamic_update_slice_in_dim(whole, part, chip * rows, 0)
        return whole

    def exchanged(values):
        return lax.ppermute(values, "seq", sibling)

    def product(left, right):
        return jnp.dot(left, right, preferred_element_type=f32)

    def product_t(left, right):
        return jnp.einsum("tk,nk->tn", left, right, preferred_element_type=f32)

    def weight_grad(left, right):
        return jnp.einsum("ta,tb->ab", left, right, preferred_element_type=f32)

    lanes = 128

    def row(values):
        return jnp.pad(values.astype(f32), (0, lanes - values.shape[0]))[None]

    small = jnp.concatenate(
        [
            row(norm_gain),
            row(mlp_gain),
            starts.astype(f32).reshape(rows // lanes, lanes),
            *[row(conv_weight[k]) for k in range(CW)],
            row(conv_bias),
            row(decay_bias),
            row(input_bias),
            row(decay_param),
            jnp.zeros((4, lanes), f32),
        ],
        axis=0,
    )
    weights_in = jnp.concatenate([by_chip(gate_branch, planes), by_chip(input_branch, planes)], axis=2)
    (swapped_in,) = plane_swap([weights_in], 2)
    small = small_gather(behind(small, swapped_in), 1)
    flags = 2 + rows // lanes
    gain_one = regrouped(small[:, :, 0, :rows_d].reshape(width), 0, n)
    gain_two = regrouped(small[:, :, 1, :rows_d].reshape(width), 0, n)
    all_flags = small[:, :, 2:flags].reshape(n * rows)
    vectors = lax.dynamic_slice_in_dim(
        small.reshape(planes, CHIPS, 2, 16, lanes), p, 1, axis=1
    )[:, 0, :, flags : flags + CW + 4, :rows_r]
    vectors = vectors.transpose(2, 1, 0, 3).reshape(CW + 4, channels)
    taps = vectors[:CW]
    bias_conv, bias_decay, bias_input, param = (vectors[CW + k] for k in range(4))

    running = jnp.ones((n * rows,), f32)
    masks_all = [running]
    for offset in range(1, CW):
        earlier = jnp.concatenate([jnp.zeros((offset - 1,), f32), all_flags[: n * rows - (offset - 1)]])
        running = running * (1.0 - earlier)
        masks_all.append(running)
    masks_all = jnp.stack(masks_all).reshape(CW, planes, CHIPS, 2, rows)

    def own_blocks(values):
        return lax.dynamic_slice(
            values,
            (0, z, 0, c, 0),
            (values.shape[0], 1, CHIPS, 1, values.shape[4]),
        )[:, 0, :, 0]

    masks = own_blocks(masks_all)
    after = masks_all[..., : CW - 1].reshape(CW, n, CW - 1)
    after = jnp.concatenate([after[:, 1:], jnp.zeros((CW, 1, CW - 1), f32)], axis=1)
    after = own_blocks(after.reshape(CW, planes, CHIPS, 2, CW - 1))
    flag_rows = own_blocks(all_flags.reshape(1, planes, CHIPS, 2, rows))[0]

    gate_parts, up_parts = by_chip(mlp_gate, planes), by_chip(mlp_up, planes)
    mlp_pieces = [
        jnp.concatenate([w[:, :, k * half_units : (k + 1) * half_units] for w in (gate_parts, up_parts)], axis=2)
        for k in range(2)
    ]
    whole_in = column_gather(swapped_in.reshape(CHIPS * rows_d, 2 * channels))
    rec_rows = column_gather(
        jnp.concatenate([regrouped(out_proj, 1, n), decay_gate, input_gate], axis=1)
    )
    whole_out, gates = rec_rows[:, :width], rec_rows[:, width:]
    gates = gates.reshape(2, planes, rows_r, 2, 2, rows_r)
    diagonal = jnp.eye(planes, dtype=bf16)[None, :, None, None, :, None]
    decay_blocks, input_blocks = (
        (gates[:, :, :, k, :, None, :] * diagonal).reshape(channels, channels) for k in range(2)
    )

    values = regrouped(tokens, 1, n).astype(f32)
    cot = regrouped(cotangent, 1, n)
    normed = rms_norm(values, gain_one).astype(bf16)
    normed_all = plane_gather(normed, 3).reshape(CHIPS * rows, width)
    swapped_mlp = plane_swap(behind(tuple(mlp_pieces), normed_all), 4)
    whole_down = column_gather(regrouped(mlp_down, 1, n))
    whole_mlp = [column_gather(part.reshape(CHIPS * rows_d, 2 * half_units)) for part in swapped_mlp]
    cot_all = plane_permuted(behind(cot, swapped_mlp[0]))

    gate_pre = product(normed_all, whole_in[:, :channels])
    gate_act = gelu_tanh(gate_pre)
    conv_input = product(normed_all, whole_in[:, channels:]).astype(bf16)
    blocks = conv_input.reshape(CHIPS, rows, channels)
    tails = blocks[:, rows - (CW - 1) :]
    from_sibling = lax.ppermute(tails, "seq", sibling)
    from_below = lax.ppermute(
        tails[CHIPS - 1 :], "seq", [(d, d + 7) for d in range(n - 8) if d % 2 == 1]
    )
    before_rows = jnp.where(
        c == 1, from_sibling, jnp.concatenate([from_below, from_sibling[: CHIPS - 1]], axis=0)
    )
    padded = jnp.concatenate([before_rows, blocks], axis=1).astype(f32)

    conv_out = bias_conv + jnp.zeros((CHIPS, rows, channels), f32)
    for offset in range(CW):
        lead = CW - 1 - offset
        conv_out = conv_out + taps[offset] * (padded[:, lead : lead + rows] * masks[offset][:, :, None])
    conv_out = conv_out.reshape(CHIPS * rows, channels)
    conv_low = conv_out.astype(bf16)
    decay_pre = product(conv_low, decay_blocks) + bias_decay
    input_pre = product(conv_low, input_blocks) + bias_input
    flat_flags = flag_rows.reshape(CHIPS * rows)
    coefficient, drive = lru_terms(decay_pre, input_pre, conv_out, param, flat_flags)
    cube = (CHIPS, rows, channels)
    cumulative, local_state = block_scan(coefficient.reshape(cube), drive.reshape(cube), False)
    entering = carry_in(cumulative[:, -1], local_state[:, -1], False, 6)
    states = local_state + cumulative * entering[:, None, :]
    flat_states = states.reshape(CHIPS * rows, channels)
    mixed = (flat_states * gate_act).astype(bf16)
    branch_parts = product(mixed, whole_out).reshape(CHIPS, rows, width)
    middle = values + plane_sum(branch_parts, 7)
    normed_two = rms_norm(middle, gain_two).astype(bf16)
    two_all = plane_gather(normed_two, 8).reshape(CHIPS * rows, width)

    cot_other = exchanged(cot_all)
    two_own, two_other = halves(two_all, 1)
    two_other = exchanged(two_other)
    grad_hidden = product_t(cot_all, whole_down)
    hiddens, grads_low, piece_grads = [], [], []
    two_now = two_all
    for k in range(2):
        weights = whole_mlp[k]
        gate_mlp = product(two_now, weights[:, :half_units])
        up_mlp = product(two_now, weights[:, half_units:])
        hidden, pull_act = jax.vjp(mlp_act, gate_mlp, up_mlp)
        hiddens.append(hidden.astype(bf16))
        grad_gate, grad_up = pull_act(grad_hidden[:, k * half_units : (k + 1) * half_units])
        low = jnp.concatenate([grad_gate.astype(bf16), grad_up.astype(bf16)], axis=1)
        grads_low.append(low)
        piece_grads.append((weight_grad(two_own, low) + weight_grad(two_other, exchanged(low))).astype(bf16))
        two_now = behind(two_now, piece_grads[-1])
    hidden = jnp.concatenate(hiddens, axis=1)
    two_parts = product_t(grads_low[0], whole_mlp[0]) + product_t(grads_low[1], whole_mlp[1])
    two_parts = behind(two_parts.astype(bf16), piece_grads[1])
    piece_grads = [line_sum(part) for part in piece_grads]
    grad_normed_two = plane_sum(two_parts.reshape(CHIPS, rows, width), 9)
    unused_norm, pull_norm = jax.vjp(rms_norm, middle, gain_two)
    grad_middle_norm, grad_mlp_gain = pull_norm(grad_normed_two)
    grad_middle = cot.astype(f32) + grad_middle_norm
    hidden_own, hidden_other = halves(behind(hidden, grad_normed_two), 1)
    down_grad = (weight_grad(hidden_own, cot_all) + weight_grad(exchanged(hidden_other), cot_other)).astype(bf16)
    grad_mlp_down = line_sum(down_grad)
    grad_branch = plane_gather(behind(grad_middle.astype(bf16), down_grad), 10).reshape(CHIPS * rows, width)
    grad_branch = behind(grad_branch, piece_grads[0])

    grad_out_proj = weight_grad(mixed, grad_branch)
    grad_mixed = product_t(grad_branch, whole_out)
    grad_states = grad_mixed * gate_act
    unused_gelu, pull_gelu = jax.vjp(gelu_tanh, gate_pre)
    grad_gate_pre = pull_gelu(grad_mixed * flat_states)[0].astype(bf16)
    coef_cube = coefficient.reshape(cube)
    shifted_coef = jnp.concatenate([coef_cube[:, 1:], jnp.ones((CHIPS, 1, channels), f32)], axis=1)
    back_cumulative, back_local = block_scan(shifted_coef, grad_states.reshape(cube), True)
    back_cumulative, back_local = lax.optimization_barrier((back_cumulative, back_local, piece_grads[1]))[:2]
    leaving = carry_in(
        coef_cube[:, 0] * back_cumulative[:, 0], coef_cube[:, 0] * back_local[:, 0], True, 12
    )
    adjoint = (back_local + back_cumulative * leaving[:, None, :]).reshape(CHIPS * rows, channels)
    previous = jnp.concatenate([entering[:, None, :], states[:, :-1]], axis=1).reshape(
        CHIPS * rows, channels
    )

    def terms_only(decay_values, input_values, conv_values, param_values):
        return lru_terms(decay_values, input_values, conv_values, param_values, flat_flags)

    unused_terms, pull_terms = jax.vjp(terms_only, decay_pre, input_pre, conv_out, param)
    grad_decay_full, grad_input_full, grad_conv_direct, grad_param = pull_terms(
        (adjoint * previous, adjoint)
    )
    grad_decay_low, grad_input_low = grad_decay_full.astype(bf16), grad_input_full.astype(bf16)

    def diagonal_blocks(left, right):
        full = weight_grad(left, right).reshape(2, planes, rows_r, 2, planes, rows_r)
        same = jnp.eye(planes, dtype=f32)[None, :, None, None, :, None]
        return jnp.sum(full * same, axis=4).reshape(channels, head)

    row_parts, row_parts_other = halves(
        jnp.concatenate(
            [
                grad_out_proj,
                diagonal_blocks(conv_low, grad_decay_low),
                diagonal_blocks(conv_low, grad_input_low),
            ],
            axis=1,
        ),
        0,
    )
    rec_row_grads = line_sum((row_parts + exchanged(row_parts_other)).astype(bf16))
    grad_conv_out = (
        grad_conv_direct
        + product_t(grad_decay_low, decay_blocks)
        + product_t(grad_input_low, input_blocks)
    ).reshape(cube)
    heads_rows = grad_conv_out[:, : CW - 1]
    from_sibling = lax.ppermute(heads_rows, "seq", sibling)
    from_above = lax.ppermute(heads_rows[:1], "seq", [(d, d - 7) for d in range(8, n) if d % 2 == 0])
    after_rows = jnp.where(c == 0, from_sibling, jnp.concatenate([from_sibling[1:], from_above], axis=0))
    extended = jnp.concatenate([grad_conv_out, after_rows], axis=1)
    grad_conv_input = jnp.zeros(cube, f32)
    grad_taps = []
    for offset in range(CW):
        lead = CW - 1 - offset
        keep = jnp.concatenate([masks[offset], after[offset]], axis=1)[:, :, None]
        grad_conv_input = grad_conv_input + taps[offset] * (extended * keep)[:, offset : offset + rows]
        grad_taps.append(
            jnp.sum(grad_conv_out * (padded[:, lead : lead + rows] * masks[offset][:, :, None]), axis=(0, 1))
        )
    grad_conv_low = grad_conv_input.reshape(CHIPS * rows, channels).astype(bf16)
    in_low = jnp.concatenate([grad_gate_pre, grad_conv_low], axis=1)
    normed_own, normed_other = halves(normed_all, 1)
    in_grads = weight_grad(normed_own, in_low) + weight_grad(exchanged(normed_other), exchanged(in_low))
    in_grads = line_sum(in_grads.astype(bf16))
    normed_parts = product_t(in_low, whole_in).astype(bf16).reshape(CHIPS, rows, width)
    grad_normed = plane_sum(behind(normed_parts, grad_mlp_down), 13)
    down_parts = product(hidden, whole_down).astype(bf16).reshape(CHIPS, rows, width)
    block_out = (middle + plane_sum(behind(down_parts, grad_normed), 11)).astype(bf16)
    unused_first, pull_first = jax.vjp(rms_norm, values, gain_one)
    grad_values_norm, grad_norm_gain = pull_first(grad_normed)
    grad_tokens = grad_middle + grad_values_norm

    mlp_out = plane_swap([part.reshape(CHIPS, rows_d, part.shape[1]) for part in piece_grads], 14)
    grad_mlp_gate, grad_mlp_up = (
        from_chips(
            jnp.concatenate([part[:, :, k * half_units : (k + 1) * half_units] for part in mlp_out], axis=2),
            planes,
        ).astype(f32)
        for k in range(2)
    )
    (in_out,) = plane_swap([in_grads.reshape(CHIPS, rows_d, 2 * channels)], 16)
    grad_gate_branch = from_chips(in_out[:, :, :channels], planes).astype(f32)
    grad_input_branch = from_chips(in_out[:, :, channels:], planes).astype(f32)

    sums = jnp.stack(
        [
            *grad_taps,
            jnp.sum(grad_conv_out, axis=(0, 1)),
            jnp.sum(grad_decay_full, axis=0),
            jnp.sum(grad_input_full, axis=0),
            grad_param,
        ]
    )
    vector_parts = sums.reshape(CW + 4, 2, planes, rows_r).transpose(2, 1, 0, 3)
    vector_parts = jnp.pad(vector_parts, ((0, 0), (0, 0), (0, 0), (0, lanes - rows_r)))
    here = (jnp.arange(CHIPS) == p).astype(f32)[None, :, None, None, None]
    vector_parts = (vector_parts[:, None] * here).reshape(planes, 8, CW + 4, lanes)
    gain_parts = jnp.stack([grad_norm_gain, grad_mlp_gain]).reshape(2, 2, planes, CHIPS, rows_d)
    gain_parts = gain_parts.transpose(2, 3, 1, 0, 4).reshape(planes, 8, 2, rows_d)
    gain_parts = jnp.pad(gain_parts, ((0, 0), (0, 0), (0, 6), (0, lanes - rows_d)))
    small_grads = small_sum(jnp.concatenate([vector_parts, gain_parts], axis=2), 15)
    vector_grads = small_grads[: CW + 4, :rows_r]
    gain_grads = small_grads[CW + 4 :, :rows_d]
    return (
        regrouped_back(block_out, 1, n),
        regrouped_back(grad_tokens, 1, n),
        gain_grads[0],
        grad_gate_branch,
        grad_input_branch,
        vector_grads[:CW],
        vector_grads[CW],
        rec_row_grads[:, width : width + head].astype(f32),
        vector_grads[CW + 1],
        rec_row_grads[:, width + head :].astype(f32),
        vector_grads[CW + 2],
        vector_grads[CW + 3],
        regrouped_back(rec_row_grads[:, :width].astype(f32), 1, n),
        gain_grads[1],
        grad_mlp_gate,
        grad_mlp_up,
        regrouped_back(grad_mlp_down.astype(f32), 1, n),
    )


def solution(mesh):
    in_specs = (
        P("seq", None),
        P("seq"),
        P("seq", None),
        P("seq"),
        P("seq", None),
        P("seq", None),
        P(None, "seq"),
        P("seq"),
        P("seq", None),
        P("seq"),
        P("seq", None),
        P("seq"),
        P("seq"),
        P("seq", None),
        P("seq"),
        P("seq", None),
        P("seq", None),
        P("seq", None),
    )
    out_specs = (
        P("seq", None),
        P("seq", None),
        P("seq"),
        P("seq", None),
        P("seq", None),
        P(None, "seq"),
        P("seq"),
        P("seq", None),
        P("seq"),
        P("seq", None),
        P("seq"),
        P("seq"),
        P("seq", None),
        P("seq"),
        P("seq", None),
        P("seq", None),
        P("seq", None),
    )
    body = plane_body if mesh.shape["seq"] == 2 * H else token_split_body
    return jax.shard_map(body, mesh=mesh, in_specs=in_specs, out_specs=out_specs, check_vma=False)
```

```python
import functools

import jax
import jax.numpy as jnp
from jax import lax
from jax.experimental import pallas as pl
from jax.experimental.pallas import tpu as pltpu
from jax.sharding import PartitionSpec as P

H = 16
CW = 4


epsilon = 1e-06
rate_scale = 8.0


def passed_along(block, axis, distance):
    devices = range(lax.axis_size(axis))
    route = [(i - distance, i) for i in devices if i - distance in devices]
    return lax.ppermute(block, axis, route)


def prefix(value, axis, combine, identity, reverse):
    peers, place = (lax.axis_size(axis), lax.axis_index(axis))
    everything = jax.tree.map(lambda part: lax.all_gather(part, axis), value)
    start = jax.tree.map(
        lambda part, zero: jnp.broadcast_to(jnp.asarray(zero, part.dtype), part.shape),
        value,
        identity,
    )

    def hop(k, before):
        at = peers - 1 - k if reverse else k
        reached = at > place if reverse else at < place
        new = combine(before, jax.tree.map(lambda part: part[at], everything))
        return jax.tree.map(lambda a, b: jnp.where(reached, a, b), new, before)

    return lax.fori_loop(0, peers, hop, start)


def gelu_tanh(values):
    return jax.nn.gelu(values, approximate=True)


def rms_norm(values, scales):
    return values * lax.rsqrt(jnp.mean(values * values, axis=-1, keepdims=True) + epsilon) * scales


def combine(earlier_part, later_part):
    return (earlier_part[0] * later_part[0], later_part[0] * earlier_part[1] + later_part[1])


def heads_product(values, weight):
    row_count, lru_width = values.shape
    shaped = values.reshape(row_count, H, lru_width // H)
    blocks = weight.reshape(H, lru_width // H, lru_width // H)
    return jnp.einsum("thi,hij->thj", shaped, blocks, preferred_element_type=jnp.float32).reshape(
        row_count, lru_width
    )


def heads_back(grads_low, weight):
    row_count, lru_width = grads_low.shape
    shaped = grads_low.reshape(row_count, H, lru_width // H)
    blocks = weight.reshape(H, lru_width // H, lru_width // H)
    return jnp.einsum("thj,hij->thi", shaped, blocks, preferred_element_type=jnp.float32).reshape(
        row_count, lru_width
    )


def heads_grad(values, grads_low):
    row_count, lru_width = values.shape
    left_side = values.reshape(row_count, H, lru_width // H)
    right_side = grads_low.reshape(row_count, H, lru_width // H)
    return jnp.einsum(
        "thi,thj->hij", left_side, right_side, preferred_element_type=jnp.float32
    ).reshape(lru_width, lru_width // H)


def lru_terms(decay_pre, input_pre, conv_out, decay_param, flag_rows):
    log_decay = -rate_scale * jax.nn.sigmoid(decay_pre) * jax.nn.softplus(decay_param)
    keep_rows = 1.0 - flag_rows[:, None]
    coefficient = jnp.exp(log_decay) * keep_rows
    scale_in = flag_rows[:, None] + keep_rows * jnp.sqrt(-jnp.expm1(2.0 * log_decay))
    drive_term = scale_in * jax.nn.sigmoid(input_pre) * conv_out
    return (coefficient, drive_term)


def build_masks(flag_rows):
    row_count = flag_rows.shape[0]
    running = jnp.ones((row_count,), jnp.float32)
    masks = [running]
    for offset in range(1, CW):
        earlier_flags = jnp.concatenate(
            [jnp.zeros((offset - 1,), jnp.float32), flag_rows[: row_count - (offset - 1)]]
        )
        running = running * (1.0 - earlier_flags)
        masks.append(running)
    return masks


def send_mask(flag_rows):
    tail_keep = 1.0 - flag_rows[flag_rows.shape[0] - (CW - 1) :]
    after_rows = jnp.cumprod(tail_keep[::-1])[::-1]
    return jnp.concatenate([after_rows[1:], jnp.ones((1,), jnp.float32)])


def conv_local(padded, weight, bias, masks):
    row_count = masks[0].shape[0]
    conv_total = bias + jnp.zeros((row_count, padded.shape[1]), jnp.float32)
    for offset in range(CW):
        lead = CW - 1 - offset
        conv_total = conv_total + weight[offset] * (
            padded[lead : lead + row_count] * masks[offset][:, None]
        )
    return conv_total


def mlp_act(gate_values, up_values):
    return gelu_tanh(gate_values) * up_values


def token_split_body(
    tokens,
    starts,
    cotangent,
    norm_gain,
    gate_branch,
    input_branch,
    conv_weight,
    conv_bias,
    decay_gate,
    decay_bias,
    input_gate,
    input_bias,
    decay_param,
    out_proj,
    mlp_gain,
    mlp_gate,
    mlp_up,
    mlp_down,
):
    (
        whole_norm_gain,
        whole_gate_branch,
        whole_input_branch,
        whole_conv_weight,
        whole_conv_bias,
        whole_decay_gate,
        whole_decay_bias,
        whole_input_gate,
        whole_input_bias,
        whole_decay_param,
        whole_out_proj,
    ) = (
        lax.all_gather(norm_gain, "seq", axis=0, tiled=True),
        lax.all_gather(gate_branch, "seq", axis=0, tiled=True),
        lax.all_gather(input_branch, "seq", axis=0, tiled=True),
        lax.all_gather(conv_weight, "seq", axis=1, tiled=True),
        lax.all_gather(conv_bias, "seq", axis=0, tiled=True),
        lax.all_gather(decay_gate, "seq", axis=0, tiled=True),
        lax.all_gather(decay_bias, "seq", axis=0, tiled=True),
        lax.all_gather(input_gate, "seq", axis=0, tiled=True),
        lax.all_gather(input_bias, "seq", axis=0, tiled=True),
        lax.all_gather(decay_param, "seq", axis=0, tiled=True),
        lax.all_gather(out_proj, "seq", axis=0, tiled=True),
    )
    flag_rows = starts.astype(jnp.float32)
    row_count = tokens.shape[0]
    values = tokens.astype(jnp.float32)
    normed = rms_norm(values, whole_norm_gain.astype(jnp.float32)).astype(jnp.bfloat16)
    gate_pre = jnp.dot(normed, whole_gate_branch, preferred_element_type=jnp.float32)
    gate_act = gelu_tanh(gate_pre)
    conv_input = jnp.dot(normed, whole_input_branch, preferred_element_type=jnp.float32).astype(
        jnp.bfloat16
    )
    lru_width = conv_input.shape[1]
    alive_rows = send_mask(flag_rows)
    masks = build_masks(flag_rows)
    outgoing = conv_input[row_count - (CW - 1) :] * alive_rows[:, None].astype(jnp.bfloat16)
    incoming = passed_along(outgoing, "seq", 1)
    padded = jnp.concatenate([incoming, conv_input], axis=0).astype(jnp.float32)
    conv_out = conv_local(
        padded, whole_conv_weight.astype(jnp.float32), whole_conv_bias.astype(jnp.float32), masks
    )
    conv_low = conv_out.astype(jnp.bfloat16)
    decay_pre = heads_product(conv_low, whole_decay_gate) + whole_decay_bias.astype(jnp.float32)
    input_pre = heads_product(conv_low, whole_input_gate) + whole_input_bias.astype(jnp.float32)
    param_full = whole_decay_param.astype(jnp.float32)
    coefficient, drive_term = lru_terms(decay_pre, input_pre, conv_out, param_full, flag_rows)
    cumulative, local_state = lax.associative_scan(combine, (coefficient, drive_term), axis=0)
    entering = prefix(
        (cumulative[-1], local_state[-1]),
        "seq",
        combine,
        (jnp.ones_like(cumulative[-1]), jnp.zeros_like(local_state[-1])),
        False,
    )
    incoming_state = entering[1]
    states = local_state + cumulative * incoming_state[None, :]
    mixed_rows = (states * gate_act).astype(jnp.bfloat16)
    middle = values + jnp.dot(mixed_rows, whole_out_proj, preferred_element_type=jnp.float32)
    whole_mlp_gain, whole_mlp_gate, whole_mlp_up, whole_mlp_down = (
        lax.all_gather(mlp_gain, "seq", axis=0, tiled=True),
        lax.all_gather(mlp_gate, "seq", axis=0, tiled=True),
        lax.all_gather(mlp_up, "seq", axis=0, tiled=True),
        lax.all_gather(mlp_down, "seq", axis=0, tiled=True),
    )
    gain_two = whole_mlp_gain.astype(jnp.float32)
    normed_two = rms_norm(middle, gain_two).astype(jnp.bfloat16)
    gate_mlp = jnp.dot(normed_two, whole_mlp_gate, preferred_element_type=jnp.float32)
    up_mlp = jnp.dot(normed_two, whole_mlp_up, preferred_element_type=jnp.float32)
    hidden = mlp_act(gate_mlp, up_mlp).astype(jnp.bfloat16)
    result = middle + jnp.dot(hidden, whole_mlp_down, preferred_element_type=jnp.float32)
    block_out = result.astype(jnp.bfloat16)
    back_mlp_gain, back_mlp_gate, back_mlp_up, back_mlp_down = (
        lax.all_gather(mlp_gain, "seq", axis=0, tiled=True),
        lax.all_gather(mlp_gate, "seq", axis=0, tiled=True),
        lax.all_gather(mlp_up, "seq", axis=0, tiled=True),
        lax.all_gather(mlp_down, "seq", axis=0, tiled=True),
    )
    grad_mlp_down = jnp.einsum("tf,td->fd", hidden, cotangent, preferred_element_type=jnp.float32)
    grad_hidden = jnp.einsum(
        "td,fd->tf", cotangent, back_mlp_down, preferred_element_type=jnp.float32
    )
    unused_act, pull_act = jax.vjp(mlp_act, gate_mlp, up_mlp)
    grad_gate_full, grad_up_full = pull_act(grad_hidden)
    grad_gate_low = grad_gate_full.astype(jnp.bfloat16)
    grad_up_low = grad_up_full.astype(jnp.bfloat16)
    grad_mlp_gate = jnp.einsum(
        "td,tf->df", normed_two, grad_gate_low, preferred_element_type=jnp.float32
    )
    grad_mlp_up = jnp.einsum(
        "td,tf->df", normed_two, grad_up_low, preferred_element_type=jnp.float32
    )
    grad_normed_two = jnp.einsum(
        "tf,df->td", grad_gate_low, back_mlp_gate, preferred_element_type=jnp.float32
    ) + jnp.einsum("tf,df->td", grad_up_low, back_mlp_up, preferred_element_type=jnp.float32)
    unused_norm, pull_norm = jax.vjp(rms_norm, middle, back_mlp_gain.astype(jnp.float32))
    grad_middle_norm, grad_mlp_gain = pull_norm(grad_normed_two)
    mlp_sums = (
        lax.psum_scatter(grad_mlp_gain, "seq", scatter_dimension=0, tiled=True),
        lax.psum_scatter(grad_mlp_gate, "seq", scatter_dimension=0, tiled=True),
        lax.psum_scatter(grad_mlp_up, "seq", scatter_dimension=0, tiled=True),
        lax.psum_scatter(grad_mlp_down, "seq", scatter_dimension=0, tiled=True),
    )
    grad_middle = cotangent.astype(jnp.float32) + grad_middle_norm
    grad_branch = grad_middle.astype(jnp.bfloat16)
    (
        back_norm_gain,
        back_gate_branch,
        back_input_branch,
        back_conv_weight,
        back_conv_bias,
        back_decay_gate,
        back_decay_bias,
        back_input_gate,
        back_input_bias,
        back_decay_param,
        back_out_proj,
    ) = (
        lax.all_gather(norm_gain, "seq", axis=0, tiled=True),
        lax.all_gather(gate_branch, "seq", axis=0, tiled=True),
        lax.all_gather(input_branch, "seq", axis=0, tiled=True),
        lax.all_gather(conv_weight, "seq", axis=1, tiled=True),
        lax.all_gather(conv_bias, "seq", axis=0, tiled=True),
        lax.all_gather(decay_gate, "seq", axis=0, tiled=True),
        lax.all_gather(decay_bias, "seq", axis=0, tiled=True),
        lax.all_gather(input_gate, "seq", axis=0, tiled=True),
        lax.all_gather(input_bias, "seq", axis=0, tiled=True),
        lax.all_gather(decay_param, "seq", axis=0, tiled=True),
        lax.all_gather(out_proj, "seq", axis=0, tiled=True),
    )
    grad_out_proj = jnp.einsum(
        "tr,td->rd", mixed_rows, grad_branch, preferred_element_type=jnp.float32
    )
    grad_mixed = jnp.einsum(
        "td,rd->tr", grad_branch, back_out_proj, preferred_element_type=jnp.float32
    )
    grad_states = grad_mixed * gate_act
    unused_gelu, pull_gelu = jax.vjp(gelu_tanh, gate_pre)
    grad_gate_pre = pull_gelu(grad_mixed * states)[0].astype(jnp.bfloat16)
    shifted_coef = jnp.concatenate([coefficient[1:], jnp.ones((1, lru_width), jnp.float32)], axis=0)
    back_cumulative, back_local = lax.associative_scan(
        combine, (shifted_coef[::-1], grad_states[::-1]), axis=0
    )
    back_cumulative = back_cumulative[::-1]
    back_local = back_local[::-1]
    leaving = prefix(
        (coefficient[0] * back_cumulative[0], coefficient[0] * back_local[0]),
        "seq",
        combine,
        (jnp.ones_like(back_local[0]), jnp.zeros_like(back_local[0])),
        True,
    )
    incoming_adjoint = leaving[1]
    adjoint = back_local + back_cumulative * incoming_adjoint[None, :]
    previous = jnp.concatenate([incoming_state[None, :], states[:-1]], axis=0)

    def terms_only(decay_values, input_values, conv_values, param_values):
        return lru_terms(decay_values, input_values, conv_values, param_values, flag_rows)

    unused_terms, pull_terms = jax.vjp(
        terms_only, decay_pre, input_pre, conv_out, back_decay_param.astype(jnp.float32)
    )
    grad_decay_full, grad_input_full, grad_conv_direct, grad_decay_param = pull_terms(
        (adjoint * previous, adjoint)
    )
    grad_decay_bias = jnp.sum(grad_decay_full, axis=0)
    grad_input_bias = jnp.sum(grad_input_full, axis=0)
    grad_decay_low = grad_decay_full.astype(jnp.bfloat16)
    grad_input_low = grad_input_full.astype(jnp.bfloat16)
    grad_decay_gate = heads_grad(conv_low, grad_decay_low)
    grad_input_gate = heads_grad(conv_low, grad_input_low)
    grad_conv_out = (
        grad_conv_direct
        + heads_back(grad_decay_low, back_decay_gate)
        + heads_back(grad_input_low, back_input_gate)
    )

    def conv_only(padded_values, weight_values, bias_values):
        return conv_local(padded_values, weight_values, bias_values, masks)

    unused_conv, pull_conv = jax.vjp(
        conv_only, padded, back_conv_weight.astype(jnp.float32), back_conv_bias.astype(jnp.float32)
    )
    grad_padded, grad_conv_weight, grad_conv_bias = pull_conv(grad_conv_out)
    returned_rows = passed_along(grad_padded[: CW - 1], "seq", -1)
    addition = jnp.concatenate(
        [
            jnp.zeros((row_count - (CW - 1), lru_width), jnp.float32),
            returned_rows * alive_rows[:, None],
        ],
        axis=0,
    )
    grad_conv_input = (grad_padded[CW - 1 :] + addition).astype(jnp.bfloat16)
    grad_input_branch = jnp.einsum(
        "td,tr->dr", normed, grad_conv_input, preferred_element_type=jnp.float32
    )
    grad_gate_branch = jnp.einsum(
        "td,tr->dr", normed, grad_gate_pre, preferred_element_type=jnp.float32
    )
    grad_normed = jnp.einsum(
        "tr,dr->td", grad_conv_input, back_input_branch, preferred_element_type=jnp.float32
    ) + jnp.einsum("tr,dr->td", grad_gate_pre, back_gate_branch, preferred_element_type=jnp.float32)
    unused_first, pull_first = jax.vjp(rms_norm, values, back_norm_gain.astype(jnp.float32))
    grad_values_norm, grad_norm_gain = pull_first(grad_normed)
    grad_tokens = grad_middle + grad_values_norm
    rec_sums = (
        lax.psum_scatter(grad_norm_gain, "seq", scatter_dimension=0, tiled=True),
        lax.psum_scatter(grad_gate_branch, "seq", scatter_dimension=0, tiled=True),
        lax.psum_scatter(grad_input_branch, "seq", scatter_dimension=0, tiled=True),
        lax.psum_scatter(grad_conv_weight, "seq", scatter_dimension=1, tiled=True),
        lax.psum_scatter(grad_conv_bias, "seq", scatter_dimension=0, tiled=True),
        lax.psum_scatter(grad_decay_gate, "seq", scatter_dimension=0, tiled=True),
        lax.psum_scatter(grad_decay_bias, "seq", scatter_dimension=0, tiled=True),
        lax.psum_scatter(grad_input_gate, "seq", scatter_dimension=0, tiled=True),
        lax.psum_scatter(grad_input_bias, "seq", scatter_dimension=0, tiled=True),
        lax.psum_scatter(grad_decay_param, "seq", scatter_dimension=0, tiled=True),
        lax.psum_scatter(grad_out_proj, "seq", scatter_dimension=0, tiled=True),
    )
    return (
        block_out,
        grad_tokens,
        rec_sums[0],
        rec_sums[1],
        rec_sums[2],
        rec_sums[3],
        rec_sums[4],
        rec_sums[5],
        rec_sums[6],
        rec_sums[7],
        rec_sums[8],
        rec_sums[9],
        rec_sums[10],
        mlp_sums[0],
        mlp_sums[1],
        mlp_sums[2],
        mlp_sums[3],
    )


CHIPS = 4
MESH = pl.DeviceIdType.MESH


def place():
    me = lax.axis_index("seq")
    core = lax.rem(me, 2)
    x = lax.rem(lax.div(me, 2), 2)
    y = lax.rem(lax.div(me, 4), 2)
    return me, lax.div(me, 8), 2 * y + x, core, x, y


def column_groups(n):
    return [[8 * z + 2 * p + c for c in range(2) for z in range(n // 8)] for p in range(CHIPS)]


def line_groups(n):
    return [[8 * z + r for z in range(n // 8)] for r in range(8)]


def greet(devices):
    barrier = pltpu.get_barrier_semaphore()
    for device in devices:
        pl.semaphore_signal(barrier, inc=1, device_id=(device,), device_id_type=MESH)
    pl.semaphore_wait(barrier, len(devices))


def remote(source, target, send_sem, recv_sem, device):
    return pltpu.make_async_remote_copy(
        src_ref=source,
        dst_ref=target,
        send_sem=send_sem,
        recv_sem=recv_sem,
        device_id=(device,),
        device_id_type=MESH,
    )


def comm_params(collective_id, vmem_mib=None):
    return pltpu.CompilerParams(
        collective_id=collective_id,
        has_side_effects=True,
        vmem_limit_bytes=None if vmem_mib is None else vmem_mib * 2**20,
    )


ANY = pl.BlockSpec(memory_space=pl.ANY)
VMEM = pl.BlockSpec(memory_space=pltpu.VMEM)


def plane_neighbours():
    me, z, p, c, x, y = place()
    x_dev, y_dev = me + 2 - 4 * x, me + 4 - 8 * y
    return (x_dev, y_dev, y_dev + 2 - 4 * x), (p + 1 - 2 * x, p + 2 - 4 * y, 3 - p)


def gather_steps(source, whole, send, recv, local, first):
    me, z, p, c, x, y = place()
    (x_dev, y_dev, d_dev), (p_x, p_y, p_d) = plane_neighbours()
    half = source.shape[0] // 2

    def copy(k, source, target, device):
        return remote(source, target, send.at[first + k], recv.at[first + k], device)

    to_x, to_y = copy(0, source, whole.at[p], x_dev), copy(1, source, whole.at[p], y_dev)
    low, high = whole.at[p_x, pl.ds(0, half)], whole.at[p_y, pl.ds(half, half)]
    on_y, on_x = copy(2, low, low, y_dev), copy(3, high, high, x_dev)
    own = pltpu.make_async_copy(source, whole.at[p], local)

    def begin():
        to_x.start()
        to_y.start()
        own.start()

    def forward():
        to_x.wait_recv()
        on_y.start()
        to_y.wait_recv()
        on_x.start()

    def end():
        to_x.wait_send()
        to_y.wait_send()
        on_y.wait()
        on_x.wait()
        own.wait()

    return begin, forward, end


def sum_scratch(rows, columns, dtype):
    whole, part = pltpu.VMEM((rows, columns), dtype), pltpu.VMEM((rows // 2, columns), dtype)
    return [whole] * 3 + [part] * 4 + [pltpu.SemaphoreType.DMA((6,)), pltpu.SemaphoreType.DMA((6,)), pltpu.SemaphoreType.DMA((3,))]


def sum_steps(part, own, from_x, from_y, diag_x, diag_y, on_x, on_y, send, recv, local):
    me, z, p, c, x, y = place()
    (x_dev, y_dev, d_dev), (p_x, p_y, p_d) = plane_neighbours()
    half = part.shape[1] // 2
    low, high = pl.ds(0, half), pl.ds(half, half)
    copies = [
        remote(part.at[p_d, low], diag_x, send.at[0], recv.at[0], x_dev),
        remote(part.at[p_d, high], diag_y, send.at[1], recv.at[1], y_dev),
        remote(part.at[p_x, low], from_x.at[low], send.at[2], recv.at[2], x_dev),
        remote(part.at[p_y, high], from_y.at[high], send.at[3], recv.at[3], y_dev),
    ]
    locals_ = [
        pltpu.make_async_copy(part.at[p_y, low], on_y, local.at[0]),
        pltpu.make_async_copy(part.at[p_x, high], on_x, local.at[1]),
        pltpu.make_async_copy(part.at[p], own, local.at[2]),
    ]
    to_y = remote(on_y, from_y.at[low], send.at[4], recv.at[4], y_dev)
    to_x = remote(on_x, from_x.at[high], send.at[5], recv.at[5], x_dev)

    def add_into(target, addend):
        @pl.loop(0, half // 16)
        def add_rows(i):
            at = pl.ds(pl.multiple_of(i * 16, 16), 16)
            target[at, :] = (
                target[at, :].astype(jnp.float32) + addend[at, :].astype(jnp.float32)
            ).astype(target.dtype)

    def begin():
        for copy in copies + locals_:
            copy.start()

    def forward():
        locals_[0].wait()
        copies[0].wait_recv()
        add_into(on_y, diag_x)
        to_y.start()
        locals_[1].wait()
        copies[1].wait_recv()
        add_into(on_x, diag_y)
        to_x.start()

    def end():
        locals_[2].wait()
        copies[2].wait_recv()
        copies[3].wait_recv()
        to_y.wait()
        to_x.wait()
        for copy in copies:
            copy.wait_send()

    return begin, forward, end


def sixteen(i):
    return pl.ds(pl.multiple_of(i * 16, 16), 16)


def middle_kernel(parts, tokens, gain, middle, whole, normed, *scratch):
    sums, (send, recv, local) = scratch[:10], scratch[10:]
    greet(plane_neighbours()[0][:2])
    own, from_x, from_y = sums[:3]
    for step in sum_steps(parts, *sums):
        step()

    @pl.loop(0, tokens.shape[0] // 16)
    def norm_rows(i):
        at = sixteen(i)
        values = tokens[at, :].astype(jnp.float32) + (own[at, :] + from_x[at, :] + from_y[at, :])
        middle[at, :] = values
        inverse = lax.rsqrt(jnp.mean(values * values, axis=-1, keepdims=True) + epsilon)
        normed[at, :] = (values * inverse * gain[...]).astype(jnp.bfloat16)

    for step in gather_steps(normed, whole, send, recv, local, 0):
        step()


def middle_of(parts, tokens, gain, collective_id):
    rows, width = tokens.shape
    return pl.pallas_call(
        middle_kernel,
        out_shape=[
            jax.ShapeDtypeStruct((rows, width), jnp.float32),
            jax.ShapeDtypeStruct((CHIPS, rows, width), jnp.bfloat16),
        ],
        in_specs=[ANY, VMEM, VMEM],
        out_specs=[VMEM, ANY],
        scratch_shapes=[
            pltpu.VMEM((rows, width), jnp.bfloat16),
            *sum_scratch(rows, width, parts.dtype),
            pltpu.SemaphoreType.DMA((4,)),
            pltpu.SemaphoreType.DMA((4,)),
            pltpu.SemaphoreType.DMA,
        ],
        compiler_params=comm_params(collective_id, 32),
        name="middle",
    )(parts, tokens, gain[None])


def norm_back_rows(values, gain, grad, rest):
    inverse = lax.rsqrt(jnp.mean(values * values, axis=-1, keepdims=True) + epsilon)
    scaled = gain * grad
    pull = jnp.mean(scaled * values, axis=-1, keepdims=True) * (inverse * inverse * inverse)
    return rest + inverse * scaled - values * pull, grad * values * inverse


def grads_of_middle_kernel(
    parts,
    middle,
    cot,
    gain,
    hidden,
    down,
    cot_all,
    cot_other,
    grad_middle,
    grad_gain,
    whole,
    down_grad,
    down_parts,
    branch,
    hidden_here,
    hidden_other,
    down_here,
    cot_here,
    cot_there,
    *scratch,
):
    sums, (send, recv, local, loads) = scratch[:10], scratch[10:]
    me, z, p, c, x, y = place()
    f32, bf16 = jnp.float32, jnp.bfloat16
    sibling = me + 1 - 2 * c
    greet((*plane_neighbours()[0][:2], sibling))
    own, from_x, from_y = sums[:3]
    begin, forward, end = sum_steps(parts, *sums)
    begin()
    units = hidden.shape[1]
    half = units // 2
    swap = remote(
        hidden.at[:, pl.ds(pl.multiple_of((1 - c) * half, 128), half)], hidden_other, send.at[4], recv.at[4], sibling
    )
    swap.start()
    fetched = [
        pltpu.make_async_copy(source, target, loads.at[k])
        for k, (source, target) in enumerate(
            ((hidden, hidden_here), (cot_all, cot_here), (cot_other, cot_there), (down, down_here))
        )
    ]
    for copy in fetched:
        copy.start()
    for copy in fetched[:3]:
        copy.wait()
    swap.wait()
    tile = 256

    def grad_tiles(m):
        rows_here = pl.ds(pl.multiple_of(c * half + m * tile, 128), tile)
        rows_there = pl.ds(pl.multiple_of(m * tile, 128), tile)

        @pl.loop(0, cot_all.shape[1] // (2 * tile))
        def grad_tile(k):
            columns = pl.ds(pl.multiple_of(k * 2 * tile, 128), 2 * tile)

            def dot_t(left, right):
                return lax.dot_general(left, right, (((0,), (0,)), ((), ())), preferred_element_type=f32)

            down_grad[rows_there, columns] = (
                dot_t(hidden_here[:, rows_here], cot_here[:, columns])
                + dot_t(hidden_other[:, rows_there], cot_there[:, columns])
            ).astype(bf16)

    pl.loop(0, 1)(grad_tiles)
    forward()
    pl.loop(1, half // tile)(grad_tiles)
    end()
    rows, width = middle.shape

    def norm_rows(i, total):
        at = sixteen(i)
        grad = own[at, :].astype(f32) + from_x[at, :].astype(f32) + from_y[at, :].astype(f32)
        given, terms = norm_back_rows(middle[at, :], gain[...], grad, cot[at, :].astype(f32))
        grad_middle[at, :] = given
        branch[at, :] = given.astype(bf16)
        return total + terms[:8] + terms[8:]

    total = lax.fori_loop(0, rows // 16, norm_rows, jnp.zeros((8, width), f32))
    grad_gain[...] = jnp.sum(total, axis=0, keepdims=True)
    begin, forward, end = gather_steps(branch, whole, send, recv, local, 0)
    begin()
    fetched[3].wait()

    def down_tiles(j):
        @pl.loop(0, width // (2 * tile))
        def down_tile(k):
            columns = pl.ds(pl.multiple_of(k * 2 * tile, 128), 2 * tile)
            down_parts[j, :, columns] = jnp.dot(
                hidden_here[pl.ds(pl.multiple_of(j * rows, 16), rows), :],
                down_here[:, columns],
                preferred_element_type=f32,
            ).astype(bf16)

    pl.loop(0, CHIPS)(down_tiles)
    forward()
    end()


def grads_of_middle(parts, middle, cot, gain, hidden, down, cot_all, cot_other, collective_id):
    rows, width = middle.shape
    tokens, units = hidden.shape
    f32, bf16 = jnp.float32, jnp.bfloat16
    return pl.pallas_call(
        grads_of_middle_kernel,
        out_shape=[
            jax.ShapeDtypeStruct((rows, width), f32),
            jax.ShapeDtypeStruct((1, width), f32),
            jax.ShapeDtypeStruct((CHIPS, rows, width), bf16),
            jax.ShapeDtypeStruct((units // 2, width), bf16),
            jax.ShapeDtypeStruct((CHIPS, rows, width), bf16),
        ],
        in_specs=[ANY, VMEM, VMEM, VMEM, ANY, ANY, ANY, ANY],
        out_specs=[VMEM, VMEM, ANY, VMEM, VMEM],
        scratch_shapes=[
            pltpu.VMEM((rows, width), bf16),
            pltpu.VMEM((tokens, units), bf16),
            pltpu.VMEM((tokens, units // 2), bf16),
            pltpu.VMEM((units, width), bf16),
            pltpu.VMEM((tokens, width), bf16),
            pltpu.VMEM((tokens, width), bf16),
            *sum_scratch(rows, width, parts.dtype),
            pltpu.SemaphoreType.DMA((5,)),
            pltpu.SemaphoreType.DMA((5,)),
            pltpu.SemaphoreType.DMA,
            pltpu.SemaphoreType.DMA((4,)),
        ],
        compiler_params=comm_params(collective_id, 56),
        name="grads_of_middle",
    )(parts, middle, cot, gain[None], hidden, down, cot_all, cot_other)


def closing_kernel(
    planes,
    parts,
    tokens,
    gain,
    rest,
    small,
    conv_here,
    conv_there,
    decay_here,
    decay_there,
    input_here,
    input_there,
    piece,
    grad_tokens,
    small_out,
    gates_out,
    swapped,
    conv_a,
    conv_b,
    low_a,
    low_b,
    low_c,
    low_d,
    gates,
    gate_lines,
    lines,
    line,
    near_parts,
    gains,
    gain_lines,
    gain_line,
    gain_near,
    *scratch,
):
    sums, (send, recv, local, loads) = scratch[:10], scratch[10:]
    me, z, p, c, x, y = place()
    f32 = jnp.float32
    r = lax.rem(me, 8)
    near = [(lax.rem(r + d, 8), me - r + lax.rem(r + d, 8)) for d in range(1, 8)]
    far = [(lax.rem(z + d, planes), 8 * lax.rem(z + d, planes) + r) for d in range(1, planes)]
    greet([device for unused, device in near + far])
    own, from_x, from_y = sums[:3]
    begin, forward, end = sum_steps(parts, *sums)
    begin()
    devices, chips = plane_neighbours()

    def copy(k, source, target, device):
        return remote(source, target, send.at[k], recv.at[k], device)

    swaps = [copy(k, piece.at[chips[k]], swapped.at[p], devices[k]) for k in range(3)]
    for swap in swaps:
        swap.start()
    swap_own = pltpu.make_async_copy(piece.at[p], swapped.at[p], local)
    swap_own.start()
    at = 3
    small_far = [copy(at + d, small.at[there], lines.at[d], device) for d, (there, device) in enumerate(far)]
    at += len(far)
    for sent in small_far:
        sent.start()
    fetched = [
        pltpu.make_async_copy(source, target, loads.at[k])
        for k, (source, target) in enumerate(
            (
                (conv_here, conv_a),
                (conv_there, conv_b),
                (decay_here, low_a),
                (decay_there, low_b),
                (input_here, low_c),
                (input_there, low_d),
            )
        )
    ]
    for fetch in fetched:
        fetch.start()
    for fetch in fetched:
        fetch.wait()

    def dot_t(left, right):
        return lax.dot_general(left, right, (((0,), (0,)), ((), ())), preferred_element_type=f32)

    block = gates.shape[1]
    count = conv_a.shape[1]
    for k, (first, second) in enumerate(((low_a, low_b), (low_c, low_d))):
        full = dot_t(conv_a[...], first[...]) + dot_t(conv_b[...], second[...])
        for j in range(planes):
            for e in range(2):
                gates[j, :, (2 * k + e) * block : (2 * k + e + 1) * block] = full[
                    j * block : (j + 1) * block, e * count + j * block : e * count + (j + 1) * block
                ]
    gate_far = [copy(at + d, gates.at[there], gate_lines.at[d], device) for d, (there, device) in enumerate(far)]
    at += len(far)
    for sent in gate_far:
        sent.start()
    forward()
    for sent in small_far:
        sent.wait()
    line[...] = small[z] + sum(lines[d] for d in range(planes - 1))
    small_near = [
        copy(at + d, line.at[there], near_parts.at[d], device) for d, (there, device) in enumerate(near)
    ]
    at += len(near)
    for sent in small_near:
        sent.start()
    end()
    rows, width = tokens.shape
    step = width // (8 * planes)

    def norm_rows(i, total):
        here = sixteen(i)
        grad = own[here, :].astype(f32) + from_x[here, :].astype(f32) + from_y[here, :].astype(f32)
        given, terms = norm_back_rows(tokens[here, :].astype(f32), gain[...], grad, rest[here, :])
        for k in range(4 * planes):
            for e in range(2):
                grad_tokens[here, (2 * k + e) * step : (2 * k + e + 1) * step] = given[
                    :, (4 * planes * e + k) * step : (4 * planes * e + k + 1) * step
                ]
        return total + terms[:8] + terms[8:]

    total = lax.fori_loop(0, rows // 16, norm_rows, jnp.zeros((8, width), f32))
    total = jnp.sum(total, axis=0, keepdims=True)
    for j in range(planes):
        for q in range(CHIPS):
            for e in range(2):
                start = ((e * planes + j) * CHIPS + q) * step
                gains[j, 2 * q + e, 0:1, 0:step] = total[:, start : start + step]
    gain_far = [copy(at + d, gains.at[there], gain_lines.at[d], device) for d, (there, device) in enumerate(far)]
    at += len(far)
    for sent in gain_far:
        sent.start()
    for sent in gain_far:
        sent.wait()
    gain_line[...] = gains[z] + sum(gain_lines[d] for d in range(planes - 1))
    last = [
        copy(at + d, gain_line.at[there], gain_near.at[d], device) for d, (there, device) in enumerate(near)
    ]
    for sent in last:
        sent.start()
    for sent in small_near + gate_far + swaps:
        sent.wait()
    swap_own.wait()
    gates_out[...] = gates[z] + sum(gate_lines[d] for d in range(planes - 1))
    for sent in last:
        sent.wait()
    rows_small = line.shape[1]
    small_out[0:rows_small, :] = line[r] + sum(near_parts[d] for d in range(7))
    small_out[rows_small : rows_small + 8, :] = gain_line[r] + sum(gain_near[d] for d in range(7))


def closing(parts, tokens, gain, rest, small, convs, decays, inputs, piece, head, collective_id):
    planes = lax.axis_size("seq") // 8
    rows, width = tokens.shape
    f32, bf16 = jnp.float32, jnp.bfloat16
    rows_small, lanes = small.shape[2:]
    block = convs[0].shape[1] // planes
    count = 3 + 3 * (planes - 1) + 14
    return pl.pallas_call(
        functools.partial(closing_kernel, planes),
        out_shape=[
            jax.ShapeDtypeStruct((rows, width), f32),
            jax.ShapeDtypeStruct((rows_small + 8, lanes), f32),
            jax.ShapeDtypeStruct((block, 2 * head), f32),
            jax.ShapeDtypeStruct(piece.shape, piece.dtype),
        ],
        in_specs=[ANY, VMEM, VMEM, VMEM, VMEM] + [ANY] * 7,
        out_specs=[VMEM, VMEM, VMEM, ANY],
        scratch_shapes=[
            pltpu.VMEM(convs[0].shape, bf16),
            pltpu.VMEM(convs[0].shape, bf16),
            *[pltpu.VMEM(decays[0].shape, bf16)] * 4,
            pltpu.VMEM((planes, block, 2 * head), f32),
            pltpu.VMEM((planes - 1, block, 2 * head), f32),
            pltpu.VMEM((planes - 1, 8, rows_small, lanes), f32),
            pltpu.VMEM((8, rows_small, lanes), f32),
            pltpu.VMEM((7, rows_small, lanes), f32),
            pltpu.VMEM((planes, 8, 8, lanes), f32),
            pltpu.VMEM((planes - 1, 8, 8, lanes), f32),
            pltpu.VMEM((8, 8, lanes), f32),
            pltpu.VMEM((7, 8, lanes), f32),
            *sum_scratch(rows, width, parts.dtype),
            pltpu.SemaphoreType.DMA((count,)),
            pltpu.SemaphoreType.DMA((count,)),
            pltpu.SemaphoreType.DMA,
            pltpu.SemaphoreType.DMA((6,)),
        ],
        compiler_params=comm_params(collective_id, 40),
        name="closing",
    )(parts, tokens, gain[None], rest, small, *convs, *decays, *inputs, piece)


def plane_gather_kernel(x_ref, o_ref, send, recv, local):
    greet(plane_neighbours()[0][:2])
    for step in gather_steps(x_ref, o_ref, send, recv, local, 0):
        step()


def plane_gather(block, collective_id):
    return pl.pallas_call(
        plane_gather_kernel,
        out_shape=jax.ShapeDtypeStruct((CHIPS,) + block.shape, block.dtype),
        in_specs=[ANY],
        out_specs=ANY,
        scratch_shapes=[
            pltpu.SemaphoreType.DMA((4,)),
            pltpu.SemaphoreType.DMA((4,)),
            pltpu.SemaphoreType.DMA,
        ],
        compiler_params=comm_params(collective_id),
        name="plane_gather",
    )(block)


def plane_swap_kernel(count, *refs):
    ins, outs = refs[:count], refs[count : 2 * count]
    send, recv, local = refs[2 * count :]
    me, z, p, c, x, y = place()
    x_dev, y_dev = me + 2 - 4 * x, me + 4 - 8 * y
    d_dev = y_dev + 2 - 4 * x
    p_x, p_y, p_d = p + 1 - 2 * x, p + 2 - 4 * y, 3 - p
    peers = ((x_dev, p_x), (y_dev, p_y), (d_dev, p_d))
    greet([device for device, unused in peers])
    copies = []
    for k in range(count):
        for j, (device, chip) in enumerate(peers):
            copies.append(remote(ins[k].at[chip], outs[k].at[p], send.at[k, j], recv.at[k, j], device))
        copies.append(pltpu.make_async_copy(ins[k].at[p], outs[k].at[p], local.at[k]))
    for copy in copies:
        copy.start()
    for copy in copies:
        copy.wait()


def plane_swap(arrays, collective_id):
    count = len(arrays)
    return pl.pallas_call(
        functools.partial(plane_swap_kernel, count),
        out_shape=[jax.ShapeDtypeStruct(a.shape, a.dtype) for a in arrays],
        in_specs=[ANY] * count,
        out_specs=[ANY] * count,
        scratch_shapes=[
            pltpu.SemaphoreType.DMA((count, 3)),
            pltpu.SemaphoreType.DMA((count, 3)),
            pltpu.SemaphoreType.DMA((count,)),
        ],
        compiler_params=comm_params(collective_id),
        name="plane_swap",
    )(*arrays)


def opening_kernel(planes, weights_ref, x_ref, swapped_ref, o_ref, send, recv, local):
    me, z, p, c, x, y = place()
    r = lax.rem(me, 8)
    base = me - r
    near = [base + lax.rem(r + d, 8) for d in range(1, 8)]
    far = [8 * lax.rem(z + d, planes) + r for d in range(1, planes)]
    greet(near + far)
    x_dev, y_dev = me + 2 - 4 * x, me + 4 - 8 * y
    d_dev = y_dev + 2 - 4 * x
    p_x, p_y, p_d = p + 1 - 2 * x, p + 2 - 4 * y, 3 - p
    lines = [
        remote(x_ref, o_ref.at[r, z], send.at[d], recv.at[d], device) for d, device in enumerate(far)
    ]
    swaps = [
        remote(weights_ref.at[chip], swapped_ref.at[p], send.at[planes + j], recv.at[planes + j], device)
        for j, (device, chip) in enumerate(((x_dev, p_x), (y_dev, p_y), (d_dev, p_d)))
    ]
    own = pltpu.make_async_copy(weights_ref.at[p], swapped_ref.at[p], local)
    for copy in lines + swaps:
        copy.start()
    own.start()
    o_ref[r, z] = x_ref[...]
    for copy in lines:
        copy.wait()
    spreads = [
        remote(o_ref.at[r], o_ref.at[r], send.at[planes + 3 + d], recv.at[planes + 3 + d], device)
        for d, device in enumerate(near)
    ]
    for copy in spreads:
        copy.start()
    for copy in spreads + swaps:
        copy.wait()
    own.wait()


def opening(weights, block, collective_id):
    planes = lax.axis_size("seq") // 8
    return pl.pallas_call(
        functools.partial(opening_kernel, planes),
        out_shape=[
            jax.ShapeDtypeStruct(weights.shape, weights.dtype),
            jax.ShapeDtypeStruct((8, planes) + block.shape, block.dtype),
        ],
        in_specs=[ANY, VMEM],
        out_specs=[ANY, VMEM],
        scratch_shapes=[
            pltpu.SemaphoreType.DMA((planes + 10,)),
            pltpu.SemaphoreType.DMA((planes + 10,)),
            pltpu.SemaphoreType.DMA,
        ],
        compiler_params=comm_params(collective_id),
        name="opening",
    )(weights, block)


def column_peers(planes, z, p, c):
    count = 2 * planes
    q = 2 * z + c
    peers = []
    for d in range(1, count):
        other = lax.rem(q + d, count)
        peers.append(8 * lax.div(other, 2) + 2 * p + lax.rem(other, 2))
    return q, peers


def carry_in(planes, reverse, z, c, q, peers, everyone, before, entering, send, recv):
    own = everyone.at[q]
    copies = [remote(own, own, send.at[d], recv.at[d], device) for d, device in enumerate(peers)]
    for copy in copies:
        copy.start()
    for copy in copies:
        copy.wait()
    carried = jnp.zeros((1, everyone.shape[2]), jnp.float32)
    order = [(k, j, e) for k in range(planes) for j in range(CHIPS) for e in range(2)]
    for k, j, e in reversed(order) if reverse else order:
        before[8 * k + 2 * j + e : 8 * k + 2 * j + e + 1, :] = carried
        part = everyone.at[2 * k + e]
        carried = part[j : j + 1, :] * carried + part[CHIPS + j : CHIPS + j + 1, :]
    for j in range(CHIPS):
        entering[j : j + 1, :] = before[pl.ds(8 * z + 2 * j + c, 1), :]


def shift_down(earlier, values, step, row):
    return jnp.where(row >= step, pltpu.roll(values, step, 0), pltpu.roll(earlier, step, 0))


def shift_up(values, later, step, row):
    return jnp.where(row < 8 - step, pltpu.roll(values, 8 - step, 0), pltpu.roll(later, 8 - step, 0))


def tile_scan(a, b, row, reverse):
    for step in (1, 2, 4):
        if reverse:
            keep = row < 8 - step
            shifted_a, shifted_b = pltpu.roll(a, 8 - step, 0), pltpu.roll(b, 8 - step, 0)
        else:
            keep = row >= step
            shifted_a, shifted_b = pltpu.roll(a, step, 0), pltpu.roll(b, step, 0)
        b = a * jnp.where(keep, shifted_b, 0.0) + b
        a = a * jnp.where(keep, shifted_a, 1.0)
    return a, b


def sigmoid(values):
    return 1.0 / (1.0 + jnp.exp(-values))


def gate_terms(decay_pre, rate, flag):
    opened = sigmoid(decay_pre)
    log_decay = rate * opened
    decay = jnp.exp(log_decay)
    keep = 1.0 - flag
    squared = decay * decay
    return opened, decay * keep, keep, squared, jnp.tanh(-log_decay) * (1.0 + squared)


GELU_A, GELU_B = 0.7978845608028654, 0.044715


def eight(i):
    return pl.ds(pl.multiple_of(i * 8, 8), 8)


def recurrence_kernel(
    planes,
    gate_pre,
    conv_input,
    masks,
    vectors,
    decay_blocks,
    input_blocks,
    cot,
    conv_out,
    conv_low,
    decay_pre,
    input_pre,
    states,
    mixed,
    entering,
    halo,
    cot_all,
    cumulative,
    sibling_tails,
    below_tail,
    everyone,
    before,
    send,
    recv,
    local,
):
    me, z, p, c, x, y = place()
    rows, channels = conv_input.shape[1:]
    q, peers = column_peers(planes, z, p, c)
    greet(peers + [*plane_neighbours()[0][:2]])
    cot_begin, cot_forward, cot_end = gather_steps(cot, cot_all, send, recv, local, 9)
    cot_begin()
    f32 = jnp.float32
    tail = pl.ds(rows - 16, 16)
    to_sibling = remote(conv_input.at[:, tail], sibling_tails, send.at[7], recv.at[7], me + 1 - 2 * c)
    to_above = remote(conv_input.at[CHIPS - 1, tail], below_tail, send.at[8], recv.at[8], me + 7)
    from_below = remote(conv_input.at[CHIPS - 1, tail], below_tail, send.at[8], recv.at[8], me - 7)
    to_sibling.start()

    @pl.when((c == 1) & (z < planes - 1))
    def send_above():
        to_above.start()

    to_sibling.wait()

    @pl.when((c == 1) & (z < planes - 1))
    def sent_above():
        to_above.wait_send()

    @pl.when((c == 0) & (z > 0))
    def had_below():
        from_below.wait_recv()

    @pl.when(c == 1)
    def halo_one():
        for j in range(CHIPS):
            halo[j] = sibling_tails[j].astype(f32)[8:]

    @pl.when(c == 0)
    def halo_zero():
        for j in range(1, CHIPS):
            halo[j] = sibling_tails[j - 1].astype(f32)[8:]

        @pl.when(z > 0)
        def halo_below():
            halo[0] = below_tail[...].astype(f32)[8:]

        @pl.when(z == 0)
        def halo_none():
            halo[0] = jnp.zeros((8, channels), f32)

    row = lax.broadcasted_iota(jnp.int32, (8, channels), 0)

    @pl.loop(0, CHIPS)
    def block(j):
        def conv_tile(i, earlier):
            both = conv_input[j, sixteen(i), :].astype(f32)
            outs = []
            for h in range(2):
                now = both[8 * h : 8 * h + 8]
                keep = masks[j, eight(2 * i + h), :]
                out = vectors[CW : CW + 1, :] + vectors[0:1, :] * now
                for k in range(1, CW):
                    out = out + vectors[k : k + 1, :] * (
                        shift_down(earlier, now, k, row) * keep[:, k : k + 1]
                    )
                conv_out[j, eight(2 * i + h), :] = out
                outs.append(out)
                earlier = now
            conv_low[j, sixteen(i), :] = jnp.concatenate(outs, axis=0).astype(jnp.bfloat16)
            return earlier

        lax.fori_loop(0, rows // 16, conv_tile, halo[j])
        low = conv_low[j]
        decay_pre[j] = jnp.dot(low, decay_blocks[...], preferred_element_type=f32) + vectors[CW + 1 : CW + 2, :]
        input_pre[j] = jnp.dot(low, input_blocks[...], preferred_element_type=f32) + vectors[CW + 2 : CW + 3, :]

        def scan_tile(i, carry):
            at = eight(i)
            flag = masks[j, at, :][:, 0:1]
            opened, coef, keep, squared, gap = gate_terms(decay_pre[j, at, :], vectors[CW + 3 : CW + 4, :], flag)
            drive = (flag + keep * jnp.sqrt(gap)) * sigmoid(input_pre[j, at, :]) * conv_out[j, at, :]
            a, b = tile_scan(coef, drive, row, False)
            before_a, before_b = carry
            b = a * before_b + b
            a = a * before_a
            cumulative[j, at, :] = a
            states[j, at, :] = b
            return a[7:8], b[7:8]

        last_a, last_b = lax.fori_loop(
            0,
            rows // 8,
            scan_tile,
            (jnp.ones((1, channels), f32), jnp.zeros((1, channels), f32)),
        )
        everyone[q, pl.ds(j, 1), :] = last_a
        everyone[q, pl.ds(CHIPS + j, 1), :] = last_b

    cot_forward()
    carry_in(planes, False, z, c, q, peers, everyone, before, entering, send, recv)

    @pl.loop(0, CHIPS)
    def finish(j):
        start = entering[pl.ds(j, 1), :]

        def state_tile(i, unused):
            at = sixteen(i)
            state = states[j, at, :] + cumulative[j, at, :] * start
            states[j, at, :] = state
            v = gate_pre[j, at, :]
            act = 0.5 * v * (1.0 + jnp.tanh(GELU_A * (v + GELU_B * (v * v * v))))
            mixed[j, at, :] = (state * act).astype(jnp.bfloat16)
            return unused

        lax.fori_loop(0, rows // 16, state_tile, 0)

    cot_end()


def recurrence(gate_pre, conv_input, masks, vectors, decay_blocks, input_blocks, cot, collective_id):
    planes = lax.axis_size("seq") // 8
    blocks, rows, channels = conv_input.shape
    f32, bf16 = jnp.float32, jnp.bfloat16
    cube = conv_input.shape

    def out(dtype, shape=cube):
        return jax.ShapeDtypeStruct(shape, dtype)

    return pl.pallas_call(
        functools.partial(recurrence_kernel, planes),
        out_shape=[
            out(f32),
            out(bf16),
            out(f32),
            out(f32),
            out(f32),
            out(bf16),
            out(f32, (CHIPS, channels)),
            out(f32, (CHIPS, 8, channels)),
            out(cot.dtype, (CHIPS,) + cot.shape),
        ],
        in_specs=[VMEM] * 6 + [ANY],
        out_specs=[VMEM] * 8 + [ANY],
        scratch_shapes=[
            pltpu.VMEM(cube, f32),
            pltpu.VMEM((CHIPS, 16, channels), bf16),
            pltpu.VMEM((16, channels), bf16),
            pltpu.VMEM((2 * planes, 2 * CHIPS, channels), f32),
            pltpu.VMEM((8 * planes, channels), f32),
            pltpu.SemaphoreType.DMA((13,)),
            pltpu.SemaphoreType.DMA((13,)),
            pltpu.SemaphoreType.DMA,
        ],
        compiler_params=comm_params(collective_id, 48),
        name="recurrence",
    )(gate_pre, conv_input, masks, vectors, decay_blocks, input_blocks, cot)


def recurrence_back_kernel(
    planes,
    grad_mixed,
    gate_pre,
    conv_input,
    conv_out,
    decay_pre,
    input_pre,
    states,
    entering,
    halo,
    masks,
    after_masks,
    vectors,
    decay_blocks,
    input_blocks,
    down_parts,
    piece,
    in_low,
    decay_low,
    input_low,
    sums,
    down_others,
    swapped,
    cumulative,
    local,
    grad_conv,
    sibling_heads,
    above_head,
    ahead,
    everyone,
    before,
    leaving,
    send,
    recv,
    piece_sem,
):
    me, z, p, c, x, y = place()
    rows, channels = conv_input.shape[1:]
    q, peers = column_peers(planes, z, p, c)
    devices, chips = plane_neighbours()
    greet(peers + [*devices])
    downs = [
        remote(down_parts.at[chips[k]], down_others.at[k], send.at[9 + k], recv.at[9 + k], devices[k])
        for k in range(3)
    ] + [
        remote(piece.at[chips[k]], swapped.at[p], send.at[12 + k], recv.at[12 + k], devices[k]) for k in range(3)
    ]
    downs.append(pltpu.make_async_copy(piece.at[p], swapped.at[p], piece_sem))
    for copy in downs:
        copy.start()
    f32, bf16 = jnp.float32, jnp.bfloat16
    row = lax.broadcasted_iota(jnp.int32, (8, channels), 0)
    rate = vectors[CW + 3 : CW + 4, :]
    nothing = jnp.zeros((8, channels), f32)

    @pl.loop(0, CHIPS)
    def scan_block(j):
        def scan_tile(i, carry):
            i = rows // 16 - 1 - i
            at = sixteen(i)
            v = gate_pre[j, at, :]
            grad = grad_mixed[j, at, :]
            t = jnp.tanh(GELU_A * (v + GELU_B * (v * v * v)))
            act = 0.5 * v * (1.0 + t)
            slope = 0.5 * (1.0 + t) + 0.5 * v * (1.0 - t * t) * (GELU_A * (1.0 + 3.0 * GELU_B * (v * v)))
            in_low[j, at, 0:channels] = (grad * states[j, at, :] * slope).astype(bf16)
            drive = grad * act
            later_a, later_b, later_coef = carry
            for h in (1, 0):
                here = eight(2 * i + h)
                flag = masks[j, here, :][:, 0:1]
                coef = gate_terms(decay_pre[j, here, :], rate, flag)[1]
                shifted = jnp.where(row < 7, pltpu.roll(coef, 7, 0), later_coef)
                a, b = tile_scan(shifted, drive[8 * h : 8 * h + 8], row, True)
                b = a * later_b + b
                a = a * later_a
                cumulative[j, here, :] = a
                local[j, here, :] = b
                later_a, later_b, later_coef = a[0:1], b[0:1], coef[0:1]
            return later_a, later_b, later_coef

        ones = jnp.ones((1, channels), f32)
        first_a, first_b, first_coef = lax.fori_loop(
            0, rows // 16, scan_tile, (ones, jnp.zeros((1, channels), f32), ones)
        )
        everyone[q, pl.ds(j, 1), :] = first_coef * first_a
        everyone[q, pl.ds(CHIPS + j, 1), :] = first_coef * first_b

    carry_in(planes, True, z, c, q, peers, everyone, before, leaving, send, recv)

    def terms_block(j, totals):
        behind_all = leaving[pl.ds(j, 1), :]

        def terms_tile(i, carry):
            previous, decay_sum, input_sum, param_sum = carry
            lows = []
            for h in range(2):
                at = eight(2 * i + h)
                adjoint = local[j, at, :] + cumulative[j, at, :] * behind_all
                state = states[j, at, :]
                earlier = jnp.where(row >= 1, pltpu.roll(state, 1, 0), previous)
                previous = state[7:8]
                flag = masks[j, at, :][:, 0:1]
                opened, coef, keep, squared, gap = gate_terms(decay_pre[j, at, :], rate, flag)
                passed = sigmoid(input_pre[j, at, :])
                conv = conv_out[j, at, :]
                inverse = lax.rsqrt(gap)
                scale = flag + keep * (gap * inverse)
                grad_log = adjoint * (earlier * coef - keep * passed * conv * squared * inverse)
                log_open = grad_log * opened
                decay_full = log_open * rate * (1.0 - opened)
                direct = adjoint * scale * passed
                input_full = direct * (1.0 - passed) * conv
                grad_conv[j, at, :] = direct
                lows.append((decay_full, input_full))
                decay_sum = decay_sum + decay_full
                input_sum = input_sum + input_full
                param_sum = param_sum + log_open
            decay_low[j, sixteen(i), :] = jnp.concatenate([low[0] for low in lows], axis=0).astype(bf16)
            input_low[j, sixteen(i), :] = jnp.concatenate([low[1] for low in lows], axis=0).astype(bf16)
            return previous, decay_sum, input_sum, param_sum

        totals = lax.fori_loop(
            0, rows // 16, terms_tile, (entering[pl.ds(j, 1), :], *totals)
        )[1:]

        def dot_t(left, right):
            return lax.dot_general(left, right, (((1,), (1,)), ((), ())), preferred_element_type=f32)

        grad_conv[j] = (
            grad_conv[j] + dot_t(decay_low[j], decay_blocks[...]) + dot_t(input_low[j], input_blocks[...])
        )
        return totals

    decay_sum, input_sum, param_sum = lax.fori_loop(0, CHIPS, terms_block, (nothing,) * 3)

    to_sibling = remote(grad_conv.at[:, pl.ds(0, 8)], sibling_heads, send.at[7], recv.at[7], me + 1 - 2 * c)
    to_below = remote(grad_conv.at[0, pl.ds(0, 8)], above_head, send.at[8], recv.at[8], me - 7)
    from_above = remote(grad_conv.at[0, pl.ds(0, 8)], above_head, send.at[8], recv.at[8], me + 7)
    to_sibling.start()

    @pl.when((c == 0) & (z > 0))
    def send_below():
        to_below.start()

    to_sibling.wait()

    @pl.when((c == 0) & (z > 0))
    def sent_below():
        to_below.wait_send()

    @pl.when((c == 1) & (z < planes - 1))
    def had_above():
        from_above.wait_recv()

    @pl.when(c == 0)
    def ahead_zero():
        for j in range(CHIPS):
            ahead[j] = sibling_heads[j]

    @pl.when(c == 1)
    def ahead_one():
        for j in range(CHIPS - 1):
            ahead[j] = sibling_heads[j + 1]

        @pl.when(z < planes - 1)
        def ahead_above():
            ahead[CHIPS - 1] = above_head[...]

        @pl.when(z == planes - 1)
        def ahead_none():
            ahead[CHIPS - 1] = nothing

    def conv_block(j, totals):
        def conv_pair(i, now, later, keep, later_keep, outs, earlier, given, totals):
            out = vectors[0:1, :] * now
            new_totals = [totals[0] + now * given]
            for k in range(1, CW):
                masked = now * keep[:, k : k + 1]
                out = out + vectors[k : k + 1, :] * shift_up(
                    masked, later * later_keep[:, k : k + 1], k, row
                )
                new_totals.append(totals[k] + masked * shift_down(earlier, given, k, row))
            new_totals.append(totals[CW] + now)
            outs.append(out)
            return tuple(new_totals)

        def conv_tile(i, carry, last):
            earlier, totals = carry
            inputs = conv_input[j, sixteen(i), :].astype(f32)
            first, second = grad_conv[j, eight(2 * i), :], grad_conv[j, eight(2 * i + 1), :]
            first_keep, second_keep = masks[j, eight(2 * i), :], masks[j, eight(2 * i + 1), :]
            if last:
                third, third_keep = ahead[j], after_masks[j]
            else:
                third, third_keep = grad_conv[j, eight(2 * i + 2), :], masks[j, eight(2 * i + 2), :]
            outs = []
            totals = conv_pair(i, first, second, first_keep, second_keep, outs, earlier, inputs[:8], totals)
            totals = conv_pair(i, second, third, second_keep, third_keep, outs, inputs[:8], inputs[8:], totals)
            in_low[j, sixteen(i), channels : 2 * channels] = jnp.concatenate(outs, axis=0).astype(bf16)
            return inputs[8:], totals

        carry = lax.fori_loop(
            0, rows // 16 - 1, lambda i, carry: conv_tile(i, carry, False), (halo[j], totals)
        )
        return conv_tile(rows // 16 - 1, carry, True)[1]

    totals = lax.fori_loop(0, CHIPS, conv_block, (nothing,) * (CW + 1))
    for k, total in enumerate((*totals, decay_sum, input_sum, param_sum)):
        sums[k : k + 1, :] = jnp.sum(total, axis=0, keepdims=True)
    for copy in downs:
        copy.wait()


def recurrence_back(
    grad_mixed,
    gate_pre,
    conv_input,
    conv_out,
    decay_pre,
    input_pre,
    states,
    entering,
    halo,
    masks,
    after_masks,
    vectors,
    decay_blocks,
    input_blocks,
    down_parts,
    piece,
    collective_id,
):
    planes = lax.axis_size("seq") // 8
    cube = conv_input.shape
    blocks, rows, channels = cube
    f32, bf16 = jnp.float32, jnp.bfloat16
    return pl.pallas_call(
        functools.partial(recurrence_back_kernel, planes),
        out_shape=[
            jax.ShapeDtypeStruct((CHIPS, rows, 2 * channels), bf16),
            jax.ShapeDtypeStruct(cube, bf16),
            jax.ShapeDtypeStruct(cube, bf16),
            jax.ShapeDtypeStruct((CW + 4, channels), f32),
            jax.ShapeDtypeStruct((CHIPS - 1,) + down_parts.shape[1:], bf16),
            jax.ShapeDtypeStruct(piece.shape, bf16),
        ],
        in_specs=[VMEM] * 14 + [ANY] * 2,
        out_specs=[VMEM] * 4 + [ANY] * 2,
        scratch_shapes=[
            pltpu.VMEM(cube, f32),
            pltpu.VMEM(cube, f32),
            pltpu.VMEM(cube, f32),
            pltpu.VMEM((CHIPS, 8, channels), f32),
            pltpu.VMEM((8, channels), f32),
            pltpu.VMEM((CHIPS, 8, channels), f32),
            pltpu.VMEM((2 * planes, 2 * CHIPS, channels), f32),
            pltpu.VMEM((8 * planes, channels), f32),
            pltpu.VMEM((CHIPS, channels), f32),
            pltpu.SemaphoreType.DMA((15,)),
            pltpu.SemaphoreType.DMA((15,)),
            pltpu.SemaphoreType.DMA,
        ],
        compiler_params=comm_params(collective_id, 52),
        name="recurrence_back",
    )(
        grad_mixed,
        gate_pre,
        conv_input,
        conv_out,
        decay_pre,
        input_pre,
        states,
        entering,
        halo,
        masks,
        after_masks,
        vectors,
        decay_blocks,
        input_blocks,
        down_parts,
        piece,
    )


def regrouped_kernel(back, devices, *refs):
    count = len(refs) // 2
    for source, target in zip(refs[:count], refs[count:]):
        step = source.shape[1] // devices
        for k in range(devices // 2):
            for e in range(2):
                split, joined = (2 * k + e) * step, (devices // 2 * e + k) * step
                start, end = (joined, split) if back else (split, joined)
                target[:, end : end + step] = source[:, start : start + step].astype(target.dtype)


def regrouped_columns(arrays, dtypes, back):
    devices = lax.axis_size("seq")
    return pl.pallas_call(
        functools.partial(regrouped_kernel, back, devices),
        out_shape=[jax.ShapeDtypeStruct(a.shape, dtype) for a, dtype in zip(arrays, dtypes)],
        in_specs=[VMEM] * len(arrays),
        out_specs=[VMEM] * len(arrays),
        compiler_params=pltpu.CompilerParams(vmem_limit_bytes=24 * 2**20),
        name="regrouped_columns",
    )(*arrays)


def to_chips_kernel(planes, pairs, *refs):
    ins, outs = refs[: len(pairs)], refs[len(pairs) :]
    for source, targets in zip(ins, pairs):
        width = source.shape[1] // (planes * 8)
        for z in range(planes):
            for p in range(CHIPS):
                for c in range(2):
                    k, at = targets[c]
                    start = ((z * CHIPS + p) * 2 + c) * width
                    outs[k][p, :, at + z * width : at + (z + 1) * width] = source[:, start : start + width]


def to_chips(weights, pairs, widths):
    planes = lax.axis_size("seq") // 8
    return pl.pallas_call(
        functools.partial(to_chips_kernel, planes, pairs),
        out_shape=[
            jax.ShapeDtypeStruct((CHIPS, weights[0].shape[0], width), weights[0].dtype) for width in widths
        ],
        in_specs=[VMEM] * len(weights),
        out_specs=[VMEM] * len(widths),
        name="to_chips",
    )(*weights)


def from_chips_kernel(planes, pairs, *refs):
    outs, ins = refs[-len(pairs) :], refs[: -len(pairs)]
    for target, sources in zip(outs, pairs):
        width = target.shape[1] // (planes * 8)
        for z in range(planes):
            for p in range(CHIPS):
                for c in range(2):
                    k, at = sources[c]
                    start = ((z * CHIPS + p) * 2 + c) * width
                    target[:, start : start + width] = ins[k][
                        p, :, at + z * width : at + (z + 1) * width
                    ].astype(jnp.float32)


def from_chips(parts, pairs, widths):
    planes = lax.axis_size("seq") // 8
    return pl.pallas_call(
        functools.partial(from_chips_kernel, planes, pairs),
        out_shape=[jax.ShapeDtypeStruct((parts[0].shape[1], width), jnp.float32) for width in widths],
        in_specs=[VMEM] * len(parts),
        out_specs=[VMEM] * len(widths),
        compiler_params=pltpu.CompilerParams(vmem_limit_bytes=32 * 2**20),
        name="from_chips",
    )(*parts)


def regrouped(values, axis, n):
    shape = values.shape
    split = shape[:axis] + (n // 2, 2, shape[axis] // n) + shape[axis + 1 :]
    return jnp.moveaxis(values.reshape(split), axis + 1, axis).reshape(shape)


def behind(value, *earlier):
    return lax.optimization_barrier((value, *earlier))[0]


def plane_body(
    tokens,
    starts,
    cotangent,
    norm_gain,
    gate_branch,
    input_branch,
    conv_weight,
    conv_bias,
    decay_gate,
    decay_bias,
    input_gate,
    input_bias,
    decay_param,
    out_proj,
    mlp_gain,
    mlp_gate,
    mlp_up,
    mlp_down,
):
    f32, bf16 = jnp.float32, jnp.bfloat16
    n = lax.axis_size("seq")
    planes = n // 8
    me, z, p, c, x, y = place()
    groups = column_groups(n)
    rows, width = tokens.shape
    rows_d, lru_width = gate_branch.shape
    head = decay_gate.shape[1]
    rows_r, rows_f = out_proj.shape[0], mlp_down.shape[0]
    channels = lru_width // CHIPS
    units = mlp_gate.shape[1] // CHIPS
    half_units = units // 2

    def column_gather(block):
        return lax.all_gather(block, "seq", axis=0, tiled=True, axis_index_groups=groups)

    def line_sum(parts):
        return lax.psum_scatter(
            parts, "seq", scatter_dimension=0, tiled=True, axis_index_groups=line_groups(n)
        )

    sibling = [(d, d + 1 - 2 * (d % 2)) for d in range(n)]

    def halves(values, axis):
        half = values.shape[axis] // 2
        return (
            lax.dynamic_slice_in_dim(values, c * half, half, axis),
            lax.dynamic_slice_in_dim(values, (1 - c) * half, half, axis),
        )

    def exchanged(values):
        return lax.ppermute(values, "seq", sibling)

    def product(left, right):
        return jnp.dot(left, right, preferred_element_type=f32)

    def product_t(left, right):
        return jnp.einsum("tk,nk->tn", left, right, preferred_element_type=f32)

    def weight_grad(left, right):
        return jnp.einsum("ta,tb->ab", left, right, preferred_element_type=f32)

    lanes = 128

    def row(values):
        return jnp.pad(values.astype(f32), (0, lanes - values.shape[0]))[None]

    small = jnp.concatenate(
        [
            row(norm_gain),
            row(mlp_gain),
            starts.astype(f32).reshape(rows // lanes, lanes),
            *[row(conv_weight[k]) for k in range(CW)],
            row(conv_bias),
            row(decay_bias),
            row(input_bias),
            row(decay_param),
            jnp.zeros((4, lanes), f32),
        ],
        axis=0,
    )
    half = channels // 2
    in_pairs = (((0, 0), (0, half)), ((0, channels), (0, channels + half)))
    (weights_in,) = to_chips([gate_branch, input_branch], in_pairs, [2 * channels])
    swapped_in, small = opening(weights_in, small, 1)
    small = small.transpose(1, 0, 2, 3)
    flags = 2 + rows // lanes
    gain_one = regrouped(small[:, :, 0, :rows_d].reshape(width), 0, n)
    gain_two = regrouped(small[:, :, 1, :rows_d].reshape(width), 0, n)
    all_flags = small[:, :, 2:flags].reshape(n * rows)
    vectors = lax.dynamic_slice_in_dim(
        small.reshape(planes, CHIPS, 2, 16, lanes), p, 1, axis=1
    )[:, 0, :, flags : flags + CW + 4, :rows_r]
    vectors = vectors.transpose(2, 1, 0, 3).reshape(CW + 4, channels)
    param = vectors[CW + 3]
    vectors = vectors.at[CW + 3].set(-rate_scale * jax.nn.softplus(param))

    running = jnp.ones((n * rows,), f32)
    masks_all = [running]
    for offset in range(1, CW):
        earlier = jnp.concatenate([jnp.zeros((offset - 1,), f32), all_flags[: n * rows - (offset - 1)]])
        running = running * (1.0 - earlier)
        masks_all.append(running)
    masks_all = jnp.stack(masks_all).reshape(CW, planes, CHIPS, 2, rows)

    def own_blocks(values):
        return lax.dynamic_slice(
            values,
            (0, z, 0, c, 0),
            (values.shape[0], 1, CHIPS, 1, values.shape[4]),
        )[:, 0, :, 0]

    after_masks = masks_all[..., :8].reshape(CW, n, 8)
    after_masks = jnp.concatenate([after_masks[:, 1:], jnp.zeros((CW, 1, 8), f32)], axis=1)
    after_masks = own_blocks(after_masks.reshape(CW, planes, CHIPS, 2, 8)).transpose(1, 2, 0)
    masks_all = jnp.concatenate([all_flags.reshape(1, planes, CHIPS, 2, rows), masks_all[1:]], axis=0)
    masks = own_blocks(masks_all).transpose(1, 2, 0)

    mlp_pairs = (((0, 0), (1, 0)), ((0, half_units), (1, half_units)))
    mlp_pieces = to_chips([mlp_gate, mlp_up], mlp_pairs, [2 * half_units] * 2)
    whole_in = column_gather(swapped_in.reshape(CHIPS * rows_d, 2 * channels))
    tokens, cot, out_proj, mlp_down = regrouped_columns(
        [tokens, cotangent, out_proj, mlp_down], [bf16] * 4, False
    )
    rec_rows = column_gather(jnp.concatenate([out_proj, decay_gate, input_gate], axis=1))
    whole_out, gates = rec_rows[:, :width], rec_rows[:, width:]
    gates = gates.reshape(2, planes, rows_r, 2, 2, rows_r)
    diagonal = jnp.eye(planes, dtype=bf16)[None, :, None, None, :, None]
    decay_blocks, input_blocks = (
        (gates[:, :, :, k, :, None, :] * diagonal).reshape(channels, channels) for k in range(2)
    )

    normed = rms_norm(tokens.astype(f32), gain_one).astype(bf16)
    normed_all = plane_gather(normed, 3).reshape(CHIPS * rows, width)
    swapped_mlp = plane_swap(behind(tuple(mlp_pieces), normed_all, decay_blocks, input_blocks), 4)
    whole_down = column_gather(mlp_down)
    whole_mlp = [column_gather(part.reshape(CHIPS * rows_d, 2 * half_units)) for part in swapped_mlp]

    gate_pre = product(normed_all, whole_in[:, :channels])
    cube = (CHIPS, rows, channels)
    gate_pre = gate_pre.reshape(cube)
    conv_input = product(normed_all, whole_in[:, channels:]).astype(bf16).reshape(cube)
    conv_out, conv_low, decay_pre, input_pre, states, mixed, entering, halo, cot_all = recurrence(
        gate_pre, conv_input, masks, vectors, decay_blocks, input_blocks, cot, 6
    )
    cot_all = cot_all.reshape(CHIPS * rows, width)
    mixed = mixed.reshape(CHIPS * rows, channels)
    branch_parts = product(mixed, whole_out).reshape(CHIPS, rows, width)
    middle, two_all = middle_of(branch_parts, tokens, gain_two, 7)
    two_all = two_all.reshape(CHIPS * rows, width)

    cot_other = exchanged(cot_all)
    two_own, two_other = halves(two_all, 1)
    two_other = exchanged(two_other)
    grad_hidden = product_t(cot_all, whole_down)
    hiddens, grads_low, piece_grads = [], [], []
    two_now = two_all
    for k in range(2):
        weights = whole_mlp[k]
        gate_mlp = product(two_now, weights[:, :half_units])
        up_mlp = product(two_now, weights[:, half_units:])
        hidden, pull_act = jax.vjp(mlp_act, gate_mlp, up_mlp)
        hiddens.append(hidden.astype(bf16))
        grad_gate, grad_up = pull_act(grad_hidden[:, k * half_units : (k + 1) * half_units])
        low = jnp.concatenate([grad_gate.astype(bf16), grad_up.astype(bf16)], axis=1)
        grads_low.append(low)
        piece_grads.append((weight_grad(two_own, low) + weight_grad(two_other, exchanged(low))).astype(bf16))
        two_now = behind(two_now, piece_grads[-1])
    hidden = jnp.concatenate(hiddens, axis=1)
    two_parts = product_t(grads_low[0], whole_mlp[0]) + product_t(grads_low[1], whole_mlp[1])
    two_parts = behind(two_parts.astype(bf16), piece_grads[1])
    piece_grads = [line_sum(part) for part in piece_grads]
    grad_middle, grad_mlp_gain, grad_branch, down_grad, down_parts = grads_of_middle(
        two_parts.reshape(CHIPS, rows, width), middle, cot, gain_two, hidden, whole_down, cot_all, cot_other, 9
    )
    grad_mlp_down = line_sum(down_grad)
    grad_branch = grad_branch.reshape(CHIPS * rows, width)

    mixed_own, mixed_other = halves(mixed, 1)
    out_grad = weight_grad(mixed_own, grad_branch) + weight_grad(
        exchanged(mixed_other), exchanged(grad_branch)
    )
    out_grad = out_grad.astype(bf16)
    grad_out_proj = line_sum(out_grad)
    grad_mixed = behind(product_t(grad_branch, whole_out), out_grad)
    in_low, grad_decay_low, grad_input_low, sums, down_others, swapped_grads = recurrence_back(
        grad_mixed.reshape(cube),
        gate_pre,
        conv_input,
        conv_out,
        decay_pre,
        input_pre,
        states,
        entering,
        halo,
        masks,
        after_masks,
        vectors,
        decay_blocks,
        input_blocks,
        down_parts,
        piece_grads[0].reshape(CHIPS, rows_d, 2 * half_units),
        12,
    )
    down_sum = lax.dynamic_index_in_dim(down_parts, p, 0, False).astype(f32) + jnp.sum(
        down_others.astype(f32), axis=0
    )
    block_out = middle + down_sum
    sums = sums.at[CW + 3].multiply(-rate_scale * jax.nn.sigmoid(param))
    in_low = in_low.reshape(CHIPS * rows, 2 * channels)
    flat = (CHIPS * rows, channels)
    conv_low, grad_decay_low, grad_input_low = (
        a.reshape(flat) for a in (conv_low, grad_decay_low, grad_input_low)
    )

    normed_own, normed_other = halves(normed_all, 1)
    in_grads = weight_grad(normed_own, in_low) + weight_grad(exchanged(normed_other), exchanged(in_low))
    in_total = in_grads.astype(bf16)
    in_grads = line_sum(in_total)
    normed_parts = product_t(in_low, whole_in).astype(bf16).reshape(CHIPS, rows, width)
    normed_parts = behind(normed_parts, in_total)
    convs, decays, inputs = (
        (own, exchanged(other))
        for own, other in (halves(conv_low, 1), (grad_decay_low, grad_decay_low), (grad_input_low, grad_input_low))
    )
    vector_parts = sums.reshape(CW + 4, 2, planes, rows_r).transpose(2, 1, 0, 3)
    vector_parts = jnp.pad(vector_parts, ((0, 0), (0, 0), (0, 0), (0, lanes - rows_r)))
    here = (jnp.arange(CHIPS) == p).astype(f32)[None, :, None, None, None]
    vector_parts = (vector_parts[:, None] * here).reshape(planes, 8, CW + 4, lanes)
    gain_parts = grad_mlp_gain.reshape(2, planes, CHIPS, 1, rows_d).transpose(1, 2, 0, 3, 4)
    gain_parts = jnp.pad(
        gain_parts.reshape(planes, 8, 1, rows_d), ((0, 0), (0, 0), (0, 7), (0, lanes - rows_d))
    )
    grad_tokens, small_grads, gate_grads, swapped_late = closing(
        normed_parts,
        tokens,
        gain_one,
        grad_middle,
        jnp.concatenate([vector_parts, gain_parts], axis=2),
        convs,
        decays,
        inputs,
        piece_grads[1].reshape(CHIPS, rows_d, 2 * half_units),
        head,
        13,
    )
    grad_mlp_gate, grad_mlp_up = from_chips(
        [swapped_grads, swapped_late], mlp_pairs, [mlp_gate.shape[1]] * 2
    )
    block_out, grad_out_proj, grad_mlp_down = regrouped_columns(
        behind((block_out, grad_out_proj, grad_mlp_down), grad_tokens), [bf16, f32, f32], True
    )
    in_out = plane_swap([in_grads.reshape(CHIPS, rows_d, 2 * channels)], 16)
    grad_gate_branch, grad_input_branch = from_chips(in_out, in_pairs, [lru_width] * 2)
    vector_grads = small_grads[: CW + 4, :rows_r]
    return (
        block_out,
        grad_tokens,
        small_grads[CW + 12, :rows_d],
        grad_gate_branch,
        grad_input_branch,
        vector_grads[:CW],
        vector_grads[CW],
        gate_grads[:, :head],
        vector_grads[CW + 1],
        gate_grads[:, head:],
        vector_grads[CW + 2],
        vector_grads[CW + 3],
        grad_out_proj,
        small_grads[CW + 4, :rows_d],
        grad_mlp_gate,
        grad_mlp_up,
        grad_mlp_down,
    )


def solution(mesh):
    in_specs = (
        P("seq", None),
        P("seq"),
        P("seq", None),
        P("seq"),
        P("seq", None),
        P("seq", None),
        P(None, "seq"),
        P("seq"),
        P("seq", None),
        P("seq"),
        P("seq", None),
        P("seq"),
        P("seq"),
        P("seq", None),
        P("seq"),
        P("seq", None),
        P("seq", None),
        P("seq", None),
    )
    out_specs = (
        P("seq", None),
        P("seq", None),
        P("seq"),
        P("seq", None),
        P("seq", None),
        P(None, "seq"),
        P("seq"),
        P("seq", None),
        P("seq"),
        P("seq", None),
        P("seq"),
        P("seq"),
        P("seq", None),
        P("seq"),
        P("seq", None),
        P("seq", None),
        P("seq", None),
    )
    body = plane_body if mesh.shape["seq"] == 2 * H else token_split_body
    return jax.shard_map(body, mesh=mesh, in_specs=in_specs, out_specs=out_specs, check_vma=False)
```

```python
import functools

import jax
import jax.numpy as jnp
from jax import lax
from jax.experimental import pallas as pl
from jax.experimental.pallas import tpu as pltpu
from jax.sharding import PartitionSpec as P

H = 16
CW = 4


epsilon = 1e-06
rate_scale = 8.0


def passed_along(block, axis, distance):
    devices = range(lax.axis_size(axis))
    route = [(i - distance, i) for i in devices if i - distance in devices]
    return lax.ppermute(block, axis, route)


def prefix(value, axis, combine, identity, reverse):
    peers, place = (lax.axis_size(axis), lax.axis_index(axis))
    everything = jax.tree.map(lambda part: lax.all_gather(part, axis), value)
    start = jax.tree.map(
        lambda part, zero: jnp.broadcast_to(jnp.asarray(zero, part.dtype), part.shape),
        value,
        identity,
    )

    def hop(k, before):
        at = peers - 1 - k if reverse else k
        reached = at > place if reverse else at < place
        new = combine(before, jax.tree.map(lambda part: part[at], everything))
        return jax.tree.map(lambda a, b: jnp.where(reached, a, b), new, before)

    return lax.fori_loop(0, peers, hop, start)


def gelu_tanh(values):
    return jax.nn.gelu(values, approximate=True)


def rms_norm(values, scales):
    return values * lax.rsqrt(jnp.mean(values * values, axis=-1, keepdims=True) + epsilon) * scales


def combine(earlier_part, later_part):
    return (earlier_part[0] * later_part[0], later_part[0] * earlier_part[1] + later_part[1])


def heads_product(values, weight):
    row_count, lru_width = values.shape
    shaped = values.reshape(row_count, H, lru_width // H)
    blocks = weight.reshape(H, lru_width // H, lru_width // H)
    return jnp.einsum("thi,hij->thj", shaped, blocks, preferred_element_type=jnp.float32).reshape(
        row_count, lru_width
    )


def heads_back(grads_low, weight):
    row_count, lru_width = grads_low.shape
    shaped = grads_low.reshape(row_count, H, lru_width // H)
    blocks = weight.reshape(H, lru_width // H, lru_width // H)
    return jnp.einsum("thj,hij->thi", shaped, blocks, preferred_element_type=jnp.float32).reshape(
        row_count, lru_width
    )


def heads_grad(values, grads_low):
    row_count, lru_width = values.shape
    left_side = values.reshape(row_count, H, lru_width // H)
    right_side = grads_low.reshape(row_count, H, lru_width // H)
    return jnp.einsum(
        "thi,thj->hij", left_side, right_side, preferred_element_type=jnp.float32
    ).reshape(lru_width, lru_width // H)


def lru_terms(decay_pre, input_pre, conv_out, decay_param, flag_rows):
    log_decay = -rate_scale * jax.nn.sigmoid(decay_pre) * jax.nn.softplus(decay_param)
    keep_rows = 1.0 - flag_rows[:, None]
    coefficient = jnp.exp(log_decay) * keep_rows
    scale_in = flag_rows[:, None] + keep_rows * jnp.sqrt(-jnp.expm1(2.0 * log_decay))
    drive_term = scale_in * jax.nn.sigmoid(input_pre) * conv_out
    return (coefficient, drive_term)


def build_masks(flag_rows):
    row_count = flag_rows.shape[0]
    running = jnp.ones((row_count,), jnp.float32)
    masks = [running]
    for offset in range(1, CW):
        earlier_flags = jnp.concatenate(
            [jnp.zeros((offset - 1,), jnp.float32), flag_rows[: row_count - (offset - 1)]]
        )
        running = running * (1.0 - earlier_flags)
        masks.append(running)
    return masks


def send_mask(flag_rows):
    tail_keep = 1.0 - flag_rows[flag_rows.shape[0] - (CW - 1) :]
    after_rows = jnp.cumprod(tail_keep[::-1])[::-1]
    return jnp.concatenate([after_rows[1:], jnp.ones((1,), jnp.float32)])


def conv_local(padded, weight, bias, masks):
    row_count = masks[0].shape[0]
    conv_total = bias + jnp.zeros((row_count, padded.shape[1]), jnp.float32)
    for offset in range(CW):
        lead = CW - 1 - offset
        conv_total = conv_total + weight[offset] * (
            padded[lead : lead + row_count] * masks[offset][:, None]
        )
    return conv_total


def mlp_act(gate_values, up_values):
    return gelu_tanh(gate_values) * up_values


def token_split_body(
    tokens,
    starts,
    cotangent,
    norm_gain,
    gate_branch,
    input_branch,
    conv_weight,
    conv_bias,
    decay_gate,
    decay_bias,
    input_gate,
    input_bias,
    decay_param,
    out_proj,
    mlp_gain,
    mlp_gate,
    mlp_up,
    mlp_down,
):
    (
        whole_norm_gain,
        whole_gate_branch,
        whole_input_branch,
        whole_conv_weight,
        whole_conv_bias,
        whole_decay_gate,
        whole_decay_bias,
        whole_input_gate,
        whole_input_bias,
        whole_decay_param,
        whole_out_proj,
    ) = (
        lax.all_gather(norm_gain, "seq", axis=0, tiled=True),
        lax.all_gather(gate_branch, "seq", axis=0, tiled=True),
        lax.all_gather(input_branch, "seq", axis=0, tiled=True),
        lax.all_gather(conv_weight, "seq", axis=1, tiled=True),
        lax.all_gather(conv_bias, "seq", axis=0, tiled=True),
        lax.all_gather(decay_gate, "seq", axis=0, tiled=True),
        lax.all_gather(decay_bias, "seq", axis=0, tiled=True),
        lax.all_gather(input_gate, "seq", axis=0, tiled=True),
        lax.all_gather(input_bias, "seq", axis=0, tiled=True),
        lax.all_gather(decay_param, "seq", axis=0, tiled=True),
        lax.all_gather(out_proj, "seq", axis=0, tiled=True),
    )
    flag_rows = starts.astype(jnp.float32)
    row_count = tokens.shape[0]
    values = tokens.astype(jnp.float32)
    normed = rms_norm(values, whole_norm_gain.astype(jnp.float32)).astype(jnp.bfloat16)
    gate_pre = jnp.dot(normed, whole_gate_branch, preferred_element_type=jnp.float32)
    gate_act = gelu_tanh(gate_pre)
    conv_input = jnp.dot(normed, whole_input_branch, preferred_element_type=jnp.float32).astype(
        jnp.bfloat16
    )
    lru_width = conv_input.shape[1]
    alive_rows = send_mask(flag_rows)
    masks = build_masks(flag_rows)
    outgoing = conv_input[row_count - (CW - 1) :] * alive_rows[:, None].astype(jnp.bfloat16)
    incoming = passed_along(outgoing, "seq", 1)
    padded = jnp.concatenate([incoming, conv_input], axis=0).astype(jnp.float32)
    conv_out = conv_local(
        padded, whole_conv_weight.astype(jnp.float32), whole_conv_bias.astype(jnp.float32), masks
    )
    conv_low = conv_out.astype(jnp.bfloat16)
    decay_pre = heads_product(conv_low, whole_decay_gate) + whole_decay_bias.astype(jnp.float32)
    input_pre = heads_product(conv_low, whole_input_gate) + whole_input_bias.astype(jnp.float32)
    param_full = whole_decay_param.astype(jnp.float32)
    coefficient, drive_term = lru_terms(decay_pre, input_pre, conv_out, param_full, flag_rows)
    cumulative, local_state = lax.associative_scan(combine, (coefficient, drive_term), axis=0)
    entering = prefix(
        (cumulative[-1], local_state[-1]),
        "seq",
        combine,
        (jnp.ones_like(cumulative[-1]), jnp.zeros_like(local_state[-1])),
        False,
    )
    incoming_state = entering[1]
    states = local_state + cumulative * incoming_state[None, :]
    mixed_rows = (states * gate_act).astype(jnp.bfloat16)
    middle = values + jnp.dot(mixed_rows, whole_out_proj, preferred_element_type=jnp.float32)
    whole_mlp_gain, whole_mlp_gate, whole_mlp_up, whole_mlp_down = (
        lax.all_gather(mlp_gain, "seq", axis=0, tiled=True),
        lax.all_gather(mlp_gate, "seq", axis=0, tiled=True),
        lax.all_gather(mlp_up, "seq", axis=0, tiled=True),
        lax.all_gather(mlp_down, "seq", axis=0, tiled=True),
    )
    gain_two = whole_mlp_gain.astype(jnp.float32)
    normed_two = rms_norm(middle, gain_two).astype(jnp.bfloat16)
    gate_mlp = jnp.dot(normed_two, whole_mlp_gate, preferred_element_type=jnp.float32)
    up_mlp = jnp.dot(normed_two, whole_mlp_up, preferred_element_type=jnp.float32)
    hidden = mlp_act(gate_mlp, up_mlp).astype(jnp.bfloat16)
    result = middle + jnp.dot(hidden, whole_mlp_down, preferred_element_type=jnp.float32)
    block_out = result.astype(jnp.bfloat16)
    back_mlp_gain, back_mlp_gate, back_mlp_up, back_mlp_down = (
        lax.all_gather(mlp_gain, "seq", axis=0, tiled=True),
        lax.all_gather(mlp_gate, "seq", axis=0, tiled=True),
        lax.all_gather(mlp_up, "seq", axis=0, tiled=True),
        lax.all_gather(mlp_down, "seq", axis=0, tiled=True),
    )
    grad_mlp_down = jnp.einsum("tf,td->fd", hidden, cotangent, preferred_element_type=jnp.float32)
    grad_hidden = jnp.einsum(
        "td,fd->tf", cotangent, back_mlp_down, preferred_element_type=jnp.float32
    )
    unused_act, pull_act = jax.vjp(mlp_act, gate_mlp, up_mlp)
    grad_gate_full, grad_up_full = pull_act(grad_hidden)
    grad_gate_low = grad_gate_full.astype(jnp.bfloat16)
    grad_up_low = grad_up_full.astype(jnp.bfloat16)
    grad_mlp_gate = jnp.einsum(
        "td,tf->df", normed_two, grad_gate_low, preferred_element_type=jnp.float32
    )
    grad_mlp_up = jnp.einsum(
        "td,tf->df", normed_two, grad_up_low, preferred_element_type=jnp.float32
    )
    grad_normed_two = jnp.einsum(
        "tf,df->td", grad_gate_low, back_mlp_gate, preferred_element_type=jnp.float32
    ) + jnp.einsum("tf,df->td", grad_up_low, back_mlp_up, preferred_element_type=jnp.float32)
    unused_norm, pull_norm = jax.vjp(rms_norm, middle, back_mlp_gain.astype(jnp.float32))
    grad_middle_norm, grad_mlp_gain = pull_norm(grad_normed_two)
    mlp_sums = (
        lax.psum_scatter(grad_mlp_gain, "seq", scatter_dimension=0, tiled=True),
        lax.psum_scatter(grad_mlp_gate, "seq", scatter_dimension=0, tiled=True),
        lax.psum_scatter(grad_mlp_up, "seq", scatter_dimension=0, tiled=True),
        lax.psum_scatter(grad_mlp_down, "seq", scatter_dimension=0, tiled=True),
    )
    grad_middle = cotangent.astype(jnp.float32) + grad_middle_norm
    grad_branch = grad_middle.astype(jnp.bfloat16)
    (
        back_norm_gain,
        back_gate_branch,
        back_input_branch,
        back_conv_weight,
        back_conv_bias,
        back_decay_gate,
        back_decay_bias,
        back_input_gate,
        back_input_bias,
        back_decay_param,
        back_out_proj,
    ) = (
        lax.all_gather(norm_gain, "seq", axis=0, tiled=True),
        lax.all_gather(gate_branch, "seq", axis=0, tiled=True),
        lax.all_gather(input_branch, "seq", axis=0, tiled=True),
        lax.all_gather(conv_weight, "seq", axis=1, tiled=True),
        lax.all_gather(conv_bias, "seq", axis=0, tiled=True),
        lax.all_gather(decay_gate, "seq", axis=0, tiled=True),
        lax.all_gather(decay_bias, "seq", axis=0, tiled=True),
        lax.all_gather(input_gate, "seq", axis=0, tiled=True),
        lax.all_gather(input_bias, "seq", axis=0, tiled=True),
        lax.all_gather(decay_param, "seq", axis=0, tiled=True),
        lax.all_gather(out_proj, "seq", axis=0, tiled=True),
    )
    grad_out_proj = jnp.einsum(
        "tr,td->rd", mixed_rows, grad_branch, preferred_element_type=jnp.float32
    )
    grad_mixed = jnp.einsum(
        "td,rd->tr", grad_branch, back_out_proj, preferred_element_type=jnp.float32
    )
    grad_states = grad_mixed * gate_act
    unused_gelu, pull_gelu = jax.vjp(gelu_tanh, gate_pre)
    grad_gate_pre = pull_gelu(grad_mixed * states)[0].astype(jnp.bfloat16)
    shifted_coef = jnp.concatenate([coefficient[1:], jnp.ones((1, lru_width), jnp.float32)], axis=0)
    back_cumulative, back_local = lax.associative_scan(
        combine, (shifted_coef[::-1], grad_states[::-1]), axis=0
    )
    back_cumulative = back_cumulative[::-1]
    back_local = back_local[::-1]
    leaving = prefix(
        (coefficient[0] * back_cumulative[0], coefficient[0] * back_local[0]),
        "seq",
        combine,
        (jnp.ones_like(back_local[0]), jnp.zeros_like(back_local[0])),
        True,
    )
    incoming_adjoint = leaving[1]
    adjoint = back_local + back_cumulative * incoming_adjoint[None, :]
    previous = jnp.concatenate([incoming_state[None, :], states[:-1]], axis=0)

    def terms_only(decay_values, input_values, conv_values, param_values):
        return lru_terms(decay_values, input_values, conv_values, param_values, flag_rows)

    unused_terms, pull_terms = jax.vjp(
        terms_only, decay_pre, input_pre, conv_out, back_decay_param.astype(jnp.float32)
    )
    grad_decay_full, grad_input_full, grad_conv_direct, grad_decay_param = pull_terms(
        (adjoint * previous, adjoint)
    )
    grad_decay_bias = jnp.sum(grad_decay_full, axis=0)
    grad_input_bias = jnp.sum(grad_input_full, axis=0)
    grad_decay_low = grad_decay_full.astype(jnp.bfloat16)
    grad_input_low = grad_input_full.astype(jnp.bfloat16)
    grad_decay_gate = heads_grad(conv_low, grad_decay_low)
    grad_input_gate = heads_grad(conv_low, grad_input_low)
    grad_conv_out = (
        grad_conv_direct
        + heads_back(grad_decay_low, back_decay_gate)
        + heads_back(grad_input_low, back_input_gate)
    )

    def conv_only(padded_values, weight_values, bias_values):
        return conv_local(padded_values, weight_values, bias_values, masks)

    unused_conv, pull_conv = jax.vjp(
        conv_only, padded, back_conv_weight.astype(jnp.float32), back_conv_bias.astype(jnp.float32)
    )
    grad_padded, grad_conv_weight, grad_conv_bias = pull_conv(grad_conv_out)
    returned_rows = passed_along(grad_padded[: CW - 1], "seq", -1)
    addition = jnp.concatenate(
        [
            jnp.zeros((row_count - (CW - 1), lru_width), jnp.float32),
            returned_rows * alive_rows[:, None],
        ],
        axis=0,
    )
    grad_conv_input = (grad_padded[CW - 1 :] + addition).astype(jnp.bfloat16)
    grad_input_branch = jnp.einsum(
        "td,tr->dr", normed, grad_conv_input, preferred_element_type=jnp.float32
    )
    grad_gate_branch = jnp.einsum(
        "td,tr->dr", normed, grad_gate_pre, preferred_element_type=jnp.float32
    )
    grad_normed = jnp.einsum(
        "tr,dr->td", grad_conv_input, back_input_branch, preferred_element_type=jnp.float32
    ) + jnp.einsum("tr,dr->td", grad_gate_pre, back_gate_branch, preferred_element_type=jnp.float32)
    unused_first, pull_first = jax.vjp(rms_norm, values, back_norm_gain.astype(jnp.float32))
    grad_values_norm, grad_norm_gain = pull_first(grad_normed)
    grad_tokens = grad_middle + grad_values_norm
    rec_sums = (
        lax.psum_scatter(grad_norm_gain, "seq", scatter_dimension=0, tiled=True),
        lax.psum_scatter(grad_gate_branch, "seq", scatter_dimension=0, tiled=True),
        lax.psum_scatter(grad_input_branch, "seq", scatter_dimension=0, tiled=True),
        lax.psum_scatter(grad_conv_weight, "seq", scatter_dimension=1, tiled=True),
        lax.psum_scatter(grad_conv_bias, "seq", scatter_dimension=0, tiled=True),
        lax.psum_scatter(grad_decay_gate, "seq", scatter_dimension=0, tiled=True),
        lax.psum_scatter(grad_decay_bias, "seq", scatter_dimension=0, tiled=True),
        lax.psum_scatter(grad_input_gate, "seq", scatter_dimension=0, tiled=True),
        lax.psum_scatter(grad_input_bias, "seq", scatter_dimension=0, tiled=True),
        lax.psum_scatter(grad_decay_param, "seq", scatter_dimension=0, tiled=True),
        lax.psum_scatter(grad_out_proj, "seq", scatter_dimension=0, tiled=True),
    )
    return (
        block_out,
        grad_tokens,
        rec_sums[0],
        rec_sums[1],
        rec_sums[2],
        rec_sums[3],
        rec_sums[4],
        rec_sums[5],
        rec_sums[6],
        rec_sums[7],
        rec_sums[8],
        rec_sums[9],
        rec_sums[10],
        mlp_sums[0],
        mlp_sums[1],
        mlp_sums[2],
        mlp_sums[3],
    )


CHIPS = 4
MESH = pl.DeviceIdType.MESH


def place():
    me = lax.axis_index("seq")
    core = lax.rem(me, 2)
    x = lax.rem(lax.div(me, 2), 2)
    y = lax.rem(lax.div(me, 4), 2)
    return me, lax.div(me, 8), 2 * y + x, core, x, y


def column_groups(n):
    return [[8 * z + 2 * p + c for c in range(2) for z in range(n // 8)] for p in range(CHIPS)]


def line_groups(n):
    return [[8 * z + r for z in range(n // 8)] for r in range(8)]


def greet(devices):
    barrier = pltpu.get_barrier_semaphore()
    for device in devices:
        pl.semaphore_signal(barrier, inc=1, device_id=(device,), device_id_type=MESH)
    pl.semaphore_wait(barrier, len(devices))


def remote(source, target, send_sem, recv_sem, device):
    return pltpu.make_async_remote_copy(
        src_ref=source,
        dst_ref=target,
        send_sem=send_sem,
        recv_sem=recv_sem,
        device_id=(device,),
        device_id_type=MESH,
    )


def comm_params(collective_id, vmem_mib=None):
    return pltpu.CompilerParams(
        collective_id=collective_id,
        has_side_effects=True,
        vmem_limit_bytes=None if vmem_mib is None else vmem_mib * 2**20,
    )


def lasting(microseconds):
    return pl.CostEstimate(
        flops=int(microseconds * 1e9), bytes_accessed=int(microseconds * 3e6), transcendentals=0
    )


ANY = pl.BlockSpec(memory_space=pl.ANY)
VMEM = pl.BlockSpec(memory_space=pltpu.VMEM)


def plane_neighbours():
    me, z, p, c, x, y = place()
    x_dev, y_dev = me + 2 - 4 * x, me + 4 - 8 * y
    return (x_dev, y_dev, y_dev + 2 - 4 * x), (p + 1 - 2 * x, p + 2 - 4 * y, 3 - p)


def gather_steps(source, whole, send, recv, local, first):
    me, z, p, c, x, y = place()
    (x_dev, y_dev, d_dev), (p_x, p_y, p_d) = plane_neighbours()
    half = source.shape[0] // 2

    def copy(k, source, target, device):
        return remote(source, target, send.at[first + k], recv.at[first + k], device)

    to_x, to_y = copy(0, source, whole.at[p], x_dev), copy(1, source, whole.at[p], y_dev)
    low, high = whole.at[p_x, pl.ds(0, half)], whole.at[p_y, pl.ds(half, half)]
    on_y, on_x = copy(2, low, low, y_dev), copy(3, high, high, x_dev)
    own = pltpu.make_async_copy(source, whole.at[p], local)

    def begin():
        to_x.start()
        to_y.start()
        own.start()

    def forward():
        to_x.wait_recv()
        on_y.start()
        to_y.wait_recv()
        on_x.start()

    def end():
        to_x.wait_send()
        to_y.wait_send()
        on_y.wait()
        on_x.wait()
        own.wait()

    return begin, forward, end


def sum_scratch(rows, columns, dtype):
    whole, part = pltpu.VMEM((rows, columns), dtype), pltpu.VMEM((rows // 2, columns), dtype)
    return [whole] * 3 + [part] * 4 + [pltpu.SemaphoreType.DMA((6,)), pltpu.SemaphoreType.DMA((6,)), pltpu.SemaphoreType.DMA((3,))]


def sum_steps(part, own, from_x, from_y, diag_x, diag_y, on_x, on_y, send, recv, local):
    me, z, p, c, x, y = place()
    (x_dev, y_dev, d_dev), (p_x, p_y, p_d) = plane_neighbours()
    half = part.shape[1] // 2
    low, high = pl.ds(0, half), pl.ds(half, half)
    copies = [
        remote(part.at[p_d, low], diag_x, send.at[0], recv.at[0], x_dev),
        remote(part.at[p_d, high], diag_y, send.at[1], recv.at[1], y_dev),
        remote(part.at[p_x, low], from_x.at[low], send.at[2], recv.at[2], x_dev),
        remote(part.at[p_y, high], from_y.at[high], send.at[3], recv.at[3], y_dev),
    ]
    locals_ = [
        pltpu.make_async_copy(part.at[p_y, low], on_y, local.at[0]),
        pltpu.make_async_copy(part.at[p_x, high], on_x, local.at[1]),
        pltpu.make_async_copy(part.at[p], own, local.at[2]),
    ]
    to_y = remote(on_y, from_y.at[low], send.at[4], recv.at[4], y_dev)
    to_x = remote(on_x, from_x.at[high], send.at[5], recv.at[5], x_dev)

    def add_into(target, addend):
        @pl.loop(0, half // 16)
        def add_rows(i):
            at = pl.ds(pl.multiple_of(i * 16, 16), 16)
            target[at, :] = (
                target[at, :].astype(jnp.float32) + addend[at, :].astype(jnp.float32)
            ).astype(target.dtype)

    def begin():
        for copy in copies + locals_:
            copy.start()

    def forward():
        locals_[0].wait()
        copies[0].wait_recv()
        add_into(on_y, diag_x)
        to_y.start()
        locals_[1].wait()
        copies[1].wait_recv()
        add_into(on_x, diag_y)
        to_x.start()

    def end():
        locals_[2].wait()
        copies[2].wait_recv()
        copies[3].wait_recv()
        to_y.wait()
        to_x.wait()
        for copy in copies:
            copy.wait_send()

    return begin, forward, end


def sixteen(i):
    return pl.ds(pl.multiple_of(i * 16, 16), 16)


def fetch_rows(rows_all, first, start, target, sems):
    count = sems.shape[0]
    rows = target.shape[0] // count
    return [
        pltpu.make_async_copy(
            rows_all.at[first + k, pl.ds(start, rows)], target.at[pl.ds(k * rows, rows)], sems.at[k]
        )
        for k in range(count)
    ]


def computed_scratch(rows, columns):
    f32, bf16 = jnp.float32, jnp.bfloat16
    whole, half = (rows, columns), (rows // 2, columns)
    shapes = [(whole, bf16)] * 3 + [(whole, f32)] + [(half, f32)] * 2 + [(whole, bf16)] * 2 + [(half, bf16)] * 2
    return [pltpu.VMEM(*shape) for shape in shapes] + [pltpu.SemaphoreType.DMA((6,))] * 2


def computed_sum(product, sent_d, sent_x, sent_y, own, kept_x, kept_y, from_x, from_y, diag_x, diag_y, send, recv):
    (x_dev, y_dev, d_dev), (p_x, p_y, p_d) = plane_neighbours()
    p = place()[2]
    rows, width = own.shape
    half = rows // 2
    low, high = pl.ds(0, half), pl.ds(half, half)
    tile = 512

    def into(chip, at, target, target_at):
        @pl.loop(0, width // tile)
        def product_tile(k):
            columns = pl.ds(pl.multiple_of(k * tile, tile), tile)
            target[target_at, columns] = product(chip, at, columns).astype(target.dtype)

    def copy(k, source, target, device):
        return remote(source, target, send.at[k], recv.at[k], device)

    first = [copy(0, sent_d.at[low], diag_x, x_dev), copy(1, sent_d.at[high], diag_y, y_dev)]
    second = [
        copy(2, sent_x.at[low], from_x.at[low], x_dev),
        copy(3, sent_y.at[high], from_y.at[high], y_dev),
    ]
    third = [
        copy(4, sent_y.at[low], from_y.at[low], y_dev),
        copy(5, sent_x.at[high], from_x.at[high], x_dev),
    ]
    everything = slice(None)

    def begin():
        into(p_d, everything, sent_d, everything)
        for sent in first:
            sent.start()
        into(p_x, low, sent_x, low)
        into(p_y, high, sent_y, high)
        for sent in second:
            sent.start()
        into(p_y, low, kept_y, everything)
        into(p_x, high, kept_x, everything)
        into(p, everything, own, everything)

    def add(target, start, kept, addend):
        @pl.loop(0, half // 16)
        def add_rows(i):
            here = sixteen(i)
            there = pl.ds(pl.multiple_of(start + i * 16, 16), 16)
            target[there, :] = (kept[here, :] + addend[here, :].astype(jnp.float32)).astype(target.dtype)

    def forward():
        first[0].wait_recv()
        add(sent_y, 0, kept_y, diag_x)
        third[0].start()
        first[1].wait_recv()
        add(sent_x, half, kept_x, diag_y)
        third[1].start()

    def end():
        for sent in first:
            sent.wait_send()
        for sent in second + third:
            sent.wait()

    return begin, forward, end


def middle_kernel(
    mixed, rows_all, tokens, gain, middle, whole, normed, out_here, send, recv, local, loads, *sums
):
    greet(plane_neighbours()[0][:2])
    f32, bf16 = jnp.float32, jnp.bfloat16
    fetched = fetch_rows(rows_all, 0, 0, out_here, loads)
    for copy in fetched:
        copy.start()
    for copy in fetched:
        copy.wait()

    def product(chip, at, columns):
        return jnp.dot(mixed[chip, at, :], out_here[:, columns], preferred_element_type=f32)

    for step in computed_sum(product, *sums):
        step()
    own, from_x, from_y = sums[3], sums[6], sums[7]

    @pl.loop(0, tokens.shape[0] // 16)
    def norm_rows(i):
        at = sixteen(i)
        values = tokens[at, :].astype(f32) + (
            own[at, :] + from_x[at, :].astype(f32) + from_y[at, :].astype(f32)
        )
        middle[at, :] = values
        inverse = lax.rsqrt(jnp.mean(values * values, axis=-1, keepdims=True) + epsilon)
        normed[at, :] = (values * inverse * gain[...]).astype(bf16)

    for step in gather_steps(normed, whole, send, recv, local, 0):
        step()


def middle_of(mixed, rows_all, tokens, gain, collective_id):
    rows, width = tokens.shape
    channels = mixed.shape[2]
    f32, bf16 = jnp.float32, jnp.bfloat16
    return pl.pallas_call(
        middle_kernel,
        out_shape=[
            jax.ShapeDtypeStruct((rows, width), f32),
            jax.ShapeDtypeStruct((CHIPS, rows, width), bf16),
        ],
        in_specs=[VMEM, ANY, VMEM, VMEM],
        out_specs=[VMEM, ANY],
        scratch_shapes=[
            pltpu.VMEM((rows, width), bf16),
            pltpu.VMEM((channels, width), bf16),
            pltpu.SemaphoreType.DMA((4,)),
            pltpu.SemaphoreType.DMA((4,)),
            pltpu.SemaphoreType.DMA,
            pltpu.SemaphoreType.DMA((rows_all.shape[0],)),
            *computed_scratch(rows, width),
        ],
        compiler_params=comm_params(collective_id, 60),
        cost_estimate=lasting(75),
        name="middle",
    )(mixed, rows_all, tokens, gain[None])


def feed_forward_kernel(
    piece,
    two,
    cot,
    weights,
    down,
    *refs,
):
    last = piece == 1
    if last:
        (
            earlier_weights,
            earlier_low,
            hidden,
            grad,
            parts,
            low,
            earlier_here,
            earlier_low_here,
            *refs,
        ) = refs
    else:
        hidden, grad, low, *refs = refs
    two_here, two_there, cot_here, weights_here, down_here, low_there, send, recv, loads, down_loads = refs
    me, z, p, c, x, y = place()
    sibling = me + 1 - 2 * c
    greet((sibling,))
    f32, bf16 = jnp.float32, jnp.bfloat16
    tokens, width = two.shape
    units = hidden.shape[1]
    half = width // 2
    pairs = [
        (two, two_here),
        (weights, weights_here),
        (cot, cot_here),
    ]
    if last:
        pairs += [(earlier_weights, earlier_here), (earlier_low, earlier_low_here)]
    fetched = [pltpu.make_async_copy(a, b, loads.at[k]) for k, (a, b) in enumerate(pairs)]
    count = down_loads.shape[0]
    fetched[3:3] = fetch_rows(down, count * piece, down.shape[1] - units // count, down_here, down_loads)
    for copy in fetched:
        copy.start()
    other_half = two.at[:, pl.ds(pl.multiple_of((1 - c) * half, 128), half)]
    two_swap = remote(other_half, two_there, send.at[0], recv.at[0], sibling)
    two_swap.start()
    for copy in fetched[: 3 + count]:
        copy.wait()
    tile, block = 256, 512

    def dot_t(left, right):
        return lax.dot_general(left, right, (((1,), (1,)), ((), ())), preferred_element_type=f32)

    def dot_first(left, right):
        return lax.dot_general(left, right, (((0,), (0,)), ((), ())), preferred_element_type=f32)

    low_swaps = []
    for t in range(units // tile):
        gate_at, up_at = pl.ds(t * tile, tile), pl.ds(units + t * tile, tile)

        @pl.loop(0, tokens // block)
        def rows_block(j):
            at = pl.ds(pl.multiple_of(j * block, block), block)
            v = jnp.dot(two_here[at, :], weights_here[:, gate_at], preferred_element_type=f32)
            up = jnp.dot(two_here[at, :], weights_here[:, up_at], preferred_element_type=f32)
            grad_hidden = dot_t(cot_here[at, :], down_here[gate_at, :])
            square = v * v
            bent = jnp.tanh(v * (GELU_A + GELU_A * GELU_B * square))
            rising = 0.5 + 0.5 * bent
            act = v * rising
            slope = rising + 0.5 * v * (1.0 - bent * bent) * (GELU_A + 3.0 * GELU_A * GELU_B * square)
            hidden[at, gate_at] = (act * up).astype(bf16)
            low[at, gate_at] = (grad_hidden * up * slope).astype(bf16)
            low[at, up_at] = (grad_hidden * act).astype(bf16)

        for k, columns in enumerate((gate_at, up_at)):
            sems = 1 + 2 * t + k
            low_swaps.append(
                remote(low.at[:, columns], low_there.at[:, columns], send.at[sems], recv.at[sems], sibling)
            )
            low_swaps[-1].start()
    if last:
        for copy in fetched[3 + count :]:
            copy.wait()

        @pl.loop(0, tokens // block)
        def parts_block(j):
            at = pl.ds(pl.multiple_of(j * block, block), block)

            @pl.loop(0, width // block)
            def parts_tile(k):
                columns = pl.ds(pl.multiple_of(k * block, block), block)
                parts[at, columns] = (
                    dot_t(earlier_low_here[at, :], earlier_here[columns, :])
                    + dot_t(low[at, :], weights_here[columns, :])
                ).astype(bf16)

    two_swap.wait()
    for copy in low_swaps:
        copy.wait()

    @pl.loop(0, half // block)
    def grad_block(m):
        here = pl.ds(pl.multiple_of(c * half + m * block, 128), block)
        there = pl.ds(pl.multiple_of(m * block, block), block)

        @pl.loop(0, 2 * units // block)
        def grad_tile(k):
            columns = pl.ds(pl.multiple_of(k * block, block), block)
            grad[there, columns] = (
                dot_first(two_here[:, here], low[:, columns]) + dot_first(two_there[:, there], low_there[:, columns])
            ).astype(bf16)


def feed_forward(piece, two, cot, weights, down, earlier, collective_id):
    tokens, width = two.shape
    units = weights.shape[1] // 2
    bf16 = jnp.bfloat16
    out_shape = [
        jax.ShapeDtypeStruct((tokens, units), bf16),
        jax.ShapeDtypeStruct((width // 2, 2 * units), bf16),
    ]
    low = pltpu.VMEM((tokens, 2 * units), bf16)
    scratch = []
    if earlier:
        out_shape.append(jax.ShapeDtypeStruct((tokens, width), bf16))
        scratch = [low, pltpu.VMEM(weights.shape, bf16), low]
    else:
        out_shape.append(jax.ShapeDtypeStruct((tokens, 2 * units), bf16))
    swaps = 1 + 2 * (units // 256)
    return pl.pallas_call(
        functools.partial(feed_forward_kernel, piece),
        out_shape=out_shape,
        in_specs=[ANY] * (4 + len(earlier)),
        out_specs=[VMEM] * 3,
        scratch_shapes=[
            *scratch,
            pltpu.VMEM((tokens, width), bf16),
            pltpu.VMEM((tokens, width // 2), bf16),
            pltpu.VMEM((tokens, width), bf16),
            pltpu.VMEM(weights.shape, bf16),
            pltpu.VMEM((units, width), bf16),
            low,
            pltpu.SemaphoreType.DMA((swaps,)),
            pltpu.SemaphoreType.DMA((swaps,)),
            pltpu.SemaphoreType.DMA((3 + len(earlier),)),
            pltpu.SemaphoreType.DMA((down.shape[0] // 2,)),
        ],
        compiler_params=comm_params(collective_id, 60),
        cost_estimate=lasting(35),
        name="feed_forward",
    )(two, cot, weights, down, *earlier)


def norm_back_rows(values, gain, grad, rest):
    inverse = lax.rsqrt(jnp.mean(values * values, axis=-1, keepdims=True) + epsilon)
    scaled = gain * grad
    pull = jnp.mean(scaled * values, axis=-1, keepdims=True) * (inverse * inverse * inverse)
    return rest + inverse * scaled - values * pull, grad * values * inverse


def grads_of_middle_kernel(
    parts,
    middle,
    cot,
    gain,
    hidden_zero,
    hidden_one,
    down,
    cot_all,
    cot_other,
    grad_middle,
    grad_gain,
    whole,
    down_grad,
    down_parts,
    branch,
    hidden_here,
    hidden_other,
    down_here,
    cot_here,
    cot_there,
    *scratch,
):
    sums, (send, recv, local, loads, down_loads) = scratch[:10], scratch[10:]
    me, z, p, c, x, y = place()
    f32, bf16 = jnp.float32, jnp.bfloat16
    sibling = me + 1 - 2 * c
    greet((*plane_neighbours()[0][:2], sibling))
    own, from_x, from_y = sums[:3]
    begin, forward, end = sum_steps(parts, *sums)
    begin()
    half = hidden_zero.shape[1]
    swaps = [remote(hidden, hidden_other, send.at[4], recv.at[4], sibling) for hidden in (hidden_one, hidden_zero)]

    @pl.when(c == 0)
    def send_one():
        swaps[0].start()

    @pl.when(c == 1)
    def send_zero():
        swaps[1].start()

    fetched = [
        pltpu.make_async_copy(source, target, loads.at[k])
        for k, (source, target) in enumerate(
            (
                (hidden_zero, hidden_here.at[:, pl.ds(0, half)]),
                (hidden_one, hidden_here.at[:, pl.ds(half, half)]),
                (cot_all, cot_here),
                (cot_other, cot_there),
            )
        )
    ]
    count = down_loads.shape[0]
    down_fetched = fetch_rows(down, 0, down.shape[1] - down_here.shape[0] // count, down_here, down_loads)
    for copy in fetched + down_fetched:
        copy.start()
    for copy in fetched[:4]:
        copy.wait()
    swaps[0].wait()
    tile = 256

    planes, units = down_grad.shape[:2]

    def grad_tiles(m):
        rows_here = pl.ds(pl.multiple_of(c * half + m * tile, 128), tile)

        @pl.loop(0, cot_all.shape[1] // (2 * tile))
        def grad_tile(k):
            columns = pl.ds(pl.multiple_of(k * 2 * tile, 128), 2 * tile)

            def dot_t(left, right):
                return lax.dot_general(left, right, (((0,), (0,)), ((), ())), preferred_element_type=f32)

            values = (
                dot_t(hidden_here[:, rows_here], cot_here[:, columns])
                + dot_t(hidden_other[:, m * tile : (m + 1) * tile], cot_there[:, columns])
            ).astype(bf16)
            for j in range(planes):
                start, stop = max(j * units, m * tile), min((j + 1) * units, (m + 1) * tile)
                if start < stop:
                    down_grad[j, start - j * units : stop - j * units, columns] = values[
                        start - m * tile : stop - m * tile
                    ]

    grad_tiles(0)
    forward()
    for m in range(1, half // tile):
        grad_tiles(m)
    end()
    rows, width = middle.shape

    def norm_rows(i, total):
        at = sixteen(i)
        grad = own[at, :].astype(f32) + from_x[at, :].astype(f32) + from_y[at, :].astype(f32)
        given, terms = norm_back_rows(middle[at, :], gain[...], grad, cot[at, :].astype(f32))
        grad_middle[at, :] = given
        branch[at, :] = given.astype(bf16)
        return total + terms[:8] + terms[8:]

    total = lax.fori_loop(0, rows // 16, norm_rows, jnp.zeros((8, width), f32))
    grad_gain[...] = jnp.sum(total, axis=0, keepdims=True)
    begin, forward, end = gather_steps(branch, whole, send, recv, local, 0)
    begin()
    for copy in down_fetched:
        copy.wait()

    def down_tiles(j):
        @pl.loop(0, width // (2 * tile))
        def down_tile(k):
            columns = pl.ds(pl.multiple_of(k * 2 * tile, 128), 2 * tile)
            down_parts[j, :, columns] = jnp.dot(
                hidden_here[pl.ds(pl.multiple_of(j * rows, 16), rows), :],
                down_here[:, columns],
                preferred_element_type=f32,
            ).astype(bf16)

    pl.loop(0, CHIPS)(down_tiles)
    forward()
    end()


def grads_of_middle(parts, middle, cot, gain, hiddens, down, cot_all, cot_other, collective_id):
    rows, width = middle.shape
    tokens, units = hiddens[0].shape[0], 2 * hiddens[0].shape[1]
    f32, bf16 = jnp.float32, jnp.bfloat16
    return pl.pallas_call(
        grads_of_middle_kernel,
        out_shape=[
            jax.ShapeDtypeStruct((rows, width), f32),
            jax.ShapeDtypeStruct((1, width), f32),
            jax.ShapeDtypeStruct((CHIPS, rows, width), bf16),
            jax.ShapeDtypeStruct((down.shape[0] // 2, 2 * hiddens[0].shape[1] // down.shape[0], width), bf16),
            jax.ShapeDtypeStruct((CHIPS, rows, width), bf16),
        ],
        in_specs=[ANY, VMEM, VMEM, VMEM] + [ANY] * 5,
        out_specs=[VMEM, VMEM, ANY, VMEM, VMEM],
        scratch_shapes=[
            pltpu.VMEM((rows, width), bf16),
            pltpu.VMEM((tokens, units), bf16),
            pltpu.VMEM((tokens, units // 2), bf16),
            pltpu.VMEM((units, width), bf16),
            pltpu.VMEM((tokens, width), bf16),
            pltpu.VMEM((tokens, width), bf16),
            *sum_scratch(rows, width, parts.dtype),
            pltpu.SemaphoreType.DMA((5,)),
            pltpu.SemaphoreType.DMA((5,)),
            pltpu.SemaphoreType.DMA,
            pltpu.SemaphoreType.DMA((4,)),
            pltpu.SemaphoreType.DMA((down.shape[0],)),
        ],
        compiler_params=comm_params(collective_id, 60),
        cost_estimate=lasting(80),
        name="grads_of_middle",
    )(parts, middle, cot, gain[None], *hiddens, down, cot_all, cot_other)


def closing_kernel(
    planes,
    in_low,
    whole_in,
    tokens,
    gain,
    rest,
    small,
    conv_low,
    decay_low,
    input_low,
    piece,
    grad_tokens,
    small_out,
    gates_out,
    swapped,
    conv_a,
    conv_b,
    decay_a,
    decay_b,
    input_a,
    input_b,
    full,
    gates,
    gate_lines,
    lines,
    line,
    near_parts,
    gains,
    gain_lines,
    gain_line,
    gain_near,
    send,
    recv,
    loads,
    swap_send,
    swap_recv,
    *sums,
):
    me, z, p, c, x, y = place()
    f32 = jnp.float32
    r = lax.rem(me, 8)
    near = [(lax.rem(r + d, 8), me - r + lax.rem(r + d, 8)) for d in range(1, 8)]
    far = [(lax.rem(z + d, planes), 8 * lax.rem(z + d, planes) + r) for d in range(1, planes)]
    greet([device for unused, device in near + far])

    def copy(k, source, target, device):
        return remote(source, target, send.at[k], recv.at[k], device)

    lows = ((conv_low, conv_a, conv_b), (decay_low, decay_a, decay_b), (input_low, input_a, input_b))
    fetched = [pltpu.make_async_copy(source, here, loads.at[k]) for k, (source, here, there) in enumerate(lows)]
    exchanges = [copy(k, source, there, me + 1 - 2 * c) for k, (source, here, there) in enumerate(lows)]
    at = 3
    small_far = [copy(at + d, small.at[there], lines.at[d], device) for d, (there, device) in enumerate(far)]
    at += len(far)
    for started in small_far + fetched + exchanges:
        started.start()

    def product(chip, rows_at, columns):
        return lax.dot_general(
            in_low[chip, rows_at, :], whole_in[columns, :], (((1,), (1,)), ((), ())), preferred_element_type=f32
        )

    begin, forward, end = computed_sum(product, *sums)
    own, from_x, from_y = sums[3], sums[6], sums[7]
    begin()
    for ended in fetched + exchanges:
        ended.wait()
    swaps = swap_copies(piece, swapped, swap_send, swap_recv, loads.at[3])

    def dot_first(left, right):
        return lax.dot_general(left, right, (((0,), (0,)), ((), ())), preferred_element_type=f32)

    block = gates.shape[1]
    count = planes * block
    for k, (first, second) in enumerate(((decay_a, decay_b), (input_a, input_b))):
        full[...] = dot_first(conv_a[...], first[...]) + dot_first(conv_b[...], second[...])
        for j in range(planes):
            rows_at = pl.ds(pl.multiple_of(c * count + j * block, 8), block)
            for e in range(2):
                gates[j, :, (2 * k + e) * block : (2 * k + e + 1) * block] = full[
                    rows_at, e * count + j * block : e * count + (j + 1) * block
                ]
    gate_far = [copy(at + d, gates.at[there], gate_lines.at[d], device) for d, (there, device) in enumerate(far)]
    at += len(far)
    for sent in gate_far:
        sent.start()
    forward()
    for sent in swaps:
        sent.start()
    for sent in small_far:
        sent.wait()
    line[...] = small[z] + sum(lines[d] for d in range(planes - 1))
    small_near = [
        copy(at + d, line.at[there], near_parts.at[d], device) for d, (there, device) in enumerate(near)
    ]
    at += len(near)
    for sent in small_near:
        sent.start()
    end()
    rows, width = tokens.shape
    step = width // (8 * planes)

    def norm_rows(i, total):
        here = sixteen(i)
        grad = own[here, :] + from_x[here, :].astype(f32) + from_y[here, :].astype(f32)
        given, terms = norm_back_rows(tokens[here, :].astype(f32), gain[...], grad, rest[here, :])
        for k in range(4 * planes):
            for e in range(2):
                grad_tokens[here, (2 * k + e) * step : (2 * k + e + 1) * step] = given[
                    :, (4 * planes * e + k) * step : (4 * planes * e + k + 1) * step
                ]
        return total + terms[:8] + terms[8:]

    total = lax.fori_loop(0, rows // 16, norm_rows, jnp.zeros((8, width), f32))
    total = jnp.sum(total, axis=0, keepdims=True)
    for j in range(planes):
        for q in range(CHIPS):
            for e in range(2):
                start = ((e * planes + j) * CHIPS + q) * step
                gains[j, 2 * q + e, 0:1, 0:step] = total[:, start : start + step]
    gain_far = [copy(at + d, gains.at[there], gain_lines.at[d], device) for d, (there, device) in enumerate(far)]
    at += len(far)
    for sent in gain_far:
        sent.start()
    for sent in gain_far:
        sent.wait()
    gain_line[...] = gains[z] + sum(gain_lines[d] for d in range(planes - 1))
    last = [
        copy(at + d, gain_line.at[there], gain_near.at[d], device) for d, (there, device) in enumerate(near)
    ]
    for sent in last:
        sent.start()
    for sent in small_near + gate_far + swaps:
        sent.wait()
    gates_out[...] = gates[z] + sum(gate_lines[d] for d in range(planes - 1))
    for sent in last:
        sent.wait()
    rows_small = line.shape[1]
    small_out[0:rows_small, :] = line[r] + sum(near_parts[d] for d in range(7))
    small_out[rows_small : rows_small + 8, :] = gain_line[r] + sum(gain_near[d] for d in range(7))


def closing(in_low, whole_in, tokens, gain, rest, small, lows, piece, head, collective_id):
    planes = lax.axis_size("seq") // 8
    rows, width = tokens.shape
    f32, bf16 = jnp.float32, jnp.bfloat16
    rows_small, lanes = small.shape[2:]
    channels = lows[0].shape[1]
    block = channels // (2 * planes)
    count = 3 + 3 * (planes - 1) + 14
    return pl.pallas_call(
        functools.partial(closing_kernel, planes),
        out_shape=[
            jax.ShapeDtypeStruct((rows, width), f32),
            jax.ShapeDtypeStruct((rows_small + 8, lanes), f32),
            jax.ShapeDtypeStruct((block, 2 * head), f32),
            jax.ShapeDtypeStruct(piece.shape, bf16),
        ],
        in_specs=[VMEM] * 6 + [ANY] * 4,
        out_specs=[VMEM] * 3 + [ANY],
        scratch_shapes=[
            *[pltpu.VMEM(lows[0].shape, bf16)] * 6,
            pltpu.VMEM((channels, channels), f32),
            pltpu.VMEM((planes, block, 2 * head), f32),
            pltpu.VMEM((planes - 1, block, 2 * head), f32),
            pltpu.VMEM((planes - 1, 8, rows_small, lanes), f32),
            pltpu.VMEM((8, rows_small, lanes), f32),
            pltpu.VMEM((7, rows_small, lanes), f32),
            pltpu.VMEM((planes, 8, 8, lanes), f32),
            pltpu.VMEM((planes - 1, 8, 8, lanes), f32),
            pltpu.VMEM((8, 8, lanes), f32),
            pltpu.VMEM((7, 8, lanes), f32),
            pltpu.SemaphoreType.DMA((count,)),
            pltpu.SemaphoreType.DMA((count,)),
            pltpu.SemaphoreType.DMA((4,)),
            pltpu.SemaphoreType.DMA((3,)),
            pltpu.SemaphoreType.DMA((3,)),
            *computed_scratch(rows, width),
        ],
        compiler_params=comm_params(collective_id, 60),
        cost_estimate=lasting(50),
        name="closing",
    )(in_low, whole_in, tokens, gain[None], rest, small, *lows, piece)


def plane_swap_kernel(count, *refs):
    ins, outs = refs[:count], refs[count : 2 * count]
    send, recv, local = refs[2 * count :]
    me, z, p, c, x, y = place()
    x_dev, y_dev = me + 2 - 4 * x, me + 4 - 8 * y
    d_dev = y_dev + 2 - 4 * x
    p_x, p_y, p_d = p + 1 - 2 * x, p + 2 - 4 * y, 3 - p
    peers = ((x_dev, p_x), (y_dev, p_y), (d_dev, p_d))
    greet([device for device, unused in peers])
    copies = []
    for k in range(count):
        for j, (device, chip) in enumerate(peers):
            copies.append(remote(ins[k].at[chip], outs[k].at[p], send.at[k, j], recv.at[k, j], device))
        copies.append(pltpu.make_async_copy(ins[k].at[p], outs[k].at[p], local.at[k]))
    for copy in copies:
        copy.start()
    for copy in copies:
        copy.wait()


def plane_swap(arrays, collective_id):
    count = len(arrays)
    return pl.pallas_call(
        functools.partial(plane_swap_kernel, count),
        out_shape=[jax.ShapeDtypeStruct(a.shape, a.dtype) for a in arrays],
        in_specs=[ANY] * count,
        out_specs=[ANY] * count,
        scratch_shapes=[
            pltpu.SemaphoreType.DMA((count, 3)),
            pltpu.SemaphoreType.DMA((count, 3)),
            pltpu.SemaphoreType.DMA((count,)),
        ],
        compiler_params=comm_params(collective_id),
        cost_estimate=lasting(10),
        name="plane_swap",
    )(*arrays)


def swap_copies(source, target, send, recv, local):
    devices, chips = plane_neighbours()
    p = place()[2]
    return [
        *[remote(source.at[chips[j]], target.at[p], send.at[j], recv.at[j], devices[j]) for j in range(3)],
        pltpu.make_async_copy(source.at[p], target.at[p], local),
    ]


def opening_kernel(
    planes,
    small,
    gates,
    tokens,
    piece,
    gathered,
    decay_blocks,
    input_blocks,
    whole,
    swapped,
    gates_all,
    gain,
    normed,
    *sems,
):
    send, recv, gate_send, gate_recv, swap_send, swap_recv, swap_local, gather_send, gather_recv, gather_local = sems
    me, z, p, c, x, y = place()
    r = lax.rem(me, 8)
    near = [me - r + lax.rem(r + d, 8) for d in range(1, 8)]
    far = [8 * lax.rem(z + d, planes) + r for d in range(1, planes)]
    greet(near + far)
    lines = [
        remote(small, gathered.at[r, z], send.at[d], recv.at[d], device) for d, device in enumerate(far)
    ]
    gate_lines = [
        remote(gates, gates_all.at[c, z], gate_send.at[d], gate_recv.at[d], device) for d, device in enumerate(far)
    ]
    for copy in lines + gate_lines:
        copy.start()
    gathered[r, z] = small[...]
    gates_all[c, z] = gates[...]
    for copy in lines:
        copy.wait()
    spreads = [
        remote(gathered.at[r], gathered.at[r], send.at[planes + d], recv.at[planes + d], device)
        for d, device in enumerate(near)
    ]
    for copy in spreads:
        copy.start()
    for copy in gate_lines:
        copy.wait()
    gate_swap = remote(
        gates_all.at[c], gates_all.at[c], gate_send.at[planes], gate_recv.at[planes], me + 1 - 2 * c
    )
    gate_swap.start()
    for copy in spreads:
        copy.wait()
    swaps = swap_copies(piece, swapped, swap_send, swap_recv, swap_local)
    rows, width = tokens.shape
    step = width // (8 * planes)
    for j in range(planes):
        for q in range(CHIPS):
            for e in range(2):
                start = ((e * planes + j) * CHIPS + q) * step
                gain[0:1, start : start + step] = gathered[2 * q + e, j, 0:1, 0:step]

    @pl.loop(0, rows // 16)
    def norm_rows(i):
        at = sixteen(i)
        values = tokens[at, :].astype(jnp.float32)
        inverse = lax.rsqrt(jnp.mean(values * values, axis=-1, keepdims=True) + epsilon)
        normed[at, :] = (values * inverse * gain[0:1, :]).astype(jnp.bfloat16)

    begin, forward, end = gather_steps(normed, whole, gather_send, gather_recv, gather_local, 0)
    begin()
    for copy in swaps:
        copy.start()
    gate_swap.wait()
    block = gates.shape[0]
    for k, target in enumerate((decay_blocks, input_blocks)):
        target[...] = jnp.zeros_like(target)
        for e in range(2):
            for j in range(planes):
                for h in range(2):
                    row, column = (e * planes + j) * block, (h * planes + j) * block
                    target[row : row + block, column : column + block] = gates_all[
                        e, j, :, (2 * k + h) * block : (2 * k + h + 1) * block
                    ]
    forward()
    end()
    for copy in swaps:
        copy.wait()


def opening(small, gates, tokens, piece, collective_id):
    planes = lax.axis_size("seq") // 8
    rows, width = tokens.shape
    channels = 2 * planes * gates.shape[0]
    return pl.pallas_call(
        functools.partial(opening_kernel, planes),
        out_shape=[
            jax.ShapeDtypeStruct((8, planes) + small.shape, small.dtype),
            jax.ShapeDtypeStruct((channels, channels), gates.dtype),
            jax.ShapeDtypeStruct((channels, channels), gates.dtype),
            jax.ShapeDtypeStruct((CHIPS, rows, width), jnp.bfloat16),
            jax.ShapeDtypeStruct(piece.shape, piece.dtype),
        ],
        in_specs=[VMEM, VMEM, VMEM, ANY],
        out_specs=[VMEM, VMEM, VMEM, ANY, ANY],
        scratch_shapes=[
            pltpu.VMEM((2, planes) + gates.shape, gates.dtype),
            pltpu.VMEM((8, width), jnp.float32),
            pltpu.VMEM((rows, width), jnp.bfloat16),
            pltpu.SemaphoreType.DMA((planes + 7,)),
            pltpu.SemaphoreType.DMA((planes + 7,)),
            pltpu.SemaphoreType.DMA((planes + 1,)),
            pltpu.SemaphoreType.DMA((planes + 1,)),
            pltpu.SemaphoreType.DMA((3,)),
            pltpu.SemaphoreType.DMA((3,)),
            pltpu.SemaphoreType.DMA,
            pltpu.SemaphoreType.DMA((4,)),
            pltpu.SemaphoreType.DMA((4,)),
            pltpu.SemaphoreType.DMA,
        ],
        compiler_params=comm_params(collective_id, 60),
        cost_estimate=lasting(65),
        name="opening",
    )(small, gates, tokens, piece)


def column_peers(planes, z, p, c):
    count = 2 * planes
    q = 2 * z + c
    peers = []
    for d in range(1, count):
        other = lax.rem(q + d, count)
        peers.append(8 * lax.div(other, 2) + 2 * p + lax.rem(other, 2))
    return q, peers


def carry_in(planes, reverse, z, c, q, peers, everyone, before, entering, send, recv):
    own = everyone.at[q]
    copies = [remote(own, own, send.at[d], recv.at[d], device) for d, device in enumerate(peers)]
    for copy in copies:
        copy.start()
    for copy in copies:
        copy.wait()
    carried = jnp.zeros((1, everyone.shape[2]), jnp.float32)
    order = [(k, j, e) for k in range(planes) for j in range(CHIPS) for e in range(2)]
    for k, j, e in reversed(order) if reverse else order:
        before[8 * k + 2 * j + e : 8 * k + 2 * j + e + 1, :] = carried
        part = everyone.at[2 * k + e]
        carried = part[j : j + 1, :] * carried + part[CHIPS + j : CHIPS + j + 1, :]
    for j in range(CHIPS):
        entering[j : j + 1, :] = before[pl.ds(8 * z + 2 * j + c, 1), :]


def shift_down(earlier, values, step, row):
    return jnp.where(row >= step, pltpu.roll(values, step, 0), pltpu.roll(earlier, step, 0))


def shift_up(values, later, step, row):
    return jnp.where(row < 8 - step, pltpu.roll(values, 8 - step, 0), pltpu.roll(later, 8 - step, 0))


def tile_scan(a, b, row, reverse):
    for step in (1, 2, 4):
        if reverse:
            keep = row < 8 - step
            shifted_a, shifted_b = pltpu.roll(a, 8 - step, 0), pltpu.roll(b, 8 - step, 0)
        else:
            keep = row >= step
            shifted_a, shifted_b = pltpu.roll(a, step, 0), pltpu.roll(b, step, 0)
        b = a * jnp.where(keep, shifted_b, 0.0) + b
        a = a * jnp.where(keep, shifted_a, 1.0)
    return a, b


def sigmoid(values):
    return 1.0 / (1.0 + jnp.exp(-values))


def gate_terms(decay_pre, rate, flag):
    opened = sigmoid(decay_pre)
    log_decay = rate * opened
    decay = jnp.exp(log_decay)
    keep = 1.0 - flag
    squared = decay * decay
    return opened, decay * keep, keep, squared, jnp.tanh(-log_decay) * (1.0 + squared)


GELU_A, GELU_B = 0.7978845608028654, 0.044715


def eight(i):
    return pl.ds(pl.multiple_of(i * 8, 8), 8)


def recurrence_kernel(
    planes,
    gate_pre,
    conv_input,
    masks,
    vectors,
    decay_blocks,
    input_blocks,
    cot,
    piece,
    conv_out,
    conv_low,
    decay_pre,
    input_pre,
    states,
    mixed,
    entering,
    halo,
    cot_all,
    swapped,
    cumulative,
    sibling_tails,
    below_tail,
    everyone,
    before,
    send,
    recv,
    local,
    swap_send,
    swap_recv,
):
    me, z, p, c, x, y = place()
    rows, channels = conv_input.shape[1:]
    q, peers = column_peers(planes, z, p, c)
    greet(peers + [*plane_neighbours()[0]])
    cot_begin, cot_forward, cot_end = gather_steps(cot, cot_all, send, recv, local.at[0], 9)
    cot_begin()
    swaps = swap_copies(piece, swapped, swap_send, swap_recv, local.at[1])
    f32 = jnp.float32
    tail = pl.ds(rows - 16, 16)
    to_sibling = remote(conv_input.at[:, tail], sibling_tails, send.at[7], recv.at[7], me + 1 - 2 * c)
    to_above = remote(conv_input.at[CHIPS - 1, tail], below_tail, send.at[8], recv.at[8], me + 7)
    from_below = remote(conv_input.at[CHIPS - 1, tail], below_tail, send.at[8], recv.at[8], me - 7)
    to_sibling.start()

    @pl.when((c == 1) & (z < planes - 1))
    def send_above():
        to_above.start()

    to_sibling.wait()

    @pl.when((c == 1) & (z < planes - 1))
    def sent_above():
        to_above.wait_send()

    @pl.when((c == 0) & (z > 0))
    def had_below():
        from_below.wait_recv()

    @pl.when(c == 1)
    def halo_one():
        for j in range(CHIPS):
            halo[j] = sibling_tails[j].astype(f32)[8:]

    @pl.when(c == 0)
    def halo_zero():
        for j in range(1, CHIPS):
            halo[j] = sibling_tails[j - 1].astype(f32)[8:]

        @pl.when(z > 0)
        def halo_below():
            halo[0] = below_tail[...].astype(f32)[8:]

        @pl.when(z == 0)
        def halo_none():
            halo[0] = jnp.zeros((8, channels), f32)

    row = lax.broadcasted_iota(jnp.int32, (8, channels), 0)

    @pl.loop(0, CHIPS)
    def block(j):
        def conv_tile(i, earlier):
            both = conv_input[j, sixteen(i), :].astype(f32)
            outs = []
            for h in range(2):
                now = both[8 * h : 8 * h + 8]
                keep = masks[j, eight(2 * i + h), :]
                out = vectors[CW : CW + 1, :] + vectors[0:1, :] * now
                for k in range(1, CW):
                    out = out + vectors[k : k + 1, :] * (
                        shift_down(earlier, now, k, row) * keep[:, k : k + 1]
                    )
                conv_out[j, eight(2 * i + h), :] = out
                outs.append(out)
                earlier = now
            conv_low[j, sixteen(i), :] = jnp.concatenate(outs, axis=0).astype(jnp.bfloat16)
            return earlier

        lax.fori_loop(0, rows // 16, conv_tile, halo[j], unroll=2)
        low = conv_low[j]
        decay_pre[j] = jnp.dot(low, decay_blocks[...], preferred_element_type=f32) + vectors[CW + 1 : CW + 2, :]
        input_pre[j] = jnp.dot(low, input_blocks[...], preferred_element_type=f32) + vectors[CW + 2 : CW + 3, :]

        def scan_tile(i, carry):
            at = eight(i)
            flag = masks[j, at, :][:, 0:1]
            opened, coef, keep, squared, gap = gate_terms(decay_pre[j, at, :], vectors[CW + 3 : CW + 4, :], flag)
            drive = (flag + keep * jnp.sqrt(gap)) * sigmoid(input_pre[j, at, :]) * conv_out[j, at, :]
            a, b = tile_scan(coef, drive, row, False)
            before_a, before_b = carry
            b = a * before_b + b
            a = a * before_a
            cumulative[j, at, :] = a
            states[j, at, :] = b
            return a[7:8], b[7:8]

        last_a, last_b = lax.fori_loop(
            0,
            rows // 8,
            scan_tile,
            (jnp.ones((1, channels), f32), jnp.zeros((1, channels), f32)),
            unroll=4,
        )
        everyone[q, pl.ds(j, 1), :] = last_a
        everyone[q, pl.ds(CHIPS + j, 1), :] = last_b

    cot_forward()
    for copy in swaps:
        copy.start()
    carry_in(planes, False, z, c, q, peers, everyone, before, entering, send, recv)

    @pl.loop(0, CHIPS)
    def finish(j):
        start = entering[pl.ds(j, 1), :]

        def state_tile(i, unused):
            at = sixteen(i)
            state = states[j, at, :] + cumulative[j, at, :] * start
            states[j, at, :] = state
            v = gate_pre[j, at, :]
            act = 0.5 * v * (1.0 + jnp.tanh(GELU_A * (v + GELU_B * (v * v * v))))
            mixed[j, at, :] = (state * act).astype(jnp.bfloat16)
            return unused

        lax.fori_loop(0, rows // 16, state_tile, 0, unroll=2)

    cot_end()
    for copy in swaps:
        copy.wait()


def recurrence(gate_pre, conv_input, masks, vectors, decay_blocks, input_blocks, cot, piece, collective_id):
    planes = lax.axis_size("seq") // 8
    blocks, rows, channels = conv_input.shape
    f32, bf16 = jnp.float32, jnp.bfloat16
    cube = conv_input.shape

    def out(dtype, shape=cube):
        return jax.ShapeDtypeStruct(shape, dtype)

    return pl.pallas_call(
        functools.partial(recurrence_kernel, planes),
        out_shape=[
            out(f32),
            out(bf16),
            out(f32),
            out(f32),
            out(f32),
            out(bf16),
            out(f32, (CHIPS, channels)),
            out(f32, (CHIPS, 8, channels)),
            out(cot.dtype, (CHIPS,) + cot.shape),
            out(piece.dtype, piece.shape),
        ],
        in_specs=[VMEM] * 6 + [ANY] * 2,
        out_specs=[VMEM] * 8 + [ANY] * 2,
        scratch_shapes=[
            pltpu.VMEM(cube, f32),
            pltpu.VMEM((CHIPS, 16, channels), bf16),
            pltpu.VMEM((16, channels), bf16),
            pltpu.VMEM((2 * planes, 2 * CHIPS, channels), f32),
            pltpu.VMEM((8 * planes, channels), f32),
            pltpu.SemaphoreType.DMA((13,)),
            pltpu.SemaphoreType.DMA((13,)),
            pltpu.SemaphoreType.DMA((2,)),
            pltpu.SemaphoreType.DMA((3,)),
            pltpu.SemaphoreType.DMA((3,)),
        ],
        compiler_params=comm_params(collective_id, 60),
        cost_estimate=lasting(46),
        name="recurrence",
    )(gate_pre, conv_input, masks, vectors, decay_blocks, input_blocks, cot, piece)


def recurrence_back_kernel(
    planes,
    grad_branch,
    rows_all,
    gate_pre,
    conv_input,
    conv_out,
    decay_pre,
    input_pre,
    states,
    entering,
    halo,
    masks,
    after_masks,
    vectors,
    decay_blocks,
    input_blocks,
    down_parts,
    piece,
    in_low,
    decay_low,
    input_low,
    sums,
    down_sum,
    swapped,
    grad_mixed,
    branch_here,
    out_here,
    cumulative,
    local,
    grad_conv,
    sibling_heads,
    above_head,
    ahead,
    everyone,
    before,
    leaving,
    send,
    recv,
    piece_sem,
    loads,
    *down_scratch,
):
    me, z, p, c, x, y = place()
    rows, channels = conv_input.shape[1:]
    q, peers = column_peers(planes, z, p, c)
    devices, chips = plane_neighbours()
    greet(peers + [*devices])
    down_begin, down_forward, down_end = sum_steps(down_parts, *down_scratch)
    down_begin()
    swaps = swap_copies(piece, swapped, send.at[pl.ds(9, 3)], recv.at[pl.ds(9, 3)], piece_sem.at[0])
    fetched = fetch_rows(rows_all, 0, 0, out_here, loads)
    fetched.append(pltpu.make_async_copy(grad_branch, branch_here, piece_sem.at[1]))
    for copy in fetched:
        copy.start()
    for copy in fetched:
        copy.wait()
    f32, bf16 = jnp.float32, jnp.bfloat16
    row = lax.broadcasted_iota(jnp.int32, (8, channels), 0)
    rate = vectors[CW + 3 : CW + 4, :]
    nothing = jnp.zeros((8, channels), f32)

    @pl.loop(0, CHIPS)
    def scan_block(j):
        grad_mixed[j] = lax.dot_general(
            branch_here[j], out_here[...], (((1,), (1,)), ((), ())), preferred_element_type=f32
        )

        def scan_tile(i, carry):
            i = rows // 16 - 1 - i
            at = sixteen(i)
            v = gate_pre[j, at, :]
            grad = grad_mixed[j, at, :]
            t = jnp.tanh(GELU_A * (v + GELU_B * (v * v * v)))
            act = 0.5 * v * (1.0 + t)
            slope = 0.5 * (1.0 + t) + 0.5 * v * (1.0 - t * t) * (GELU_A * (1.0 + 3.0 * GELU_B * (v * v)))
            in_low[j, at, 0:channels] = (grad * states[j, at, :] * slope).astype(bf16)
            drive = grad * act
            later_a, later_b, later_coef = carry
            for h in (1, 0):
                here = eight(2 * i + h)
                flag = masks[j, here, :][:, 0:1]
                coef = gate_terms(decay_pre[j, here, :], rate, flag)[1]
                shifted = jnp.where(row < 7, pltpu.roll(coef, 7, 0), later_coef)
                a, b = tile_scan(shifted, drive[8 * h : 8 * h + 8], row, True)
                b = a * later_b + b
                a = a * later_a
                cumulative[j, here, :] = a
                local[j, here, :] = b
                later_a, later_b, later_coef = a[0:1], b[0:1], coef[0:1]
            return later_a, later_b, later_coef

        ones = jnp.ones((1, channels), f32)
        first_a, first_b, first_coef = lax.fori_loop(
            0, rows // 16, scan_tile, (ones, jnp.zeros((1, channels), f32), ones), unroll=2
        )
        everyone[q, pl.ds(j, 1), :] = first_coef * first_a
        everyone[q, pl.ds(CHIPS + j, 1), :] = first_coef * first_b

    carry_in(planes, True, z, c, q, peers, everyone, before, leaving, send, recv)
    down_forward()
    for copy in swaps:
        copy.start()

    def terms_block(j, totals):
        behind_all = leaving[pl.ds(j, 1), :]

        def terms_tile(i, carry):
            previous, decay_sum, input_sum, param_sum = carry
            lows = []
            for h in range(2):
                at = eight(2 * i + h)
                adjoint = local[j, at, :] + cumulative[j, at, :] * behind_all
                state = states[j, at, :]
                earlier = jnp.where(row >= 1, pltpu.roll(state, 1, 0), previous)
                previous = state[7:8]
                flag = masks[j, at, :][:, 0:1]
                opened, coef, keep, squared, gap = gate_terms(decay_pre[j, at, :], rate, flag)
                passed = sigmoid(input_pre[j, at, :])
                conv = conv_out[j, at, :]
                inverse = lax.rsqrt(gap)
                scale = flag + keep * (gap * inverse)
                grad_log = adjoint * (earlier * coef - keep * passed * conv * squared * inverse)
                log_open = grad_log * opened
                decay_full = log_open * rate * (1.0 - opened)
                direct = adjoint * scale * passed
                input_full = direct * (1.0 - passed) * conv
                grad_conv[j, at, :] = direct
                lows.append((decay_full, input_full))
                decay_sum = decay_sum + decay_full
                input_sum = input_sum + input_full
                param_sum = param_sum + log_open
            decay_low[j, sixteen(i), :] = jnp.concatenate([low[0] for low in lows], axis=0).astype(bf16)
            input_low[j, sixteen(i), :] = jnp.concatenate([low[1] for low in lows], axis=0).astype(bf16)
            return previous, decay_sum, input_sum, param_sum

        totals = lax.fori_loop(
            0, rows // 16, terms_tile, (entering[pl.ds(j, 1), :], *totals), unroll=2
        )[1:]

        def dot_t(left, right):
            return lax.dot_general(left, right, (((1,), (1,)), ((), ())), preferred_element_type=f32)

        grad_conv[j] = (
            grad_conv[j] + dot_t(decay_low[j], decay_blocks[...]) + dot_t(input_low[j], input_blocks[...])
        )
        return totals

    decay_sum, input_sum, param_sum = lax.fori_loop(0, CHIPS, terms_block, (nothing,) * 3)

    to_sibling = remote(grad_conv.at[:, pl.ds(0, 8)], sibling_heads, send.at[7], recv.at[7], me + 1 - 2 * c)
    to_below = remote(grad_conv.at[0, pl.ds(0, 8)], above_head, send.at[8], recv.at[8], me - 7)
    from_above = remote(grad_conv.at[0, pl.ds(0, 8)], above_head, send.at[8], recv.at[8], me + 7)
    to_sibling.start()

    @pl.when((c == 0) & (z > 0))
    def send_below():
        to_below.start()

    to_sibling.wait()

    @pl.when((c == 0) & (z > 0))
    def sent_below():
        to_below.wait_send()

    @pl.when((c == 1) & (z < planes - 1))
    def had_above():
        from_above.wait_recv()

    @pl.when(c == 0)
    def ahead_zero():
        for j in range(CHIPS):
            ahead[j] = sibling_heads[j]

    @pl.when(c == 1)
    def ahead_one():
        for j in range(CHIPS - 1):
            ahead[j] = sibling_heads[j + 1]

        @pl.when(z < planes - 1)
        def ahead_above():
            ahead[CHIPS - 1] = above_head[...]

        @pl.when(z == planes - 1)
        def ahead_none():
            ahead[CHIPS - 1] = nothing

    def conv_block(j, totals):
        def conv_pair(i, now, later, keep, later_keep, outs, earlier, given, totals):
            out = vectors[0:1, :] * now
            new_totals = [totals[0] + now * given]
            for k in range(1, CW):
                masked = now * keep[:, k : k + 1]
                out = out + vectors[k : k + 1, :] * shift_up(
                    masked, later * later_keep[:, k : k + 1], k, row
                )
                new_totals.append(totals[k] + masked * shift_down(earlier, given, k, row))
            new_totals.append(totals[CW] + now)
            outs.append(out)
            return tuple(new_totals)

        def conv_tile(i, carry, last):
            earlier, totals = carry
            inputs = conv_input[j, sixteen(i), :].astype(f32)
            first, second = grad_conv[j, eight(2 * i), :], grad_conv[j, eight(2 * i + 1), :]
            first_keep, second_keep = masks[j, eight(2 * i), :], masks[j, eight(2 * i + 1), :]
            if last:
                third, third_keep = ahead[j], after_masks[j]
            else:
                third, third_keep = grad_conv[j, eight(2 * i + 2), :], masks[j, eight(2 * i + 2), :]
            outs = []
            totals = conv_pair(i, first, second, first_keep, second_keep, outs, earlier, inputs[:8], totals)
            totals = conv_pair(i, second, third, second_keep, third_keep, outs, inputs[:8], inputs[8:], totals)
            in_low[j, sixteen(i), channels : 2 * channels] = jnp.concatenate(outs, axis=0).astype(bf16)
            return inputs[8:], totals

        carry = lax.fori_loop(
            0, rows // 16 - 1, lambda i, carry: conv_tile(i, carry, False), (halo[j], totals)
        )
        return conv_tile(rows // 16 - 1, carry, True)[1]

    totals = lax.fori_loop(0, CHIPS, conv_block, (nothing,) * (CW + 1))
    for k, total in enumerate((*totals, decay_sum, input_sum, param_sum)):
        sums[k : k + 1, :] = jnp.sum(total, axis=0, keepdims=True)
    down_end()
    own, from_x, from_y = down_scratch[:3]

    @pl.loop(0, own.shape[0] // 16)
    def sum_rows(i):
        at = sixteen(i)
        down_sum[at, :] = own[at, :].astype(f32) + from_x[at, :].astype(f32) + from_y[at, :].astype(f32)

    for copy in swaps:
        copy.wait()


def recurrence_back(
    grad_branch,
    rows_all,
    gate_pre,
    conv_input,
    conv_out,
    decay_pre,
    input_pre,
    states,
    entering,
    halo,
    masks,
    after_masks,
    vectors,
    decay_blocks,
    input_blocks,
    down_parts,
    piece,
    collective_id,
):
    planes = lax.axis_size("seq") // 8
    cube = conv_input.shape
    blocks, rows, channels = cube
    f32, bf16 = jnp.float32, jnp.bfloat16
    return pl.pallas_call(
        functools.partial(recurrence_back_kernel, planes),
        out_shape=[
            jax.ShapeDtypeStruct((CHIPS, rows, 2 * channels), bf16),
            jax.ShapeDtypeStruct(cube, bf16),
            jax.ShapeDtypeStruct(cube, bf16),
            jax.ShapeDtypeStruct((CW + 4, channels), f32),
            jax.ShapeDtypeStruct(down_parts.shape[1:], f32),
            jax.ShapeDtypeStruct(piece.shape, bf16),
        ],
        in_specs=[ANY] * 2 + [VMEM] * 13 + [ANY] * 2,
        out_specs=[VMEM] * 5 + [ANY],
        scratch_shapes=[
            pltpu.VMEM(cube, f32),
            pltpu.VMEM(grad_branch.shape, bf16),
            pltpu.VMEM((channels, grad_branch.shape[2]), bf16),
            pltpu.VMEM(cube, f32),
            pltpu.VMEM(cube, f32),
            pltpu.VMEM(cube, f32),
            pltpu.VMEM((CHIPS, 8, channels), f32),
            pltpu.VMEM((8, channels), f32),
            pltpu.VMEM((CHIPS, 8, channels), f32),
            pltpu.VMEM((2 * planes, 2 * CHIPS, channels), f32),
            pltpu.VMEM((8 * planes, channels), f32),
            pltpu.VMEM((CHIPS, channels), f32),
            pltpu.SemaphoreType.DMA((12,)),
            pltpu.SemaphoreType.DMA((12,)),
            pltpu.SemaphoreType.DMA((2,)),
            pltpu.SemaphoreType.DMA((rows_all.shape[0],)),
            *sum_scratch(*down_parts.shape[1:], bf16),
        ],
        compiler_params=comm_params(collective_id, 60),
        cost_estimate=lasting(58),
        name="recurrence_back",
    )(
        grad_branch,
        rows_all,
        gate_pre,
        conv_input,
        conv_out,
        decay_pre,
        input_pre,
        states,
        entering,
        halo,
        masks,
        after_masks,
        vectors,
        decay_blocks,
        input_blocks,
        down_parts,
        piece,
    )


def regrouped_kernel(back, devices, *refs):
    count = len(refs) // 2
    for source, target in zip(refs[:count], refs[count:]):
        step = source.shape[1] // devices
        for k in range(devices // 2):
            for e in range(2):
                split, joined = (2 * k + e) * step, (devices // 2 * e + k) * step
                start, end = (joined, split) if back else (split, joined)
                target[:, end : end + step] = source[:, start : start + step].astype(target.dtype)


def regrouped_columns(arrays, dtypes, back):
    devices = lax.axis_size("seq")
    return pl.pallas_call(
        functools.partial(regrouped_kernel, back, devices),
        out_shape=[jax.ShapeDtypeStruct(a.shape, dtype) for a, dtype in zip(arrays, dtypes)],
        in_specs=[VMEM] * len(arrays),
        out_specs=[VMEM] * len(arrays),
        compiler_params=pltpu.CompilerParams(vmem_limit_bytes=24 * 2**20),
        name="regrouped_columns",
    )(*arrays)


def to_chips_kernel(planes, pairs, *refs):
    ins, outs = refs[: len(pairs)], refs[len(pairs) :]
    for source, targets in zip(ins, pairs):
        width = source.shape[1] // (planes * 8)
        for z in range(planes):
            for p in range(CHIPS):
                for c in range(2):
                    k, at = targets[c]
                    start = ((z * CHIPS + p) * 2 + c) * width
                    outs[k][p, :, at + z * width : at + (z + 1) * width] = source[:, start : start + width]


def to_chips(weights, pairs, widths):
    planes = lax.axis_size("seq") // 8
    return pl.pallas_call(
        functools.partial(to_chips_kernel, planes, pairs),
        out_shape=[
            jax.ShapeDtypeStruct((CHIPS, weights[0].shape[0], width), weights[0].dtype) for width in widths
        ],
        in_specs=[VMEM] * len(weights),
        out_specs=[VMEM] * len(widths),
        name="to_chips",
    )(*weights)


def from_chips_kernel(planes, pairs, *refs):
    outs, ins = refs[-len(pairs) :], refs[: -len(pairs)]
    for target, sources in zip(outs, pairs):
        width = target.shape[1] // (planes * 8)
        for z in range(planes):
            for p in range(CHIPS):
                for c in range(2):
                    k, at = sources[c]
                    start = ((z * CHIPS + p) * 2 + c) * width
                    target[:, start : start + width] = ins[k][
                        p, :, at + z * width : at + (z + 1) * width
                    ].astype(jnp.float32)


def from_chips(parts, pairs, widths):
    planes = lax.axis_size("seq") // 8
    return pl.pallas_call(
        functools.partial(from_chips_kernel, planes, pairs),
        out_shape=[jax.ShapeDtypeStruct((parts[0].shape[1], width), jnp.float32) for width in widths],
        in_specs=[VMEM] * len(parts),
        out_specs=[VMEM] * len(widths),
        compiler_params=pltpu.CompilerParams(vmem_limit_bytes=32 * 2**20),
        name="from_chips",
    )(*parts)


def regrouped(values, axis, n):
    shape = values.shape
    split = shape[:axis] + (n // 2, 2, shape[axis] // n) + shape[axis + 1 :]
    return jnp.moveaxis(values.reshape(split), axis + 1, axis).reshape(shape)


def behind(value, *earlier):
    return lax.optimization_barrier((value, *earlier))[0]


def plane_body(
    tokens,
    starts,
    cotangent,
    norm_gain,
    gate_branch,
    input_branch,
    conv_weight,
    conv_bias,
    decay_gate,
    decay_bias,
    input_gate,
    input_bias,
    decay_param,
    out_proj,
    mlp_gain,
    mlp_gate,
    mlp_up,
    mlp_down,
):
    f32, bf16 = jnp.float32, jnp.bfloat16
    n = lax.axis_size("seq")
    planes = n // 8
    me, z, p, c, x, y = place()
    groups = column_groups(n)
    rows, width = tokens.shape
    rows_d, lru_width = gate_branch.shape
    head = decay_gate.shape[1]
    rows_r, rows_f = out_proj.shape[0], mlp_down.shape[0]
    channels = lru_width // CHIPS
    units = mlp_gate.shape[1] // CHIPS
    half_units = units // 2

    def column_gather(block):
        return lax.all_gather(block, "seq", axis=0, tiled=True, axis_index_groups=groups)

    def line_sum(parts):
        return lax.psum_scatter(
            parts, "seq", scatter_dimension=0, tiled=True, axis_index_groups=line_groups(n)
        )

    sibling = [(d, d + 1 - 2 * (d % 2)) for d in range(n)]

    def halves(values, axis):
        half = values.shape[axis] // 2
        return (
            lax.dynamic_slice_in_dim(values, c * half, half, axis),
            lax.dynamic_slice_in_dim(values, (1 - c) * half, half, axis),
        )

    def exchanged(values):
        return lax.ppermute(values, "seq", sibling)

    def product(left, right):
        return jnp.dot(left, right, preferred_element_type=f32)

    def product_t(left, right):
        return jnp.einsum("tk,nk->tn", left, right, preferred_element_type=f32)

    def weight_grad(left, right):
        return jnp.einsum("ta,tb->ab", left, right, preferred_element_type=f32)

    lanes = 128

    def row(values):
        return jnp.pad(values.astype(f32), (0, lanes - values.shape[0]))[None]

    small = jnp.concatenate(
        [
            row(norm_gain),
            row(mlp_gain),
            starts.astype(f32).reshape(rows // lanes, lanes),
            *[row(conv_weight[k]) for k in range(CW)],
            row(conv_bias),
            row(decay_bias),
            row(input_bias),
            row(decay_param),
            jnp.zeros((4, lanes), f32),
        ],
        axis=0,
    )
    half = channels // 2
    in_pairs = (((0, 0), (0, half)), ((0, channels), (0, channels + half)))
    (weights_in,) = to_chips([gate_branch, input_branch], in_pairs, [2 * channels])
    (swapped_in,) = plane_swap([weights_in], 2)
    whole_in = column_gather(swapped_in.reshape(CHIPS * rows_d, 2 * channels))
    tokens, cot, out_proj, mlp_down = regrouped_columns(
        [tokens, cotangent, out_proj, mlp_down], [bf16] * 4, False
    )
    mlp_pairs = (((0, 0), (1, 0)), ((0, half_units), (1, half_units)))
    mlp_pieces = to_chips([mlp_gate, mlp_up], mlp_pairs, [2 * half_units] * 2)
    gates = jnp.concatenate([decay_gate, input_gate], axis=1)
    small, decay_blocks, input_blocks, normed_all, first_piece = opening(
        behind(small, swapped_in), gates, tokens, mlp_pieces[0], 1
    )
    normed_all = normed_all.reshape(CHIPS * rows, width)
    small = small.transpose(1, 0, 2, 3)
    flags = 2 + rows // lanes
    gain_one = regrouped(small[:, :, 0, :rows_d].reshape(width), 0, n)
    gain_two = regrouped(small[:, :, 1, :rows_d].reshape(width), 0, n)
    all_flags = small[:, :, 2:flags].reshape(n * rows)
    vectors = lax.dynamic_slice_in_dim(
        small.reshape(planes, CHIPS, 2, 16, lanes), p, 1, axis=1
    )[:, 0, :, flags : flags + CW + 4, :rows_r]
    vectors = vectors.transpose(2, 1, 0, 3).reshape(CW + 4, channels)
    param = vectors[CW + 3]
    vectors = vectors.at[CW + 3].set(-rate_scale * jax.nn.softplus(param))

    running = jnp.ones((n * rows,), f32)
    masks_all = [running]
    for offset in range(1, CW):
        earlier = jnp.concatenate([jnp.zeros((offset - 1,), f32), all_flags[: n * rows - (offset - 1)]])
        running = running * (1.0 - earlier)
        masks_all.append(running)
    masks_all = jnp.stack(masks_all).reshape(CW, planes, CHIPS, 2, rows)

    def own_blocks(values):
        return lax.dynamic_slice(
            values,
            (0, z, 0, c, 0),
            (values.shape[0], 1, CHIPS, 1, values.shape[4]),
        )[:, 0, :, 0]

    after_masks = masks_all[..., :8].reshape(CW, n, 8)
    after_masks = jnp.concatenate([after_masks[:, 1:], jnp.zeros((CW, 1, 8), f32)], axis=1)
    after_masks = own_blocks(after_masks.reshape(CW, planes, CHIPS, 2, 8)).transpose(1, 2, 0)
    masks_all = jnp.concatenate([all_flags.reshape(1, planes, CHIPS, 2, rows), masks_all[1:]], axis=0)
    masks = own_blocks(masks_all).transpose(1, 2, 0)

    rows_all = column_gather(behind(jnp.concatenate([out_proj, mlp_down], axis=0), swapped_in))
    rows_all = rows_all.reshape(2 * planes, rows_r + rows_f, width)

    gate_pre = product(normed_all, whole_in[:, :channels])
    cube = (CHIPS, rows, channels)
    gate_pre = gate_pre.reshape(cube)
    conv_input = product(normed_all, whole_in[:, channels:]).astype(bf16).reshape(cube)
    conv_out, conv_low, decay_pre, input_pre, states, mixed, entering, halo, cot_all, second_piece = recurrence(
        gate_pre,
        conv_input,
        masks,
        vectors,
        decay_blocks,
        input_blocks,
        cot,
        mlp_pieces[1],
        6,
    )
    whole_mlp = [
        column_gather(part.reshape(CHIPS * rows_d, 2 * half_units)) for part in (first_piece, second_piece)
    ]
    cot_all = cot_all.reshape(CHIPS * rows, width)
    middle, two_all = middle_of(mixed, rows_all, tokens, gain_two, 7)
    mixed = mixed.reshape(CHIPS * rows, channels)
    two_all = two_all.reshape(CHIPS * rows, width)

    cot_other = exchanged(cot_all)
    hidden_zero, first_grad, first_low = feed_forward(0, two_all, cot_all, whole_mlp[0], rows_all, (), 8)
    hidden_one, second_grad, two_parts = feed_forward(
        1, two_all, cot_all, whole_mlp[1], rows_all, (whole_mlp[0], first_low), 14
    )
    piece_grads = [line_sum(first_grad), line_sum(second_grad)]
    grad_middle, grad_mlp_gain, grad_branch, down_grad, down_parts = grads_of_middle(
        two_parts.reshape(CHIPS, rows, width),
        middle,
        cot,
        gain_two,
        (hidden_zero, hidden_one),
        rows_all,
        cot_all,
        cot_other,
        9,
    )
    branch_cube, grad_branch = grad_branch, grad_branch.reshape(CHIPS * rows, width)

    mixed_own, mixed_other = halves(mixed, 1)
    out_grad = weight_grad(mixed_own, grad_branch) + weight_grad(
        exchanged(mixed_other), exchanged(grad_branch)
    )
    out_grad = out_grad.astype(bf16)
    grad_out_proj = line_sum(out_grad)
    grad_mlp_down = line_sum(down_grad.reshape(planes * rows_f, width))
    branch_cube = behind(branch_cube, out_grad)
    in_low, grad_decay_low, grad_input_low, sums, down_sum, first_swapped = recurrence_back(
        branch_cube,
        rows_all,
        gate_pre,
        conv_input,
        conv_out,
        decay_pre,
        input_pre,
        states,
        entering,
        halo,
        masks,
        after_masks,
        vectors,
        decay_blocks,
        input_blocks,
        down_parts,
        piece_grads[0].reshape(CHIPS, rows_d, 2 * half_units),
        12,
    )
    sums = sums.at[CW + 3].multiply(-rate_scale * jax.nn.sigmoid(param))
    low_cube = in_low
    in_low = low_cube.reshape(CHIPS * rows, 2 * channels)
    flat = (CHIPS * rows, channels)
    conv_low, grad_decay_low, grad_input_low = (
        a.reshape(flat) for a in (conv_low, grad_decay_low, grad_input_low)
    )

    normed_own, normed_other = halves(normed_all, 1)
    in_grads = weight_grad(normed_own, in_low) + weight_grad(exchanged(normed_other), exchanged(in_low))
    in_total = in_grads.astype(bf16)
    in_grads = line_sum(in_total)
    low_cube = behind(low_cube, in_total)
    vector_parts = sums.reshape(CW + 4, 2, planes, rows_r).transpose(2, 1, 0, 3)
    vector_parts = jnp.pad(vector_parts, ((0, 0), (0, 0), (0, 0), (0, lanes - rows_r)))
    here = (jnp.arange(CHIPS) == p).astype(f32)[None, :, None, None, None]
    vector_parts = (vector_parts[:, None] * here).reshape(planes, 8, CW + 4, lanes)
    gain_parts = grad_mlp_gain.reshape(2, planes, CHIPS, 1, rows_d).transpose(1, 2, 0, 3, 4)
    gain_parts = jnp.pad(
        gain_parts.reshape(planes, 8, 1, rows_d), ((0, 0), (0, 0), (0, 7), (0, lanes - rows_d))
    )
    grad_tokens, small_grads, gate_grads, second_swapped = closing(
        low_cube,
        whole_in,
        tokens,
        gain_one,
        grad_middle,
        jnp.concatenate([vector_parts, gain_parts], axis=2),
        (conv_low, grad_decay_low, grad_input_low),
        piece_grads[1].reshape(CHIPS, rows_d, 2 * half_units),
        head,
        13,
    )
    grad_mlp_gate, grad_mlp_up = from_chips(
        [first_swapped, second_swapped], mlp_pairs, [mlp_gate.shape[1]] * 2
    )
    block_out = middle + behind(down_sum, grad_tokens)
    block_out, grad_out_proj, grad_mlp_down = regrouped_columns(
        (block_out, *behind((grad_out_proj, grad_mlp_down), grad_tokens)), [bf16, f32, f32], True
    )
    in_out = plane_swap([in_grads.reshape(CHIPS, rows_d, 2 * channels)], 16)
    grad_gate_branch, grad_input_branch = from_chips(in_out, in_pairs, [lru_width] * 2)
    vector_grads = small_grads[: CW + 4, :rows_r]
    return (
        block_out,
        grad_tokens,
        small_grads[CW + 12, :rows_d],
        grad_gate_branch,
        grad_input_branch,
        vector_grads[:CW],
        vector_grads[CW],
        gate_grads[:, :head],
        vector_grads[CW + 1],
        gate_grads[:, head:],
        vector_grads[CW + 2],
        vector_grads[CW + 3],
        grad_out_proj,
        small_grads[CW + 4, :rows_d],
        grad_mlp_gate,
        grad_mlp_up,
        grad_mlp_down,
    )


def solution(mesh):
    in_specs = (
        P("seq", None),
        P("seq"),
        P("seq", None),
        P("seq"),
        P("seq", None),
        P("seq", None),
        P(None, "seq"),
        P("seq"),
        P("seq", None),
        P("seq"),
        P("seq", None),
        P("seq"),
        P("seq"),
        P("seq", None),
        P("seq"),
        P("seq", None),
        P("seq", None),
        P("seq", None),
    )
    out_specs = (
        P("seq", None),
        P("seq", None),
        P("seq"),
        P("seq", None),
        P("seq", None),
        P(None, "seq"),
        P("seq"),
        P("seq", None),
        P("seq"),
        P("seq", None),
        P("seq"),
        P("seq"),
        P("seq", None),
        P("seq"),
        P("seq", None),
        P("seq", None),
        P("seq", None),
    )
    body = plane_body if mesh.shape["seq"] == 2 * H else token_split_body
    return jax.shard_map(body, mesh=mesh, in_specs=in_specs, out_specs=out_specs, check_vma=False)
```

```python
import functools

import jax
import jax.numpy as jnp
from jax import lax
from jax.experimental import pallas as pl
from jax.experimental.pallas import tpu as pltpu
from jax.sharding import PartitionSpec as P

H = 16
CW = 4


epsilon = 1e-06
rate_scale = 8.0


def passed_along(block, axis, distance):
    devices = range(lax.axis_size(axis))
    route = [(i - distance, i) for i in devices if i - distance in devices]
    return lax.ppermute(block, axis, route)


def prefix(value, axis, combine, identity, reverse):
    peers, place = (lax.axis_size(axis), lax.axis_index(axis))
    everything = jax.tree.map(lambda part: lax.all_gather(part, axis), value)
    start = jax.tree.map(
        lambda part, zero: jnp.broadcast_to(jnp.asarray(zero, part.dtype), part.shape),
        value,
        identity,
    )

    def hop(k, before):
        at = peers - 1 - k if reverse else k
        reached = at > place if reverse else at < place
        new = combine(before, jax.tree.map(lambda part: part[at], everything))
        return jax.tree.map(lambda a, b: jnp.where(reached, a, b), new, before)

    return lax.fori_loop(0, peers, hop, start)


def gelu_tanh(values):
    return jax.nn.gelu(values, approximate=True)


def rms_norm(values, scales):
    return values * lax.rsqrt(jnp.mean(values * values, axis=-1, keepdims=True) + epsilon) * scales


def combine(earlier_part, later_part):
    return (earlier_part[0] * later_part[0], later_part[0] * earlier_part[1] + later_part[1])


def heads_product(values, weight):
    row_count, lru_width = values.shape
    shaped = values.reshape(row_count, H, lru_width // H)
    blocks = weight.reshape(H, lru_width // H, lru_width // H)
    return jnp.einsum("thi,hij->thj", shaped, blocks, preferred_element_type=jnp.float32).reshape(
        row_count, lru_width
    )


def heads_back(grads_low, weight):
    row_count, lru_width = grads_low.shape
    shaped = grads_low.reshape(row_count, H, lru_width // H)
    blocks = weight.reshape(H, lru_width // H, lru_width // H)
    return jnp.einsum("thj,hij->thi", shaped, blocks, preferred_element_type=jnp.float32).reshape(
        row_count, lru_width
    )


def heads_grad(values, grads_low):
    row_count, lru_width = values.shape
    left_side = values.reshape(row_count, H, lru_width // H)
    right_side = grads_low.reshape(row_count, H, lru_width // H)
    return jnp.einsum(
        "thi,thj->hij", left_side, right_side, preferred_element_type=jnp.float32
    ).reshape(lru_width, lru_width // H)


def lru_terms(decay_pre, input_pre, conv_out, decay_param, flag_rows):
    log_decay = -rate_scale * jax.nn.sigmoid(decay_pre) * jax.nn.softplus(decay_param)
    keep_rows = 1.0 - flag_rows[:, None]
    coefficient = jnp.exp(log_decay) * keep_rows
    scale_in = flag_rows[:, None] + keep_rows * jnp.sqrt(-jnp.expm1(2.0 * log_decay))
    drive_term = scale_in * jax.nn.sigmoid(input_pre) * conv_out
    return (coefficient, drive_term)


def build_masks(flag_rows):
    row_count = flag_rows.shape[0]
    running = jnp.ones((row_count,), jnp.float32)
    masks = [running]
    for offset in range(1, CW):
        earlier_flags = jnp.concatenate(
            [jnp.zeros((offset - 1,), jnp.float32), flag_rows[: row_count - (offset - 1)]]
        )
        running = running * (1.0 - earlier_flags)
        masks.append(running)
    return masks


def send_mask(flag_rows):
    tail_keep = 1.0 - flag_rows[flag_rows.shape[0] - (CW - 1) :]
    after_rows = jnp.cumprod(tail_keep[::-1])[::-1]
    return jnp.concatenate([after_rows[1:], jnp.ones((1,), jnp.float32)])


def conv_local(padded, weight, bias, masks):
    row_count = masks[0].shape[0]
    conv_total = bias + jnp.zeros((row_count, padded.shape[1]), jnp.float32)
    for offset in range(CW):
        lead = CW - 1 - offset
        conv_total = conv_total + weight[offset] * (
            padded[lead : lead + row_count] * masks[offset][:, None]
        )
    return conv_total


def mlp_act(gate_values, up_values):
    return gelu_tanh(gate_values) * up_values


def token_split_body(
    tokens,
    starts,
    cotangent,
    norm_gain,
    gate_branch,
    input_branch,
    conv_weight,
    conv_bias,
    decay_gate,
    decay_bias,
    input_gate,
    input_bias,
    decay_param,
    out_proj,
    mlp_gain,
    mlp_gate,
    mlp_up,
    mlp_down,
):
    (
        whole_norm_gain,
        whole_gate_branch,
        whole_input_branch,
        whole_conv_weight,
        whole_conv_bias,
        whole_decay_gate,
        whole_decay_bias,
        whole_input_gate,
        whole_input_bias,
        whole_decay_param,
        whole_out_proj,
    ) = (
        lax.all_gather(norm_gain, "seq", axis=0, tiled=True),
        lax.all_gather(gate_branch, "seq", axis=0, tiled=True),
        lax.all_gather(input_branch, "seq", axis=0, tiled=True),
        lax.all_gather(conv_weight, "seq", axis=1, tiled=True),
        lax.all_gather(conv_bias, "seq", axis=0, tiled=True),
        lax.all_gather(decay_gate, "seq", axis=0, tiled=True),
        lax.all_gather(decay_bias, "seq", axis=0, tiled=True),
        lax.all_gather(input_gate, "seq", axis=0, tiled=True),
        lax.all_gather(input_bias, "seq", axis=0, tiled=True),
        lax.all_gather(decay_param, "seq", axis=0, tiled=True),
        lax.all_gather(out_proj, "seq", axis=0, tiled=True),
    )
    flag_rows = starts.astype(jnp.float32)
    row_count = tokens.shape[0]
    values = tokens.astype(jnp.float32)
    normed = rms_norm(values, whole_norm_gain.astype(jnp.float32)).astype(jnp.bfloat16)
    gate_pre = jnp.dot(normed, whole_gate_branch, preferred_element_type=jnp.float32)
    gate_act = gelu_tanh(gate_pre)
    conv_input = jnp.dot(normed, whole_input_branch, preferred_element_type=jnp.float32).astype(
        jnp.bfloat16
    )
    lru_width = conv_input.shape[1]
    alive_rows = send_mask(flag_rows)
    masks = build_masks(flag_rows)
    outgoing = conv_input[row_count - (CW - 1) :] * alive_rows[:, None].astype(jnp.bfloat16)
    incoming = passed_along(outgoing, "seq", 1)
    padded = jnp.concatenate([incoming, conv_input], axis=0).astype(jnp.float32)
    conv_out = conv_local(
        padded, whole_conv_weight.astype(jnp.float32), whole_conv_bias.astype(jnp.float32), masks
    )
    conv_low = conv_out.astype(jnp.bfloat16)
    decay_pre = heads_product(conv_low, whole_decay_gate) + whole_decay_bias.astype(jnp.float32)
    input_pre = heads_product(conv_low, whole_input_gate) + whole_input_bias.astype(jnp.float32)
    param_full = whole_decay_param.astype(jnp.float32)
    coefficient, drive_term = lru_terms(decay_pre, input_pre, conv_out, param_full, flag_rows)
    cumulative, local_state = lax.associative_scan(combine, (coefficient, drive_term), axis=0)
    entering = prefix(
        (cumulative[-1], local_state[-1]),
        "seq",
        combine,
        (jnp.ones_like(cumulative[-1]), jnp.zeros_like(local_state[-1])),
        False,
    )
    incoming_state = entering[1]
    states = local_state + cumulative * incoming_state[None, :]
    mixed_rows = (states * gate_act).astype(jnp.bfloat16)
    middle = values + jnp.dot(mixed_rows, whole_out_proj, preferred_element_type=jnp.float32)
    whole_mlp_gain, whole_mlp_gate, whole_mlp_up, whole_mlp_down = (
        lax.all_gather(mlp_gain, "seq", axis=0, tiled=True),
        lax.all_gather(mlp_gate, "seq", axis=0, tiled=True),
        lax.all_gather(mlp_up, "seq", axis=0, tiled=True),
        lax.all_gather(mlp_down, "seq", axis=0, tiled=True),
    )
    gain_two = whole_mlp_gain.astype(jnp.float32)
    normed_two = rms_norm(middle, gain_two).astype(jnp.bfloat16)
    gate_mlp = jnp.dot(normed_two, whole_mlp_gate, preferred_element_type=jnp.float32)
    up_mlp = jnp.dot(normed_two, whole_mlp_up, preferred_element_type=jnp.float32)
    hidden = mlp_act(gate_mlp, up_mlp).astype(jnp.bfloat16)
    result = middle + jnp.dot(hidden, whole_mlp_down, preferred_element_type=jnp.float32)
    block_out = result.astype(jnp.bfloat16)
    back_mlp_gain, back_mlp_gate, back_mlp_up, back_mlp_down = (
        lax.all_gather(mlp_gain, "seq", axis=0, tiled=True),
        lax.all_gather(mlp_gate, "seq", axis=0, tiled=True),
        lax.all_gather(mlp_up, "seq", axis=0, tiled=True),
        lax.all_gather(mlp_down, "seq", axis=0, tiled=True),
    )
    grad_mlp_down = jnp.einsum("tf,td->fd", hidden, cotangent, preferred_element_type=jnp.float32)
    grad_hidden = jnp.einsum(
        "td,fd->tf", cotangent, back_mlp_down, preferred_element_type=jnp.float32
    )
    unused_act, pull_act = jax.vjp(mlp_act, gate_mlp, up_mlp)
    grad_gate_full, grad_up_full = pull_act(grad_hidden)
    grad_gate_low = grad_gate_full.astype(jnp.bfloat16)
    grad_up_low = grad_up_full.astype(jnp.bfloat16)
    grad_mlp_gate = jnp.einsum(
        "td,tf->df", normed_two, grad_gate_low, preferred_element_type=jnp.float32
    )
    grad_mlp_up = jnp.einsum(
        "td,tf->df", normed_two, grad_up_low, preferred_element_type=jnp.float32
    )
    grad_normed_two = jnp.einsum(
        "tf,df->td", grad_gate_low, back_mlp_gate, preferred_element_type=jnp.float32
    ) + jnp.einsum("tf,df->td", grad_up_low, back_mlp_up, preferred_element_type=jnp.float32)
    unused_norm, pull_norm = jax.vjp(rms_norm, middle, back_mlp_gain.astype(jnp.float32))
    grad_middle_norm, grad_mlp_gain = pull_norm(grad_normed_two)
    mlp_sums = (
        lax.psum_scatter(grad_mlp_gain, "seq", scatter_dimension=0, tiled=True),
        lax.psum_scatter(grad_mlp_gate, "seq", scatter_dimension=0, tiled=True),
        lax.psum_scatter(grad_mlp_up, "seq", scatter_dimension=0, tiled=True),
        lax.psum_scatter(grad_mlp_down, "seq", scatter_dimension=0, tiled=True),
    )
    grad_middle = cotangent.astype(jnp.float32) + grad_middle_norm
    grad_branch = grad_middle.astype(jnp.bfloat16)
    (
        back_norm_gain,
        back_gate_branch,
        back_input_branch,
        back_conv_weight,
        back_conv_bias,
        back_decay_gate,
        back_decay_bias,
        back_input_gate,
        back_input_bias,
        back_decay_param,
        back_out_proj,
    ) = (
        lax.all_gather(norm_gain, "seq", axis=0, tiled=True),
        lax.all_gather(gate_branch, "seq", axis=0, tiled=True),
        lax.all_gather(input_branch, "seq", axis=0, tiled=True),
        lax.all_gather(conv_weight, "seq", axis=1, tiled=True),
        lax.all_gather(conv_bias, "seq", axis=0, tiled=True),
        lax.all_gather(decay_gate, "seq", axis=0, tiled=True),
        lax.all_gather(decay_bias, "seq", axis=0, tiled=True),
        lax.all_gather(input_gate, "seq", axis=0, tiled=True),
        lax.all_gather(input_bias, "seq", axis=0, tiled=True),
        lax.all_gather(decay_param, "seq", axis=0, tiled=True),
        lax.all_gather(out_proj, "seq", axis=0, tiled=True),
    )
    grad_out_proj = jnp.einsum(
        "tr,td->rd", mixed_rows, grad_branch, preferred_element_type=jnp.float32
    )
    grad_mixed = jnp.einsum(
        "td,rd->tr", grad_branch, back_out_proj, preferred_element_type=jnp.float32
    )
    grad_states = grad_mixed * gate_act
    unused_gelu, pull_gelu = jax.vjp(gelu_tanh, gate_pre)
    grad_gate_pre = pull_gelu(grad_mixed * states)[0].astype(jnp.bfloat16)
    shifted_coef = jnp.concatenate([coefficient[1:], jnp.ones((1, lru_width), jnp.float32)], axis=0)
    back_cumulative, back_local = lax.associative_scan(
        combine, (shifted_coef[::-1], grad_states[::-1]), axis=0
    )
    back_cumulative = back_cumulative[::-1]
    back_local = back_local[::-1]
    leaving = prefix(
        (coefficient[0] * back_cumulative[0], coefficient[0] * back_local[0]),
        "seq",
        combine,
        (jnp.ones_like(back_local[0]), jnp.zeros_like(back_local[0])),
        True,
    )
    incoming_adjoint = leaving[1]
    adjoint = back_local + back_cumulative * incoming_adjoint[None, :]
    previous = jnp.concatenate([incoming_state[None, :], states[:-1]], axis=0)

    def terms_only(decay_values, input_values, conv_values, param_values):
        return lru_terms(decay_values, input_values, conv_values, param_values, flag_rows)

    unused_terms, pull_terms = jax.vjp(
        terms_only, decay_pre, input_pre, conv_out, back_decay_param.astype(jnp.float32)
    )
    grad_decay_full, grad_input_full, grad_conv_direct, grad_decay_param = pull_terms(
        (adjoint * previous, adjoint)
    )
    grad_decay_bias = jnp.sum(grad_decay_full, axis=0)
    grad_input_bias = jnp.sum(grad_input_full, axis=0)
    grad_decay_low = grad_decay_full.astype(jnp.bfloat16)
    grad_input_low = grad_input_full.astype(jnp.bfloat16)
    grad_decay_gate = heads_grad(conv_low, grad_decay_low)
    grad_input_gate = heads_grad(conv_low, grad_input_low)
    grad_conv_out = (
        grad_conv_direct
        + heads_back(grad_decay_low, back_decay_gate)
        + heads_back(grad_input_low, back_input_gate)
    )

    def conv_only(padded_values, weight_values, bias_values):
        return conv_local(padded_values, weight_values, bias_values, masks)

    unused_conv, pull_conv = jax.vjp(
        conv_only, padded, back_conv_weight.astype(jnp.float32), back_conv_bias.astype(jnp.float32)
    )
    grad_padded, grad_conv_weight, grad_conv_bias = pull_conv(grad_conv_out)
    returned_rows = passed_along(grad_padded[: CW - 1], "seq", -1)
    addition = jnp.concatenate(
        [
            jnp.zeros((row_count - (CW - 1), lru_width), jnp.float32),
            returned_rows * alive_rows[:, None],
        ],
        axis=0,
    )
    grad_conv_input = (grad_padded[CW - 1 :] + addition).astype(jnp.bfloat16)
    grad_input_branch = jnp.einsum(
        "td,tr->dr", normed, grad_conv_input, preferred_element_type=jnp.float32
    )
    grad_gate_branch = jnp.einsum(
        "td,tr->dr", normed, grad_gate_pre, preferred_element_type=jnp.float32
    )
    grad_normed = jnp.einsum(
        "tr,dr->td", grad_conv_input, back_input_branch, preferred_element_type=jnp.float32
    ) + jnp.einsum("tr,dr->td", grad_gate_pre, back_gate_branch, preferred_element_type=jnp.float32)
    unused_first, pull_first = jax.vjp(rms_norm, values, back_norm_gain.astype(jnp.float32))
    grad_values_norm, grad_norm_gain = pull_first(grad_normed)
    grad_tokens = grad_middle + grad_values_norm
    rec_sums = (
        lax.psum_scatter(grad_norm_gain, "seq", scatter_dimension=0, tiled=True),
        lax.psum_scatter(grad_gate_branch, "seq", scatter_dimension=0, tiled=True),
        lax.psum_scatter(grad_input_branch, "seq", scatter_dimension=0, tiled=True),
        lax.psum_scatter(grad_conv_weight, "seq", scatter_dimension=1, tiled=True),
        lax.psum_scatter(grad_conv_bias, "seq", scatter_dimension=0, tiled=True),
        lax.psum_scatter(grad_decay_gate, "seq", scatter_dimension=0, tiled=True),
        lax.psum_scatter(grad_decay_bias, "seq", scatter_dimension=0, tiled=True),
        lax.psum_scatter(grad_input_gate, "seq", scatter_dimension=0, tiled=True),
        lax.psum_scatter(grad_input_bias, "seq", scatter_dimension=0, tiled=True),
        lax.psum_scatter(grad_decay_param, "seq", scatter_dimension=0, tiled=True),
        lax.psum_scatter(grad_out_proj, "seq", scatter_dimension=0, tiled=True),
    )
    return (
        block_out,
        grad_tokens,
        rec_sums[0],
        rec_sums[1],
        rec_sums[2],
        rec_sums[3],
        rec_sums[4],
        rec_sums[5],
        rec_sums[6],
        rec_sums[7],
        rec_sums[8],
        rec_sums[9],
        rec_sums[10],
        mlp_sums[0],
        mlp_sums[1],
        mlp_sums[2],
        mlp_sums[3],
    )


CHIPS = 4
MESH = pl.DeviceIdType.MESH


def place():
    me = lax.axis_index("seq")
    core = lax.rem(me, 2)
    x = lax.rem(lax.div(me, 2), 2)
    y = lax.rem(lax.div(me, 4), 2)
    return me, lax.div(me, 8), 2 * y + x, core, x, y


def column_groups(n):
    return [[8 * z + 2 * p + c for c in range(2) for z in range(n // 8)] for p in range(CHIPS)]


def line_groups(n):
    return [[8 * z + r for z in range(n // 8)] for r in range(8)]


def greet(devices):
    barrier = pltpu.get_barrier_semaphore()
    for device in devices:
        pl.semaphore_signal(barrier, inc=1, device_id=(device,), device_id_type=MESH)
    pl.semaphore_wait(barrier, len(devices))


def remote(source, target, send_sem, recv_sem, device):
    return pltpu.make_async_remote_copy(
        src_ref=source,
        dst_ref=target,
        send_sem=send_sem,
        recv_sem=recv_sem,
        device_id=(device,),
        device_id_type=MESH,
    )


def comm_params(collective_id, vmem_mib=None):
    return pltpu.CompilerParams(
        collective_id=collective_id,
        has_side_effects=True,
        vmem_limit_bytes=None if vmem_mib is None else vmem_mib * 2**20,
    )


def lasting(microseconds):
    return pl.CostEstimate(
        flops=int(microseconds * 1e9), bytes_accessed=int(microseconds * 3e6), transcendentals=0
    )


ANY = pl.BlockSpec(memory_space=pl.ANY)
VMEM = pl.BlockSpec(memory_space=pltpu.VMEM)


def plane_neighbours():
    me, z, p, c, x, y = place()
    x_dev, y_dev = me + 2 - 4 * x, me + 4 - 8 * y
    return (x_dev, y_dev, y_dev + 2 - 4 * x), (p + 1 - 2 * x, p + 2 - 4 * y, 3 - p)


def gather_steps(source, whole, send, recv, local, first):
    me, z, p, c, x, y = place()
    (x_dev, y_dev, d_dev), (p_x, p_y, p_d) = plane_neighbours()
    half = source.shape[0] // 2

    def copy(k, source, target, device):
        return remote(source, target, send.at[first + k], recv.at[first + k], device)

    to_x, to_y = copy(0, source, whole.at[p], x_dev), copy(1, source, whole.at[p], y_dev)
    low, high = whole.at[p_x, pl.ds(0, half)], whole.at[p_y, pl.ds(half, half)]
    on_y, on_x = copy(2, low, low, y_dev), copy(3, high, high, x_dev)
    own = pltpu.make_async_copy(source, whole.at[p], local)

    def begin():
        to_x.start()
        to_y.start()
        own.start()

    def forward():
        to_x.wait_recv()
        on_y.start()
        to_y.wait_recv()
        on_x.start()

    def end():
        to_x.wait_send()
        to_y.wait_send()
        on_y.wait()
        on_x.wait()
        own.wait()

    return begin, forward, end


def sum_scratch(rows, columns, dtype):
    whole, part = pltpu.VMEM((rows, columns), dtype), pltpu.VMEM((rows // 2, columns), dtype)
    return [whole] * 3 + [part] * 4 + [pltpu.SemaphoreType.DMA((6,)), pltpu.SemaphoreType.DMA((6,)), pltpu.SemaphoreType.DMA((3,))]


def sum_steps(part, own, from_x, from_y, diag_x, diag_y, on_x, on_y, send, recv, local):
    me, z, p, c, x, y = place()
    (x_dev, y_dev, d_dev), (p_x, p_y, p_d) = plane_neighbours()
    half = part.shape[1] // 2
    low, high = pl.ds(0, half), pl.ds(half, half)
    copies = [
        remote(part.at[p_d, low], diag_x, send.at[0], recv.at[0], x_dev),
        remote(part.at[p_d, high], diag_y, send.at[1], recv.at[1], y_dev),
        remote(part.at[p_x, low], from_x.at[low], send.at[2], recv.at[2], x_dev),
        remote(part.at[p_y, high], from_y.at[high], send.at[3], recv.at[3], y_dev),
    ]
    locals_ = [
        pltpu.make_async_copy(part.at[p_y, low], on_y, local.at[0]),
        pltpu.make_async_copy(part.at[p_x, high], on_x, local.at[1]),
        pltpu.make_async_copy(part.at[p], own, local.at[2]),
    ]
    to_y = remote(on_y, from_y.at[low], send.at[4], recv.at[4], y_dev)
    to_x = remote(on_x, from_x.at[high], send.at[5], recv.at[5], x_dev)

    def add_into(target, addend):
        @pl.loop(0, half // 16)
        def add_rows(i):
            at = pl.ds(pl.multiple_of(i * 16, 16), 16)
            target[at, :] = (
                target[at, :].astype(jnp.float32) + addend[at, :].astype(jnp.float32)
            ).astype(target.dtype)

    def begin():
        for copy in copies + locals_:
            copy.start()

    def forward():
        locals_[0].wait()
        copies[0].wait_recv()
        add_into(on_y, diag_x)
        to_y.start()
        locals_[1].wait()
        copies[1].wait_recv()
        add_into(on_x, diag_y)
        to_x.start()

    def end():
        locals_[2].wait()
        copies[2].wait_recv()
        copies[3].wait_recv()
        to_y.wait()
        to_x.wait()
        for copy in copies:
            copy.wait_send()

    return begin, forward, end


def sixteen(i):
    return pl.ds(pl.multiple_of(i * 16, 16), 16)


def fetch_rows(rows_all, first, start, target, sems):
    count = sems.shape[0]
    rows = target.shape[0] // count
    return [
        pltpu.make_async_copy(
            rows_all.at[first + k, pl.ds(start, rows)], target.at[pl.ds(k * rows, rows)], sems.at[k]
        )
        for k in range(count)
    ]


def computed_scratch(rows, columns, dtype):
    f32, bf16 = jnp.float32, jnp.bfloat16
    whole, half = (rows, columns), (rows // 2, columns)
    shapes = [(whole, bf16), (whole, f32)] + [(half, f32)] * 2 + [(half, bf16)] * 6 + [(half, dtype)] * 4
    return [pltpu.VMEM(*shape) for shape in shapes] + [pltpu.SemaphoreType.DMA((6,))] * 2


def computed_sum(product, sent_d, own, kept_x, kept_y, *refs):
    sent_x, sent_y, from_x, from_y, diag_x, diag_y, joint_x, joint_y, also_x, also_y, send, recv = refs
    (x_dev, y_dev, d_dev), (p_x, p_y, p_d) = plane_neighbours()
    p = place()[2]
    rows, width = own.shape
    half = rows // 2
    low, high = pl.ds(0, half), pl.ds(half, half)
    tile = 512

    def into(chip, at, target):
        @pl.loop(0, width // tile)
        def product_tile(k):
            columns = pl.ds(pl.multiple_of(k * tile, tile), tile)
            target[:, columns] = product(chip, at, columns).astype(target.dtype)

    def copy(k, source, target, device):
        return remote(source, target, send.at[k], recv.at[k], device)

    first = [copy(0, sent_d.at[low], diag_x, x_dev), copy(1, sent_d.at[high], diag_y, y_dev)]
    second = [copy(2, sent_x, from_x, x_dev), copy(3, sent_y, from_y, y_dev)]
    third = [copy(4, joint_y, also_y, y_dev), copy(5, joint_x, also_x, x_dev)]

    def begin():
        into(p_d, slice(None), sent_d)
        for sent in first:
            sent.start()
        into(p_x, low, sent_x)
        into(p_y, high, sent_y)
        for sent in second:
            sent.start()
        into(p_y, low, kept_y)
        into(p_x, high, kept_x)
        into(p, slice(None), own)

    def add(target, kept, addend):
        @pl.loop(0, half // 16)
        def add_rows(i):
            at = sixteen(i)
            target[at, :] = (kept[at, :] + addend[at, :].astype(jnp.float32)).astype(target.dtype)

    def forward():
        first[0].wait_recv()
        add(joint_y, kept_y, diag_x)
        third[0].start()
        first[1].wait_recv()
        add(joint_x, kept_x, diag_y)
        third[1].start()

    def end():
        for sent in first:
            sent.wait_send()
        for sent in second + third:
            sent.wait()

    def total(i, j):
        at = sixteen(j)
        parts = (from_x, also_y) if i == 0 else (also_x, from_y)
        here = pl.ds(pl.multiple_of(i * half + j * 16, 16), 16)
        return here, own[here, :] + parts[0][at, :].astype(jnp.float32) + parts[1][at, :].astype(jnp.float32)

    return begin, forward, end, total


def middle_kernel(
    mixed, rows_all, tokens, gain, cot, middle, whole, cot_other, normed, out_here, send, recv, local, loads, *sums
):
    me, z, p, c, x, y = place()
    sibling = me + 1 - 2 * c
    greet((*plane_neighbours()[0][:2], sibling))
    to_sibling = remote(cot, cot_other, send.at[4], recv.at[4], sibling)
    to_sibling.start()
    f32, bf16 = jnp.float32, jnp.bfloat16
    fetched = fetch_rows(rows_all, 0, 0, out_here, loads)
    for copy in fetched:
        copy.start()
    for copy in fetched:
        copy.wait()

    def product(chip, at, columns):
        return jnp.dot(mixed[chip, at, :], out_here[:, columns], preferred_element_type=f32)

    *steps, total = computed_sum(product, *sums)
    for step in steps:
        step()
    for i in range(2):

        @pl.loop(0, tokens.shape[0] // 32)
        def norm_rows(j):
            at, values = total(i, j)
            values = tokens[at, :].astype(f32) + values
            middle[at, :] = values
            inverse = lax.rsqrt(jnp.mean(values * values, axis=-1, keepdims=True) + epsilon)
            normed[at, :] = (values * inverse * gain[...]).astype(bf16)

    for step in gather_steps(normed, whole, send, recv, local, 0):
        step()
    to_sibling.wait()


def middle_of(mixed, rows_all, tokens, gain, cot, collective_id):
    rows, width = tokens.shape
    channels = mixed.shape[2]
    f32, bf16 = jnp.float32, jnp.bfloat16
    return pl.pallas_call(
        middle_kernel,
        out_shape=[
            jax.ShapeDtypeStruct((rows, width), f32),
            jax.ShapeDtypeStruct((CHIPS, rows, width), bf16),
            jax.ShapeDtypeStruct(cot.shape, cot.dtype),
        ],
        in_specs=[VMEM, ANY, VMEM, VMEM, ANY],
        out_specs=[VMEM, ANY, ANY],
        scratch_shapes=[
            pltpu.VMEM((rows, width), bf16),
            pltpu.VMEM((channels, width), bf16),
            pltpu.SemaphoreType.DMA((5,)),
            pltpu.SemaphoreType.DMA((5,)),
            pltpu.SemaphoreType.DMA,
            pltpu.SemaphoreType.DMA((rows_all.shape[0],)),
            *computed_scratch(rows, width, f32),
        ],
        compiler_params=comm_params(collective_id, 60),
        cost_estimate=lasting(75),
        name="middle",
    )(mixed, rows_all, tokens, gain[None], cot)


def feed_forward_kernel(
    piece,
    two,
    cot,
    weights,
    down,
    *refs,
):
    last = piece == 1
    if last:
        earlier, hidden, grad, parts, earlier_here, *refs = refs
    else:
        hidden, grad, parts, *refs = refs
    low, two_here, two_there, cot_here, weights_here, down_here, low_there, send, recv, loads, down_loads = refs
    me, z, p, c, x, y = place()
    sibling = me + 1 - 2 * c
    greet((sibling,))
    f32, bf16 = jnp.float32, jnp.bfloat16
    tokens, width = two.shape
    units = hidden.shape[1]
    half = width // 2
    pairs = [
        (two, two_here),
        (weights, weights_here),
        (cot, cot_here),
    ]
    if last:
        pairs.append((earlier, earlier_here))
    fetched = [pltpu.make_async_copy(a, b, loads.at[k]) for k, (a, b) in enumerate(pairs)]
    count = down_loads.shape[0]
    fetched[3:3] = fetch_rows(down, count * piece, down.shape[1] - units // count, down_here, down_loads)
    for copy in fetched:
        copy.start()
    other_half = two.at[:, pl.ds(pl.multiple_of((1 - c) * half, 128), half)]
    two_swap = remote(other_half, two_there, send.at[0], recv.at[0], sibling)
    two_swap.start()
    for copy in fetched[: 3 + count]:
        copy.wait()
    tile, block = 256, 512

    def dot_t(left, right):
        return lax.dot_general(left, right, (((1,), (1,)), ((), ())), preferred_element_type=f32)

    def dot_first(left, right):
        return lax.dot_general(left, right, (((0,), (0,)), ((), ())), preferred_element_type=f32)

    low_swaps = []
    for t in range(units // tile):
        gate_at, up_at = pl.ds(t * tile, tile), pl.ds(units + t * tile, tile)

        @pl.loop(0, tokens // block)
        def rows_block(j):
            at = pl.ds(pl.multiple_of(j * block, block), block)
            v = jnp.dot(two_here[at, :], weights_here[:, gate_at], preferred_element_type=f32)
            up = jnp.dot(two_here[at, :], weights_here[:, up_at], preferred_element_type=f32)
            grad_hidden = dot_t(cot_here[at, :], down_here[gate_at, :])
            square = v * v
            bent = jnp.tanh(v * (GELU_A + GELU_A * GELU_B * square))
            rising = 0.5 + 0.5 * bent
            act = v * rising
            slope = rising + 0.5 * v * (1.0 - bent * bent) * (GELU_A + 3.0 * GELU_A * GELU_B * square)
            hidden[at, gate_at] = (act * up).astype(bf16)
            low[at, gate_at] = (grad_hidden * up * slope).astype(bf16)
            low[at, up_at] = (grad_hidden * act).astype(bf16)

        for k, columns in enumerate((gate_at, up_at)):
            sems = 1 + 2 * t + k
            low_swaps.append(
                remote(low.at[:, columns], low_there.at[:, columns], send.at[sems], recv.at[sems], sibling)
            )
            low_swaps[-1].start()
    for copy in fetched[3 + count :]:
        copy.wait()

    @pl.loop(0, tokens // block)
    def parts_block(j):
        at = pl.ds(pl.multiple_of(j * block, block), block)

        @pl.loop(0, width // block)
        def parts_tile(k):
            columns = pl.ds(pl.multiple_of(k * block, block), block)
            values = dot_t(low[at, :], weights_here[columns, :])
            if last:
                values = values + earlier_here[at, columns]
            parts[at, columns] = values.astype(parts.dtype)

    two_swap.wait()
    for copy in low_swaps:
        copy.wait()

    @pl.loop(0, half // block)
    def grad_block(m):
        here = pl.ds(pl.multiple_of(c * half + m * block, 128), block)
        there = pl.ds(pl.multiple_of(m * block, block), block)

        @pl.loop(0, 2 * units // block)
        def grad_tile(k):
            columns = pl.ds(pl.multiple_of(k * block, block), block)
            grad[there, columns] = (
                dot_first(two_here[:, here], low[:, columns]) + dot_first(two_there[:, there], low_there[:, columns])
            ).astype(bf16)


def feed_forward(piece, two, cot, weights, down, earlier, collective_id):
    tokens, width = two.shape
    units = weights.shape[1] // 2
    bf16 = jnp.bfloat16
    out_shape = [
        jax.ShapeDtypeStruct((tokens, units), bf16),
        jax.ShapeDtypeStruct((width // 2, 2 * units), bf16),
    ]
    low = pltpu.VMEM((tokens, 2 * units), bf16)
    scratch = []
    if earlier:
        out_shape.append(jax.ShapeDtypeStruct((tokens, width), bf16))
        scratch = [pltpu.VMEM((tokens, width), jnp.float32)]
    else:
        out_shape.append(jax.ShapeDtypeStruct((tokens, width), jnp.float32))
    swaps = 1 + 2 * (units // 256)
    return pl.pallas_call(
        functools.partial(feed_forward_kernel, piece),
        out_shape=out_shape,
        in_specs=[ANY] * (4 + len(earlier)),
        out_specs=[VMEM] * 3,
        scratch_shapes=[
            *scratch,
            low,
            pltpu.VMEM((tokens, width), bf16),
            pltpu.VMEM((tokens, width // 2), bf16),
            pltpu.VMEM((tokens, width), bf16),
            pltpu.VMEM(weights.shape, bf16),
            pltpu.VMEM((units, width), bf16),
            low,
            pltpu.SemaphoreType.DMA((swaps,)),
            pltpu.SemaphoreType.DMA((swaps,)),
            pltpu.SemaphoreType.DMA((3 + len(earlier),)),
            pltpu.SemaphoreType.DMA((down.shape[0] // 2,)),
        ],
        compiler_params=comm_params(collective_id, 60),
        cost_estimate=lasting(35),
        name="feed_forward",
    )(two, cot, weights, down, *earlier)


def norm_back_rows(values, gain, grad, rest):
    inverse = lax.rsqrt(jnp.mean(values * values, axis=-1, keepdims=True) + epsilon)
    scaled = gain * grad
    pull = jnp.mean(scaled * values, axis=-1, keepdims=True) * (inverse * inverse * inverse)
    return rest + inverse * scaled - values * pull, grad * values * inverse


def grads_of_middle_kernel(
    parts,
    middle,
    cot,
    gain,
    hidden_zero,
    hidden_one,
    down,
    cot_all,
    cot_other,
    mixed_zero,
    mixed_one,
    grad_middle,
    grad_gain,
    whole,
    row_grads,
    down_parts,
    branch,
    branch_all,
    branch_other,
    mixed_here,
    mixed_there,
    out_sum,
    hidden_here,
    hidden_other,
    down_here,
    cot_here,
    cot_there,
    *scratch,
):
    sums, (send, recv, local, loads, down_loads) = scratch[:10], scratch[10:]
    me, z, p, c, x, y = place()
    f32, bf16 = jnp.float32, jnp.bfloat16
    sibling = me + 1 - 2 * c
    greet((*plane_neighbours()[0][:2], sibling))
    own, from_x, from_y = sums[:3]
    begin, forward, end = sum_steps(parts, *sums)
    begin()
    half = hidden_zero.shape[1]
    swaps = [remote(hidden, hidden_other, send.at[4], recv.at[4], sibling) for hidden in (hidden_one, hidden_zero)]
    mixed_swaps = [remote(mixed, mixed_there, send.at[9], recv.at[9], sibling) for mixed in (mixed_one, mixed_zero)]
    mixed_loads = [pltpu.make_async_copy(mixed, mixed_here, loads.at[4]) for mixed in (mixed_zero, mixed_one)]

    @pl.when(c == 0)
    def send_one():
        swaps[0].start()
        mixed_swaps[0].start()
        mixed_loads[0].start()

    @pl.when(c == 1)
    def send_zero():
        swaps[1].start()
        mixed_swaps[1].start()
        mixed_loads[1].start()

    fetched = [
        pltpu.make_async_copy(source, target, loads.at[k])
        for k, (source, target) in enumerate(
            (
                (hidden_zero, hidden_here.at[:, pl.ds(0, half)]),
                (hidden_one, hidden_here.at[:, pl.ds(half, half)]),
                (cot_all, cot_here),
                (cot_other, cot_there),
            )
        )
    ]
    count = down_loads.shape[0]
    down_fetched = fetch_rows(down, 0, down.shape[1] - down_here.shape[0] // count, down_here, down_loads)
    for copy in fetched + down_fetched:
        copy.start()
    for copy in fetched[:4]:
        copy.wait()
    swaps[0].wait()
    tile = 256

    planes = row_grads.shape[0]
    units = half // planes
    above = row_grads.shape[1] - units

    def grad_tiles(m):
        rows_here = pl.ds(pl.multiple_of(c * half + m * tile, 128), tile)

        @pl.loop(0, cot_all.shape[1] // (2 * tile))
        def grad_tile(k):
            columns = pl.ds(pl.multiple_of(k * 2 * tile, 128), 2 * tile)

            def dot_t(left, right):
                return lax.dot_general(left, right, (((0,), (0,)), ((), ())), preferred_element_type=f32)

            values = (
                dot_t(hidden_here[:, rows_here], cot_here[:, columns])
                + dot_t(hidden_other[:, m * tile : (m + 1) * tile], cot_there[:, columns])
            ).astype(bf16)
            for j in range(planes):
                start, stop = max(j * units, m * tile), min((j + 1) * units, (m + 1) * tile)
                if start < stop:
                    row_grads[j, above + start - j * units : above + stop - j * units, columns] = values[
                        start - m * tile : stop - m * tile
                    ]

    grad_tiles(0)
    forward()
    for m in range(1, half // tile):
        grad_tiles(m)
    end()
    rows, width = middle.shape

    def norm_rows(i, total):
        at = sixteen(i)
        grad = own[at, :].astype(f32) + from_x[at, :].astype(f32) + from_y[at, :].astype(f32)
        given, terms = norm_back_rows(middle[at, :], gain[...], grad, cot[at, :].astype(f32))
        grad_middle[at, :] = given
        branch[at, :] = given.astype(bf16)
        return total + terms[:8] + terms[8:]

    total = lax.fori_loop(0, rows // 16, norm_rows, jnp.zeros((8, width), f32))
    grad_gain[...] = jnp.sum(total, axis=0, keepdims=True)
    begin, forward, end = gather_steps(branch, branch_all, send, recv, local, 0)
    (p_x, p_y, p_d) = plane_neighbours()[1]

    def to_sibling(k, chip, source):
        return remote(source, branch_other.at[chip], send.at[5 + k], recv.at[5 + k], sibling)

    shares = [to_sibling(0, p, branch)] + [
        to_sibling(1 + k, chip, branch_all.at[chip]) for k, chip in enumerate((p_x, p_y, p_d))
    ]
    begin()
    shares[0].start()
    for copy in down_fetched + [mixed_loads[0], mixed_swaps[0]]:
        copy.wait()

    def down_tiles(j):
        @pl.loop(0, width // (2 * tile))
        def down_tile(k):
            columns = pl.ds(pl.multiple_of(k * 2 * tile, 128), 2 * tile)
            down_parts[j, :, columns] = jnp.dot(
                hidden_here[pl.ds(pl.multiple_of(j * rows, 16), rows), :],
                down_here[:, columns],
                preferred_element_type=f32,
            ).astype(bf16)

    pl.loop(0, CHIPS)(down_tiles)

    def out_tiles(mixed, branches, chips, finish):
        @pl.loop(0, width // (2 * tile))
        def out_tile(k):
            columns = pl.ds(pl.multiple_of(k * 2 * tile, 128), 2 * tile)
            values = out_sum[:, columns]
            for chip in chips:
                values = values + lax.dot_general(
                    mixed[pl.ds(pl.multiple_of(chip * rows, 16), rows), :],
                    branches[chip, :, columns],
                    (((0,), (0,)), ((), ())),
                    preferred_element_type=f32,
                )
            if finish:
                for j in range(planes):
                    row_grads[j, 0:above, columns] = values[j * above : (j + 1) * above].astype(bf16)
            else:
                out_sum[:, columns] = values

    forward()
    shares[1].start()
    shares[2].start()
    out_sum[...] = jnp.zeros_like(out_sum)
    out_tiles(mixed_here, branch_all, (p_x, p_y), False)
    end()
    shares[3].start()
    to_whole = pltpu.make_async_copy(branch_all, whole, local)
    to_whole.start()
    out_tiles(mixed_here, branch_all, (p, p_d), False)
    for copy in shares:
        copy.wait()
    out_tiles(mixed_there, branch_other, range(CHIPS), True)
    to_whole.wait()


def grads_of_middle(parts, middle, cot, gain, hiddens, down, cots, mixeds, collective_id):
    rows, width = middle.shape
    tokens, units = hiddens[0].shape[0], 2 * hiddens[0].shape[1]
    f32, bf16 = jnp.float32, jnp.bfloat16
    return pl.pallas_call(
        grads_of_middle_kernel,
        out_shape=[
            jax.ShapeDtypeStruct((rows, width), f32),
            jax.ShapeDtypeStruct((1, width), f32),
            jax.ShapeDtypeStruct((CHIPS, rows, width), bf16),
            jax.ShapeDtypeStruct((down.shape[0] // 2, down.shape[1], width), bf16),
            jax.ShapeDtypeStruct((CHIPS, rows, width), bf16),
        ],
        in_specs=[ANY, VMEM, VMEM, VMEM] + [ANY] * 7,
        out_specs=[VMEM, VMEM, ANY, VMEM, VMEM],
        scratch_shapes=[
            pltpu.VMEM((rows, width), bf16),
            pltpu.VMEM((CHIPS, rows, width), bf16),
            pltpu.VMEM((CHIPS, rows, width), bf16),
            pltpu.VMEM(mixeds[0].shape, bf16),
            pltpu.VMEM(mixeds[0].shape, bf16),
            pltpu.VMEM((mixeds[0].shape[1], width), f32),
            pltpu.VMEM((tokens, units), bf16),
            pltpu.VMEM((tokens, units // 2), bf16),
            pltpu.VMEM((units, width), bf16),
            pltpu.VMEM((tokens, width), bf16),
            pltpu.VMEM((tokens, width), bf16),
            *sum_scratch(rows, width, parts.dtype),
            pltpu.SemaphoreType.DMA((10,)),
            pltpu.SemaphoreType.DMA((10,)),
            pltpu.SemaphoreType.DMA,
            pltpu.SemaphoreType.DMA((5,)),
            pltpu.SemaphoreType.DMA((down.shape[0],)),
        ],
        compiler_params=comm_params(collective_id, 60),
        cost_estimate=lasting(80),
        name="grads_of_middle",
    )(parts, middle, cot, gain[None], *hiddens, down, *cots, *mixeds)


def closing_kernel(
    planes,
    in_low,
    whole_in,
    tokens,
    gain,
    rest,
    small,
    conv_low,
    decay_low,
    input_low,
    piece,
    grad_tokens,
    small_out,
    gates_out,
    swapped,
    conv_a,
    conv_b,
    decay_a,
    decay_b,
    input_a,
    input_b,
    full,
    gates,
    gate_lines,
    lines,
    line,
    near_parts,
    gains,
    gain_lines,
    gain_line,
    gain_near,
    send,
    recv,
    loads,
    swap_send,
    swap_recv,
    *sums,
):
    me, z, p, c, x, y = place()
    f32 = jnp.float32
    r = lax.rem(me, 8)
    near = [(lax.rem(r + d, 8), me - r + lax.rem(r + d, 8)) for d in range(1, 8)]
    far = [(lax.rem(z + d, planes), 8 * lax.rem(z + d, planes) + r) for d in range(1, planes)]
    greet([device for unused, device in near + far])

    def copy(k, source, target, device):
        return remote(source, target, send.at[k], recv.at[k], device)

    lows = ((conv_low, conv_a, conv_b), (decay_low, decay_a, decay_b), (input_low, input_a, input_b))
    fetched = [pltpu.make_async_copy(source, here, loads.at[k]) for k, (source, here, there) in enumerate(lows)]
    exchanges = [copy(k, source, there, me + 1 - 2 * c) for k, (source, here, there) in enumerate(lows)]
    at = 3
    small_far = [copy(at + d, small.at[there], lines.at[d], device) for d, (there, device) in enumerate(far)]
    at += len(far)
    for started in small_far + fetched + exchanges:
        started.start()

    def product(chip, rows_at, columns):
        return lax.dot_general(
            in_low[chip, rows_at, :], whole_in[columns, :], (((1,), (1,)), ((), ())), preferred_element_type=f32
        )

    begin, forward, end, part_of = computed_sum(product, *sums)
    begin()
    for ended in fetched + exchanges:
        ended.wait()
    swaps = swap_copies(piece, swapped, swap_send, swap_recv, loads.at[3])

    def dot_first(left, right):
        return lax.dot_general(left, right, (((0,), (0,)), ((), ())), preferred_element_type=f32)

    block = gates.shape[1]
    count = planes * block
    for k, (first, second) in enumerate(((decay_a, decay_b), (input_a, input_b))):
        full[...] = dot_first(conv_a[...], first[...]) + dot_first(conv_b[...], second[...])
        for j in range(planes):
            rows_at = pl.ds(pl.multiple_of(c * count + j * block, 8), block)
            for e in range(2):
                gates[j, :, (2 * k + e) * block : (2 * k + e + 1) * block] = full[
                    rows_at, e * count + j * block : e * count + (j + 1) * block
                ]
    gate_far = [copy(at + d, gates.at[there], gate_lines.at[d], device) for d, (there, device) in enumerate(far)]
    at += len(far)
    for sent in gate_far:
        sent.start()
    forward()
    for sent in swaps:
        sent.start()
    for sent in small_far:
        sent.wait()
    line[...] = small[z] + sum(lines[d] for d in range(planes - 1))
    small_near = [
        copy(at + d, line.at[there], near_parts.at[d], device) for d, (there, device) in enumerate(near)
    ]
    at += len(near)
    for sent in small_near:
        sent.start()
    end()
    rows, width = tokens.shape
    step = width // (8 * planes)

    def norm_rows(i, j, total):
        here, grad = part_of(i, j)
        given, terms = norm_back_rows(tokens[here, :].astype(f32), gain[...], grad, rest[here, :])
        for k in range(4 * planes):
            for e in range(2):
                grad_tokens[here, (2 * k + e) * step : (2 * k + e + 1) * step] = given[
                    :, (4 * planes * e + k) * step : (4 * planes * e + k + 1) * step
                ]
        return total + terms[:8] + terms[8:]

    total = jnp.zeros((8, width), f32)
    for i in range(2):
        total = lax.fori_loop(0, rows // 32, functools.partial(norm_rows, i), total)
    total = jnp.sum(total, axis=0, keepdims=True)
    for j in range(planes):
        for q in range(CHIPS):
            for e in range(2):
                start = ((e * planes + j) * CHIPS + q) * step
                gains[j, 2 * q + e, 0:1, 0:step] = total[:, start : start + step]
    gain_far = [copy(at + d, gains.at[there], gain_lines.at[d], device) for d, (there, device) in enumerate(far)]
    at += len(far)
    for sent in gain_far:
        sent.start()
    for sent in gain_far:
        sent.wait()
    gain_line[...] = gains[z] + sum(gain_lines[d] for d in range(planes - 1))
    last = [
        copy(at + d, gain_line.at[there], gain_near.at[d], device) for d, (there, device) in enumerate(near)
    ]
    for sent in last:
        sent.start()
    for sent in small_near + gate_far + swaps:
        sent.wait()
    gates_out[...] = gates[z] + sum(gate_lines[d] for d in range(planes - 1))
    for sent in last:
        sent.wait()
    rows_small = line.shape[1]
    small_out[0:rows_small, :] = line[r] + sum(near_parts[d] for d in range(7))
    small_out[rows_small : rows_small + 8, :] = gain_line[r] + sum(gain_near[d] for d in range(7))


def closing(in_low, whole_in, tokens, gain, rest, small, lows, piece, head, collective_id):
    planes = lax.axis_size("seq") // 8
    rows, width = tokens.shape
    f32, bf16 = jnp.float32, jnp.bfloat16
    rows_small, lanes = small.shape[2:]
    channels = lows[0].shape[1]
    block = channels // (2 * planes)
    count = 3 + 3 * (planes - 1) + 14
    return pl.pallas_call(
        functools.partial(closing_kernel, planes),
        out_shape=[
            jax.ShapeDtypeStruct((rows, width), f32),
            jax.ShapeDtypeStruct((rows_small + 8, lanes), f32),
            jax.ShapeDtypeStruct((block, 2 * head), f32),
            jax.ShapeDtypeStruct(piece.shape, bf16),
        ],
        in_specs=[VMEM] * 6 + [ANY] * 4,
        out_specs=[VMEM] * 3 + [ANY],
        scratch_shapes=[
            *[pltpu.VMEM(lows[0].shape, bf16)] * 6,
            pltpu.VMEM((channels, channels), f32),
            pltpu.VMEM((planes, block, 2 * head), f32),
            pltpu.VMEM((planes - 1, block, 2 * head), f32),
            pltpu.VMEM((planes - 1, 8, rows_small, lanes), f32),
            pltpu.VMEM((8, rows_small, lanes), f32),
            pltpu.VMEM((7, rows_small, lanes), f32),
            pltpu.VMEM((planes, 8, 8, lanes), f32),
            pltpu.VMEM((planes - 1, 8, 8, lanes), f32),
            pltpu.VMEM((8, 8, lanes), f32),
            pltpu.VMEM((7, 8, lanes), f32),
            pltpu.SemaphoreType.DMA((count,)),
            pltpu.SemaphoreType.DMA((count,)),
            pltpu.SemaphoreType.DMA((4,)),
            pltpu.SemaphoreType.DMA((3,)),
            pltpu.SemaphoreType.DMA((3,)),
            *computed_scratch(rows, width, bf16),
        ],
        compiler_params=comm_params(collective_id, 60),
        cost_estimate=lasting(50),
        name="closing",
    )(in_low, whole_in, tokens, gain[None], rest, small, *lows, piece)


def plane_swap_kernel(count, *refs):
    ins, outs = refs[:count], refs[count : 2 * count]
    send, recv, local = refs[2 * count :]
    me, z, p, c, x, y = place()
    x_dev, y_dev = me + 2 - 4 * x, me + 4 - 8 * y
    d_dev = y_dev + 2 - 4 * x
    p_x, p_y, p_d = p + 1 - 2 * x, p + 2 - 4 * y, 3 - p
    peers = ((x_dev, p_x), (y_dev, p_y), (d_dev, p_d))
    greet([device for device, unused in peers])
    copies = []
    for k in range(count):
        for j, (device, chip) in enumerate(peers):
            copies.append(remote(ins[k].at[chip], outs[k].at[p], send.at[k, j], recv.at[k, j], device))
        copies.append(pltpu.make_async_copy(ins[k].at[p], outs[k].at[p], local.at[k]))
    for copy in copies:
        copy.start()
    for copy in copies:
        copy.wait()


def plane_swap(arrays, collective_id):
    count = len(arrays)
    return pl.pallas_call(
        functools.partial(plane_swap_kernel, count),
        out_shape=[jax.ShapeDtypeStruct(a.shape, a.dtype) for a in arrays],
        in_specs=[ANY] * count,
        out_specs=[ANY] * count,
        scratch_shapes=[
            pltpu.SemaphoreType.DMA((count, 3)),
            pltpu.SemaphoreType.DMA((count, 3)),
            pltpu.SemaphoreType.DMA((count,)),
        ],
        compiler_params=comm_params(collective_id),
        cost_estimate=lasting(10),
        name="plane_swap",
    )(*arrays)


def swap_copies(source, target, send, recv, local):
    devices, chips = plane_neighbours()
    p = place()[2]
    return [
        *[remote(source.at[chips[j]], target.at[p], send.at[j], recv.at[j], devices[j]) for j in range(3)],
        pltpu.make_async_copy(source.at[p], target.at[p], local),
    ]


def opening_kernel(
    planes,
    small,
    gates,
    tokens,
    piece,
    gathered,
    decay_blocks,
    input_blocks,
    whole,
    swapped,
    gates_all,
    gain,
    normed,
    *sems,
):
    send, recv, gate_send, gate_recv, swap_send, swap_recv, swap_local, gather_send, gather_recv, gather_local = sems
    me, z, p, c, x, y = place()
    r = lax.rem(me, 8)
    near = [me - r + lax.rem(r + d, 8) for d in range(1, 8)]
    far = [8 * lax.rem(z + d, planes) + r for d in range(1, planes)]
    greet(near + far)
    lines = [
        remote(small, gathered.at[r, z], send.at[d], recv.at[d], device) for d, device in enumerate(far)
    ]
    gate_lines = [
        remote(gates, gates_all.at[c, z], gate_send.at[d], gate_recv.at[d], device) for d, device in enumerate(far)
    ]
    for copy in lines + gate_lines:
        copy.start()
    gathered[r, z] = small[...]
    gates_all[c, z] = gates[...]
    for copy in lines:
        copy.wait()
    spreads = [
        remote(gathered.at[r], gathered.at[r], send.at[planes + d], recv.at[planes + d], device)
        for d, device in enumerate(near)
    ]
    for copy in spreads:
        copy.start()
    for copy in gate_lines:
        copy.wait()
    gate_swap = remote(
        gates_all.at[c], gates_all.at[c], gate_send.at[planes], gate_recv.at[planes], me + 1 - 2 * c
    )
    gate_swap.start()
    for copy in spreads:
        copy.wait()
    swaps = swap_copies(piece, swapped, swap_send, swap_recv, swap_local)
    rows, width = tokens.shape
    step = width // (8 * planes)
    for j in range(planes):
        for q in range(CHIPS):
            for e in range(2):
                start = ((e * planes + j) * CHIPS + q) * step
                gain[0:1, start : start + step] = gathered[2 * q + e, j, 0:1, 0:step]

    @pl.loop(0, rows // 16)
    def norm_rows(i):
        at = sixteen(i)
        values = tokens[at, :].astype(jnp.float32)
        inverse = lax.rsqrt(jnp.mean(values * values, axis=-1, keepdims=True) + epsilon)
        normed[at, :] = (values * inverse * gain[0:1, :]).astype(jnp.bfloat16)

    begin, forward, end = gather_steps(normed, whole, gather_send, gather_recv, gather_local, 0)
    begin()
    for copy in swaps:
        copy.start()
    gate_swap.wait()
    block = gates.shape[0]
    for k, target in enumerate((decay_blocks, input_blocks)):
        target[...] = jnp.zeros_like(target)
        for e in range(2):
            for j in range(planes):
                for h in range(2):
                    row, column = (e * planes + j) * block, (h * planes + j) * block
                    target[row : row + block, column : column + block] = gates_all[
                        e, j, :, (2 * k + h) * block : (2 * k + h + 1) * block
                    ]
    forward()
    end()
    for copy in swaps:
        copy.wait()


def opening(small, gates, tokens, piece, collective_id):
    planes = lax.axis_size("seq") // 8
    rows, width = tokens.shape
    channels = 2 * planes * gates.shape[0]
    return pl.pallas_call(
        functools.partial(opening_kernel, planes),
        out_shape=[
            jax.ShapeDtypeStruct((8, planes) + small.shape, small.dtype),
            jax.ShapeDtypeStruct((channels, channels), gates.dtype),
            jax.ShapeDtypeStruct((channels, channels), gates.dtype),
            jax.ShapeDtypeStruct((CHIPS, rows, width), jnp.bfloat16),
            jax.ShapeDtypeStruct(piece.shape, piece.dtype),
        ],
        in_specs=[VMEM, VMEM, VMEM, ANY],
        out_specs=[VMEM, VMEM, VMEM, ANY, ANY],
        scratch_shapes=[
            pltpu.VMEM((2, planes) + gates.shape, gates.dtype),
            pltpu.VMEM((8, width), jnp.float32),
            pltpu.VMEM((rows, width), jnp.bfloat16),
            pltpu.SemaphoreType.DMA((planes + 7,)),
            pltpu.SemaphoreType.DMA((planes + 7,)),
            pltpu.SemaphoreType.DMA((planes + 1,)),
            pltpu.SemaphoreType.DMA((planes + 1,)),
            pltpu.SemaphoreType.DMA((3,)),
            pltpu.SemaphoreType.DMA((3,)),
            pltpu.SemaphoreType.DMA,
            pltpu.SemaphoreType.DMA((4,)),
            pltpu.SemaphoreType.DMA((4,)),
            pltpu.SemaphoreType.DMA,
        ],
        compiler_params=comm_params(collective_id, 60),
        cost_estimate=lasting(65),
        name="opening",
    )(small, gates, tokens, piece)


def column_peers(planes, z, p, c):
    count = 2 * planes
    q = 2 * z + c
    peers = []
    for d in range(1, count):
        other = lax.rem(q + d, count)
        peers.append(8 * lax.div(other, 2) + 2 * p + lax.rem(other, 2))
    return q, peers


def carry_in(planes, reverse, z, c, q, peers, everyone, before, entering, send, recv):
    own = everyone.at[q]
    copies = [remote(own, own, send.at[d], recv.at[d], device) for d, device in enumerate(peers)]
    for copy in copies:
        copy.start()
    for copy in copies:
        copy.wait()
    carried = jnp.zeros((1, everyone.shape[2]), jnp.float32)
    order = [(k, j, e) for k in range(planes) for j in range(CHIPS) for e in range(2)]
    for k, j, e in reversed(order) if reverse else order:
        before[8 * k + 2 * j + e : 8 * k + 2 * j + e + 1, :] = carried
        part = everyone.at[2 * k + e]
        carried = part[j : j + 1, :] * carried + part[CHIPS + j : CHIPS + j + 1, :]
    for j in range(CHIPS):
        entering[j : j + 1, :] = before[pl.ds(8 * z + 2 * j + c, 1), :]


def shift_down(earlier, values, step, row):
    return jnp.where(row >= step, pltpu.roll(values, step, 0), pltpu.roll(earlier, step, 0))


def shift_up(values, later, step, row):
    return jnp.where(row < 8 - step, pltpu.roll(values, 8 - step, 0), pltpu.roll(later, 8 - step, 0))


def tile_scan(a, b, row, reverse):
    for step in (1, 2, 4):
        if reverse:
            keep = row < 8 - step
            shifted_a, shifted_b = pltpu.roll(a, 8 - step, 0), pltpu.roll(b, 8 - step, 0)
        else:
            keep = row >= step
            shifted_a, shifted_b = pltpu.roll(a, step, 0), pltpu.roll(b, step, 0)
        b = a * jnp.where(keep, shifted_b, 0.0) + b
        a = a * jnp.where(keep, shifted_a, 1.0)
    return a, b


def sigmoid(values):
    return 1.0 / (1.0 + jnp.exp(-values))


def gate_terms(decay_pre, rate, flag):
    opened = sigmoid(decay_pre)
    log_decay = rate * opened
    decay = jnp.exp(log_decay)
    keep = 1.0 - flag
    squared = decay * decay
    return opened, decay * keep, keep, squared, jnp.tanh(-log_decay) * (1.0 + squared)


GELU_A, GELU_B = 0.7978845608028654, 0.044715


def eight(i):
    return pl.ds(pl.multiple_of(i * 8, 8), 8)


def recurrence_kernel(
    planes,
    gate_pre,
    conv_input,
    masks,
    vectors,
    decay_blocks,
    input_blocks,
    cot,
    piece,
    normed,
    conv_out,
    conv_low,
    decay_pre,
    input_pre,
    states,
    mixed,
    mixed_zero,
    mixed_one,
    entering,
    halo,
    cot_all,
    swapped,
    normed_other,
    cumulative,
    sibling_tails,
    below_tail,
    everyone,
    before,
    send,
    recv,
    local,
    swap_send,
    swap_recv,
    other_send,
    other_recv,
):
    me, z, p, c, x, y = place()
    rows, channels = conv_input.shape[1:]
    q, peers = column_peers(planes, z, p, c)
    greet(peers + [*plane_neighbours()[0]])
    cot_begin, cot_forward, cot_end = gather_steps(cot, cot_all, send, recv, local.at[0], 9)
    cot_begin()
    half = normed.shape[1] // 2
    other = remote(
        normed.at[:, pl.ds(pl.multiple_of((1 - c) * half, 128), half)],
        normed_other,
        other_send,
        other_recv,
        me + 1 - 2 * c,
    )
    other.start()
    swaps = swap_copies(piece, swapped, swap_send, swap_recv, local.at[1])
    f32 = jnp.float32
    tail = pl.ds(rows - 16, 16)
    to_sibling = remote(conv_input.at[:, tail], sibling_tails, send.at[7], recv.at[7], me + 1 - 2 * c)
    to_above = remote(conv_input.at[CHIPS - 1, tail], below_tail, send.at[8], recv.at[8], me + 7)
    from_below = remote(conv_input.at[CHIPS - 1, tail], below_tail, send.at[8], recv.at[8], me - 7)
    to_sibling.start()

    @pl.when((c == 1) & (z < planes - 1))
    def send_above():
        to_above.start()

    to_sibling.wait()

    @pl.when((c == 1) & (z < planes - 1))
    def sent_above():
        to_above.wait_send()

    @pl.when((c == 0) & (z > 0))
    def had_below():
        from_below.wait_recv()

    @pl.when(c == 1)
    def halo_one():
        for j in range(CHIPS):
            halo[j] = sibling_tails[j].astype(f32)[8:]

    @pl.when(c == 0)
    def halo_zero():
        for j in range(1, CHIPS):
            halo[j] = sibling_tails[j - 1].astype(f32)[8:]

        @pl.when(z > 0)
        def halo_below():
            halo[0] = below_tail[...].astype(f32)[8:]

        @pl.when(z == 0)
        def halo_none():
            halo[0] = jnp.zeros((8, channels), f32)

    row = lax.broadcasted_iota(jnp.int32, (8, channels), 0)

    @pl.loop(0, CHIPS)
    def block(j):
        def conv_tile(i, earlier):
            both = conv_input[j, sixteen(i), :].astype(f32)
            outs = []
            for h in range(2):
                now = both[8 * h : 8 * h + 8]
                keep = masks[j, eight(2 * i + h), :]
                out = vectors[CW : CW + 1, :] + vectors[0:1, :] * now
                for k in range(1, CW):
                    out = out + vectors[k : k + 1, :] * (
                        shift_down(earlier, now, k, row) * keep[:, k : k + 1]
                    )
                conv_out[j, eight(2 * i + h), :] = out
                outs.append(out)
                earlier = now
            conv_low[j, sixteen(i), :] = jnp.concatenate(outs, axis=0).astype(jnp.bfloat16)
            return earlier

        lax.fori_loop(0, rows // 16, conv_tile, halo[j], unroll=2)
        low = conv_low[j]
        decay_pre[j] = jnp.dot(low, decay_blocks[...], preferred_element_type=f32) + vectors[CW + 1 : CW + 2, :]
        input_pre[j] = jnp.dot(low, input_blocks[...], preferred_element_type=f32) + vectors[CW + 2 : CW + 3, :]

        def scan_tile(i, carry):
            at = eight(i)
            flag = masks[j, at, :][:, 0:1]
            opened, coef, keep, squared, gap = gate_terms(decay_pre[j, at, :], vectors[CW + 3 : CW + 4, :], flag)
            drive = (flag + keep * jnp.sqrt(gap)) * sigmoid(input_pre[j, at, :]) * conv_out[j, at, :]
            a, b = tile_scan(coef, drive, row, False)
            before_a, before_b = carry
            b = a * before_b + b
            a = a * before_a
            cumulative[j, at, :] = a
            states[j, at, :] = b
            return a[7:8], b[7:8]

        last_a, last_b = lax.fori_loop(
            0,
            rows // 8,
            scan_tile,
            (jnp.ones((1, channels), f32), jnp.zeros((1, channels), f32)),
            unroll=4,
        )
        everyone[q, pl.ds(j, 1), :] = last_a
        everyone[q, pl.ds(CHIPS + j, 1), :] = last_b

    cot_forward()
    for copy in swaps:
        copy.start()
    carry_in(planes, False, z, c, q, peers, everyone, before, entering, send, recv)

    @pl.loop(0, CHIPS)
    def finish(j):
        start = entering[pl.ds(j, 1), :]

        def state_tile(i, unused):
            at = sixteen(i)
            state = states[j, at, :] + cumulative[j, at, :] * start
            states[j, at, :] = state
            v = gate_pre[j, at, :]
            act = 0.5 * v * (1.0 + jnp.tanh(GELU_A * (v + GELU_B * (v * v * v))))
            product = (state * act).astype(jnp.bfloat16)
            mixed[j, at, :] = product
            mixed_zero[j, at, :] = product[:, : channels // 2]
            mixed_one[j, at, :] = product[:, channels // 2 :]
            return unused

        lax.fori_loop(0, rows // 16, state_tile, 0, unroll=2)

    cot_end()
    other.wait()
    for copy in swaps:
        copy.wait()


def recurrence(gate_pre, conv_input, masks, vectors, decay_blocks, input_blocks, cot, piece, normed, collective_id):
    planes = lax.axis_size("seq") // 8
    blocks, rows, channels = conv_input.shape
    f32, bf16 = jnp.float32, jnp.bfloat16
    cube = conv_input.shape

    def out(dtype, shape=cube):
        return jax.ShapeDtypeStruct(shape, dtype)

    return pl.pallas_call(
        functools.partial(recurrence_kernel, planes),
        out_shape=[
            out(f32),
            out(bf16),
            out(f32),
            out(f32),
            out(f32),
            out(bf16),
            *[out(bf16, (CHIPS, rows, channels // 2))] * 2,
            out(f32, (CHIPS, channels)),
            out(f32, (CHIPS, 8, channels)),
            out(cot.dtype, (CHIPS,) + cot.shape),
            out(piece.dtype, piece.shape),
            out(normed.dtype, (normed.shape[0], normed.shape[1] // 2)),
        ],
        in_specs=[VMEM] * 6 + [ANY] * 3,
        out_specs=[VMEM] * 10 + [ANY] * 3,
        scratch_shapes=[
            pltpu.VMEM(cube, f32),
            pltpu.VMEM((CHIPS, 16, channels), bf16),
            pltpu.VMEM((16, channels), bf16),
            pltpu.VMEM((2 * planes, 2 * CHIPS, channels), f32),
            pltpu.VMEM((8 * planes, channels), f32),
            pltpu.SemaphoreType.DMA((13,)),
            pltpu.SemaphoreType.DMA((13,)),
            pltpu.SemaphoreType.DMA((2,)),
            pltpu.SemaphoreType.DMA((3,)),
            pltpu.SemaphoreType.DMA((3,)),
            pltpu.SemaphoreType.DMA,
            pltpu.SemaphoreType.DMA,
        ],
        compiler_params=comm_params(collective_id, 60),
        cost_estimate=lasting(46),
        name="recurrence",
    )(gate_pre, conv_input, masks, vectors, decay_blocks, input_blocks, cot, piece, normed)


def recurrence_back_kernel(
    planes,
    grad_branch,
    rows_all,
    gate_pre,
    conv_input,
    conv_out,
    decay_pre,
    input_pre,
    states,
    entering,
    halo,
    masks,
    after_masks,
    vectors,
    decay_blocks,
    input_blocks,
    down_parts,
    piece,
    in_low,
    decay_low,
    input_low,
    sums,
    down_sum,
    swapped,
    grad_mixed,
    branch_here,
    out_here,
    cumulative,
    local,
    grad_conv,
    sibling_heads,
    above_head,
    ahead,
    everyone,
    before,
    leaving,
    send,
    recv,
    piece_sem,
    loads,
    *down_scratch,
):
    me, z, p, c, x, y = place()
    rows, channels = conv_input.shape[1:]
    q, peers = column_peers(planes, z, p, c)
    devices, chips = plane_neighbours()
    greet(peers + [*devices])
    down_begin, down_forward, down_end = sum_steps(down_parts, *down_scratch)
    down_begin()
    swaps = swap_copies(piece, swapped, send.at[pl.ds(9, 3)], recv.at[pl.ds(9, 3)], piece_sem.at[0])
    fetched = fetch_rows(rows_all, 0, 0, out_here, loads)
    fetched.append(pltpu.make_async_copy(grad_branch, branch_here, piece_sem.at[1]))
    for copy in fetched:
        copy.start()
    for copy in fetched:
        copy.wait()
    f32, bf16 = jnp.float32, jnp.bfloat16
    row = lax.broadcasted_iota(jnp.int32, (8, channels), 0)
    rate = vectors[CW + 3 : CW + 4, :]
    nothing = jnp.zeros((8, channels), f32)

    @pl.loop(0, CHIPS)
    def scan_block(j):
        grad_mixed[j] = lax.dot_general(
            branch_here[j], out_here[...], (((1,), (1,)), ((), ())), preferred_element_type=f32
        )

        def scan_tile(i, carry):
            i = rows // 16 - 1 - i
            at = sixteen(i)
            v = gate_pre[j, at, :]
            grad = grad_mixed[j, at, :]
            t = jnp.tanh(GELU_A * (v + GELU_B * (v * v * v)))
            act = 0.5 * v * (1.0 + t)
            slope = 0.5 * (1.0 + t) + 0.5 * v * (1.0 - t * t) * (GELU_A * (1.0 + 3.0 * GELU_B * (v * v)))
            in_low[j, at, 0:channels] = (grad * states[j, at, :] * slope).astype(bf16)
            drive = grad * act
            later_a, later_b, later_coef = carry
            for h in (1, 0):
                here = eight(2 * i + h)
                flag = masks[j, here, :][:, 0:1]
                coef = gate_terms(decay_pre[j, here, :], rate, flag)[1]
                shifted = jnp.where(row < 7, pltpu.roll(coef, 7, 0), later_coef)
                a, b = tile_scan(shifted, drive[8 * h : 8 * h + 8], row, True)
                b = a * later_b + b
                a = a * later_a
                cumulative[j, here, :] = a
                local[j, here, :] = b
                later_a, later_b, later_coef = a[0:1], b[0:1], coef[0:1]
            return later_a, later_b, later_coef

        ones = jnp.ones((1, channels), f32)
        first_a, first_b, first_coef = lax.fori_loop(
            0, rows // 16, scan_tile, (ones, jnp.zeros((1, channels), f32), ones), unroll=2
        )
        everyone[q, pl.ds(j, 1), :] = first_coef * first_a
        everyone[q, pl.ds(CHIPS + j, 1), :] = first_coef * first_b

    carry_in(planes, True, z, c, q, peers, everyone, before, leaving, send, recv)
    down_forward()
    for copy in swaps:
        copy.start()

    def terms_block(j, totals):
        behind_all = leaving[pl.ds(j, 1), :]

        def terms_tile(i, carry):
            previous, decay_sum, input_sum, param_sum = carry
            lows = []
            for h in range(2):
                at = eight(2 * i + h)
                adjoint = local[j, at, :] + cumulative[j, at, :] * behind_all
                state = states[j, at, :]
                earlier = jnp.where(row >= 1, pltpu.roll(state, 1, 0), previous)
                previous = state[7:8]
                flag = masks[j, at, :][:, 0:1]
                opened, coef, keep, squared, gap = gate_terms(decay_pre[j, at, :], rate, flag)
                passed = sigmoid(input_pre[j, at, :])
                conv = conv_out[j, at, :]
                inverse = lax.rsqrt(gap)
                scale = flag + keep * (gap * inverse)
                grad_log = adjoint * (earlier * coef - keep * passed * conv * squared * inverse)
                log_open = grad_log * opened
                decay_full = log_open * rate * (1.0 - opened)
                direct = adjoint * scale * passed
                input_full = direct * (1.0 - passed) * conv
                grad_conv[j, at, :] = direct
                lows.append((decay_full, input_full))
                decay_sum = decay_sum + decay_full
                input_sum = input_sum + input_full
                param_sum = param_sum + log_open
            decay_low[j, sixteen(i), :] = jnp.concatenate([low[0] for low in lows], axis=0).astype(bf16)
            input_low[j, sixteen(i), :] = jnp.concatenate([low[1] for low in lows], axis=0).astype(bf16)
            return previous, decay_sum, input_sum, param_sum

        totals = lax.fori_loop(
            0, rows // 16, terms_tile, (entering[pl.ds(j, 1), :], *totals), unroll=2
        )[1:]

        def dot_t(left, right):
            return lax.dot_general(left, right, (((1,), (1,)), ((), ())), preferred_element_type=f32)

        grad_conv[j] = (
            grad_conv[j] + dot_t(decay_low[j], decay_blocks[...]) + dot_t(input_low[j], input_blocks[...])
        )
        return totals

    decay_sum, input_sum, param_sum = lax.fori_loop(0, CHIPS, terms_block, (nothing,) * 3)

    to_sibling = remote(grad_conv.at[:, pl.ds(0, 8)], sibling_heads, send.at[7], recv.at[7], me + 1 - 2 * c)
    to_below = remote(grad_conv.at[0, pl.ds(0, 8)], above_head, send.at[8], recv.at[8], me - 7)
    from_above = remote(grad_conv.at[0, pl.ds(0, 8)], above_head, send.at[8], recv.at[8], me + 7)
    to_sibling.start()

    @pl.when((c == 0) & (z > 0))
    def send_below():
        to_below.start()

    to_sibling.wait()

    @pl.when((c == 0) & (z > 0))
    def sent_below():
        to_below.wait_send()

    @pl.when((c == 1) & (z < planes - 1))
    def had_above():
        from_above.wait_recv()

    @pl.when(c == 0)
    def ahead_zero():
        for j in range(CHIPS):
            ahead[j] = sibling_heads[j]

    @pl.when(c == 1)
    def ahead_one():
        for j in range(CHIPS - 1):
            ahead[j] = sibling_heads[j + 1]

        @pl.when(z < planes - 1)
        def ahead_above():
            ahead[CHIPS - 1] = above_head[...]

        @pl.when(z == planes - 1)
        def ahead_none():
            ahead[CHIPS - 1] = nothing

    def conv_block(j, totals):
        def conv_pair(i, now, later, keep, later_keep, outs, earlier, given, totals):
            out = vectors[0:1, :] * now
            new_totals = [totals[0] + now * given]
            for k in range(1, CW):
                masked = now * keep[:, k : k + 1]
                out = out + vectors[k : k + 1, :] * shift_up(
                    masked, later * later_keep[:, k : k + 1], k, row
                )
                new_totals.append(totals[k] + masked * shift_down(earlier, given, k, row))
            new_totals.append(totals[CW] + now)
            outs.append(out)
            return tuple(new_totals)

        def conv_tile(i, carry, last):
            earlier, totals = carry
            inputs = conv_input[j, sixteen(i), :].astype(f32)
            first, second = grad_conv[j, eight(2 * i), :], grad_conv[j, eight(2 * i + 1), :]
            first_keep, second_keep = masks[j, eight(2 * i), :], masks[j, eight(2 * i + 1), :]
            if last:
                third, third_keep = ahead[j], after_masks[j]
            else:
                third, third_keep = grad_conv[j, eight(2 * i + 2), :], masks[j, eight(2 * i + 2), :]
            outs = []
            totals = conv_pair(i, first, second, first_keep, second_keep, outs, earlier, inputs[:8], totals)
            totals = conv_pair(i, second, third, second_keep, third_keep, outs, inputs[:8], inputs[8:], totals)
            in_low[j, sixteen(i), channels : 2 * channels] = jnp.concatenate(outs, axis=0).astype(bf16)
            return inputs[8:], totals

        carry = lax.fori_loop(
            0, rows // 16 - 1, lambda i, carry: conv_tile(i, carry, False), (halo[j], totals)
        )
        return conv_tile(rows // 16 - 1, carry, True)[1]

    totals = lax.fori_loop(0, CHIPS, conv_block, (nothing,) * (CW + 1))
    for k, total in enumerate((*totals, decay_sum, input_sum, param_sum)):
        sums[k : k + 1, :] = jnp.sum(total, axis=0, keepdims=True)
    down_end()
    own, from_x, from_y = down_scratch[:3]

    @pl.loop(0, own.shape[0] // 16)
    def sum_rows(i):
        at = sixteen(i)
        down_sum[at, :] = own[at, :].astype(f32) + from_x[at, :].astype(f32) + from_y[at, :].astype(f32)

    for copy in swaps:
        copy.wait()


def recurrence_back(
    grad_branch,
    rows_all,
    gate_pre,
    conv_input,
    conv_out,
    decay_pre,
    input_pre,
    states,
    entering,
    halo,
    masks,
    after_masks,
    vectors,
    decay_blocks,
    input_blocks,
    down_parts,
    piece,
    collective_id,
):
    planes = lax.axis_size("seq") // 8
    cube = conv_input.shape
    blocks, rows, channels = cube
    f32, bf16 = jnp.float32, jnp.bfloat16
    return pl.pallas_call(
        functools.partial(recurrence_back_kernel, planes),
        out_shape=[
            jax.ShapeDtypeStruct((CHIPS, rows, 2 * channels), bf16),
            jax.ShapeDtypeStruct(cube, bf16),
            jax.ShapeDtypeStruct(cube, bf16),
            jax.ShapeDtypeStruct((CW + 4, channels), f32),
            jax.ShapeDtypeStruct(down_parts.shape[1:], f32),
            jax.ShapeDtypeStruct(piece.shape, bf16),
        ],
        in_specs=[ANY] * 2 + [VMEM] * 13 + [ANY] * 2,
        out_specs=[VMEM] * 5 + [ANY],
        scratch_shapes=[
            pltpu.VMEM(cube, f32),
            pltpu.VMEM(grad_branch.shape, bf16),
            pltpu.VMEM((channels, grad_branch.shape[2]), bf16),
            pltpu.VMEM(cube, f32),
            pltpu.VMEM(cube, f32),
            pltpu.VMEM(cube, f32),
            pltpu.VMEM((CHIPS, 8, channels), f32),
            pltpu.VMEM((8, channels), f32),
            pltpu.VMEM((CHIPS, 8, channels), f32),
            pltpu.VMEM((2 * planes, 2 * CHIPS, channels), f32),
            pltpu.VMEM((8 * planes, channels), f32),
            pltpu.VMEM((CHIPS, channels), f32),
            pltpu.SemaphoreType.DMA((12,)),
            pltpu.SemaphoreType.DMA((12,)),
            pltpu.SemaphoreType.DMA((2,)),
            pltpu.SemaphoreType.DMA((rows_all.shape[0],)),
            *sum_scratch(*down_parts.shape[1:], bf16),
        ],
        compiler_params=comm_params(collective_id, 60),
        cost_estimate=lasting(58),
        name="recurrence_back",
    )(
        grad_branch,
        rows_all,
        gate_pre,
        conv_input,
        conv_out,
        decay_pre,
        input_pre,
        states,
        entering,
        halo,
        masks,
        after_masks,
        vectors,
        decay_blocks,
        input_blocks,
        down_parts,
        piece,
    )


def input_grads_kernel(
    normed, normed_other, low, grad, here, there, low_here, low_there, kept, send, recv, loads
):
    me, z, p, c, x, y = place()
    sibling = me + 1 - 2 * c
    greet((sibling,))
    swap = remote(low, low_there, send, recv, sibling)
    swap.start()
    half, columns = grad.shape
    fetched = [
        pltpu.make_async_copy(source, target, loads.at[k])
        for k, (source, target) in enumerate(
            (
                (normed.at[:, pl.ds(pl.multiple_of(c * half, 128), half)], here),
                (low, low_here),
                (normed_other, there),
            )
        )
    ]
    for copy in fetched:
        copy.start()
    for copy in fetched[:2]:
        copy.wait()
    block, tile = 512, 256

    def products(left, right, keep):
        @pl.loop(0, half // block)
        def product_block(m):
            at = pl.ds(pl.multiple_of(m * block, block), block)

            @pl.loop(0, columns // tile)
            def product_tile(k):
                across = pl.ds(pl.multiple_of(k * tile, tile), tile)
                keep(
                    at,
                    across,
                    lax.dot_general(
                        left[:, at], right[:, across], (((0,), (0,)), ((), ())), preferred_element_type=jnp.float32
                    ),
                )

    def keep_first(at, across, values):
        kept[at, across] = values

    def keep_sum(at, across, values):
        grad[at, across] = (kept[at, across] + values).astype(grad.dtype)

    products(here, low_here, keep_first)
    fetched[2].wait()
    swap.wait()
    products(there, low_there, keep_sum)


def input_grads(normed, normed_other, low, collective_id):
    tokens, width = normed.shape
    columns = low.shape[1]
    bf16 = low.dtype
    return pl.pallas_call(
        input_grads_kernel,
        out_shape=jax.ShapeDtypeStruct((width // 2, columns), bf16),
        in_specs=[ANY] * 3,
        out_specs=VMEM,
        scratch_shapes=[
            pltpu.VMEM((tokens, width // 2), bf16),
            pltpu.VMEM((tokens, width // 2), bf16),
            pltpu.VMEM((tokens, columns), bf16),
            pltpu.VMEM((tokens, columns), bf16),
            pltpu.VMEM((width // 2, columns), jnp.float32),
            pltpu.SemaphoreType.DMA,
            pltpu.SemaphoreType.DMA,
            pltpu.SemaphoreType.DMA((3,)),
        ],
        compiler_params=comm_params(collective_id, 60),
        name="input_grads",
    )(normed, normed_other, low)


def regrouped_kernel(back, devices, *refs):
    count = len(refs) // 2
    for source, target in zip(refs[:count], refs[count:]):
        step = source.shape[1] // devices
        for k in range(devices // 2):
            for e in range(2):
                split, joined = (2 * k + e) * step, (devices // 2 * e + k) * step
                start, end = (joined, split) if back else (split, joined)
                target[:, end : end + step] = source[:, start : start + step].astype(target.dtype)


def regrouped_columns(arrays, dtypes, back):
    devices = lax.axis_size("seq")
    return pl.pallas_call(
        functools.partial(regrouped_kernel, back, devices),
        out_shape=[jax.ShapeDtypeStruct(a.shape, dtype) for a, dtype in zip(arrays, dtypes)],
        in_specs=[VMEM] * len(arrays),
        out_specs=[VMEM] * len(arrays),
        compiler_params=pltpu.CompilerParams(vmem_limit_bytes=24 * 2**20),
        name="regrouped_columns",
    )(*arrays)


def to_chips_kernel(planes, pairs, *refs):
    ins, outs = refs[: len(pairs)], refs[len(pairs) :]
    for source, targets in zip(ins, pairs):
        width = source.shape[1] // (planes * 8)
        for z in range(planes):
            for p in range(CHIPS):
                for c in range(2):
                    k, at = targets[c]
                    start = ((z * CHIPS + p) * 2 + c) * width
                    outs[k][p, :, at + z * width : at + (z + 1) * width] = source[:, start : start + width]


def to_chips(weights, pairs, widths):
    planes = lax.axis_size("seq") // 8
    return pl.pallas_call(
        functools.partial(to_chips_kernel, planes, pairs),
        out_shape=[
            jax.ShapeDtypeStruct((CHIPS, weights[0].shape[0], width), weights[0].dtype) for width in widths
        ],
        in_specs=[VMEM] * len(weights),
        out_specs=[VMEM] * len(widths),
        name="to_chips",
    )(*weights)


def from_chips_kernel(planes, pairs, *refs):
    outs, ins = refs[-len(pairs) :], refs[: -len(pairs)]
    for target, sources in zip(outs, pairs):
        width = target.shape[1] // (planes * 8)
        for z in range(planes):
            for p in range(CHIPS):
                for c in range(2):
                    k, at = sources[c]
                    start = ((z * CHIPS + p) * 2 + c) * width
                    target[:, start : start + width] = ins[k][
                        p, :, at + z * width : at + (z + 1) * width
                    ].astype(jnp.float32)


def from_chips(parts, pairs, widths):
    planes = lax.axis_size("seq") // 8
    return pl.pallas_call(
        functools.partial(from_chips_kernel, planes, pairs),
        out_shape=[jax.ShapeDtypeStruct((parts[0].shape[1], width), jnp.float32) for width in widths],
        in_specs=[VMEM] * len(parts),
        out_specs=[VMEM] * len(widths),
        compiler_params=pltpu.CompilerParams(vmem_limit_bytes=32 * 2**20),
        name="from_chips",
    )(*parts)


def regrouped(values, axis, n):
    shape = values.shape
    split = shape[:axis] + (n // 2, 2, shape[axis] // n) + shape[axis + 1 :]
    return jnp.moveaxis(values.reshape(split), axis + 1, axis).reshape(shape)


def behind(value, *earlier):
    return lax.optimization_barrier((value, *earlier))[0]


def plane_body(
    tokens,
    starts,
    cotangent,
    norm_gain,
    gate_branch,
    input_branch,
    conv_weight,
    conv_bias,
    decay_gate,
    decay_bias,
    input_gate,
    input_bias,
    decay_param,
    out_proj,
    mlp_gain,
    mlp_gate,
    mlp_up,
    mlp_down,
):
    f32, bf16 = jnp.float32, jnp.bfloat16
    n = lax.axis_size("seq")
    planes = n // 8
    me, z, p, c, x, y = place()
    groups = column_groups(n)
    rows, width = tokens.shape
    rows_d, lru_width = gate_branch.shape
    head = decay_gate.shape[1]
    rows_r, rows_f = out_proj.shape[0], mlp_down.shape[0]
    channels = lru_width // CHIPS
    units = mlp_gate.shape[1] // CHIPS
    half_units = units // 2

    def column_gather(block):
        return lax.all_gather(block, "seq", axis=0, tiled=True, axis_index_groups=groups)

    def line_sum(parts):
        return lax.psum_scatter(
            parts, "seq", scatter_dimension=0, tiled=True, axis_index_groups=line_groups(n)
        )

    def product(left, right):
        return jnp.dot(left, right, preferred_element_type=f32)

    def product_t(left, right):
        return jnp.einsum("tk,nk->tn", left, right, preferred_element_type=f32)

    def weight_grad(left, right):
        return jnp.einsum("ta,tb->ab", left, right, preferred_element_type=f32)

    lanes = 128

    def row(values):
        return jnp.pad(values.astype(f32), (0, lanes - values.shape[0]))[None]

    small = jnp.concatenate(
        [
            row(norm_gain),
            row(mlp_gain),
            starts.astype(f32).reshape(rows // lanes, lanes),
            *[row(conv_weight[k]) for k in range(CW)],
            row(conv_bias),
            row(decay_bias),
            row(input_bias),
            row(decay_param),
            jnp.zeros((4, lanes), f32),
        ],
        axis=0,
    )
    half = channels // 2
    in_pairs = (((0, 0), (0, half)), ((0, channels), (0, channels + half)))
    (weights_in,) = to_chips([gate_branch, input_branch], in_pairs, [2 * channels])
    (swapped_in,) = plane_swap([weights_in], 2)
    whole_in = column_gather(swapped_in.reshape(CHIPS * rows_d, 2 * channels))
    tokens, cot, out_proj, mlp_down = regrouped_columns(
        [tokens, cotangent, out_proj, mlp_down], [bf16] * 4, False
    )
    mlp_pairs = (((0, 0), (1, 0)), ((0, half_units), (1, half_units)))
    mlp_pieces = to_chips([mlp_gate, mlp_up], mlp_pairs, [2 * half_units] * 2)
    gates = jnp.concatenate([decay_gate, input_gate], axis=1)
    small, decay_blocks, input_blocks, normed_all, first_piece = opening(
        behind(small, swapped_in), gates, tokens, mlp_pieces[0], 1
    )
    normed_all = normed_all.reshape(CHIPS * rows, width)
    small = small.transpose(1, 0, 2, 3)
    flags = 2 + rows // lanes
    gain_one = regrouped(small[:, :, 0, :rows_d].reshape(width), 0, n)
    gain_two = regrouped(small[:, :, 1, :rows_d].reshape(width), 0, n)
    all_flags = small[:, :, 2:flags].reshape(n * rows)
    vectors = lax.dynamic_slice_in_dim(
        small.reshape(planes, CHIPS, 2, 16, lanes), p, 1, axis=1
    )[:, 0, :, flags : flags + CW + 4, :rows_r]
    vectors = vectors.transpose(2, 1, 0, 3).reshape(CW + 4, channels)
    param = vectors[CW + 3]
    vectors = vectors.at[CW + 3].set(-rate_scale * jax.nn.softplus(param))

    running = jnp.ones((n * rows,), f32)
    masks_all = [running]
    for offset in range(1, CW):
        earlier = jnp.concatenate([jnp.zeros((offset - 1,), f32), all_flags[: n * rows - (offset - 1)]])
        running = running * (1.0 - earlier)
        masks_all.append(running)
    masks_all = jnp.stack(masks_all).reshape(CW, planes, CHIPS, 2, rows)

    def own_blocks(values):
        return lax.dynamic_slice(
            values,
            (0, z, 0, c, 0),
            (values.shape[0], 1, CHIPS, 1, values.shape[4]),
        )[:, 0, :, 0]

    after_masks = masks_all[..., :8].reshape(CW, n, 8)
    after_masks = jnp.concatenate([after_masks[:, 1:], jnp.zeros((CW, 1, 8), f32)], axis=1)
    after_masks = own_blocks(after_masks.reshape(CW, planes, CHIPS, 2, 8)).transpose(1, 2, 0)
    masks_all = jnp.concatenate([all_flags.reshape(1, planes, CHIPS, 2, rows), masks_all[1:]], axis=0)
    masks = own_blocks(masks_all).transpose(1, 2, 0)

    rows_all = column_gather(behind(jnp.concatenate([out_proj, mlp_down], axis=0), swapped_in))
    rows_all = rows_all.reshape(2 * planes, rows_r + rows_f, width)

    gate_pre = product(normed_all, whole_in[:, :channels])
    cube = (CHIPS, rows, channels)
    gate_pre = gate_pre.reshape(cube)
    conv_input = product(normed_all, whole_in[:, channels:]).astype(bf16).reshape(cube)
    conv_out, conv_low, decay_pre, input_pre, states, mixed, *mixeds, entering, halo, cot_all, second_piece, normed_other = recurrence(
        gate_pre,
        conv_input,
        masks,
        vectors,
        decay_blocks,
        input_blocks,
        cot,
        mlp_pieces[1],
        normed_all,
        6,
    )
    whole_mlp = [
        column_gather(part.reshape(CHIPS * rows_d, 2 * half_units)) for part in (first_piece, second_piece)
    ]
    cot_all = cot_all.reshape(CHIPS * rows, width)
    middle, two_all, cot_other = middle_of(mixed, rows_all, tokens, gain_two, cot_all, 7)
    mixeds = [part.reshape(CHIPS * rows, channels // 2) for part in mixeds]
    two_all = two_all.reshape(CHIPS * rows, width)

    hidden_zero, first_grad, first_parts = feed_forward(0, two_all, cot_all, whole_mlp[0], rows_all, (), 8)
    hidden_one, second_grad, two_parts = feed_forward(
        1, two_all, cot_all, whole_mlp[1], rows_all, (first_parts,), 14
    )
    piece_grads = [line_sum(first_grad), line_sum(second_grad)]
    grad_middle, grad_mlp_gain, grad_branch, row_grads, down_parts = grads_of_middle(
        two_parts.reshape(CHIPS, rows, width),
        middle,
        cot,
        gain_two,
        (hidden_zero, hidden_one),
        rows_all,
        (cot_all, cot_other),
        mixeds,
        9,
    )
    grad_rows = line_sum(row_grads.reshape(planes * (rows_r + rows_f), width))

    in_low, grad_decay_low, grad_input_low, sums, down_sum, first_swapped = recurrence_back(
        grad_branch,
        rows_all,
        gate_pre,
        conv_input,
        conv_out,
        decay_pre,
        input_pre,
        states,
        entering,
        halo,
        masks,
        after_masks,
        vectors,
        decay_blocks,
        input_blocks,
        down_parts,
        piece_grads[0].reshape(CHIPS, rows_d, 2 * half_units),
        12,
    )
    sums = sums.at[CW + 3].multiply(-rate_scale * jax.nn.sigmoid(param))
    low_cube = in_low
    in_low = low_cube.reshape(CHIPS * rows, 2 * channels)
    flat = (CHIPS * rows, channels)
    conv_low, grad_decay_low, grad_input_low = (
        a.reshape(flat) for a in (conv_low, grad_decay_low, grad_input_low)
    )

    in_total = input_grads(normed_all, normed_other, in_low, 15)
    in_grads = line_sum(in_total)
    low_cube = behind(low_cube, in_total)
    vector_parts = sums.reshape(CW + 4, 2, planes, rows_r).transpose(2, 1, 0, 3)
    vector_parts = jnp.pad(vector_parts, ((0, 0), (0, 0), (0, 0), (0, lanes - rows_r)))
    here = (jnp.arange(CHIPS) == p).astype(f32)[None, :, None, None, None]
    vector_parts = (vector_parts[:, None] * here).reshape(planes, 8, CW + 4, lanes)
    gain_parts = grad_mlp_gain.reshape(2, planes, CHIPS, 1, rows_d).transpose(1, 2, 0, 3, 4)
    gain_parts = jnp.pad(
        gain_parts.reshape(planes, 8, 1, rows_d), ((0, 0), (0, 0), (0, 7), (0, lanes - rows_d))
    )
    grad_tokens, small_grads, gate_grads, second_swapped = closing(
        low_cube,
        whole_in,
        tokens,
        gain_one,
        grad_middle,
        jnp.concatenate([vector_parts, gain_parts], axis=2),
        (conv_low, grad_decay_low, grad_input_low),
        piece_grads[1].reshape(CHIPS, rows_d, 2 * half_units),
        head,
        13,
    )
    grad_mlp_gate, grad_mlp_up = from_chips(
        [first_swapped, second_swapped], mlp_pairs, [mlp_gate.shape[1]] * 2
    )
    block_out = middle + behind(down_sum, grad_tokens)
    block_out, grad_out_proj, grad_mlp_down = regrouped_columns(
        (block_out, *behind((grad_rows[:rows_r], grad_rows[rows_r:]), grad_tokens)), [bf16, f32, f32], True
    )
    in_grads = behind(in_grads, grad_out_proj)
    in_out = plane_swap([in_grads.reshape(CHIPS, rows_d, 2 * channels)], 16)
    grad_gate_branch, grad_input_branch = from_chips(in_out, in_pairs, [lru_width] * 2)
    vector_grads = small_grads[: CW + 4, :rows_r]
    return (
        block_out,
        grad_tokens,
        small_grads[CW + 12, :rows_d],
        grad_gate_branch,
        grad_input_branch,
        vector_grads[:CW],
        vector_grads[CW],
        gate_grads[:, :head],
        vector_grads[CW + 1],
        gate_grads[:, head:],
        vector_grads[CW + 2],
        vector_grads[CW + 3],
        grad_out_proj,
        small_grads[CW + 4, :rows_d],
        grad_mlp_gate,
        grad_mlp_up,
        grad_mlp_down,
    )


def solution(mesh):
    in_specs = (
        P("seq", None),
        P("seq"),
        P("seq", None),
        P("seq"),
        P("seq", None),
        P("seq", None),
        P(None, "seq"),
        P("seq"),
        P("seq", None),
        P("seq"),
        P("seq", None),
        P("seq"),
        P("seq"),
        P("seq", None),
        P("seq"),
        P("seq", None),
        P("seq", None),
        P("seq", None),
    )
    out_specs = (
        P("seq", None),
        P("seq", None),
        P("seq"),
        P("seq", None),
        P("seq", None),
        P(None, "seq"),
        P("seq"),
        P("seq", None),
        P("seq"),
        P("seq", None),
        P("seq"),
        P("seq"),
        P("seq", None),
        P("seq"),
        P("seq", None),
        P("seq", None),
        P("seq", None),
    )
    body = plane_body if mesh.shape["seq"] == 2 * H else token_split_body
    return jax.shard_map(body, mesh=mesh, in_specs=in_specs, out_specs=out_specs, check_vma=False)
```

```python
import functools

import jax
import jax.numpy as jnp
from jax import lax
from jax.experimental import pallas as pl
from jax.experimental.pallas import tpu as pltpu
from jax.sharding import PartitionSpec as P

H = 16
CW = 4


epsilon = 1e-06
rate_scale = 8.0


def passed_along(block, axis, distance):
    devices = range(lax.axis_size(axis))
    route = [(i - distance, i) for i in devices if i - distance in devices]
    return lax.ppermute(block, axis, route)


def prefix(value, axis, combine, identity, reverse):
    peers, place = (lax.axis_size(axis), lax.axis_index(axis))
    everything = jax.tree.map(lambda part: lax.all_gather(part, axis), value)
    start = jax.tree.map(
        lambda part, zero: jnp.broadcast_to(jnp.asarray(zero, part.dtype), part.shape),
        value,
        identity,
    )

    def hop(k, before):
        at = peers - 1 - k if reverse else k
        reached = at > place if reverse else at < place
        new = combine(before, jax.tree.map(lambda part: part[at], everything))
        return jax.tree.map(lambda a, b: jnp.where(reached, a, b), new, before)

    return lax.fori_loop(0, peers, hop, start)


def gelu_tanh(values):
    return jax.nn.gelu(values, approximate=True)


def rms_norm(values, scales):
    return values * lax.rsqrt(jnp.mean(values * values, axis=-1, keepdims=True) + epsilon) * scales


def combine(earlier_part, later_part):
    return (earlier_part[0] * later_part[0], later_part[0] * earlier_part[1] + later_part[1])


def heads_product(values, weight):
    row_count, lru_width = values.shape
    shaped = values.reshape(row_count, H, lru_width // H)
    blocks = weight.reshape(H, lru_width // H, lru_width // H)
    return jnp.einsum("thi,hij->thj", shaped, blocks, preferred_element_type=jnp.float32).reshape(
        row_count, lru_width
    )


def heads_back(grads_low, weight):
    row_count, lru_width = grads_low.shape
    shaped = grads_low.reshape(row_count, H, lru_width // H)
    blocks = weight.reshape(H, lru_width // H, lru_width // H)
    return jnp.einsum("thj,hij->thi", shaped, blocks, preferred_element_type=jnp.float32).reshape(
        row_count, lru_width
    )


def heads_grad(values, grads_low):
    row_count, lru_width = values.shape
    left_side = values.reshape(row_count, H, lru_width // H)
    right_side = grads_low.reshape(row_count, H, lru_width // H)
    return jnp.einsum(
        "thi,thj->hij", left_side, right_side, preferred_element_type=jnp.float32
    ).reshape(lru_width, lru_width // H)


def lru_terms(decay_pre, input_pre, conv_out, decay_param, flag_rows):
    log_decay = -rate_scale * jax.nn.sigmoid(decay_pre) * jax.nn.softplus(decay_param)
    keep_rows = 1.0 - flag_rows[:, None]
    coefficient = jnp.exp(log_decay) * keep_rows
    scale_in = flag_rows[:, None] + keep_rows * jnp.sqrt(-jnp.expm1(2.0 * log_decay))
    drive_term = scale_in * jax.nn.sigmoid(input_pre) * conv_out
    return (coefficient, drive_term)


def build_masks(flag_rows):
    row_count = flag_rows.shape[0]
    running = jnp.ones((row_count,), jnp.float32)
    masks = [running]
    for offset in range(1, CW):
        earlier_flags = jnp.concatenate(
            [jnp.zeros((offset - 1,), jnp.float32), flag_rows[: row_count - (offset - 1)]]
        )
        running = running * (1.0 - earlier_flags)
        masks.append(running)
    return masks


def send_mask(flag_rows):
    tail_keep = 1.0 - flag_rows[flag_rows.shape[0] - (CW - 1) :]
    after_rows = jnp.cumprod(tail_keep[::-1])[::-1]
    return jnp.concatenate([after_rows[1:], jnp.ones((1,), jnp.float32)])


def conv_local(padded, weight, bias, masks):
    row_count = masks[0].shape[0]
    conv_total = bias + jnp.zeros((row_count, padded.shape[1]), jnp.float32)
    for offset in range(CW):
        lead = CW - 1 - offset
        conv_total = conv_total + weight[offset] * (
            padded[lead : lead + row_count] * masks[offset][:, None]
        )
    return conv_total


def mlp_act(gate_values, up_values):
    return gelu_tanh(gate_values) * up_values


def token_split_body(
    tokens,
    starts,
    cotangent,
    norm_gain,
    gate_branch,
    input_branch,
    conv_weight,
    conv_bias,
    decay_gate,
    decay_bias,
    input_gate,
    input_bias,
    decay_param,
    out_proj,
    mlp_gain,
    mlp_gate,
    mlp_up,
    mlp_down,
):
    (
        whole_norm_gain,
        whole_gate_branch,
        whole_input_branch,
        whole_conv_weight,
        whole_conv_bias,
        whole_decay_gate,
        whole_decay_bias,
        whole_input_gate,
        whole_input_bias,
        whole_decay_param,
        whole_out_proj,
    ) = (
        lax.all_gather(norm_gain, "seq", axis=0, tiled=True),
        lax.all_gather(gate_branch, "seq", axis=0, tiled=True),
        lax.all_gather(input_branch, "seq", axis=0, tiled=True),
        lax.all_gather(conv_weight, "seq", axis=1, tiled=True),
        lax.all_gather(conv_bias, "seq", axis=0, tiled=True),
        lax.all_gather(decay_gate, "seq", axis=0, tiled=True),
        lax.all_gather(decay_bias, "seq", axis=0, tiled=True),
        lax.all_gather(input_gate, "seq", axis=0, tiled=True),
        lax.all_gather(input_bias, "seq", axis=0, tiled=True),
        lax.all_gather(decay_param, "seq", axis=0, tiled=True),
        lax.all_gather(out_proj, "seq", axis=0, tiled=True),
    )
    flag_rows = starts.astype(jnp.float32)
    row_count = tokens.shape[0]
    values = tokens.astype(jnp.float32)
    normed = rms_norm(values, whole_norm_gain.astype(jnp.float32)).astype(jnp.bfloat16)
    gate_pre = jnp.dot(normed, whole_gate_branch, preferred_element_type=jnp.float32)
    gate_act = gelu_tanh(gate_pre)
    conv_input = jnp.dot(normed, whole_input_branch, preferred_element_type=jnp.float32).astype(
        jnp.bfloat16
    )
    lru_width = conv_input.shape[1]
    alive_rows = send_mask(flag_rows)
    masks = build_masks(flag_rows)
    outgoing = conv_input[row_count - (CW - 1) :] * alive_rows[:, None].astype(jnp.bfloat16)
    incoming = passed_along(outgoing, "seq", 1)
    padded = jnp.concatenate([incoming, conv_input], axis=0).astype(jnp.float32)
    conv_out = conv_local(
        padded, whole_conv_weight.astype(jnp.float32), whole_conv_bias.astype(jnp.float32), masks
    )
    conv_low = conv_out.astype(jnp.bfloat16)
    decay_pre = heads_product(conv_low, whole_decay_gate) + whole_decay_bias.astype(jnp.float32)
    input_pre = heads_product(conv_low, whole_input_gate) + whole_input_bias.astype(jnp.float32)
    param_full = whole_decay_param.astype(jnp.float32)
    coefficient, drive_term = lru_terms(decay_pre, input_pre, conv_out, param_full, flag_rows)
    cumulative, local_state = lax.associative_scan(combine, (coefficient, drive_term), axis=0)
    entering = prefix(
        (cumulative[-1], local_state[-1]),
        "seq",
        combine,
        (jnp.ones_like(cumulative[-1]), jnp.zeros_like(local_state[-1])),
        False,
    )
    incoming_state = entering[1]
    states = local_state + cumulative * incoming_state[None, :]
    mixed_rows = (states * gate_act).astype(jnp.bfloat16)
    middle = values + jnp.dot(mixed_rows, whole_out_proj, preferred_element_type=jnp.float32)
    whole_mlp_gain, whole_mlp_gate, whole_mlp_up, whole_mlp_down = (
        lax.all_gather(mlp_gain, "seq", axis=0, tiled=True),
        lax.all_gather(mlp_gate, "seq", axis=0, tiled=True),
        lax.all_gather(mlp_up, "seq", axis=0, tiled=True),
        lax.all_gather(mlp_down, "seq", axis=0, tiled=True),
    )
    gain_two = whole_mlp_gain.astype(jnp.float32)
    normed_two = rms_norm(middle, gain_two).astype(jnp.bfloat16)
    gate_mlp = jnp.dot(normed_two, whole_mlp_gate, preferred_element_type=jnp.float32)
    up_mlp = jnp.dot(normed_two, whole_mlp_up, preferred_element_type=jnp.float32)
    hidden = mlp_act(gate_mlp, up_mlp).astype(jnp.bfloat16)
    result = middle + jnp.dot(hidden, whole_mlp_down, preferred_element_type=jnp.float32)
    block_out = result.astype(jnp.bfloat16)
    back_mlp_gain, back_mlp_gate, back_mlp_up, back_mlp_down = (
        lax.all_gather(mlp_gain, "seq", axis=0, tiled=True),
        lax.all_gather(mlp_gate, "seq", axis=0, tiled=True),
        lax.all_gather(mlp_up, "seq", axis=0, tiled=True),
        lax.all_gather(mlp_down, "seq", axis=0, tiled=True),
    )
    grad_mlp_down = jnp.einsum("tf,td->fd", hidden, cotangent, preferred_element_type=jnp.float32)
    grad_hidden = jnp.einsum(
        "td,fd->tf", cotangent, back_mlp_down, preferred_element_type=jnp.float32
    )
    unused_act, pull_act = jax.vjp(mlp_act, gate_mlp, up_mlp)
    grad_gate_full, grad_up_full = pull_act(grad_hidden)
    grad_gate_low = grad_gate_full.astype(jnp.bfloat16)
    grad_up_low = grad_up_full.astype(jnp.bfloat16)
    grad_mlp_gate = jnp.einsum(
        "td,tf->df", normed_two, grad_gate_low, preferred_element_type=jnp.float32
    )
    grad_mlp_up = jnp.einsum(
        "td,tf->df", normed_two, grad_up_low, preferred_element_type=jnp.float32
    )
    grad_normed_two = jnp.einsum(
        "tf,df->td", grad_gate_low, back_mlp_gate, preferred_element_type=jnp.float32
    ) + jnp.einsum("tf,df->td", grad_up_low, back_mlp_up, preferred_element_type=jnp.float32)
    unused_norm, pull_norm = jax.vjp(rms_norm, middle, back_mlp_gain.astype(jnp.float32))
    grad_middle_norm, grad_mlp_gain = pull_norm(grad_normed_two)
    mlp_sums = (
        lax.psum_scatter(grad_mlp_gain, "seq", scatter_dimension=0, tiled=True),
        lax.psum_scatter(grad_mlp_gate, "seq", scatter_dimension=0, tiled=True),
        lax.psum_scatter(grad_mlp_up, "seq", scatter_dimension=0, tiled=True),
        lax.psum_scatter(grad_mlp_down, "seq", scatter_dimension=0, tiled=True),
    )
    grad_middle = cotangent.astype(jnp.float32) + grad_middle_norm
    grad_branch = grad_middle.astype(jnp.bfloat16)
    (
        back_norm_gain,
        back_gate_branch,
        back_input_branch,
        back_conv_weight,
        back_conv_bias,
        back_decay_gate,
        back_decay_bias,
        back_input_gate,
        back_input_bias,
        back_decay_param,
        back_out_proj,
    ) = (
        lax.all_gather(norm_gain, "seq", axis=0, tiled=True),
        lax.all_gather(gate_branch, "seq", axis=0, tiled=True),
        lax.all_gather(input_branch, "seq", axis=0, tiled=True),
        lax.all_gather(conv_weight, "seq", axis=1, tiled=True),
        lax.all_gather(conv_bias, "seq", axis=0, tiled=True),
        lax.all_gather(decay_gate, "seq", axis=0, tiled=True),
        lax.all_gather(decay_bias, "seq", axis=0, tiled=True),
        lax.all_gather(input_gate, "seq", axis=0, tiled=True),
        lax.all_gather(input_bias, "seq", axis=0, tiled=True),
        lax.all_gather(decay_param, "seq", axis=0, tiled=True),
        lax.all_gather(out_proj, "seq", axis=0, tiled=True),
    )
    grad_out_proj = jnp.einsum(
        "tr,td->rd", mixed_rows, grad_branch, preferred_element_type=jnp.float32
    )
    grad_mixed = jnp.einsum(
        "td,rd->tr", grad_branch, back_out_proj, preferred_element_type=jnp.float32
    )
    grad_states = grad_mixed * gate_act
    unused_gelu, pull_gelu = jax.vjp(gelu_tanh, gate_pre)
    grad_gate_pre = pull_gelu(grad_mixed * states)[0].astype(jnp.bfloat16)
    shifted_coef = jnp.concatenate([coefficient[1:], jnp.ones((1, lru_width), jnp.float32)], axis=0)
    back_cumulative, back_local = lax.associative_scan(
        combine, (shifted_coef[::-1], grad_states[::-1]), axis=0
    )
    back_cumulative = back_cumulative[::-1]
    back_local = back_local[::-1]
    leaving = prefix(
        (coefficient[0] * back_cumulative[0], coefficient[0] * back_local[0]),
        "seq",
        combine,
        (jnp.ones_like(back_local[0]), jnp.zeros_like(back_local[0])),
        True,
    )
    incoming_adjoint = leaving[1]
    adjoint = back_local + back_cumulative * incoming_adjoint[None, :]
    previous = jnp.concatenate([incoming_state[None, :], states[:-1]], axis=0)

    def terms_only(decay_values, input_values, conv_values, param_values):
        return lru_terms(decay_values, input_values, conv_values, param_values, flag_rows)

    unused_terms, pull_terms = jax.vjp(
        terms_only, decay_pre, input_pre, conv_out, back_decay_param.astype(jnp.float32)
    )
    grad_decay_full, grad_input_full, grad_conv_direct, grad_decay_param = pull_terms(
        (adjoint * previous, adjoint)
    )
    grad_decay_bias = jnp.sum(grad_decay_full, axis=0)
    grad_input_bias = jnp.sum(grad_input_full, axis=0)
    grad_decay_low = grad_decay_full.astype(jnp.bfloat16)
    grad_input_low = grad_input_full.astype(jnp.bfloat16)
    grad_decay_gate = heads_grad(conv_low, grad_decay_low)
    grad_input_gate = heads_grad(conv_low, grad_input_low)
    grad_conv_out = (
        grad_conv_direct
        + heads_back(grad_decay_low, back_decay_gate)
        + heads_back(grad_input_low, back_input_gate)
    )

    def conv_only(padded_values, weight_values, bias_values):
        return conv_local(padded_values, weight_values, bias_values, masks)

    unused_conv, pull_conv = jax.vjp(
        conv_only, padded, back_conv_weight.astype(jnp.float32), back_conv_bias.astype(jnp.float32)
    )
    grad_padded, grad_conv_weight, grad_conv_bias = pull_conv(grad_conv_out)
    returned_rows = passed_along(grad_padded[: CW - 1], "seq", -1)
    addition = jnp.concatenate(
        [
            jnp.zeros((row_count - (CW - 1), lru_width), jnp.float32),
            returned_rows * alive_rows[:, None],
        ],
        axis=0,
    )
    grad_conv_input = (grad_padded[CW - 1 :] + addition).astype(jnp.bfloat16)
    grad_input_branch = jnp.einsum(
        "td,tr->dr", normed, grad_conv_input, preferred_element_type=jnp.float32
    )
    grad_gate_branch = jnp.einsum(
        "td,tr->dr", normed, grad_gate_pre, preferred_element_type=jnp.float32
    )
    grad_normed = jnp.einsum(
        "tr,dr->td", grad_conv_input, back_input_branch, preferred_element_type=jnp.float32
    ) + jnp.einsum("tr,dr->td", grad_gate_pre, back_gate_branch, preferred_element_type=jnp.float32)
    unused_first, pull_first = jax.vjp(rms_norm, values, back_norm_gain.astype(jnp.float32))
    grad_values_norm, grad_norm_gain = pull_first(grad_normed)
    grad_tokens = grad_middle + grad_values_norm
    rec_sums = (
        lax.psum_scatter(grad_norm_gain, "seq", scatter_dimension=0, tiled=True),
        lax.psum_scatter(grad_gate_branch, "seq", scatter_dimension=0, tiled=True),
        lax.psum_scatter(grad_input_branch, "seq", scatter_dimension=0, tiled=True),
        lax.psum_scatter(grad_conv_weight, "seq", scatter_dimension=1, tiled=True),
        lax.psum_scatter(grad_conv_bias, "seq", scatter_dimension=0, tiled=True),
        lax.psum_scatter(grad_decay_gate, "seq", scatter_dimension=0, tiled=True),
        lax.psum_scatter(grad_decay_bias, "seq", scatter_dimension=0, tiled=True),
        lax.psum_scatter(grad_input_gate, "seq", scatter_dimension=0, tiled=True),
        lax.psum_scatter(grad_input_bias, "seq", scatter_dimension=0, tiled=True),
        lax.psum_scatter(grad_decay_param, "seq", scatter_dimension=0, tiled=True),
        lax.psum_scatter(grad_out_proj, "seq", scatter_dimension=0, tiled=True),
    )
    return (
        block_out,
        grad_tokens,
        rec_sums[0],
        rec_sums[1],
        rec_sums[2],
        rec_sums[3],
        rec_sums[4],
        rec_sums[5],
        rec_sums[6],
        rec_sums[7],
        rec_sums[8],
        rec_sums[9],
        rec_sums[10],
        mlp_sums[0],
        mlp_sums[1],
        mlp_sums[2],
        mlp_sums[3],
    )


CHIPS = 4
MESH = pl.DeviceIdType.MESH


def place():
    me = lax.axis_index("seq")
    core = lax.rem(me, 2)
    x = lax.rem(lax.div(me, 2), 2)
    y = lax.rem(lax.div(me, 4), 2)
    return me, lax.div(me, 8), 2 * y + x, core, x, y


def column_groups(n):
    return [[8 * z + 2 * p + c for c in range(2) for z in range(n // 8)] for p in range(CHIPS)]


def line_groups(n):
    return [[8 * z + r for z in range(n // 8)] for r in range(8)]


def greet(devices):
    barrier = pltpu.get_barrier_semaphore()
    for device in devices:
        pl.semaphore_signal(barrier, inc=1, device_id=(device,), device_id_type=MESH)
    pl.semaphore_wait(barrier, len(devices))


def remote(source, target, send_sem, recv_sem, device):
    return pltpu.make_async_remote_copy(
        src_ref=source,
        dst_ref=target,
        send_sem=send_sem,
        recv_sem=recv_sem,
        device_id=(device,),
        device_id_type=MESH,
    )


def comm_params(collective_id, vmem_mib=None):
    return pltpu.CompilerParams(
        collective_id=collective_id,
        has_side_effects=True,
        vmem_limit_bytes=None if vmem_mib is None else vmem_mib * 2**20,
    )


def lasting(microseconds):
    return pl.CostEstimate(
        flops=int(microseconds * 1e9), bytes_accessed=int(microseconds * 3e6), transcendentals=0
    )


ANY = pl.BlockSpec(memory_space=pl.ANY)
VMEM = pl.BlockSpec(memory_space=pltpu.VMEM)


def plane_neighbours():
    me, z, p, c, x, y = place()
    x_dev, y_dev = me + 2 - 4 * x, me + 4 - 8 * y
    return (x_dev, y_dev, y_dev + 2 - 4 * x), (p + 1 - 2 * x, p + 2 - 4 * y, 3 - p)


def gather_steps(source, whole, send, recv, local, first):
    me, z, p, c, x, y = place()
    (x_dev, y_dev, d_dev), (p_x, p_y, p_d) = plane_neighbours()
    half = source.shape[0] // 2

    def copy(k, source, target, device):
        return remote(source, target, send.at[first + k], recv.at[first + k], device)

    to_x, to_y = copy(0, source, whole.at[p], x_dev), copy(1, source, whole.at[p], y_dev)
    low, high = whole.at[p_x, pl.ds(0, half)], whole.at[p_y, pl.ds(half, half)]
    on_y, on_x = copy(2, low, low, y_dev), copy(3, high, high, x_dev)
    own = pltpu.make_async_copy(source, whole.at[p], local)

    def begin():
        to_x.start()
        to_y.start()
        own.start()

    def forward():
        to_x.wait_recv()
        on_y.start()
        to_y.wait_recv()
        on_x.start()

    def end():
        to_x.wait_send()
        to_y.wait_send()
        on_y.wait()
        on_x.wait()
        own.wait()

    return begin, forward, end


def sum_scratch(rows, columns, dtype):
    whole, part = pltpu.VMEM((rows, columns), dtype), pltpu.VMEM((rows // 2, columns), dtype)
    return [whole] * 3 + [part] * 4 + [pltpu.SemaphoreType.DMA((6,)), pltpu.SemaphoreType.DMA((6,)), pltpu.SemaphoreType.DMA((3,))]


def sum_steps(part, own, from_x, from_y, diag_x, diag_y, on_x, on_y, send, recv, local):
    me, z, p, c, x, y = place()
    (x_dev, y_dev, d_dev), (p_x, p_y, p_d) = plane_neighbours()
    half = part.shape[1] // 2
    low, high = pl.ds(0, half), pl.ds(half, half)
    copies = [
        remote(part.at[p_d, low], diag_x, send.at[0], recv.at[0], x_dev),
        remote(part.at[p_d, high], diag_y, send.at[1], recv.at[1], y_dev),
        remote(part.at[p_x, low], from_x.at[low], send.at[2], recv.at[2], x_dev),
        remote(part.at[p_y, high], from_y.at[high], send.at[3], recv.at[3], y_dev),
    ]
    locals_ = [
        pltpu.make_async_copy(part.at[p_y, low], on_y, local.at[0]),
        pltpu.make_async_copy(part.at[p_x, high], on_x, local.at[1]),
        pltpu.make_async_copy(part.at[p], own, local.at[2]),
    ]
    to_y = remote(on_y, from_y.at[low], send.at[4], recv.at[4], y_dev)
    to_x = remote(on_x, from_x.at[high], send.at[5], recv.at[5], x_dev)

    def add_into(target, addend):
        @pl.loop(0, half // 16)
        def add_rows(i):
            at = pl.ds(pl.multiple_of(i * 16, 16), 16)
            target[at, :] = (
                target[at, :].astype(jnp.float32) + addend[at, :].astype(jnp.float32)
            ).astype(target.dtype)

    def begin():
        for copy in copies + locals_:
            copy.start()

    def forward():
        locals_[0].wait()
        copies[0].wait_recv()
        add_into(on_y, diag_x)
        to_y.start()
        locals_[1].wait()
        copies[1].wait_recv()
        add_into(on_x, diag_y)
        to_x.start()

    def end():
        locals_[2].wait()
        copies[2].wait_recv()
        copies[3].wait_recv()
        to_y.wait()
        to_x.wait()
        for copy in copies:
            copy.wait_send()

    return begin, forward, end


def sixteen(i):
    return pl.ds(pl.multiple_of(i * 16, 16), 16)


def fetch_rows(rows_all, first, start, target, sems):
    count = sems.shape[0]
    rows = target.shape[0] // count
    return [
        pltpu.make_async_copy(
            rows_all.at[first + k, pl.ds(start, rows)], target.at[pl.ds(k * rows, rows)], sems.at[k]
        )
        for k in range(count)
    ]


def computed_scratch(rows, columns, dtype):
    f32, bf16 = jnp.float32, jnp.bfloat16
    whole, half = (rows, columns), (rows // 2, columns)
    shapes = [(whole, bf16), (whole, f32)] + [(half, f32)] * 2 + [(half, bf16)] * 6 + [(half, dtype)] * 4
    return [pltpu.VMEM(*shape) for shape in shapes] + [pltpu.SemaphoreType.DMA((6,))] * 2


def computed_sum(product, sent_d, own, kept_x, kept_y, *refs):
    sent_x, sent_y, from_x, from_y, diag_x, diag_y, joint_x, joint_y, also_x, also_y, send, recv = refs
    (x_dev, y_dev, d_dev), (p_x, p_y, p_d) = plane_neighbours()
    p = place()[2]
    rows, width = own.shape
    half = rows // 2
    low, high = pl.ds(0, half), pl.ds(half, half)
    tile = 512

    def into(chip, at, target):
        @pl.loop(0, width // tile)
        def product_tile(k):
            columns = pl.ds(pl.multiple_of(k * tile, tile), tile)
            target[:, columns] = product(chip, at, columns).astype(target.dtype)

    def copy(k, source, target, device):
        return remote(source, target, send.at[k], recv.at[k], device)

    first = [copy(0, sent_d.at[low], diag_x, x_dev), copy(1, sent_d.at[high], diag_y, y_dev)]
    second = [copy(2, sent_x, from_x, x_dev), copy(3, sent_y, from_y, y_dev)]
    third = [copy(4, joint_y, also_y, y_dev), copy(5, joint_x, also_x, x_dev)]

    def begin():
        into(p_d, slice(None), sent_d)
        for sent in first:
            sent.start()
        into(p_x, low, sent_x)
        into(p_y, high, sent_y)
        for sent in second:
            sent.start()
        into(p_y, low, kept_y)
        into(p_x, high, kept_x)
        into(p, slice(None), own)

    def add(target, kept, addend):
        @pl.loop(0, half // 16)
        def add_rows(i):
            at = sixteen(i)
            target[at, :] = (kept[at, :] + addend[at, :].astype(jnp.float32)).astype(target.dtype)

    def forward():
        first[0].wait_recv()
        add(joint_y, kept_y, diag_x)
        third[0].start()
        first[1].wait_recv()
        add(joint_x, kept_x, diag_y)
        third[1].start()

    def end():
        for sent in first:
            sent.wait_send()
        for sent in second + third:
            sent.wait()

    def total(i, j):
        at = sixteen(j)
        parts = (from_x, also_y) if i == 0 else (also_x, from_y)
        here = pl.ds(pl.multiple_of(i * half + j * 16, 16), 16)
        return here, own[here, :] + parts[0][at, :].astype(jnp.float32) + parts[1][at, :].astype(jnp.float32)

    return begin, forward, end, total


def middle_kernel(
    mixed, rows_all, tokens, gain, cot, middle, whole, cot_other, normed, out_here, send, recv, local, loads, *sums
):
    me, z, p, c, x, y = place()
    sibling = me + 1 - 2 * c
    greet((*plane_neighbours()[0][:2], sibling))
    to_sibling = remote(cot, cot_other, send.at[4], recv.at[4], sibling)
    to_sibling.start()
    f32, bf16 = jnp.float32, jnp.bfloat16
    fetched = fetch_rows(rows_all, 0, 0, out_here, loads)
    for copy in fetched:
        copy.start()
    for copy in fetched:
        copy.wait()

    def product(chip, at, columns):
        return jnp.dot(mixed[chip, at, :], out_here[:, columns], preferred_element_type=f32)

    *steps, total = computed_sum(product, *sums)
    for step in steps:
        step()
    for i in range(2):

        @pl.loop(0, tokens.shape[0] // 32)
        def norm_rows(j):
            at, values = total(i, j)
            values = tokens[at, :].astype(f32) + values
            middle[at, :] = values
            inverse = lax.rsqrt(jnp.mean(values * values, axis=-1, keepdims=True) + epsilon)
            normed[at, :] = (values * inverse * gain[...]).astype(bf16)

    for step in gather_steps(normed, whole, send, recv, local, 0):
        step()
    to_sibling.wait()


def middle_of(mixed, rows_all, tokens, gain, cot, collective_id):
    rows, width = tokens.shape
    channels = mixed.shape[2]
    f32, bf16 = jnp.float32, jnp.bfloat16
    return pl.pallas_call(
        middle_kernel,
        out_shape=[
            jax.ShapeDtypeStruct((rows, width), f32),
            jax.ShapeDtypeStruct((CHIPS, rows, width), bf16),
            jax.ShapeDtypeStruct(cot.shape, cot.dtype),
        ],
        in_specs=[VMEM, ANY, VMEM, VMEM, ANY],
        out_specs=[VMEM, ANY, ANY],
        scratch_shapes=[
            pltpu.VMEM((rows, width), bf16),
            pltpu.VMEM((channels, width), bf16),
            pltpu.SemaphoreType.DMA((5,)),
            pltpu.SemaphoreType.DMA((5,)),
            pltpu.SemaphoreType.DMA,
            pltpu.SemaphoreType.DMA((rows_all.shape[0],)),
            *computed_scratch(rows, width, f32),
        ],
        compiler_params=comm_params(collective_id, 60),
        cost_estimate=lasting(75),
        name="middle",
    )(mixed, rows_all, tokens, gain[None], cot)


def feed_forward_kernel(
    piece,
    two,
    cot,
    weights,
    down,
    *refs,
):
    last = piece == 1
    if last:
        earlier, hidden, grad, parts, earlier_here, *refs = refs
    else:
        hidden, grad, parts, *refs = refs
    low, two_here, two_there, cot_here, weights_here, down_here, low_there, send, recv, loads, down_loads = refs
    me, z, p, c, x, y = place()
    sibling = me + 1 - 2 * c
    greet((sibling,))
    f32, bf16 = jnp.float32, jnp.bfloat16
    tokens, width = two.shape
    units = hidden.shape[1]
    half = width // 2
    pairs = [
        (two, two_here),
        (weights, weights_here),
        (cot, cot_here),
    ]
    if last:
        pairs.append((earlier, earlier_here))
    fetched = [pltpu.make_async_copy(a, b, loads.at[k]) for k, (a, b) in enumerate(pairs)]
    count = down_loads.shape[0]
    fetched[3:3] = fetch_rows(down, count * piece, down.shape[1] - units // count, down_here, down_loads)
    for copy in fetched:
        copy.start()
    other_half = two.at[:, pl.ds(pl.multiple_of((1 - c) * half, 128), half)]
    two_swap = remote(other_half, two_there, send.at[0], recv.at[0], sibling)
    two_swap.start()
    for copy in fetched[: 3 + count]:
        copy.wait()
    tile, block = 256, 512

    def dot_t(left, right):
        return lax.dot_general(left, right, (((1,), (1,)), ((), ())), preferred_element_type=f32)

    def dot_first(left, right):
        return lax.dot_general(left, right, (((0,), (0,)), ((), ())), preferred_element_type=f32)

    low_swaps = []
    for t in range(units // tile):
        gate_at, up_at = pl.ds(t * tile, tile), pl.ds(units + t * tile, tile)

        @pl.loop(0, tokens // block)
        def rows_block(j):
            at = pl.ds(pl.multiple_of(j * block, block), block)
            v = jnp.dot(two_here[at, :], weights_here[:, gate_at], preferred_element_type=f32)
            up = jnp.dot(two_here[at, :], weights_here[:, up_at], preferred_element_type=f32)
            grad_hidden = dot_t(cot_here[at, :], down_here[gate_at, :])
            square = v * v
            bent = jnp.tanh(v * (GELU_A + GELU_A * GELU_B * square))
            rising = 0.5 + 0.5 * bent
            act = v * rising
            slope = rising + 0.5 * v * (1.0 - bent * bent) * (GELU_A + 3.0 * GELU_A * GELU_B * square)
            hidden[at, gate_at] = (act * up).astype(bf16)
            low[at, gate_at] = (grad_hidden * up * slope).astype(bf16)
            low[at, up_at] = (grad_hidden * act).astype(bf16)

        for k, columns in enumerate((gate_at, up_at)):
            sems = 1 + 2 * t + k
            low_swaps.append(
                remote(low.at[:, columns], low_there.at[:, columns], send.at[sems], recv.at[sems], sibling)
            )
            low_swaps[-1].start()
    for copy in fetched[3 + count :]:
        copy.wait()

    @pl.loop(0, tokens // block)
    def parts_block(j):
        at = pl.ds(pl.multiple_of(j * block, block), block)

        @pl.loop(0, width // block)
        def parts_tile(k):
            columns = pl.ds(pl.multiple_of(k * block, block), block)
            values = dot_t(low[at, :], weights_here[columns, :])
            if last:
                values = values + earlier_here[at, columns]
            parts[at, columns] = values.astype(parts.dtype)

    two_swap.wait()
    for copy in low_swaps:
        copy.wait()

    @pl.loop(0, half // block)
    def grad_block(m):
        here = pl.ds(pl.multiple_of(c * half + m * block, 128), block)
        there = pl.ds(pl.multiple_of(m * block, block), block)

        @pl.loop(0, 2 * units // block)
        def grad_tile(k):
            columns = pl.ds(pl.multiple_of(k * block, block), block)
            grad[there, columns] = (
                dot_first(two_here[:, here], low[:, columns]) + dot_first(two_there[:, there], low_there[:, columns])
            ).astype(bf16)


def feed_forward(piece, two, cot, weights, down, earlier, collective_id):
    tokens, width = two.shape
    units = weights.shape[1] // 2
    bf16 = jnp.bfloat16
    out_shape = [
        jax.ShapeDtypeStruct((tokens, units), bf16),
        jax.ShapeDtypeStruct((width // 2, 2 * units), bf16),
    ]
    low = pltpu.VMEM((tokens, 2 * units), bf16)
    scratch = []
    if earlier:
        out_shape.append(jax.ShapeDtypeStruct((tokens, width), bf16))
        scratch = [pltpu.VMEM((tokens, width), jnp.float32)]
    else:
        out_shape.append(jax.ShapeDtypeStruct((tokens, width), jnp.float32))
    swaps = 1 + 2 * (units // 256)
    return pl.pallas_call(
        functools.partial(feed_forward_kernel, piece),
        out_shape=out_shape,
        in_specs=[ANY] * (4 + len(earlier)),
        out_specs=[VMEM] * 3,
        scratch_shapes=[
            *scratch,
            low,
            pltpu.VMEM((tokens, width), bf16),
            pltpu.VMEM((tokens, width // 2), bf16),
            pltpu.VMEM((tokens, width), bf16),
            pltpu.VMEM(weights.shape, bf16),
            pltpu.VMEM((units, width), bf16),
            low,
            pltpu.SemaphoreType.DMA((swaps,)),
            pltpu.SemaphoreType.DMA((swaps,)),
            pltpu.SemaphoreType.DMA((3 + len(earlier),)),
            pltpu.SemaphoreType.DMA((down.shape[0] // 2,)),
        ],
        compiler_params=comm_params(collective_id, 60),
        cost_estimate=lasting(35),
        name="feed_forward",
    )(two, cot, weights, down, *earlier)


def norm_back_rows(values, gain, grad, rest):
    inverse = lax.rsqrt(jnp.mean(values * values, axis=-1, keepdims=True) + epsilon)
    scaled = gain * grad
    pull = jnp.mean(scaled * values, axis=-1, keepdims=True) * (inverse * inverse * inverse)
    return rest + inverse * scaled - values * pull, grad * values * inverse


def grads_of_middle_kernel(
    parts,
    middle,
    cot,
    gain,
    hidden_zero,
    hidden_one,
    down,
    cot_all,
    cot_other,
    mixed_zero,
    mixed_one,
    grad_middle,
    grad_gain,
    whole,
    row_grads,
    down_parts,
    branch,
    branch_all,
    branch_other,
    mixed_here,
    mixed_there,
    out_sum,
    hidden_here,
    hidden_other,
    down_here,
    cot_here,
    cot_there,
    *scratch,
):
    sums, (send, recv, local, loads, down_loads) = scratch[:10], scratch[10:]
    me, z, p, c, x, y = place()
    f32, bf16 = jnp.float32, jnp.bfloat16
    sibling = me + 1 - 2 * c
    greet((*plane_neighbours()[0][:2], sibling))
    own, from_x, from_y = sums[:3]
    begin, forward, end = sum_steps(parts, *sums)
    begin()
    half = hidden_zero.shape[1]
    swaps = [remote(hidden, hidden_other, send.at[4], recv.at[4], sibling) for hidden in (hidden_one, hidden_zero)]
    mixed_swaps = [remote(mixed, mixed_there, send.at[9], recv.at[9], sibling) for mixed in (mixed_one, mixed_zero)]
    mixed_loads = [pltpu.make_async_copy(mixed, mixed_here, loads.at[4]) for mixed in (mixed_zero, mixed_one)]

    @pl.when(c == 0)
    def send_one():
        swaps[0].start()
        mixed_swaps[0].start()
        mixed_loads[0].start()

    @pl.when(c == 1)
    def send_zero():
        swaps[1].start()
        mixed_swaps[1].start()
        mixed_loads[1].start()

    fetched = [
        pltpu.make_async_copy(source, target, loads.at[k])
        for k, (source, target) in enumerate(
            (
                (hidden_zero, hidden_here.at[:, pl.ds(0, half)]),
                (hidden_one, hidden_here.at[:, pl.ds(half, half)]),
                (cot_all, cot_here),
                (cot_other, cot_there),
            )
        )
    ]
    count = down_loads.shape[0]
    down_fetched = fetch_rows(down, 0, down.shape[1] - down_here.shape[0] // count, down_here, down_loads)
    for copy in fetched + down_fetched:
        copy.start()
    for copy in fetched[:4]:
        copy.wait()
    swaps[0].wait()
    tile = 256

    planes = row_grads.shape[0]
    units = half // planes
    above = row_grads.shape[1] - units

    def grad_tiles(m):
        rows_here = pl.ds(pl.multiple_of(c * half + m * tile, 128), tile)

        @pl.loop(0, cot_all.shape[1] // (2 * tile))
        def grad_tile(k):
            columns = pl.ds(pl.multiple_of(k * 2 * tile, 128), 2 * tile)

            def dot_t(left, right):
                return lax.dot_general(left, right, (((0,), (0,)), ((), ())), preferred_element_type=f32)

            values = (
                dot_t(hidden_here[:, rows_here], cot_here[:, columns])
                + dot_t(hidden_other[:, m * tile : (m + 1) * tile], cot_there[:, columns])
            ).astype(bf16)
            for j in range(planes):
                start, stop = max(j * units, m * tile), min((j + 1) * units, (m + 1) * tile)
                if start < stop:
                    row_grads[j, above + start - j * units : above + stop - j * units, columns] = values[
                        start - m * tile : stop - m * tile
                    ]

    grad_tiles(0)
    forward()
    for m in range(1, half // tile):
        grad_tiles(m)
    end()
    rows, width = middle.shape

    def norm_rows(i, total):
        at = sixteen(i)
        grad = own[at, :].astype(f32) + from_x[at, :].astype(f32) + from_y[at, :].astype(f32)
        given, terms = norm_back_rows(middle[at, :], gain[...], grad, cot[at, :].astype(f32))
        grad_middle[at, :] = given
        branch[at, :] = given.astype(bf16)
        return total + terms[:8] + terms[8:]

    total = lax.fori_loop(0, rows // 16, norm_rows, jnp.zeros((8, width), f32))
    grad_gain[...] = jnp.sum(total, axis=0, keepdims=True)
    begin, forward, end = gather_steps(branch, branch_all, send, recv, local, 0)
    (p_x, p_y, p_d) = plane_neighbours()[1]

    def to_sibling(k, chip, source):
        return remote(source, branch_other.at[chip], send.at[5 + k], recv.at[5 + k], sibling)

    shares = [to_sibling(0, p, branch)] + [
        to_sibling(1 + k, chip, branch_all.at[chip]) for k, chip in enumerate((p_x, p_y, p_d))
    ]
    begin()
    shares[0].start()
    for copy in down_fetched + [mixed_loads[0], mixed_swaps[0]]:
        copy.wait()

    def down_tiles(j):
        @pl.loop(0, width // (2 * tile))
        def down_tile(k):
            columns = pl.ds(pl.multiple_of(k * 2 * tile, 128), 2 * tile)
            down_parts[j, :, columns] = jnp.dot(
                hidden_here[pl.ds(pl.multiple_of(j * rows, 16), rows), :],
                down_here[:, columns],
                preferred_element_type=f32,
            ).astype(bf16)

    pl.loop(0, CHIPS)(down_tiles)

    def out_tiles(mixed, branches, chips, finish):
        @pl.loop(0, width // (2 * tile))
        def out_tile(k):
            columns = pl.ds(pl.multiple_of(k * 2 * tile, 128), 2 * tile)
            values = out_sum[:, columns]
            for chip in chips:
                values = values + lax.dot_general(
                    mixed[pl.ds(pl.multiple_of(chip * rows, 16), rows), :],
                    branches[chip, :, columns],
                    (((0,), (0,)), ((), ())),
                    preferred_element_type=f32,
                )
            if finish:
                for j in range(planes):
                    row_grads[j, 0:above, columns] = values[j * above : (j + 1) * above].astype(bf16)
            else:
                out_sum[:, columns] = values

    forward()
    shares[1].start()
    shares[2].start()
    out_sum[...] = jnp.zeros_like(out_sum)
    out_tiles(mixed_here, branch_all, (p_x, p_y), False)
    end()
    shares[3].start()
    to_whole = pltpu.make_async_copy(branch_all, whole, local)
    to_whole.start()
    out_tiles(mixed_here, branch_all, (p, p_d), False)
    for copy in shares:
        copy.wait()
    out_tiles(mixed_there, branch_other, range(CHIPS), True)
    to_whole.wait()


def grads_of_middle(parts, middle, cot, gain, hiddens, down, cots, mixeds, collective_id):
    rows, width = middle.shape
    tokens, units = hiddens[0].shape[0], 2 * hiddens[0].shape[1]
    f32, bf16 = jnp.float32, jnp.bfloat16
    return pl.pallas_call(
        grads_of_middle_kernel,
        out_shape=[
            jax.ShapeDtypeStruct((rows, width), f32),
            jax.ShapeDtypeStruct((1, width), f32),
            jax.ShapeDtypeStruct((CHIPS, rows, width), bf16),
            jax.ShapeDtypeStruct(
                (down.shape[0] // 2, down.shape[1], width), bf16
            ),
            jax.ShapeDtypeStruct((CHIPS, rows, width), bf16),
        ],
        in_specs=[ANY, VMEM, VMEM, VMEM] + [ANY] * 7,
        out_specs=[VMEM, VMEM, ANY, VMEM, VMEM],
        scratch_shapes=[
            pltpu.VMEM((rows, width), bf16),
            pltpu.VMEM((CHIPS, rows, width), bf16),
            pltpu.VMEM((CHIPS, rows, width), bf16),
            pltpu.VMEM(mixeds[0].shape, bf16),
            pltpu.VMEM(mixeds[0].shape, bf16),
            pltpu.VMEM((mixeds[0].shape[1], width), f32),
            pltpu.VMEM((tokens, units), bf16),
            pltpu.VMEM((tokens, units // 2), bf16),
            pltpu.VMEM((units, width), bf16),
            pltpu.VMEM((tokens, width), bf16),
            pltpu.VMEM((tokens, width), bf16),
            *sum_scratch(rows, width, parts.dtype),
            pltpu.SemaphoreType.DMA((10,)),
            pltpu.SemaphoreType.DMA((10,)),
            pltpu.SemaphoreType.DMA,
            pltpu.SemaphoreType.DMA((5,)),
            pltpu.SemaphoreType.DMA((down.shape[0],)),
        ],
        compiler_params=comm_params(collective_id, 60),
        cost_estimate=lasting(80),
        name="grads_of_middle",
    )(parts, middle, cot, gain[None], *hiddens, down, *cots, *mixeds)


def closing_kernel(
    planes,
    in_low,
    whole_in,
    tokens,
    gain,
    rest,
    small,
    mlp_gain,
    conv_low,
    decay_low,
    input_low,
    piece,
    grad_tokens,
    small_out,
    gates_out,
    swapped,
    conv_a,
    conv_b,
    decay_a,
    decay_b,
    input_a,
    input_b,
    full,
    gates,
    gate_lines,
    lines,
    line,
    near_part,
    gains,
    gain_lines,
    gain_line,
    gain_near,
    gain_sum,
    send,
    recv,
    loads,
    swap_send,
    swap_recv,
    *sums,
):
    me, z, p, c, x, y = place()
    f32 = jnp.float32
    r = lax.rem(me, 8)
    near = [(lax.rem(r + d, 8), me - r + lax.rem(r + d, 8)) for d in range(1, 8)]
    far = [(lax.rem(z + d, planes), 8 * lax.rem(z + d, planes) + r) for d in range(1, planes)]
    greet([device for unused, device in near + far])

    def copy(k, source, target, device):
        return remote(source, target, send.at[k], recv.at[k], device)

    lows = ((conv_low, conv_a, conv_b), (decay_low, decay_a, decay_b), (input_low, input_a, input_b))
    fetched = [pltpu.make_async_copy(source, here, loads.at[k]) for k, (source, here, there) in enumerate(lows)]
    exchanges = [copy(k, source, there, me + 1 - 2 * c) for k, (source, here, there) in enumerate(lows)]
    at = 3
    small_far = [copy(at + d, small.at[there], lines.at[d], device) for d, (there, device) in enumerate(far)]
    at += len(far)
    for started in small_far + fetched + exchanges:
        started.start()

    def product(chip, rows_at, columns):
        return lax.dot_general(
            in_low[chip, rows_at, :], whole_in[columns, :], (((1,), (1,)), ((), ())), preferred_element_type=f32
        )

    begin, forward, end, part_of = computed_sum(product, *sums)
    begin()
    for ended in fetched + exchanges:
        ended.wait()
    swaps = swap_copies(piece, swapped, swap_send, swap_recv, loads.at[3])

    def dot_first(left, right):
        return lax.dot_general(left, right, (((0,), (0,)), ((), ())), preferred_element_type=f32)

    block = gates.shape[1]
    count = planes * block
    for k, (first, second) in enumerate(((decay_a, decay_b), (input_a, input_b))):
        full[...] = dot_first(conv_a[...], first[...]) + dot_first(conv_b[...], second[...])
        for j in range(planes):
            rows_at = pl.ds(pl.multiple_of(c * count + j * block, 8), block)
            for e in range(2):
                gates[j, :, (2 * k + e) * block : (2 * k + e + 1) * block] = full[
                    rows_at, e * count + j * block : e * count + (j + 1) * block
                ].astype(gates.dtype)
    gate_far = [copy(at + d, gates.at[there], gate_lines.at[d], device) for d, (there, device) in enumerate(far)]
    at += len(far)
    for sent in gate_far:
        sent.start()
    forward()
    for sent in swaps:
        sent.start()
    for sent in small_far:
        sent.wait()
    line[...] = small[z] + sum(lines[d] for d in range(planes - 1))
    small_near = copy(at, line.at[1 - c], near_part, me + 1 - 2 * c)
    small_near.start()
    at += 1
    end()
    rows, width = tokens.shape
    step = width // (8 * planes)

    def norm_rows(i, j, total):
        here, grad = part_of(i, j)
        given, terms = norm_back_rows(tokens[here, :].astype(f32), gain[...], grad, rest[here, :])
        for k in range(4 * planes):
            for e in range(2):
                grad_tokens[here, (2 * k + e) * step : (2 * k + e + 1) * step] = given[
                    :, (4 * planes * e + k) * step : (4 * planes * e + k + 1) * step
                ]
        return total + terms[:8] + terms[8:]

    total = jnp.zeros((8, width), f32)
    for i in range(2):
        total = lax.fori_loop(0, rows // 32, functools.partial(norm_rows, i), total)
    total = jnp.sum(total, axis=0, keepdims=True)
    for j in range(planes):
        for q in range(CHIPS):
            for e in range(2):
                start = ((e * planes + j) * CHIPS + q) * step
                gains[j, 2 * q + e : 2 * q + e + 1, 0:step] = total[:, start : start + step]
                gains[j, 2 * q + e : 2 * q + e + 1, step : 2 * step] = mlp_gain[:, start : start + step]
    gain_far = [copy(at + d, gains.at[there], gain_lines.at[d], device) for d, (there, device) in enumerate(far)]
    at += len(far)
    for sent in gain_far:
        sent.start()
    for sent in gain_far:
        sent.wait()
    gain_line[...] = gains[z] + sum(gain_lines[d] for d in range(planes - 1))
    last = [copy(at + d, gain_line, gain_near.at[d], device) for d, (there, device) in enumerate(near)]
    for sent in last:
        sent.start()
    for sent in gate_far + swaps + [small_near]:
        sent.wait()
    gates_out[...] = gates[z].astype(f32) + sum(gate_lines[d].astype(f32) for d in range(planes - 1))
    for sent in last:
        sent.wait()
    rows_small = line.shape[1]
    small_out[0:rows_small, :] = line[c] + near_part[...]
    gain_sum[...] = gain_line[...] + sum(gain_near[d] for d in range(7))
    small_out[rows_small : rows_small + 1, :] = gain_sum[pl.ds(r, 1), :]


def closing(in_low, whole_in, tokens, gain, rest, small, mlp_gain, lows, piece, head, collective_id):
    planes = lax.axis_size("seq") // 8
    rows, width = tokens.shape
    f32, bf16 = jnp.float32, jnp.bfloat16
    rows_small, lanes = small.shape[2:]
    channels = lows[0].shape[1]
    block = channels // (2 * planes)
    count = 3 + 3 * (planes - 1) + 8
    return pl.pallas_call(
        functools.partial(closing_kernel, planes),
        out_shape=[
            jax.ShapeDtypeStruct((rows, width), f32),
            jax.ShapeDtypeStruct((rows_small + 1, lanes), f32),
            jax.ShapeDtypeStruct((block, 2 * head), f32),
            jax.ShapeDtypeStruct(piece.shape, bf16),
        ],
        in_specs=[VMEM] * 7 + [ANY] * 4,
        out_specs=[VMEM] * 3 + [ANY],
        scratch_shapes=[
            *[pltpu.VMEM(lows[0].shape, bf16)] * 6,
            pltpu.VMEM((channels, channels), f32),
            pltpu.VMEM((planes, block, 2 * head), bf16),
            pltpu.VMEM((planes - 1, block, 2 * head), bf16),
            pltpu.VMEM((planes - 1, 2, rows_small, lanes), f32),
            pltpu.VMEM((2, rows_small, lanes), f32),
            pltpu.VMEM((rows_small, lanes), f32),
            pltpu.VMEM((planes, 8, lanes), f32),
            pltpu.VMEM((planes - 1, 8, lanes), f32),
            pltpu.VMEM((8, lanes), f32),
            pltpu.VMEM((7, 8, lanes), f32),
            pltpu.VMEM((8, lanes), f32),
            pltpu.SemaphoreType.DMA((count,)),
            pltpu.SemaphoreType.DMA((count,)),
            pltpu.SemaphoreType.DMA((4,)),
            pltpu.SemaphoreType.DMA((3,)),
            pltpu.SemaphoreType.DMA((3,)),
            *computed_scratch(rows, width, bf16),
        ],
        compiler_params=comm_params(collective_id, 60),
        cost_estimate=lasting(50),
        name="closing",
    )(in_low, whole_in, tokens, gain[None], rest, small, mlp_gain, *lows, piece)


def first_swap_kernel(planes, pairs, *refs):
    count = len(pairs)
    ins, (out, parts, send, recv, local) = refs[:count], refs[count:]
    to_chips_kernel(planes, pairs, *ins, parts)
    greet(plane_neighbours()[0])
    copies = swap_copies(parts, out, send, recv, local)
    for copy in copies:
        copy.start()
    for copy in copies:
        copy.wait()


def first_swap(weights, pairs, width, collective_id):
    planes = lax.axis_size("seq") // 8
    shape = (CHIPS, weights[0].shape[0], width)
    return pl.pallas_call(
        functools.partial(first_swap_kernel, planes, pairs),
        out_shape=jax.ShapeDtypeStruct(shape, weights[0].dtype),
        in_specs=[VMEM] * len(weights),
        out_specs=ANY,
        scratch_shapes=[
            pltpu.VMEM(shape, weights[0].dtype),
            pltpu.SemaphoreType.DMA((3,)),
            pltpu.SemaphoreType.DMA((3,)),
            pltpu.SemaphoreType.DMA,
        ],
        compiler_params=comm_params(collective_id, 60),
        name="first_swap",
    )(*weights)


def plane_swap_kernel(count, *refs):
    ins, outs = refs[:count], refs[count : 2 * count]
    send, recv, local = refs[2 * count :]
    me, z, p, c, x, y = place()
    x_dev, y_dev = me + 2 - 4 * x, me + 4 - 8 * y
    d_dev = y_dev + 2 - 4 * x
    p_x, p_y, p_d = p + 1 - 2 * x, p + 2 - 4 * y, 3 - p
    peers = ((x_dev, p_x), (y_dev, p_y), (d_dev, p_d))
    greet([device for device, unused in peers])
    copies = []
    for k in range(count):
        for j, (device, chip) in enumerate(peers):
            copies.append(remote(ins[k].at[chip], outs[k].at[p], send.at[k, j], recv.at[k, j], device))
        copies.append(pltpu.make_async_copy(ins[k].at[p], outs[k].at[p], local.at[k]))
    for copy in copies:
        copy.start()
    for copy in copies:
        copy.wait()


def plane_swap(arrays, collective_id):
    count = len(arrays)
    return pl.pallas_call(
        functools.partial(plane_swap_kernel, count),
        out_shape=[jax.ShapeDtypeStruct(a.shape, a.dtype) for a in arrays],
        in_specs=[ANY] * count,
        out_specs=[ANY] * count,
        scratch_shapes=[
            pltpu.SemaphoreType.DMA((count, 3)),
            pltpu.SemaphoreType.DMA((count, 3)),
            pltpu.SemaphoreType.DMA((count,)),
        ],
        compiler_params=comm_params(collective_id, 60),
        cost_estimate=lasting(10),
        name="plane_swap",
    )(*arrays)


def swap_copies(source, target, send, recv, local):
    devices, chips = plane_neighbours()
    p = place()[2]
    return [
        *[remote(source.at[chips[j]], target.at[p], send.at[j], recv.at[j], devices[j]) for j in range(3)],
        pltpu.make_async_copy(source.at[p], target.at[p], local),
    ]


def opening_kernel(
    planes,
    pairs,
    small,
    gates,
    tokens,
    mlp_gate,
    mlp_up,
    gathered,
    decay_blocks,
    input_blocks,
    second_piece,
    whole,
    swapped,
    piece,
    gates_all,
    gain,
    normed,
    *sems,
):
    send, recv, gate_send, gate_recv, swap_send, swap_recv, swap_local, gather_send, gather_recv, gather_local = sems
    me, z, p, c, x, y = place()
    r = lax.rem(me, 8)
    near = [me - r + lax.rem(r + d, 8) for d in range(1, 8)]
    far = [8 * lax.rem(z + d, planes) + r for d in range(1, planes)]
    greet(near + far)
    lines = [
        remote(small, gathered.at[r, z], send.at[d], recv.at[d], device) for d, device in enumerate(far)
    ]
    gate_lines = [
        remote(gates, gates_all.at[c, z], gate_send.at[d], gate_recv.at[d], device) for d, device in enumerate(far)
    ]
    for copy in lines + gate_lines:
        copy.start()
    gathered[r, z] = small[...]
    gates_all[c, z] = gates[...]
    to_chips_kernel(planes, pairs, mlp_gate, mlp_up, piece, second_piece)
    for copy in lines:
        copy.wait()
    spreads = [
        remote(gathered.at[r], gathered.at[r], send.at[planes + d], recv.at[planes + d], device)
        for d, device in enumerate(near)
    ]
    for copy in spreads:
        copy.start()
    for copy in gate_lines:
        copy.wait()
    gate_swap = remote(
        gates_all.at[c], gates_all.at[c], gate_send.at[planes], gate_recv.at[planes], me + 1 - 2 * c
    )
    gate_swap.start()
    for copy in spreads:
        copy.wait()
    swaps = swap_copies(piece, swapped, swap_send, swap_recv, swap_local)
    rows, width = tokens.shape
    step = width // (8 * planes)
    for j in range(planes):
        for q in range(CHIPS):
            for e in range(2):
                start = ((e * planes + j) * CHIPS + q) * step
                gain[0:1, start : start + step] = gathered[2 * q + e, j, 0:1, 0:step]

    @pl.loop(0, rows // 16)
    def norm_rows(i):
        at = sixteen(i)
        values = tokens[at, :].astype(jnp.float32)
        inverse = lax.rsqrt(jnp.mean(values * values, axis=-1, keepdims=True) + epsilon)
        normed[at, :] = (values * inverse * gain[0:1, :]).astype(jnp.bfloat16)

    begin, forward, end = gather_steps(normed, whole, gather_send, gather_recv, gather_local, 0)
    begin()
    for copy in swaps:
        copy.start()
    gate_swap.wait()
    block = gates.shape[0]
    for k, target in enumerate((decay_blocks, input_blocks)):
        target[...] = jnp.zeros_like(target)
        for e in range(2):
            for j in range(planes):
                for h in range(2):
                    row, column = (e * planes + j) * block, (h * planes + j) * block
                    target[row : row + block, column : column + block] = gates_all[
                        e, j, :, (2 * k + h) * block : (2 * k + h + 1) * block
                    ]
    forward()
    end()
    for copy in swaps:
        copy.wait()


def opening(small, gates, tokens, mlp_gate, mlp_up, pairs, collective_id):
    planes = lax.axis_size("seq") // 8
    rows, width = tokens.shape
    channels = 2 * planes * gates.shape[0]
    piece = (CHIPS, mlp_gate.shape[0], mlp_gate.shape[1] // CHIPS)
    return pl.pallas_call(
        functools.partial(opening_kernel, planes, pairs),
        out_shape=[
            jax.ShapeDtypeStruct((8, planes) + small.shape, small.dtype),
            jax.ShapeDtypeStruct((channels, channels), gates.dtype),
            jax.ShapeDtypeStruct((channels, channels), gates.dtype),
            jax.ShapeDtypeStruct(piece, mlp_gate.dtype),
            jax.ShapeDtypeStruct((CHIPS, rows, width), jnp.bfloat16),
            jax.ShapeDtypeStruct(piece, mlp_gate.dtype),
        ],
        in_specs=[VMEM] * 5,
        out_specs=[VMEM] * 4 + [ANY, ANY],
        scratch_shapes=[
            pltpu.VMEM(piece, mlp_gate.dtype),
            pltpu.VMEM((2, planes) + gates.shape, gates.dtype),
            pltpu.VMEM((8, width), jnp.float32),
            pltpu.VMEM((rows, width), jnp.bfloat16),
            pltpu.SemaphoreType.DMA((planes + 7,)),
            pltpu.SemaphoreType.DMA((planes + 7,)),
            pltpu.SemaphoreType.DMA((planes + 1,)),
            pltpu.SemaphoreType.DMA((planes + 1,)),
            pltpu.SemaphoreType.DMA((3,)),
            pltpu.SemaphoreType.DMA((3,)),
            pltpu.SemaphoreType.DMA,
            pltpu.SemaphoreType.DMA((4,)),
            pltpu.SemaphoreType.DMA((4,)),
            pltpu.SemaphoreType.DMA,
        ],
        compiler_params=comm_params(collective_id, 60),
        cost_estimate=lasting(65),
        name="opening",
    )(small, gates, tokens, mlp_gate, mlp_up)


def column_peers(planes, z, p, c):
    count = 2 * planes
    q = 2 * z + c
    peers = []
    for d in range(1, count):
        other = lax.rem(q + d, count)
        peers.append(8 * lax.div(other, 2) + 2 * p + lax.rem(other, 2))
    return q, peers


def carry_in(planes, reverse, z, c, q, peers, everyone, before, entering, send, recv):
    own = everyone.at[q]
    copies = [remote(own, own, send.at[d], recv.at[d], device) for d, device in enumerate(peers)]
    for copy in copies:
        copy.start()
    for copy in copies:
        copy.wait()
    carried = jnp.zeros((1, everyone.shape[2]), jnp.float32)
    order = [(k, j, e) for k in range(planes) for j in range(CHIPS) for e in range(2)]
    for k, j, e in reversed(order) if reverse else order:
        before[8 * k + 2 * j + e : 8 * k + 2 * j + e + 1, :] = carried
        part = everyone.at[2 * k + e]
        carried = part[j : j + 1, :] * carried + part[CHIPS + j : CHIPS + j + 1, :]
    for j in range(CHIPS):
        entering[j : j + 1, :] = before[pl.ds(8 * z + 2 * j + c, 1), :]


def shift_down(earlier, values, step, row):
    return jnp.where(row >= step, pltpu.roll(values, step, 0), pltpu.roll(earlier, step, 0))


def shift_up(values, later, step, row):
    return jnp.where(row < 8 - step, pltpu.roll(values, 8 - step, 0), pltpu.roll(later, 8 - step, 0))


def tile_scan(a, b, row, reverse):
    for step in (1, 2, 4):
        if reverse:
            keep = row < 8 - step
            shifted_a, shifted_b = pltpu.roll(a, 8 - step, 0), pltpu.roll(b, 8 - step, 0)
        else:
            keep = row >= step
            shifted_a, shifted_b = pltpu.roll(a, step, 0), pltpu.roll(b, step, 0)
        b = a * jnp.where(keep, shifted_b, 0.0) + b
        a = a * jnp.where(keep, shifted_a, 1.0)
    return a, b


def sigmoid(values):
    return 1.0 / (1.0 + jnp.exp(-values))


def gate_terms(decay_pre, rate, flag):
    opened = sigmoid(decay_pre)
    log_decay = rate * opened
    decay = jnp.exp(log_decay)
    keep = 1.0 - flag
    squared = decay * decay
    return opened, decay * keep, keep, squared, jnp.tanh(-log_decay) * (1.0 + squared)


GELU_A, GELU_B = 0.7978845608028654, 0.044715


def eight(i):
    return pl.ds(pl.multiple_of(i * 8, 8), 8)


def recurrence_kernel(
    planes,
    gate_pre,
    conv_input,
    masks,
    vectors,
    decay_blocks,
    input_blocks,
    cot,
    piece,
    normed,
    conv_out,
    conv_low,
    decay_pre,
    input_pre,
    states,
    mixed,
    mixed_zero,
    mixed_one,
    entering,
    halo,
    cot_all,
    swapped,
    normed_other,
    cumulative,
    sibling_tails,
    below_tail,
    everyone,
    before,
    send,
    recv,
    local,
    swap_send,
    swap_recv,
    other_send,
    other_recv,
):
    me, z, p, c, x, y = place()
    rows, channels = conv_input.shape[1:]
    q, peers = column_peers(planes, z, p, c)
    greet(peers + [*plane_neighbours()[0]])
    cot_begin, cot_forward, cot_end = gather_steps(cot, cot_all, send, recv, local.at[0], 9)
    cot_begin()
    half = normed.shape[1] // 2
    other = remote(
        normed.at[:, pl.ds(pl.multiple_of((1 - c) * half, 128), half)],
        normed_other,
        other_send,
        other_recv,
        me + 1 - 2 * c,
    )
    other.start()
    swaps = swap_copies(piece, swapped, swap_send, swap_recv, local.at[1])
    f32 = jnp.float32
    tail = pl.ds(rows - 16, 16)
    to_sibling = remote(conv_input.at[:, tail], sibling_tails, send.at[7], recv.at[7], me + 1 - 2 * c)
    to_above = remote(conv_input.at[CHIPS - 1, tail], below_tail, send.at[8], recv.at[8], me + 7)
    from_below = remote(conv_input.at[CHIPS - 1, tail], below_tail, send.at[8], recv.at[8], me - 7)
    to_sibling.start()

    @pl.when((c == 1) & (z < planes - 1))
    def send_above():
        to_above.start()

    to_sibling.wait()

    @pl.when((c == 1) & (z < planes - 1))
    def sent_above():
        to_above.wait_send()

    @pl.when((c == 0) & (z > 0))
    def had_below():
        from_below.wait_recv()

    @pl.when(c == 1)
    def halo_one():
        for j in range(CHIPS):
            halo[j] = sibling_tails[j].astype(f32)[8:]

    @pl.when(c == 0)
    def halo_zero():
        for j in range(1, CHIPS):
            halo[j] = sibling_tails[j - 1].astype(f32)[8:]

        @pl.when(z > 0)
        def halo_below():
            halo[0] = below_tail[...].astype(f32)[8:]

        @pl.when(z == 0)
        def halo_none():
            halo[0] = jnp.zeros((8, channels), f32)

    row = lax.broadcasted_iota(jnp.int32, (8, channels), 0)

    @pl.loop(0, CHIPS)
    def block(j):
        def conv_tile(i, earlier):
            both = conv_input[j, sixteen(i), :].astype(f32)
            outs = []
            for h in range(2):
                now = both[8 * h : 8 * h + 8]
                keep = masks[j, eight(2 * i + h), :]
                out = vectors[CW : CW + 1, :] + vectors[0:1, :] * now
                for k in range(1, CW):
                    out = out + vectors[k : k + 1, :] * (
                        shift_down(earlier, now, k, row) * keep[:, k : k + 1]
                    )
                conv_out[j, eight(2 * i + h), :] = out
                outs.append(out)
                earlier = now
            conv_low[j, sixteen(i), :] = jnp.concatenate(outs, axis=0).astype(jnp.bfloat16)
            return earlier

        lax.fori_loop(0, rows // 16, conv_tile, halo[j], unroll=2)
        low = conv_low[j]
        decay_pre[j] = jnp.dot(low, decay_blocks[...], preferred_element_type=f32) + vectors[CW + 1 : CW + 2, :]
        input_pre[j] = jnp.dot(low, input_blocks[...], preferred_element_type=f32) + vectors[CW + 2 : CW + 3, :]

        def scan_tile(i, carry):
            at = eight(i)
            flag = masks[j, at, :][:, 0:1]
            opened, coef, keep, squared, gap = gate_terms(decay_pre[j, at, :], vectors[CW + 3 : CW + 4, :], flag)
            drive = (flag + keep * jnp.sqrt(gap)) * sigmoid(input_pre[j, at, :]) * conv_out[j, at, :]
            a, b = tile_scan(coef, drive, row, False)
            before_a, before_b = carry
            b = a * before_b + b
            a = a * before_a
            cumulative[j, at, :] = a
            states[j, at, :] = b
            return a[7:8], b[7:8]

        last_a, last_b = lax.fori_loop(
            0,
            rows // 8,
            scan_tile,
            (jnp.ones((1, channels), f32), jnp.zeros((1, channels), f32)),
            unroll=4,
        )
        everyone[q, pl.ds(j, 1), :] = last_a
        everyone[q, pl.ds(CHIPS + j, 1), :] = last_b

    cot_forward()
    for copy in swaps:
        copy.start()
    carry_in(planes, False, z, c, q, peers, everyone, before, entering, send, recv)

    @pl.loop(0, CHIPS)
    def finish(j):
        start = entering[pl.ds(j, 1), :]

        def state_tile(i, unused):
            at = sixteen(i)
            state = states[j, at, :] + cumulative[j, at, :] * start
            states[j, at, :] = state
            v = gate_pre[j, at, :]
            act = 0.5 * v * (1.0 + jnp.tanh(GELU_A * (v + GELU_B * (v * v * v))))
            product = (state * act).astype(jnp.bfloat16)
            mixed[j, at, :] = product
            mixed_zero[j, at, :] = product[:, : channels // 2]
            mixed_one[j, at, :] = product[:, channels // 2 :]
            return unused

        lax.fori_loop(0, rows // 16, state_tile, 0, unroll=2)

    cot_end()
    other.wait()
    for copy in swaps:
        copy.wait()


def recurrence(gate_pre, conv_input, masks, vectors, decay_blocks, input_blocks, cot, piece, normed, collective_id):
    planes = lax.axis_size("seq") // 8
    blocks, rows, channels = conv_input.shape
    f32, bf16 = jnp.float32, jnp.bfloat16
    cube = conv_input.shape

    def out(dtype, shape=cube):
        return jax.ShapeDtypeStruct(shape, dtype)

    return pl.pallas_call(
        functools.partial(recurrence_kernel, planes),
        out_shape=[
            out(f32),
            out(bf16),
            out(f32),
            out(f32),
            out(f32),
            out(bf16),
            *[out(bf16, (CHIPS, rows, channels // 2))] * 2,
            out(f32, (CHIPS, channels)),
            out(f32, (CHIPS, 8, channels)),
            out(cot.dtype, (CHIPS,) + cot.shape),
            out(piece.dtype, piece.shape),
            out(normed.dtype, (normed.shape[0], normed.shape[1] // 2)),
        ],
        in_specs=[VMEM] * 6 + [ANY] * 3,
        out_specs=[VMEM] * 10 + [ANY] * 3,
        scratch_shapes=[
            pltpu.VMEM(cube, f32),
            pltpu.VMEM((CHIPS, 16, channels), bf16),
            pltpu.VMEM((16, channels), bf16),
            pltpu.VMEM((2 * planes, 2 * CHIPS, channels), f32),
            pltpu.VMEM((8 * planes, channels), f32),
            pltpu.SemaphoreType.DMA((13,)),
            pltpu.SemaphoreType.DMA((13,)),
            pltpu.SemaphoreType.DMA((2,)),
            pltpu.SemaphoreType.DMA((3,)),
            pltpu.SemaphoreType.DMA((3,)),
            pltpu.SemaphoreType.DMA,
            pltpu.SemaphoreType.DMA,
        ],
        compiler_params=comm_params(collective_id, 60),
        cost_estimate=lasting(46),
        name="recurrence",
    )(gate_pre, conv_input, masks, vectors, decay_blocks, input_blocks, cot, piece, normed)


def recurrence_back_kernel(
    planes,
    grad_branch,
    rows_all,
    gate_pre,
    conv_input,
    conv_out,
    decay_pre,
    input_pre,
    states,
    entering,
    halo,
    masks,
    after_masks,
    vectors,
    decay_blocks,
    input_blocks,
    middle,
    down_parts,
    piece,
    in_low,
    decay_low,
    input_low,
    sums,
    block_out,
    swapped,
    grad_mixed,
    branch_here,
    out_here,
    cumulative,
    local,
    grad_conv,
    sibling_heads,
    above_head,
    ahead,
    everyone,
    before,
    leaving,
    send,
    recv,
    piece_sem,
    loads,
    *down_scratch,
):
    me, z, p, c, x, y = place()
    rows, channels = conv_input.shape[1:]
    q, peers = column_peers(planes, z, p, c)
    devices, chips = plane_neighbours()
    greet(peers + [*devices])
    down_begin, down_forward, down_end = sum_steps(down_parts, *down_scratch)
    down_begin()
    swaps = swap_copies(piece, swapped, send.at[pl.ds(9, 3)], recv.at[pl.ds(9, 3)], piece_sem.at[0])
    fetched = fetch_rows(rows_all, 0, 0, out_here, loads)
    fetched.append(pltpu.make_async_copy(grad_branch, branch_here, piece_sem.at[1]))
    for copy in fetched:
        copy.start()
    for copy in fetched:
        copy.wait()
    f32, bf16 = jnp.float32, jnp.bfloat16
    row = lax.broadcasted_iota(jnp.int32, (8, channels), 0)
    rate = vectors[CW + 3 : CW + 4, :]
    nothing = jnp.zeros((8, channels), f32)

    @pl.loop(0, CHIPS)
    def scan_block(j):
        grad_mixed[j] = lax.dot_general(
            branch_here[j], out_here[...], (((1,), (1,)), ((), ())), preferred_element_type=f32
        )

        def scan_tile(i, carry):
            i = rows // 16 - 1 - i
            at = sixteen(i)
            v = gate_pre[j, at, :]
            grad = grad_mixed[j, at, :]
            t = jnp.tanh(GELU_A * (v + GELU_B * (v * v * v)))
            act = 0.5 * v * (1.0 + t)
            slope = 0.5 * (1.0 + t) + 0.5 * v * (1.0 - t * t) * (GELU_A * (1.0 + 3.0 * GELU_B * (v * v)))
            in_low[j, at, 0:channels] = (grad * states[j, at, :] * slope).astype(bf16)
            drive = grad * act
            later_a, later_b, later_coef = carry
            for h in (1, 0):
                here = eight(2 * i + h)
                flag = masks[j, here, :][:, 0:1]
                coef = gate_terms(decay_pre[j, here, :], rate, flag)[1]
                shifted = jnp.where(row < 7, pltpu.roll(coef, 7, 0), later_coef)
                a, b = tile_scan(shifted, drive[8 * h : 8 * h + 8], row, True)
                b = a * later_b + b
                a = a * later_a
                cumulative[j, here, :] = a
                local[j, here, :] = b
                later_a, later_b, later_coef = a[0:1], b[0:1], coef[0:1]
            return later_a, later_b, later_coef

        ones = jnp.ones((1, channels), f32)
        first_a, first_b, first_coef = lax.fori_loop(
            0, rows // 16, scan_tile, (ones, jnp.zeros((1, channels), f32), ones), unroll=2
        )
        everyone[q, pl.ds(j, 1), :] = first_coef * first_a
        everyone[q, pl.ds(CHIPS + j, 1), :] = first_coef * first_b

    carry_in(planes, True, z, c, q, peers, everyone, before, leaving, send, recv)
    down_forward()
    for copy in swaps:
        copy.start()

    def terms_block(j, totals):
        behind_all = leaving[pl.ds(j, 1), :]

        def terms_tile(i, carry):
            previous, decay_sum, input_sum, param_sum = carry
            lows = []
            for h in range(2):
                at = eight(2 * i + h)
                adjoint = local[j, at, :] + cumulative[j, at, :] * behind_all
                state = states[j, at, :]
                earlier = jnp.where(row >= 1, pltpu.roll(state, 1, 0), previous)
                previous = state[7:8]
                flag = masks[j, at, :][:, 0:1]
                opened, coef, keep, squared, gap = gate_terms(decay_pre[j, at, :], rate, flag)
                passed = sigmoid(input_pre[j, at, :])
                conv = conv_out[j, at, :]
                inverse = lax.rsqrt(gap)
                scale = flag + keep * (gap * inverse)
                grad_log = adjoint * (earlier * coef - keep * passed * conv * squared * inverse)
                log_open = grad_log * opened
                decay_full = log_open * rate * (1.0 - opened)
                direct = adjoint * scale * passed
                input_full = direct * (1.0 - passed) * conv
                grad_conv[j, at, :] = direct
                lows.append((decay_full, input_full))
                decay_sum = decay_sum + decay_full
                input_sum = input_sum + input_full
                param_sum = param_sum + log_open
            decay_low[j, sixteen(i), :] = jnp.concatenate([low[0] for low in lows], axis=0).astype(bf16)
            input_low[j, sixteen(i), :] = jnp.concatenate([low[1] for low in lows], axis=0).astype(bf16)
            return previous, decay_sum, input_sum, param_sum

        totals = lax.fori_loop(
            0, rows // 16, terms_tile, (entering[pl.ds(j, 1), :], *totals), unroll=2
        )[1:]

        def dot_t(left, right):
            return lax.dot_general(left, right, (((1,), (1,)), ((), ())), preferred_element_type=f32)

        grad_conv[j] = (
            grad_conv[j] + dot_t(decay_low[j], decay_blocks[...]) + dot_t(input_low[j], input_blocks[...])
        )
        return totals

    decay_sum, input_sum, param_sum = lax.fori_loop(0, CHIPS, terms_block, (nothing,) * 3)

    to_sibling = remote(grad_conv.at[:, pl.ds(0, 8)], sibling_heads, send.at[7], recv.at[7], me + 1 - 2 * c)
    to_below = remote(grad_conv.at[0, pl.ds(0, 8)], above_head, send.at[8], recv.at[8], me - 7)
    from_above = remote(grad_conv.at[0, pl.ds(0, 8)], above_head, send.at[8], recv.at[8], me + 7)
    to_sibling.start()

    @pl.when((c == 0) & (z > 0))
    def send_below():
        to_below.start()

    to_sibling.wait()

    @pl.when((c == 0) & (z > 0))
    def sent_below():
        to_below.wait_send()

    @pl.when((c == 1) & (z < planes - 1))
    def had_above():
        from_above.wait_recv()

    @pl.when(c == 0)
    def ahead_zero():
        for j in range(CHIPS):
            ahead[j] = sibling_heads[j]

    @pl.when(c == 1)
    def ahead_one():
        for j in range(CHIPS - 1):
            ahead[j] = sibling_heads[j + 1]

        @pl.when(z < planes - 1)
        def ahead_above():
            ahead[CHIPS - 1] = above_head[...]

        @pl.when(z == planes - 1)
        def ahead_none():
            ahead[CHIPS - 1] = nothing

    def conv_block(j, totals):
        def conv_pair(i, now, later, keep, later_keep, outs, earlier, given, totals):
            out = vectors[0:1, :] * now
            new_totals = [totals[0] + now * given]
            for k in range(1, CW):
                masked = now * keep[:, k : k + 1]
                out = out + vectors[k : k + 1, :] * shift_up(
                    masked, later * later_keep[:, k : k + 1], k, row
                )
                new_totals.append(totals[k] + masked * shift_down(earlier, given, k, row))
            new_totals.append(totals[CW] + now)
            outs.append(out)
            return tuple(new_totals)

        def conv_tile(i, carry, last):
            earlier, totals = carry
            inputs = conv_input[j, sixteen(i), :].astype(f32)
            first, second = grad_conv[j, eight(2 * i), :], grad_conv[j, eight(2 * i + 1), :]
            first_keep, second_keep = masks[j, eight(2 * i), :], masks[j, eight(2 * i + 1), :]
            if last:
                third, third_keep = ahead[j], after_masks[j]
            else:
                third, third_keep = grad_conv[j, eight(2 * i + 2), :], masks[j, eight(2 * i + 2), :]
            outs = []
            totals = conv_pair(i, first, second, first_keep, second_keep, outs, earlier, inputs[:8], totals)
            totals = conv_pair(i, second, third, second_keep, third_keep, outs, inputs[:8], inputs[8:], totals)
            in_low[j, sixteen(i), channels : 2 * channels] = jnp.concatenate(outs, axis=0).astype(bf16)
            return inputs[8:], totals

        carry = lax.fori_loop(
            0, rows // 16 - 1, lambda i, carry: conv_tile(i, carry, False), (halo[j], totals)
        )
        return conv_tile(rows // 16 - 1, carry, True)[1]

    totals = lax.fori_loop(0, CHIPS, conv_block, (nothing,) * (CW + 1))
    for k, total in enumerate((*totals, decay_sum, input_sum, param_sum)):
        sums[k : k + 1, :] = jnp.sum(total, axis=0, keepdims=True)
    down_end()
    own, from_x, from_y = down_scratch[:3]

    @pl.loop(0, own.shape[0] // 16)
    def sum_rows(i):
        at = sixteen(i)
        block_out[at, :] = middle[at, :] + (
            own[at, :].astype(f32) + from_x[at, :].astype(f32) + from_y[at, :].astype(f32)
        )

    for copy in swaps:
        copy.wait()


def recurrence_back(
    grad_branch,
    rows_all,
    gate_pre,
    conv_input,
    conv_out,
    decay_pre,
    input_pre,
    states,
    entering,
    halo,
    masks,
    after_masks,
    vectors,
    decay_blocks,
    input_blocks,
    middle,
    down_parts,
    piece,
    collective_id,
):
    planes = lax.axis_size("seq") // 8
    cube = conv_input.shape
    blocks, rows, channels = cube
    f32, bf16 = jnp.float32, jnp.bfloat16
    return pl.pallas_call(
        functools.partial(recurrence_back_kernel, planes),
        out_shape=[
            jax.ShapeDtypeStruct((CHIPS, rows, 2 * channels), bf16),
            jax.ShapeDtypeStruct(cube, bf16),
            jax.ShapeDtypeStruct(cube, bf16),
            jax.ShapeDtypeStruct((CW + 4, channels), f32),
            jax.ShapeDtypeStruct(down_parts.shape[1:], f32),
            jax.ShapeDtypeStruct(piece.shape, bf16),
        ],
        in_specs=[ANY] * 2 + [VMEM] * 14 + [ANY] * 2,
        out_specs=[VMEM] * 5 + [ANY],
        scratch_shapes=[
            pltpu.VMEM(cube, f32),
            pltpu.VMEM(grad_branch.shape, bf16),
            pltpu.VMEM((channels, grad_branch.shape[2]), bf16),
            pltpu.VMEM(cube, f32),
            pltpu.VMEM(cube, f32),
            pltpu.VMEM(cube, f32),
            pltpu.VMEM((CHIPS, 8, channels), f32),
            pltpu.VMEM((8, channels), f32),
            pltpu.VMEM((CHIPS, 8, channels), f32),
            pltpu.VMEM((2 * planes, 2 * CHIPS, channels), f32),
            pltpu.VMEM((8 * planes, channels), f32),
            pltpu.VMEM((CHIPS, channels), f32),
            pltpu.SemaphoreType.DMA((12,)),
            pltpu.SemaphoreType.DMA((12,)),
            pltpu.SemaphoreType.DMA((2,)),
            pltpu.SemaphoreType.DMA((rows_all.shape[0],)),
            *sum_scratch(*down_parts.shape[1:], bf16),
        ],
        compiler_params=comm_params(collective_id, 60),
        cost_estimate=lasting(58),
        name="recurrence_back",
    )(
        grad_branch,
        rows_all,
        gate_pre,
        conv_input,
        conv_out,
        decay_pre,
        input_pre,
        states,
        entering,
        halo,
        masks,
        after_masks,
        vectors,
        decay_blocks,
        input_blocks,
        middle,
        down_parts,
        piece,
    )


def input_grads_kernel(
    normed, normed_other, low, grad, here, there, low_here, low_there, kept, send, recv, loads
):
    me, z, p, c, x, y = place()
    sibling = me + 1 - 2 * c
    greet((sibling,))
    swap = remote(low, low_there, send, recv, sibling)
    swap.start()
    half, columns = grad.shape
    fetched = [
        pltpu.make_async_copy(source, target, loads.at[k])
        for k, (source, target) in enumerate(
            (
                (normed.at[:, pl.ds(pl.multiple_of(c * half, 128), half)], here),
                (low, low_here),
                (normed_other, there),
            )
        )
    ]
    for copy in fetched:
        copy.start()
    for copy in fetched[:2]:
        copy.wait()
    block, tile = 512, 256

    def products(left, right, keep):
        @pl.loop(0, half // block)
        def product_block(m):
            at = pl.ds(pl.multiple_of(m * block, block), block)

            @pl.loop(0, columns // tile)
            def product_tile(k):
                across = pl.ds(pl.multiple_of(k * tile, tile), tile)
                keep(
                    at,
                    across,
                    lax.dot_general(
                        left[:, at], right[:, across], (((0,), (0,)), ((), ())), preferred_element_type=jnp.float32
                    ),
                )

    def keep_first(at, across, values):
        kept[at, across] = values

    def keep_sum(at, across, values):
        grad[at, across] = (kept[at, across] + values).astype(grad.dtype)

    products(here, low_here, keep_first)
    fetched[2].wait()
    swap.wait()
    products(there, low_there, keep_sum)


def input_grads(normed, normed_other, low, collective_id):
    tokens, width = normed.shape
    columns = low.shape[1]
    bf16 = low.dtype
    return pl.pallas_call(
        input_grads_kernel,
        out_shape=jax.ShapeDtypeStruct((width // 2, columns), bf16),
        in_specs=[ANY] * 3,
        out_specs=VMEM,
        scratch_shapes=[
            pltpu.VMEM((tokens, width // 2), bf16),
            pltpu.VMEM((tokens, width // 2), bf16),
            pltpu.VMEM((tokens, columns), bf16),
            pltpu.VMEM((tokens, columns), bf16),
            pltpu.VMEM((width // 2, columns), jnp.float32),
            pltpu.SemaphoreType.DMA,
            pltpu.SemaphoreType.DMA,
            pltpu.SemaphoreType.DMA((3,)),
        ],
        compiler_params=comm_params(collective_id, 60),
        name="input_grads",
    )(normed, normed_other, low)


def regrouped_kernel(back, devices, places, *refs):
    count = 1 + max(place[0] for place in places)
    for source, first, rows, target, row in places:
        source, target = refs[source], refs[count + target]
        step = source.shape[1] // devices
        for k in range(devices // 2):
            for e in range(2):
                split, joined = (2 * k + e) * step, (devices // 2 * e + k) * step
                start, end = (joined, split) if back else (split, joined)
                target[row : row + rows, end : end + step] = source[
                    first : first + rows, start : start + step
                ].astype(target.dtype)


def regrouped_columns(arrays, places, dtypes, back, vmem_mib):
    devices = lax.axis_size("seq")
    sizes = [max(row + rows for unused, unused, rows, m, row in places if m == k) for k in range(len(dtypes))]
    return pl.pallas_call(
        functools.partial(regrouped_kernel, back, devices, places),
        out_shape=[jax.ShapeDtypeStruct((r, arrays[0].shape[1]), dtype) for r, dtype in zip(sizes, dtypes)],
        in_specs=[VMEM] * len(arrays),
        out_specs=[VMEM] * len(dtypes),
        compiler_params=pltpu.CompilerParams(vmem_limit_bytes=vmem_mib * 2**20),
        name="regrouped_columns",
    )(*arrays)


def to_chips_kernel(planes, pairs, *refs):
    ins, outs = refs[: len(pairs)], refs[len(pairs) :]
    for source, targets in zip(ins, pairs):
        width = source.shape[1] // (planes * 8)
        for z in range(planes):
            for p in range(CHIPS):
                for c in range(2):
                    k, at = targets[c]
                    start = ((z * CHIPS + p) * 2 + c) * width
                    outs[k][p, :, at + z * width : at + (z + 1) * width] = source[:, start : start + width]


def from_chips_kernel(planes, pairs, *refs):
    outs, ins = refs[-len(pairs) :], refs[: -len(pairs)]
    for target, sources in zip(outs, pairs):
        width = target.shape[1] // (planes * 8)
        for z in range(planes):
            for p in range(CHIPS):
                for c in range(2):
                    k, at = sources[c]
                    start = ((z * CHIPS + p) * 2 + c) * width
                    target[:, start : start + width] = ins[k][
                        p, :, at + z * width : at + (z + 1) * width
                    ].astype(jnp.float32)


def from_chips(parts, pairs, widths):
    planes = lax.axis_size("seq") // 8
    return pl.pallas_call(
        functools.partial(from_chips_kernel, planes, pairs),
        out_shape=[jax.ShapeDtypeStruct((parts[0].shape[1], width), jnp.float32) for width in widths],
        in_specs=[VMEM] * len(parts),
        out_specs=[VMEM] * len(widths),
        compiler_params=pltpu.CompilerParams(vmem_limit_bytes=32 * 2**20),
        name="from_chips",
    )(*parts)


def regrouped(values, axis, n):
    shape = values.shape
    split = shape[:axis] + (n // 2, 2, shape[axis] // n) + shape[axis + 1 :]
    return jnp.moveaxis(values.reshape(split), axis + 1, axis).reshape(shape)


def behind(value, *earlier):
    return lax.optimization_barrier((value, *earlier))[0]


def plane_body(
    tokens,
    starts,
    cotangent,
    norm_gain,
    gate_branch,
    input_branch,
    conv_weight,
    conv_bias,
    decay_gate,
    decay_bias,
    input_gate,
    input_bias,
    decay_param,
    out_proj,
    mlp_gain,
    mlp_gate,
    mlp_up,
    mlp_down,
):
    f32, bf16 = jnp.float32, jnp.bfloat16
    n = lax.axis_size("seq")
    planes = n // 8
    me, z, p, c, x, y = place()
    groups = column_groups(n)
    rows, width = tokens.shape
    rows_d, lru_width = gate_branch.shape
    head = decay_gate.shape[1]
    rows_r, rows_f = out_proj.shape[0], mlp_down.shape[0]
    channels = lru_width // CHIPS
    units = mlp_gate.shape[1] // CHIPS
    half_units = units // 2

    def column_gather(block):
        return lax.all_gather(block, "seq", axis=0, tiled=True, axis_index_groups=groups)

    def line_sum(parts):
        return lax.psum_scatter(
            parts, "seq", scatter_dimension=0, tiled=True, axis_index_groups=line_groups(n)
        )

    def product(left, right):
        return jnp.dot(left, right, preferred_element_type=f32)

    def product_t(left, right):
        return jnp.einsum("tk,nk->tn", left, right, preferred_element_type=f32)

    def weight_grad(left, right):
        return jnp.einsum("ta,tb->ab", left, right, preferred_element_type=f32)

    lanes = 128

    def row(values):
        return jnp.pad(values.astype(f32), (0, lanes - values.shape[0]))[None]

    small = jnp.concatenate(
        [
            row(norm_gain),
            row(mlp_gain),
            starts.astype(f32).reshape(rows // lanes, lanes),
            *[row(conv_weight[k]) for k in range(CW)],
            row(conv_bias),
            row(decay_bias),
            row(input_bias),
            row(decay_param),
            jnp.zeros((4, lanes), f32),
        ],
        axis=0,
    )
    half = channels // 2
    in_pairs = (((0, 0), (0, half)), ((0, channels), (0, channels + half)))
    swapped_in = first_swap([gate_branch, input_branch], in_pairs, 2 * channels, 2)
    whole_in = column_gather(swapped_in.reshape(CHIPS * rows_d, 2 * channels))
    tokens, cot, row_shards = regrouped_columns(
        [tokens, cotangent, out_proj, mlp_down],
        [(0, 0, rows, 0, 0), (1, 0, rows, 1, 0), (2, 0, rows_r, 2, 0), (3, 0, rows_f, 2, rows_r)],
        [bf16] * 3,
        False,
        60,
    )
    mlp_pairs = (((0, 0), (1, 0)), ((0, half_units), (1, half_units)))
    gates = jnp.concatenate([decay_gate, input_gate], axis=1)
    small, decay_blocks, input_blocks, second_part, normed_all, first_piece = opening(
        behind(small, swapped_in), gates, tokens, mlp_gate, mlp_up, mlp_pairs, 1
    )
    normed_all = normed_all.reshape(CHIPS * rows, width)
    small = small.transpose(1, 0, 2, 3)
    flags = 2 + rows // lanes
    gain_one = regrouped(small[:, :, 0, :rows_d].reshape(width), 0, n)
    gain_two = regrouped(small[:, :, 1, :rows_d].reshape(width), 0, n)
    all_flags = small[:, :, 2:flags].reshape(n * rows)
    vectors = lax.dynamic_slice_in_dim(
        small.reshape(planes, CHIPS, 2, 16, lanes), p, 1, axis=1
    )[:, 0, :, flags : flags + CW + 4, :rows_r]
    vectors = vectors.transpose(2, 1, 0, 3).reshape(CW + 4, channels)
    param = vectors[CW + 3]
    vectors = vectors.at[CW + 3].set(-rate_scale * jax.nn.softplus(param))

    running = jnp.ones((n * rows,), f32)
    masks_all = [running]
    for offset in range(1, CW):
        earlier = jnp.concatenate([jnp.zeros((offset - 1,), f32), all_flags[: n * rows - (offset - 1)]])
        running = running * (1.0 - earlier)
        masks_all.append(running)
    masks_all = jnp.stack(masks_all).reshape(CW, planes, CHIPS, 2, rows)

    def own_blocks(values):
        return lax.dynamic_slice(
            values,
            (0, z, 0, c, 0),
            (values.shape[0], 1, CHIPS, 1, values.shape[4]),
        )[:, 0, :, 0]

    after_masks = masks_all[..., :8].reshape(CW, n, 8)
    after_masks = jnp.concatenate([after_masks[:, 1:], jnp.zeros((CW, 1, 8), f32)], axis=1)
    after_masks = own_blocks(after_masks.reshape(CW, planes, CHIPS, 2, 8)).transpose(1, 2, 0)
    masks_all = jnp.concatenate([all_flags.reshape(1, planes, CHIPS, 2, rows), masks_all[1:]], axis=0)
    masks = own_blocks(masks_all).transpose(1, 2, 0)

    rows_all = column_gather(behind(row_shards, swapped_in)).reshape(2 * planes, rows_r + rows_f, width)

    gate_pre = product(normed_all, whole_in[:, :channels])
    cube = (CHIPS, rows, channels)
    gate_pre = gate_pre.reshape(cube)
    conv_input = product(normed_all, whole_in[:, channels:]).astype(bf16).reshape(cube)
    conv_out, conv_low, decay_pre, input_pre, states, mixed, *mixeds, entering, halo, cot_all, second_piece, normed_other = recurrence(
        gate_pre,
        conv_input,
        masks,
        vectors,
        decay_blocks,
        input_blocks,
        cot,
        second_part,
        normed_all,
        6,
    )
    whole_mlp = [
        column_gather(part.reshape(CHIPS * rows_d, 2 * half_units)) for part in (first_piece, second_piece)
    ]
    cot_all = cot_all.reshape(CHIPS * rows, width)
    middle, two_all, cot_other = middle_of(mixed, rows_all, tokens, gain_two, cot_all, 7)
    mixeds = [part.reshape(CHIPS * rows, channels // 2) for part in mixeds]
    two_all = two_all.reshape(CHIPS * rows, width)

    hidden_zero, first_grad, first_parts = feed_forward(0, two_all, cot_all, whole_mlp[0], rows_all, (), 8)
    hidden_one, second_grad, two_parts = feed_forward(
        1, two_all, cot_all, whole_mlp[1], rows_all, (first_parts,), 14
    )
    piece_grads = [line_sum(first_grad), line_sum(second_grad)]
    grad_middle, grad_mlp_gain, grad_branch, row_grads, down_parts = grads_of_middle(
        two_parts.reshape(CHIPS, rows, width),
        middle,
        cot,
        gain_two,
        (hidden_zero, hidden_one),
        rows_all,
        (cot_all, cot_other),
        mixeds,
        9,
    )
    grad_rows = line_sum(row_grads.reshape(planes * (rows_r + rows_f), width))

    in_low, grad_decay_low, grad_input_low, sums, block_out, first_swapped = recurrence_back(
        grad_branch,
        rows_all,
        gate_pre,
        conv_input,
        conv_out,
        decay_pre,
        input_pre,
        states,
        entering,
        halo,
        masks,
        after_masks,
        vectors,
        decay_blocks,
        input_blocks,
        middle,
        down_parts,
        piece_grads[0].reshape(CHIPS, rows_d, 2 * half_units),
        12,
    )
    sums = sums.at[CW + 3].multiply(-rate_scale * jax.nn.sigmoid(param))
    low_cube = in_low
    in_low = low_cube.reshape(CHIPS * rows, 2 * channels)
    flat = (CHIPS * rows, channels)
    conv_low, grad_decay_low, grad_input_low = (
        a.reshape(flat) for a in (conv_low, grad_decay_low, grad_input_low)
    )

    in_total = input_grads(normed_all, normed_other, in_low, 15)
    in_grads = line_sum(in_total)
    low_cube = behind(low_cube, in_total)
    vector_parts = sums.reshape(CW + 4, 2, planes, rows_r).transpose(2, 1, 0, 3)
    vector_parts = jnp.pad(vector_parts, ((0, 0), (0, 0), (0, 0), (0, lanes - rows_r)))
    grad_tokens, small_grads, gate_grads, second_swapped = closing(
        low_cube,
        whole_in,
        tokens,
        gain_one,
        grad_middle,
        vector_parts,
        grad_mlp_gain,
        (conv_low, grad_decay_low, grad_input_low),
        piece_grads[1].reshape(CHIPS, rows_d, 2 * half_units),
        head,
        13,
    )
    grad_mlp_gate, grad_mlp_up = from_chips(
        [first_swapped, second_swapped], mlp_pairs, [mlp_gate.shape[1]] * 2
    )
    block_out, grad_out_proj, grad_mlp_down = regrouped_columns(
        [block_out, behind(grad_rows, grad_tokens)],
        [(0, 0, rows, 0, 0), (1, 0, rows_r, 1, 0), (1, rows_r, rows_f, 2, 0)],
        [bf16, f32, f32],
        True,
        24,
    )
    in_grads = behind(in_grads, grad_out_proj)
    in_out = plane_swap([in_grads.reshape(CHIPS, rows_d, 2 * channels)], 16)
    grad_gate_branch, grad_input_branch = from_chips(in_out, in_pairs, [lru_width] * 2)
    vector_grads = small_grads[: CW + 4, :rows_r]
    return (
        block_out,
        grad_tokens,
        small_grads[CW + 4, :rows_d],
        grad_gate_branch,
        grad_input_branch,
        vector_grads[:CW],
        vector_grads[CW],
        gate_grads[:, :head],
        vector_grads[CW + 1],
        gate_grads[:, head:],
        vector_grads[CW + 2],
        vector_grads[CW + 3],
        grad_out_proj,
        small_grads[CW + 4, rows_d : 2 * rows_d],
        grad_mlp_gate,
        grad_mlp_up,
        grad_mlp_down,
    )


def solution(mesh):
    in_specs = (
        P("seq", None),
        P("seq"),
        P("seq", None),
        P("seq"),
        P("seq", None),
        P("seq", None),
        P(None, "seq"),
        P("seq"),
        P("seq", None),
        P("seq"),
        P("seq", None),
        P("seq"),
        P("seq"),
        P("seq", None),
        P("seq"),
        P("seq", None),
        P("seq", None),
        P("seq", None),
    )
    out_specs = (
        P("seq", None),
        P("seq", None),
        P("seq"),
        P("seq", None),
        P("seq", None),
        P(None, "seq"),
        P("seq"),
        P("seq", None),
        P("seq"),
        P("seq", None),
        P("seq"),
        P("seq"),
        P("seq", None),
        P("seq"),
        P("seq", None),
        P("seq", None),
        P("seq", None),
    )
    body = plane_body if mesh.shape["seq"] == 2 * H else token_split_body
    return jax.shard_map(body, mesh=mesh, in_specs=in_specs, out_specs=out_specs, check_vma=False)
```

```python
import functools

import jax
import jax.numpy as jnp
from jax import lax
from jax.experimental import pallas as pl
from jax.experimental.pallas import tpu as pltpu
from jax.sharding import PartitionSpec as P

H = 16
CW = 4


epsilon = 1e-06
rate_scale = 8.0


def passed_along(block, axis, distance):
    devices = range(lax.axis_size(axis))
    route = [(i - distance, i) for i in devices if i - distance in devices]
    return lax.ppermute(block, axis, route)


def prefix(value, axis, combine, identity, reverse):
    peers, place = (lax.axis_size(axis), lax.axis_index(axis))
    everything = jax.tree.map(lambda part: lax.all_gather(part, axis), value)
    start = jax.tree.map(
        lambda part, zero: jnp.broadcast_to(jnp.asarray(zero, part.dtype), part.shape),
        value,
        identity,
    )

    def hop(k, before):
        at = peers - 1 - k if reverse else k
        reached = at > place if reverse else at < place
        new = combine(before, jax.tree.map(lambda part: part[at], everything))
        return jax.tree.map(lambda a, b: jnp.where(reached, a, b), new, before)

    return lax.fori_loop(0, peers, hop, start)


def gelu_tanh(values):
    return jax.nn.gelu(values, approximate=True)


def rms_norm(values, scales):
    return values * lax.rsqrt(jnp.mean(values * values, axis=-1, keepdims=True) + epsilon) * scales


def combine(earlier_part, later_part):
    return (earlier_part[0] * later_part[0], later_part[0] * earlier_part[1] + later_part[1])


def heads_product(values, weight):
    row_count, lru_width = values.shape
    shaped = values.reshape(row_count, H, lru_width // H)
    blocks = weight.reshape(H, lru_width // H, lru_width // H)
    return jnp.einsum("thi,hij->thj", shaped, blocks, preferred_element_type=jnp.float32).reshape(
        row_count, lru_width
    )


def heads_back(grads_low, weight):
    row_count, lru_width = grads_low.shape
    shaped = grads_low.reshape(row_count, H, lru_width // H)
    blocks = weight.reshape(H, lru_width // H, lru_width // H)
    return jnp.einsum("thj,hij->thi", shaped, blocks, preferred_element_type=jnp.float32).reshape(
        row_count, lru_width
    )


def heads_grad(values, grads_low):
    row_count, lru_width = values.shape
    left_side = values.reshape(row_count, H, lru_width // H)
    right_side = grads_low.reshape(row_count, H, lru_width // H)
    return jnp.einsum(
        "thi,thj->hij", left_side, right_side, preferred_element_type=jnp.float32
    ).reshape(lru_width, lru_width // H)


def lru_terms(decay_pre, input_pre, conv_out, decay_param, flag_rows):
    log_decay = -rate_scale * jax.nn.sigmoid(decay_pre) * jax.nn.softplus(decay_param)
    keep_rows = 1.0 - flag_rows[:, None]
    coefficient = jnp.exp(log_decay) * keep_rows
    scale_in = flag_rows[:, None] + keep_rows * jnp.sqrt(-jnp.expm1(2.0 * log_decay))
    drive_term = scale_in * jax.nn.sigmoid(input_pre) * conv_out
    return (coefficient, drive_term)


def build_masks(flag_rows):
    row_count = flag_rows.shape[0]
    running = jnp.ones((row_count,), jnp.float32)
    masks = [running]
    for offset in range(1, CW):
        earlier_flags = jnp.concatenate(
            [jnp.zeros((offset - 1,), jnp.float32), flag_rows[: row_count - (offset - 1)]]
        )
        running = running * (1.0 - earlier_flags)
        masks.append(running)
    return masks


def send_mask(flag_rows):
    tail_keep = 1.0 - flag_rows[flag_rows.shape[0] - (CW - 1) :]
    after_rows = jnp.cumprod(tail_keep[::-1])[::-1]
    return jnp.concatenate([after_rows[1:], jnp.ones((1,), jnp.float32)])


def conv_local(padded, weight, bias, masks):
    row_count = masks[0].shape[0]
    conv_total = bias + jnp.zeros((row_count, padded.shape[1]), jnp.float32)
    for offset in range(CW):
        lead = CW - 1 - offset
        conv_total = conv_total + weight[offset] * (
            padded[lead : lead + row_count] * masks[offset][:, None]
        )
    return conv_total


def mlp_act(gate_values, up_values):
    return gelu_tanh(gate_values) * up_values


def token_split_body(
    tokens,
    starts,
    cotangent,
    norm_gain,
    gate_branch,
    input_branch,
    conv_weight,
    conv_bias,
    decay_gate,
    decay_bias,
    input_gate,
    input_bias,
    decay_param,
    out_proj,
    mlp_gain,
    mlp_gate,
    mlp_up,
    mlp_down,
):
    (
        whole_norm_gain,
        whole_gate_branch,
        whole_input_branch,
        whole_conv_weight,
        whole_conv_bias,
        whole_decay_gate,
        whole_decay_bias,
        whole_input_gate,
        whole_input_bias,
        whole_decay_param,
        whole_out_proj,
    ) = (
        lax.all_gather(norm_gain, "seq", axis=0, tiled=True),
        lax.all_gather(gate_branch, "seq", axis=0, tiled=True),
        lax.all_gather(input_branch, "seq", axis=0, tiled=True),
        lax.all_gather(conv_weight, "seq", axis=1, tiled=True),
        lax.all_gather(conv_bias, "seq", axis=0, tiled=True),
        lax.all_gather(decay_gate, "seq", axis=0, tiled=True),
        lax.all_gather(decay_bias, "seq", axis=0, tiled=True),
        lax.all_gather(input_gate, "seq", axis=0, tiled=True),
        lax.all_gather(input_bias, "seq", axis=0, tiled=True),
        lax.all_gather(decay_param, "seq", axis=0, tiled=True),
        lax.all_gather(out_proj, "seq", axis=0, tiled=True),
    )
    flag_rows = starts.astype(jnp.float32)
    row_count = tokens.shape[0]
    values = tokens.astype(jnp.float32)
    normed = rms_norm(values, whole_norm_gain.astype(jnp.float32)).astype(jnp.bfloat16)
    gate_pre = jnp.dot(normed, whole_gate_branch, preferred_element_type=jnp.float32)
    gate_act = gelu_tanh(gate_pre)
    conv_input = jnp.dot(normed, whole_input_branch, preferred_element_type=jnp.float32).astype(
        jnp.bfloat16
    )
    lru_width = conv_input.shape[1]
    alive_rows = send_mask(flag_rows)
    masks = build_masks(flag_rows)
    outgoing = conv_input[row_count - (CW - 1) :] * alive_rows[:, None].astype(jnp.bfloat16)
    incoming = passed_along(outgoing, "seq", 1)
    padded = jnp.concatenate([incoming, conv_input], axis=0).astype(jnp.float32)
    conv_out = conv_local(
        padded, whole_conv_weight.astype(jnp.float32), whole_conv_bias.astype(jnp.float32), masks
    )
    conv_low = conv_out.astype(jnp.bfloat16)
    decay_pre = heads_product(conv_low, whole_decay_gate) + whole_decay_bias.astype(jnp.float32)
    input_pre = heads_product(conv_low, whole_input_gate) + whole_input_bias.astype(jnp.float32)
    param_full = whole_decay_param.astype(jnp.float32)
    coefficient, drive_term = lru_terms(decay_pre, input_pre, conv_out, param_full, flag_rows)
    cumulative, local_state = lax.associative_scan(combine, (coefficient, drive_term), axis=0)
    entering = prefix(
        (cumulative[-1], local_state[-1]),
        "seq",
        combine,
        (jnp.ones_like(cumulative[-1]), jnp.zeros_like(local_state[-1])),
        False,
    )
    incoming_state = entering[1]
    states = local_state + cumulative * incoming_state[None, :]
    mixed_rows = (states * gate_act).astype(jnp.bfloat16)
    middle = values + jnp.dot(mixed_rows, whole_out_proj, preferred_element_type=jnp.float32)
    whole_mlp_gain, whole_mlp_gate, whole_mlp_up, whole_mlp_down = (
        lax.all_gather(mlp_gain, "seq", axis=0, tiled=True),
        lax.all_gather(mlp_gate, "seq", axis=0, tiled=True),
        lax.all_gather(mlp_up, "seq", axis=0, tiled=True),
        lax.all_gather(mlp_down, "seq", axis=0, tiled=True),
    )
    gain_two = whole_mlp_gain.astype(jnp.float32)
    normed_two = rms_norm(middle, gain_two).astype(jnp.bfloat16)
    gate_mlp = jnp.dot(normed_two, whole_mlp_gate, preferred_element_type=jnp.float32)
    up_mlp = jnp.dot(normed_two, whole_mlp_up, preferred_element_type=jnp.float32)
    hidden = mlp_act(gate_mlp, up_mlp).astype(jnp.bfloat16)
    result = middle + jnp.dot(hidden, whole_mlp_down, preferred_element_type=jnp.float32)
    block_out = result.astype(jnp.bfloat16)
    back_mlp_gain, back_mlp_gate, back_mlp_up, back_mlp_down = (
        lax.all_gather(mlp_gain, "seq", axis=0, tiled=True),
        lax.all_gather(mlp_gate, "seq", axis=0, tiled=True),
        lax.all_gather(mlp_up, "seq", axis=0, tiled=True),
        lax.all_gather(mlp_down, "seq", axis=0, tiled=True),
    )
    grad_mlp_down = jnp.einsum("tf,td->fd", hidden, cotangent, preferred_element_type=jnp.float32)
    grad_hidden = jnp.einsum(
        "td,fd->tf", cotangent, back_mlp_down, preferred_element_type=jnp.float32
    )
    unused_act, pull_act = jax.vjp(mlp_act, gate_mlp, up_mlp)
    grad_gate_full, grad_up_full = pull_act(grad_hidden)
    grad_gate_low = grad_gate_full.astype(jnp.bfloat16)
    grad_up_low = grad_up_full.astype(jnp.bfloat16)
    grad_mlp_gate = jnp.einsum(
        "td,tf->df", normed_two, grad_gate_low, preferred_element_type=jnp.float32
    )
    grad_mlp_up = jnp.einsum(
        "td,tf->df", normed_two, grad_up_low, preferred_element_type=jnp.float32
    )
    grad_normed_two = jnp.einsum(
        "tf,df->td", grad_gate_low, back_mlp_gate, preferred_element_type=jnp.float32
    ) + jnp.einsum("tf,df->td", grad_up_low, back_mlp_up, preferred_element_type=jnp.float32)
    unused_norm, pull_norm = jax.vjp(rms_norm, middle, back_mlp_gain.astype(jnp.float32))
    grad_middle_norm, grad_mlp_gain = pull_norm(grad_normed_two)
    mlp_sums = (
        lax.psum_scatter(grad_mlp_gain, "seq", scatter_dimension=0, tiled=True),
        lax.psum_scatter(grad_mlp_gate, "seq", scatter_dimension=0, tiled=True),
        lax.psum_scatter(grad_mlp_up, "seq", scatter_dimension=0, tiled=True),
        lax.psum_scatter(grad_mlp_down, "seq", scatter_dimension=0, tiled=True),
    )
    grad_middle = cotangent.astype(jnp.float32) + grad_middle_norm
    grad_branch = grad_middle.astype(jnp.bfloat16)
    (
        back_norm_gain,
        back_gate_branch,
        back_input_branch,
        back_conv_weight,
        back_conv_bias,
        back_decay_gate,
        back_decay_bias,
        back_input_gate,
        back_input_bias,
        back_decay_param,
        back_out_proj,
    ) = (
        lax.all_gather(norm_gain, "seq", axis=0, tiled=True),
        lax.all_gather(gate_branch, "seq", axis=0, tiled=True),
        lax.all_gather(input_branch, "seq", axis=0, tiled=True),
        lax.all_gather(conv_weight, "seq", axis=1, tiled=True),
        lax.all_gather(conv_bias, "seq", axis=0, tiled=True),
        lax.all_gather(decay_gate, "seq", axis=0, tiled=True),
        lax.all_gather(decay_bias, "seq", axis=0, tiled=True),
        lax.all_gather(input_gate, "seq", axis=0, tiled=True),
        lax.all_gather(input_bias, "seq", axis=0, tiled=True),
        lax.all_gather(decay_param, "seq", axis=0, tiled=True),
        lax.all_gather(out_proj, "seq", axis=0, tiled=True),
    )
    grad_out_proj = jnp.einsum(
        "tr,td->rd", mixed_rows, grad_branch, preferred_element_type=jnp.float32
    )
    grad_mixed = jnp.einsum(
        "td,rd->tr", grad_branch, back_out_proj, preferred_element_type=jnp.float32
    )
    grad_states = grad_mixed * gate_act
    unused_gelu, pull_gelu = jax.vjp(gelu_tanh, gate_pre)
    grad_gate_pre = pull_gelu(grad_mixed * states)[0].astype(jnp.bfloat16)
    shifted_coef = jnp.concatenate([coefficient[1:], jnp.ones((1, lru_width), jnp.float32)], axis=0)
    back_cumulative, back_local = lax.associative_scan(
        combine, (shifted_coef[::-1], grad_states[::-1]), axis=0
    )
    back_cumulative = back_cumulative[::-1]
    back_local = back_local[::-1]
    leaving = prefix(
        (coefficient[0] * back_cumulative[0], coefficient[0] * back_local[0]),
        "seq",
        combine,
        (jnp.ones_like(back_local[0]), jnp.zeros_like(back_local[0])),
        True,
    )
    incoming_adjoint = leaving[1]
    adjoint = back_local + back_cumulative * incoming_adjoint[None, :]
    previous = jnp.concatenate([incoming_state[None, :], states[:-1]], axis=0)

    def terms_only(decay_values, input_values, conv_values, param_values):
        return lru_terms(decay_values, input_values, conv_values, param_values, flag_rows)

    unused_terms, pull_terms = jax.vjp(
        terms_only, decay_pre, input_pre, conv_out, back_decay_param.astype(jnp.float32)
    )
    grad_decay_full, grad_input_full, grad_conv_direct, grad_decay_param = pull_terms(
        (adjoint * previous, adjoint)
    )
    grad_decay_bias = jnp.sum(grad_decay_full, axis=0)
    grad_input_bias = jnp.sum(grad_input_full, axis=0)
    grad_decay_low = grad_decay_full.astype(jnp.bfloat16)
    grad_input_low = grad_input_full.astype(jnp.bfloat16)
    grad_decay_gate = heads_grad(conv_low, grad_decay_low)
    grad_input_gate = heads_grad(conv_low, grad_input_low)
    grad_conv_out = (
        grad_conv_direct
        + heads_back(grad_decay_low, back_decay_gate)
        + heads_back(grad_input_low, back_input_gate)
    )

    def conv_only(padded_values, weight_values, bias_values):
        return conv_local(padded_values, weight_values, bias_values, masks)

    unused_conv, pull_conv = jax.vjp(
        conv_only, padded, back_conv_weight.astype(jnp.float32), back_conv_bias.astype(jnp.float32)
    )
    grad_padded, grad_conv_weight, grad_conv_bias = pull_conv(grad_conv_out)
    returned_rows = passed_along(grad_padded[: CW - 1], "seq", -1)
    addition = jnp.concatenate(
        [
            jnp.zeros((row_count - (CW - 1), lru_width), jnp.float32),
            returned_rows * alive_rows[:, None],
        ],
        axis=0,
    )
    grad_conv_input = (grad_padded[CW - 1 :] + addition).astype(jnp.bfloat16)
    grad_input_branch = jnp.einsum(
        "td,tr->dr", normed, grad_conv_input, preferred_element_type=jnp.float32
    )
    grad_gate_branch = jnp.einsum(
        "td,tr->dr", normed, grad_gate_pre, preferred_element_type=jnp.float32
    )
    grad_normed = jnp.einsum(
        "tr,dr->td", grad_conv_input, back_input_branch, preferred_element_type=jnp.float32
    ) + jnp.einsum("tr,dr->td", grad_gate_pre, back_gate_branch, preferred_element_type=jnp.float32)
    unused_first, pull_first = jax.vjp(rms_norm, values, back_norm_gain.astype(jnp.float32))
    grad_values_norm, grad_norm_gain = pull_first(grad_normed)
    grad_tokens = grad_middle + grad_values_norm
    rec_sums = (
        lax.psum_scatter(grad_norm_gain, "seq", scatter_dimension=0, tiled=True),
        lax.psum_scatter(grad_gate_branch, "seq", scatter_dimension=0, tiled=True),
        lax.psum_scatter(grad_input_branch, "seq", scatter_dimension=0, tiled=True),
        lax.psum_scatter(grad_conv_weight, "seq", scatter_dimension=1, tiled=True),
        lax.psum_scatter(grad_conv_bias, "seq", scatter_dimension=0, tiled=True),
        lax.psum_scatter(grad_decay_gate, "seq", scatter_dimension=0, tiled=True),
        lax.psum_scatter(grad_decay_bias, "seq", scatter_dimension=0, tiled=True),
        lax.psum_scatter(grad_input_gate, "seq", scatter_dimension=0, tiled=True),
        lax.psum_scatter(grad_input_bias, "seq", scatter_dimension=0, tiled=True),
        lax.psum_scatter(grad_decay_param, "seq", scatter_dimension=0, tiled=True),
        lax.psum_scatter(grad_out_proj, "seq", scatter_dimension=0, tiled=True),
    )
    return (
        block_out,
        grad_tokens,
        rec_sums[0],
        rec_sums[1],
        rec_sums[2],
        rec_sums[3],
        rec_sums[4],
        rec_sums[5],
        rec_sums[6],
        rec_sums[7],
        rec_sums[8],
        rec_sums[9],
        rec_sums[10],
        mlp_sums[0],
        mlp_sums[1],
        mlp_sums[2],
        mlp_sums[3],
    )


CHIPS = 4
MESH = pl.DeviceIdType.MESH


def place():
    me = lax.axis_index("seq")
    core = lax.rem(me, 2)
    x = lax.rem(lax.div(me, 2), 2)
    y = lax.rem(lax.div(me, 4), 2)
    return me, lax.div(me, 8), 2 * y + x, core, x, y


def column_groups(n):
    return [[8 * z + 2 * p + c for c in range(2) for z in range(n // 8)] for p in range(CHIPS)]


def line_groups(n):
    return [[8 * z + r for z in range(n // 8)] for r in range(8)]


def greet(devices):
    barrier = pltpu.get_barrier_semaphore()
    for device in devices:
        pl.semaphore_signal(barrier, inc=1, device_id=(device,), device_id_type=MESH)
    pl.semaphore_wait(barrier, len(devices))


def remote(source, target, send_sem, recv_sem, device):
    return pltpu.make_async_remote_copy(
        src_ref=source,
        dst_ref=target,
        send_sem=send_sem,
        recv_sem=recv_sem,
        device_id=(device,),
        device_id_type=MESH,
    )


def comm_params(collective_id, vmem_mib=None):
    return pltpu.CompilerParams(
        collective_id=collective_id,
        has_side_effects=True,
        vmem_limit_bytes=None if vmem_mib is None else vmem_mib * 2**20,
    )


def lasting(microseconds):
    return pl.CostEstimate(
        flops=int(microseconds * 1e9), bytes_accessed=int(microseconds * 3e6), transcendentals=0
    )


ANY = pl.BlockSpec(memory_space=pl.ANY)
VMEM = pl.BlockSpec(memory_space=pltpu.VMEM)


def plane_neighbours():
    me, z, p, c, x, y = place()
    x_dev, y_dev = me + 2 - 4 * x, me + 4 - 8 * y
    return (x_dev, y_dev, y_dev + 2 - 4 * x), (p + 1 - 2 * x, p + 2 - 4 * y, 3 - p)


def gather_steps(source, whole, send, recv, local, first):
    me, z, p, c, x, y = place()
    (x_dev, y_dev, d_dev), (p_x, p_y, p_d) = plane_neighbours()
    half = source.shape[0] // 2

    def copy(k, source, target, device):
        return remote(source, target, send.at[first + k], recv.at[first + k], device)

    to_x, to_y = copy(0, source, whole.at[p], x_dev), copy(1, source, whole.at[p], y_dev)
    low, high = whole.at[p_x, pl.ds(0, half)], whole.at[p_y, pl.ds(half, half)]
    on_y, on_x = copy(2, low, low, y_dev), copy(3, high, high, x_dev)
    own = pltpu.make_async_copy(source, whole.at[p], local)

    def begin():
        to_x.start()
        to_y.start()
        own.start()

    def forward():
        to_x.wait_recv()
        on_y.start()
        to_y.wait_recv()
        on_x.start()

    def end():
        to_x.wait_send()
        to_y.wait_send()
        on_y.wait()
        on_x.wait()
        own.wait()

    return begin, forward, end


def sum_scratch(rows, columns, dtype):
    whole, part = pltpu.VMEM((rows, columns), dtype), pltpu.VMEM((rows // 2, columns), dtype)
    return [whole] * 3 + [part] * 4 + [pltpu.SemaphoreType.DMA((6,)), pltpu.SemaphoreType.DMA((6,)), pltpu.SemaphoreType.DMA((3,))]


def sum_steps(part, own, from_x, from_y, diag_x, diag_y, on_x, on_y, send, recv, local):
    me, z, p, c, x, y = place()
    (x_dev, y_dev, d_dev), (p_x, p_y, p_d) = plane_neighbours()
    half = part.shape[1] // 2
    low, high = pl.ds(0, half), pl.ds(half, half)
    copies = [
        remote(part.at[p_d, low], diag_x, send.at[0], recv.at[0], x_dev),
        remote(part.at[p_d, high], diag_y, send.at[1], recv.at[1], y_dev),
        remote(part.at[p_x, low], from_x.at[low], send.at[2], recv.at[2], x_dev),
        remote(part.at[p_y, high], from_y.at[high], send.at[3], recv.at[3], y_dev),
    ]
    locals_ = [
        pltpu.make_async_copy(part.at[p_y, low], on_y, local.at[0]),
        pltpu.make_async_copy(part.at[p_x, high], on_x, local.at[1]),
        pltpu.make_async_copy(part.at[p], own, local.at[2]),
    ]
    to_y = remote(on_y, from_y.at[low], send.at[4], recv.at[4], y_dev)
    to_x = remote(on_x, from_x.at[high], send.at[5], recv.at[5], x_dev)

    def add_into(target, addend):
        @pl.loop(0, half // 16)
        def add_rows(i):
            at = pl.ds(pl.multiple_of(i * 16, 16), 16)
            target[at, :] = (
                target[at, :].astype(jnp.float32) + addend[at, :].astype(jnp.float32)
            ).astype(target.dtype)

    def begin():
        for copy in copies + locals_:
            copy.start()

    def forward():
        locals_[0].wait()
        copies[0].wait_recv()
        add_into(on_y, diag_x)
        to_y.start()
        locals_[1].wait()
        copies[1].wait_recv()
        add_into(on_x, diag_y)
        to_x.start()

    def end():
        locals_[2].wait()
        copies[2].wait_recv()
        copies[3].wait_recv()
        to_y.wait()
        to_x.wait()
        for copy in copies:
            copy.wait_send()

    return begin, forward, end


def sixteen(i):
    return pl.ds(pl.multiple_of(i * 16, 16), 16)


def fetch_rows(rows_all, first, start, target, sems):
    count = sems.shape[0]
    rows = target.shape[0] // count
    return [
        pltpu.make_async_copy(
            rows_all.at[first + k, pl.ds(start, rows)], target.at[pl.ds(k * rows, rows)], sems.at[k]
        )
        for k in range(count)
    ]


def computed_scratch(rows, columns, dtype):
    f32, bf16 = jnp.float32, jnp.bfloat16
    whole, half = (rows, columns), (rows // 2, columns)
    shapes = [(whole, bf16), (whole, f32)] + [(half, f32)] * 2 + [(half, bf16)] * 6 + [(half, dtype)] * 4
    return [pltpu.VMEM(*shape) for shape in shapes] + [pltpu.SemaphoreType.DMA((6,))] * 2


def computed_sum(product, sent_d, own, kept_x, kept_y, *refs):
    sent_x, sent_y, from_x, from_y, diag_x, diag_y, joint_x, joint_y, also_x, also_y, send, recv = refs
    (x_dev, y_dev, d_dev), (p_x, p_y, p_d) = plane_neighbours()
    p = place()[2]
    rows, width = own.shape
    half = rows // 2
    low, high = pl.ds(0, half), pl.ds(half, half)
    tile = 512

    def into(chip, at, target):
        @pl.loop(0, width // tile)
        def product_tile(k):
            columns = pl.ds(pl.multiple_of(k * tile, tile), tile)
            target[:, columns] = product(chip, at, columns).astype(target.dtype)

    def copy(k, source, target, device):
        return remote(source, target, send.at[k], recv.at[k], device)

    first = [copy(0, sent_d.at[low], diag_x, x_dev), copy(1, sent_d.at[high], diag_y, y_dev)]
    second = [copy(2, sent_x, from_x, x_dev), copy(3, sent_y, from_y, y_dev)]
    third = [copy(4, joint_y, also_y, y_dev), copy(5, joint_x, also_x, x_dev)]

    def begin():
        into(p_d, slice(None), sent_d)
        for sent in first:
            sent.start()
        into(p_x, low, sent_x)
        into(p_y, high, sent_y)
        for sent in second:
            sent.start()
        into(p_y, low, kept_y)
        into(p_x, high, kept_x)
        into(p, slice(None), own)

    def add(target, kept, addend):
        @pl.loop(0, half // 16)
        def add_rows(i):
            at = sixteen(i)
            target[at, :] = (kept[at, :] + addend[at, :].astype(jnp.float32)).astype(target.dtype)

    def forward():
        first[0].wait_recv()
        add(joint_y, kept_y, diag_x)
        third[0].start()
        first[1].wait_recv()
        add(joint_x, kept_x, diag_y)
        third[1].start()

    def end():
        for sent in first:
            sent.wait_send()
        for sent in second + third:
            sent.wait()

    def total(i, j):
        at = sixteen(j)
        parts = (from_x, also_y) if i == 0 else (also_x, from_y)
        here = pl.ds(pl.multiple_of(i * half + j * 16, 16), 16)
        return here, own[here, :] + parts[0][at, :].astype(jnp.float32) + parts[1][at, :].astype(jnp.float32)

    return begin, forward, end, total


def middle_kernel(
    mixed, rows_all, tokens, gain, cot, middle, whole, cot_other, normed, out_here, send, recv, local, loads, *sums
):
    me, z, p, c, x, y = place()
    sibling = me + 1 - 2 * c
    greet((*plane_neighbours()[0][:2], sibling))
    to_sibling = remote(cot, cot_other, send.at[4], recv.at[4], sibling)
    to_sibling.start()
    f32, bf16 = jnp.float32, jnp.bfloat16
    fetched = fetch_rows(rows_all, 0, 0, out_here, loads)
    for copy in fetched:
        copy.start()
    for copy in fetched:
        copy.wait()

    def product(chip, at, columns):
        return jnp.dot(mixed[chip, at, :], out_here[:, columns], preferred_element_type=f32)

    *steps, total = computed_sum(product, *sums)
    for step in steps:
        step()
    for i in range(2):

        @pl.loop(0, tokens.shape[0] // 32)
        def norm_rows(j):
            at, values = total(i, j)
            values = tokens[at, :].astype(f32) + values
            middle[at, :] = values
            inverse = lax.rsqrt(jnp.mean(values * values, axis=-1, keepdims=True) + epsilon)
            normed[at, :] = (values * inverse * gain[...]).astype(bf16)

    for step in gather_steps(normed, whole, send, recv, local, 0):
        step()
    to_sibling.wait()


def middle_of(mixed, rows_all, tokens, gain, cot, collective_id):
    rows, width = tokens.shape
    channels = mixed.shape[2]
    f32, bf16 = jnp.float32, jnp.bfloat16
    return pl.pallas_call(
        middle_kernel,
        out_shape=[
            jax.ShapeDtypeStruct((rows, width), f32),
            jax.ShapeDtypeStruct((CHIPS, rows, width), bf16),
            jax.ShapeDtypeStruct(cot.shape, cot.dtype),
        ],
        in_specs=[VMEM, ANY, VMEM, VMEM, ANY],
        out_specs=[VMEM, ANY, ANY],
        scratch_shapes=[
            pltpu.VMEM((rows, width), bf16),
            pltpu.VMEM((channels, width), bf16),
            pltpu.SemaphoreType.DMA((5,)),
            pltpu.SemaphoreType.DMA((5,)),
            pltpu.SemaphoreType.DMA,
            pltpu.SemaphoreType.DMA((rows_all.shape[0],)),
            *computed_scratch(rows, width, f32),
        ],
        compiler_params=comm_params(collective_id, 60),
        cost_estimate=lasting(75),
        name="middle",
    )(mixed, rows_all, tokens, gain[None], cot)


def feed_forward_kernel(
    piece,
    two,
    cot,
    weights,
    down,
    *refs,
):
    last = piece == 1
    if last:
        earlier, hidden, grad, parts, earlier_here, *refs = refs
    else:
        hidden, grad, parts, *refs = refs
    low, two_here, two_there, cot_here, weights_here, down_here, low_there, send, recv, loads, down_loads = refs
    me, z, p, c, x, y = place()
    sibling = me + 1 - 2 * c
    greet((sibling,))
    f32, bf16 = jnp.float32, jnp.bfloat16
    tokens, width = two.shape
    units = hidden.shape[1]
    half = width // 2
    pairs = [
        (two, two_here),
        (weights, weights_here),
        (cot, cot_here),
    ]
    if last:
        pairs.append((earlier, earlier_here))
    fetched = [pltpu.make_async_copy(a, b, loads.at[k]) for k, (a, b) in enumerate(pairs)]
    count = down_loads.shape[0]
    fetched[3:3] = fetch_rows(down, count * piece, down.shape[1] - units // count, down_here, down_loads)
    for copy in fetched:
        copy.start()
    other_half = two.at[:, pl.ds(pl.multiple_of((1 - c) * half, 128), half)]
    two_swap = remote(other_half, two_there, send.at[0], recv.at[0], sibling)
    two_swap.start()
    for copy in fetched[: 3 + count]:
        copy.wait()
    tile, block = 256, 512

    def dot_t(left, right):
        return lax.dot_general(left, right, (((1,), (1,)), ((), ())), preferred_element_type=f32)

    def dot_first(left, right):
        return lax.dot_general(left, right, (((0,), (0,)), ((), ())), preferred_element_type=f32)

    low_swaps = []
    for t in range(units // tile):
        gate_at, up_at = pl.ds(t * tile, tile), pl.ds(units + t * tile, tile)

        @pl.loop(0, tokens // block)
        def rows_block(j):
            at = pl.ds(pl.multiple_of(j * block, block), block)
            v = jnp.dot(two_here[at, :], weights_here[:, gate_at], preferred_element_type=f32)
            up = jnp.dot(two_here[at, :], weights_here[:, up_at], preferred_element_type=f32)
            grad_hidden = dot_t(cot_here[at, :], down_here[gate_at, :])
            square = v * v
            bent = jnp.tanh(v * (GELU_A + GELU_A * GELU_B * square))
            rising = 0.5 + 0.5 * bent
            act = v * rising
            slope = rising + 0.5 * v * (1.0 - bent * bent) * (GELU_A + 3.0 * GELU_A * GELU_B * square)
            hidden[at, gate_at] = (act * up).astype(bf16)
            low[at, gate_at] = (grad_hidden * up * slope).astype(bf16)
            low[at, up_at] = (grad_hidden * act).astype(bf16)

        for k, columns in enumerate((gate_at, up_at)):
            sems = 1 + 2 * t + k
            low_swaps.append(
                remote(low.at[:, columns], low_there.at[:, columns], send.at[sems], recv.at[sems], sibling)
            )
            low_swaps[-1].start()
    for copy in fetched[3 + count :]:
        copy.wait()

    @pl.loop(0, tokens // block)
    def parts_block(j):
        at = pl.ds(pl.multiple_of(j * block, block), block)

        @pl.loop(0, width // block)
        def parts_tile(k):
            columns = pl.ds(pl.multiple_of(k * block, block), block)
            values = dot_t(low[at, :], weights_here[columns, :])
            if last:
                values = values + earlier_here[at, columns]
            parts[at, columns] = values.astype(parts.dtype)

    two_swap.wait()
    for copy in low_swaps:
        copy.wait()

    @pl.loop(0, half // block)
    def grad_block(m):
        here = pl.ds(pl.multiple_of(c * half + m * block, 128), block)
        there = pl.ds(pl.multiple_of(m * block, block), block)

        @pl.loop(0, 2 * units // block)
        def grad_tile(k):
            columns = pl.ds(pl.multiple_of(k * block, block), block)
            grad[there, columns] = (
                dot_first(two_here[:, here], low[:, columns]) + dot_first(two_there[:, there], low_there[:, columns])
            ).astype(bf16)


def feed_forward(piece, two, cot, weights, down, earlier, collective_id):
    tokens, width = two.shape
    units = weights.shape[1] // 2
    bf16 = jnp.bfloat16
    out_shape = [
        jax.ShapeDtypeStruct((tokens, units), bf16),
        jax.ShapeDtypeStruct((width // 2, 2 * units), bf16),
    ]
    low = pltpu.VMEM((tokens, 2 * units), bf16)
    scratch = []
    if earlier:
        out_shape.append(jax.ShapeDtypeStruct((tokens, width), bf16))
        scratch = [pltpu.VMEM((tokens, width), jnp.float32)]
    else:
        out_shape.append(jax.ShapeDtypeStruct((tokens, width), jnp.float32))
    swaps = 1 + 2 * (units // 256)
    return pl.pallas_call(
        functools.partial(feed_forward_kernel, piece),
        out_shape=out_shape,
        in_specs=[ANY] * (4 + len(earlier)),
        out_specs=[VMEM] * 3,
        scratch_shapes=[
            *scratch,
            low,
            pltpu.VMEM((tokens, width), bf16),
            pltpu.VMEM((tokens, width // 2), bf16),
            pltpu.VMEM((tokens, width), bf16),
            pltpu.VMEM(weights.shape, bf16),
            pltpu.VMEM((units, width), bf16),
            low,
            pltpu.SemaphoreType.DMA((swaps,)),
            pltpu.SemaphoreType.DMA((swaps,)),
            pltpu.SemaphoreType.DMA((3 + len(earlier),)),
            pltpu.SemaphoreType.DMA((down.shape[0] // 2,)),
        ],
        compiler_params=comm_params(collective_id, 60),
        cost_estimate=lasting(35),
        name="feed_forward",
    )(two, cot, weights, down, *earlier)


def norm_back_rows(values, gain, grad, rest):
    inverse = lax.rsqrt(jnp.mean(values * values, axis=-1, keepdims=True) + epsilon)
    scaled = gain * grad
    pull = jnp.mean(scaled * values, axis=-1, keepdims=True) * (inverse * inverse * inverse)
    return rest + inverse * scaled - values * pull, grad * values * inverse


def grads_of_middle_kernel(
    parts,
    middle,
    cot,
    gain,
    hidden_zero,
    hidden_one,
    down,
    cot_all,
    cot_other,
    mixed_zero,
    mixed_one,
    grad_middle,
    grad_gain,
    whole,
    row_grads,
    down_parts,
    branch,
    branch_all,
    branch_other,
    mixed_here,
    mixed_there,
    out_sum,
    hidden_here,
    hidden_other,
    down_here,
    cot_here,
    cot_there,
    *scratch,
):
    sums, (send, recv, local, loads, down_loads) = scratch[:10], scratch[10:]
    me, z, p, c, x, y = place()
    f32, bf16 = jnp.float32, jnp.bfloat16
    sibling = me + 1 - 2 * c
    greet((*plane_neighbours()[0][:2], sibling))
    own, from_x, from_y = sums[:3]
    begin, forward, end = sum_steps(parts, *sums)
    begin()
    half = hidden_zero.shape[1]
    swaps = [remote(hidden, hidden_other, send.at[4], recv.at[4], sibling) for hidden in (hidden_one, hidden_zero)]
    mixed_swaps = [remote(mixed, mixed_there, send.at[9], recv.at[9], sibling) for mixed in (mixed_one, mixed_zero)]
    mixed_loads = [pltpu.make_async_copy(mixed, mixed_here, loads.at[4]) for mixed in (mixed_zero, mixed_one)]

    @pl.when(c == 0)
    def send_one():
        swaps[0].start()
        mixed_swaps[0].start()
        mixed_loads[0].start()

    @pl.when(c == 1)
    def send_zero():
        swaps[1].start()
        mixed_swaps[1].start()
        mixed_loads[1].start()

    fetched = [
        pltpu.make_async_copy(source, target, loads.at[k])
        for k, (source, target) in enumerate(
            (
                (hidden_zero, hidden_here.at[:, pl.ds(0, half)]),
                (hidden_one, hidden_here.at[:, pl.ds(half, half)]),
                (cot_all, cot_here),
                (cot_other, cot_there),
            )
        )
    ]
    count = down_loads.shape[0]
    down_fetched = fetch_rows(down, 0, down.shape[1] - down_here.shape[0] // count, down_here, down_loads)
    for copy in fetched + down_fetched:
        copy.start()
    for copy in fetched[:4]:
        copy.wait()
    swaps[0].wait()
    tile = 256

    planes = row_grads.shape[0]
    units = half // planes
    above = row_grads.shape[1] - units

    def grad_tiles(m):
        rows_here = pl.ds(pl.multiple_of(c * half + m * tile, 128), tile)

        @pl.loop(0, cot_all.shape[1] // (2 * tile))
        def grad_tile(k):
            columns = pl.ds(pl.multiple_of(k * 2 * tile, 128), 2 * tile)

            def dot_t(left, right):
                return lax.dot_general(left, right, (((0,), (0,)), ((), ())), preferred_element_type=f32)

            values = (
                dot_t(hidden_here[:, rows_here], cot_here[:, columns])
                + dot_t(hidden_other[:, m * tile : (m + 1) * tile], cot_there[:, columns])
            ).astype(bf16)
            for j in range(planes):
                start, stop = max(j * units, m * tile), min((j + 1) * units, (m + 1) * tile)
                if start < stop:
                    row_grads[j, above + start - j * units : above + stop - j * units, columns] = values[
                        start - m * tile : stop - m * tile
                    ]

    grad_tiles(0)
    forward()
    for m in range(1, half // tile):
        grad_tiles(m)
    end()
    rows, width = middle.shape

    def norm_rows(i, total):
        at = sixteen(i)
        grad = own[at, :].astype(f32) + from_x[at, :].astype(f32) + from_y[at, :].astype(f32)
        given, terms = norm_back_rows(middle[at, :], gain[...], grad, cot[at, :].astype(f32))
        grad_middle[at, :] = given
        branch[at, :] = given.astype(bf16)
        return total + terms[:8] + terms[8:]

    total = lax.fori_loop(0, rows // 16, norm_rows, jnp.zeros((8, width), f32))
    grad_gain[...] = jnp.sum(total, axis=0, keepdims=True)
    begin, forward, end = gather_steps(branch, branch_all, send, recv, local, 0)
    (p_x, p_y, p_d) = plane_neighbours()[1]

    def to_sibling(k, chip, source):
        return remote(source, branch_other.at[chip], send.at[5 + k], recv.at[5 + k], sibling)

    shares = [to_sibling(0, p, branch)] + [
        to_sibling(1 + k, chip, branch_all.at[chip]) for k, chip in enumerate((p_x, p_y, p_d))
    ]
    begin()
    shares[0].start()
    for copy in down_fetched + [mixed_loads[0], mixed_swaps[0]]:
        copy.wait()

    def down_tiles(j):
        @pl.loop(0, width // (2 * tile))
        def down_tile(k):
            columns = pl.ds(pl.multiple_of(k * 2 * tile, 128), 2 * tile)
            down_parts[j, :, columns] = jnp.dot(
                hidden_here[pl.ds(pl.multiple_of(j * rows, 16), rows), :],
                down_here[:, columns],
                preferred_element_type=f32,
            ).astype(bf16)

    pl.loop(0, CHIPS)(down_tiles)

    def out_tiles(mixed, branches, chips, finish):
        @pl.loop(0, width // (2 * tile))
        def out_tile(k):
            columns = pl.ds(pl.multiple_of(k * 2 * tile, 128), 2 * tile)
            values = out_sum[:, columns]
            for chip in chips:
                values = values + lax.dot_general(
                    mixed[pl.ds(pl.multiple_of(chip * rows, 16), rows), :],
                    branches[chip, :, columns],
                    (((0,), (0,)), ((), ())),
                    preferred_element_type=f32,
                )
            if finish:
                for j in range(planes):
                    row_grads[j, 0:above, columns] = values[j * above : (j + 1) * above].astype(bf16)
            else:
                out_sum[:, columns] = values

    forward()
    shares[1].start()
    shares[2].start()
    out_sum[...] = jnp.zeros_like(out_sum)
    out_tiles(mixed_here, branch_all, (p_x, p_y), False)
    end()
    shares[3].start()
    to_whole = pltpu.make_async_copy(branch_all, whole, local)
    to_whole.start()
    out_tiles(mixed_here, branch_all, (p, p_d), False)
    for copy in shares:
        copy.wait()
    out_tiles(mixed_there, branch_other, range(CHIPS), True)
    to_whole.wait()


def grads_of_middle(parts, middle, cot, gain, hiddens, down, cots, mixeds, collective_id):
    rows, width = middle.shape
    tokens, units = hiddens[0].shape[0], 2 * hiddens[0].shape[1]
    f32, bf16 = jnp.float32, jnp.bfloat16
    return pl.pallas_call(
        grads_of_middle_kernel,
        out_shape=[
            jax.ShapeDtypeStruct((rows, width), f32),
            jax.ShapeDtypeStruct((1, width), f32),
            jax.ShapeDtypeStruct((CHIPS, rows, width), bf16),
            jax.ShapeDtypeStruct(
                (down.shape[0] // 2, down.shape[1], width), bf16
            ),
            jax.ShapeDtypeStruct((CHIPS, rows, width), bf16),
        ],
        in_specs=[ANY, VMEM, VMEM, VMEM] + [ANY] * 7,
        out_specs=[VMEM, VMEM, ANY, VMEM, VMEM],
        scratch_shapes=[
            pltpu.VMEM((rows, width), bf16),
            pltpu.VMEM((CHIPS, rows, width), bf16),
            pltpu.VMEM((CHIPS, rows, width), bf16),
            pltpu.VMEM(mixeds[0].shape, bf16),
            pltpu.VMEM(mixeds[0].shape, bf16),
            pltpu.VMEM((mixeds[0].shape[1], width), f32),
            pltpu.VMEM((tokens, units), bf16),
            pltpu.VMEM((tokens, units // 2), bf16),
            pltpu.VMEM((units, width), bf16),
            pltpu.VMEM((tokens, width), bf16),
            pltpu.VMEM((tokens, width), bf16),
            *sum_scratch(rows, width, parts.dtype),
            pltpu.SemaphoreType.DMA((10,)),
            pltpu.SemaphoreType.DMA((10,)),
            pltpu.SemaphoreType.DMA,
            pltpu.SemaphoreType.DMA((5,)),
            pltpu.SemaphoreType.DMA((down.shape[0],)),
        ],
        compiler_params=comm_params(collective_id, 60),
        cost_estimate=lasting(80),
        name="grads_of_middle",
    )(parts, middle, cot, gain[None], *hiddens, down, *cots, *mixeds)


def closing_kernel(
    planes,
    in_low,
    whole_in,
    tokens,
    gain,
    rest,
    small,
    mlp_gain,
    conv_low,
    decay_low,
    input_low,
    piece,
    grad_tokens,
    small_out,
    gates_out,
    swapped,
    conv_a,
    conv_b,
    decay_a,
    decay_b,
    input_a,
    input_b,
    full,
    gates,
    gate_lines,
    lines,
    line,
    near_part,
    gains,
    gain_lines,
    gain_line,
    gain_near,
    gain_sum,
    send,
    recv,
    loads,
    swap_send,
    swap_recv,
    *sums,
):
    me, z, p, c, x, y = place()
    f32 = jnp.float32
    r = lax.rem(me, 8)
    near = [(lax.rem(r + d, 8), me - r + lax.rem(r + d, 8)) for d in range(1, 8)]
    far = [(lax.rem(z + d, planes), 8 * lax.rem(z + d, planes) + r) for d in range(1, planes)]
    greet([device for unused, device in near + far])

    def copy(k, source, target, device):
        return remote(source, target, send.at[k], recv.at[k], device)

    lows = ((conv_low, conv_a, conv_b), (decay_low, decay_a, decay_b), (input_low, input_a, input_b))
    fetched = [pltpu.make_async_copy(source, here, loads.at[k]) for k, (source, here, there) in enumerate(lows)]
    exchanges = [copy(k, source, there, me + 1 - 2 * c) for k, (source, here, there) in enumerate(lows)]
    at = 3
    small_far = [copy(at + d, small.at[there], lines.at[d], device) for d, (there, device) in enumerate(far)]
    at += len(far)
    for started in small_far + fetched + exchanges:
        started.start()

    def product(chip, rows_at, columns):
        return lax.dot_general(
            in_low[chip, rows_at, :], whole_in[columns, :], (((1,), (1,)), ((), ())), preferred_element_type=f32
        )

    begin, forward, end, part_of = computed_sum(product, *sums)
    begin()
    for ended in fetched + exchanges:
        ended.wait()
    swaps = swap_copies(piece, swapped, swap_send, swap_recv, loads.at[3])

    def dot_first(left, right):
        return lax.dot_general(left, right, (((0,), (0,)), ((), ())), preferred_element_type=f32)

    block = gates.shape[1]
    count = planes * block
    for k, (first, second) in enumerate(((decay_a, decay_b), (input_a, input_b))):
        full[...] = dot_first(conv_a[...], first[...]) + dot_first(conv_b[...], second[...])
        for j in range(planes):
            rows_at = pl.ds(pl.multiple_of(c * count + j * block, 8), block)
            for e in range(2):
                gates[j, :, (2 * k + e) * block : (2 * k + e + 1) * block] = full[
                    rows_at, e * count + j * block : e * count + (j + 1) * block
                ].astype(gates.dtype)
    gate_far = [copy(at + d, gates.at[there], gate_lines.at[d], device) for d, (there, device) in enumerate(far)]
    at += len(far)
    for sent in gate_far:
        sent.start()
    forward()
    for sent in swaps:
        sent.start()
    for sent in small_far:
        sent.wait()
    line[...] = small[z] + sum(lines[d] for d in range(planes - 1))
    small_near = copy(at, line.at[1 - c], near_part, me + 1 - 2 * c)
    small_near.start()
    at += 1
    end()
    rows, width = tokens.shape
    step = width // (8 * planes)

    def norm_rows(i, j, total):
        here, grad = part_of(i, j)
        given, terms = norm_back_rows(tokens[here, :].astype(f32), gain[...], grad, rest[here, :])
        for k in range(4 * planes):
            for e in range(2):
                grad_tokens[here, (2 * k + e) * step : (2 * k + e + 1) * step] = given[
                    :, (4 * planes * e + k) * step : (4 * planes * e + k + 1) * step
                ]
        return total + terms[:8] + terms[8:]

    total = jnp.zeros((8, width), f32)
    for i in range(2):
        total = lax.fori_loop(0, rows // 32, functools.partial(norm_rows, i), total)
    total = jnp.sum(total, axis=0, keepdims=True)
    for j in range(planes):
        for q in range(CHIPS):
            for e in range(2):
                start = ((e * planes + j) * CHIPS + q) * step
                gains[j, 2 * q + e : 2 * q + e + 1, 0:step] = total[:, start : start + step]
                gains[j, 2 * q + e : 2 * q + e + 1, step : 2 * step] = mlp_gain[:, start : start + step]
    gain_far = [copy(at + d, gains.at[there], gain_lines.at[d], device) for d, (there, device) in enumerate(far)]
    at += len(far)
    for sent in gain_far:
        sent.start()
    for sent in gain_far:
        sent.wait()
    gain_line[...] = gains[z] + sum(gain_lines[d] for d in range(planes - 1))
    last = [copy(at + d, gain_line, gain_near.at[d], device) for d, (there, device) in enumerate(near)]
    for sent in last:
        sent.start()
    for sent in gate_far + swaps + [small_near]:
        sent.wait()
    gates_out[...] = gates[z].astype(f32) + sum(gate_lines[d].astype(f32) for d in range(planes - 1))
    for sent in last:
        sent.wait()
    rows_small = line.shape[1]
    small_out[0:rows_small, :] = line[c] + near_part[...]
    gain_sum[...] = gain_line[...] + sum(gain_near[d] for d in range(7))
    small_out[rows_small : rows_small + 1, :] = gain_sum[pl.ds(r, 1), :]


def closing(in_low, whole_in, tokens, gain, rest, small, mlp_gain, lows, piece, head, collective_id):
    planes = lax.axis_size("seq") // 8
    rows, width = tokens.shape
    f32, bf16 = jnp.float32, jnp.bfloat16
    rows_small, lanes = small.shape[2:]
    channels = lows[0].shape[1]
    block = channels // (2 * planes)
    count = 3 + 3 * (planes - 1) + 8
    return pl.pallas_call(
        functools.partial(closing_kernel, planes),
        out_shape=[
            jax.ShapeDtypeStruct((rows, width), f32),
            jax.ShapeDtypeStruct((rows_small + 1, lanes), f32),
            jax.ShapeDtypeStruct((block, 2 * head), f32),
            jax.ShapeDtypeStruct(piece.shape, bf16),
        ],
        in_specs=[VMEM] * 7 + [ANY] * 4,
        out_specs=[VMEM] * 3 + [ANY],
        scratch_shapes=[
            *[pltpu.VMEM(lows[0].shape, bf16)] * 6,
            pltpu.VMEM((channels, channels), f32),
            pltpu.VMEM((planes, block, 2 * head), bf16),
            pltpu.VMEM((planes - 1, block, 2 * head), bf16),
            pltpu.VMEM((planes - 1, 2, rows_small, lanes), f32),
            pltpu.VMEM((2, rows_small, lanes), f32),
            pltpu.VMEM((rows_small, lanes), f32),
            pltpu.VMEM((planes, 8, lanes), f32),
            pltpu.VMEM((planes - 1, 8, lanes), f32),
            pltpu.VMEM((8, lanes), f32),
            pltpu.VMEM((7, 8, lanes), f32),
            pltpu.VMEM((8, lanes), f32),
            pltpu.SemaphoreType.DMA((count,)),
            pltpu.SemaphoreType.DMA((count,)),
            pltpu.SemaphoreType.DMA((4,)),
            pltpu.SemaphoreType.DMA((3,)),
            pltpu.SemaphoreType.DMA((3,)),
            *computed_scratch(rows, width, bf16),
        ],
        compiler_params=comm_params(collective_id, 60),
        cost_estimate=lasting(50),
        name="closing",
    )(in_low, whole_in, tokens, gain[None], rest, small, mlp_gain, *lows, piece)


def first_swap_kernel(planes, pairs, *refs):
    count = len(pairs)
    ins, refs = refs[:count], refs[count:]
    decay_gate, input_gate, out, line, gates, parts, send, recv, local, line_send, line_recv = refs
    me, z, p, c, x, y = place()
    far = [8 * lax.rem(z + d, planes) + lax.rem(me, 8) for d in range(1, planes)]
    head = decay_gate.shape[1]
    gates[:, :head] = decay_gate[...]
    gates[:, head:] = input_gate[...]
    to_chips_kernel(planes, pairs, *ins, parts)
    greet([*plane_neighbours()[0], *far])
    copies = swap_copies(parts, out, send, recv, local) + [
        remote(gates, line.at[z], line_send.at[d], line_recv.at[d], device) for d, device in enumerate(far)
    ]
    for copy in copies:
        copy.start()
    line[z] = gates[...]
    for copy in copies:
        copy.wait()


def first_swap(weights, pairs, width, gates, collective_id):
    planes = lax.axis_size("seq") // 8
    rows, head = gates[0].shape
    shape = (CHIPS, weights[0].shape[0], width)
    return pl.pallas_call(
        functools.partial(first_swap_kernel, planes, pairs),
        out_shape=[
            jax.ShapeDtypeStruct(shape, weights[0].dtype),
            jax.ShapeDtypeStruct((planes, rows, 2 * head), gates[0].dtype),
        ],
        in_specs=[VMEM] * (len(weights) + 2),
        out_specs=[ANY, VMEM],
        scratch_shapes=[
            pltpu.VMEM((rows, 2 * head), gates[0].dtype),
            pltpu.VMEM(shape, weights[0].dtype),
            pltpu.SemaphoreType.DMA((3,)),
            pltpu.SemaphoreType.DMA((3,)),
            pltpu.SemaphoreType.DMA,
            pltpu.SemaphoreType.DMA((planes - 1,)),
            pltpu.SemaphoreType.DMA((planes - 1,)),
        ],
        compiler_params=comm_params(collective_id, 60),
        name="first_swap",
    )(*weights, *gates)


def plane_swap_kernel(count, *refs):
    ins, outs = refs[:count], refs[count : 2 * count]
    send, recv, local = refs[2 * count :]
    me, z, p, c, x, y = place()
    x_dev, y_dev = me + 2 - 4 * x, me + 4 - 8 * y
    d_dev = y_dev + 2 - 4 * x
    p_x, p_y, p_d = p + 1 - 2 * x, p + 2 - 4 * y, 3 - p
    peers = ((x_dev, p_x), (y_dev, p_y), (d_dev, p_d))
    greet([device for device, unused in peers])
    copies = []
    for k in range(count):
        for j, (device, chip) in enumerate(peers):
            copies.append(remote(ins[k].at[chip], outs[k].at[p], send.at[k, j], recv.at[k, j], device))
        copies.append(pltpu.make_async_copy(ins[k].at[p], outs[k].at[p], local.at[k]))
    for copy in copies:
        copy.start()
    for copy in copies:
        copy.wait()


def plane_swap(arrays, collective_id):
    count = len(arrays)
    return pl.pallas_call(
        functools.partial(plane_swap_kernel, count),
        out_shape=[jax.ShapeDtypeStruct(a.shape, a.dtype) for a in arrays],
        in_specs=[ANY] * count,
        out_specs=[ANY] * count,
        scratch_shapes=[
            pltpu.SemaphoreType.DMA((count, 3)),
            pltpu.SemaphoreType.DMA((count, 3)),
            pltpu.SemaphoreType.DMA((count,)),
        ],
        compiler_params=comm_params(collective_id, 60),
        cost_estimate=lasting(10),
        name="plane_swap",
    )(*arrays)


def swap_copies(source, target, send, recv, local):
    devices, chips = plane_neighbours()
    p = place()[2]
    return [
        *[remote(source.at[chips[j]], target.at[p], send.at[j], recv.at[j], devices[j]) for j in range(3)],
        pltpu.make_async_copy(source.at[p], target.at[p], local),
    ]


def opening_kernel(
    planes,
    pairs,
    small,
    gates,
    tokens,
    mlp_gate,
    mlp_up,
    gathered,
    decay_blocks,
    input_blocks,
    second_piece,
    whole,
    swapped,
    piece,
    gates_all,
    gain,
    normed,
    *sems,
):
    send, recv, gate_send, gate_recv, swap_send, swap_recv, swap_local, gather_send, gather_recv, gather_local = sems
    me, z, p, c, x, y = place()
    r = lax.rem(me, 8)
    near = [me - r + lax.rem(r + d, 8) for d in range(1, 8)]
    far = [8 * lax.rem(z + d, planes) + r for d in range(1, planes)]
    greet(near + far)
    lines = [
        remote(small, gathered.at[r, z], send.at[d], recv.at[d], device) for d, device in enumerate(far)
    ]
    gate_swap = remote(gates, gates_all.at[c], gate_send, gate_recv, me + 1 - 2 * c)
    for copy in lines + [gate_swap]:
        copy.start()
    gathered[r, z] = small[...]
    gates_all[c] = gates[...]
    to_chips_kernel(planes, pairs, mlp_gate, mlp_up, piece, second_piece)
    swaps = swap_copies(piece, swapped, swap_send, swap_recv, swap_local)
    for copy in swaps:
        copy.start()
    for copy in lines:
        copy.wait()
    spreads = [
        remote(gathered.at[r], gathered.at[r], send.at[planes + d], recv.at[planes + d], device)
        for d, device in enumerate(near)
    ]
    for copy in spreads:
        copy.start()
    for copy in spreads:
        copy.wait()
    rows, width = tokens.shape
    step = width // (8 * planes)
    for j in range(planes):
        for q in range(CHIPS):
            for e in range(2):
                start = ((e * planes + j) * CHIPS + q) * step
                gain[0:1, start : start + step] = gathered[2 * q + e, j, 0:1, 0:step]

    @pl.loop(0, rows // 16)
    def norm_rows(i):
        at = sixteen(i)
        values = tokens[at, :].astype(jnp.float32)
        inverse = lax.rsqrt(jnp.mean(values * values, axis=-1, keepdims=True) + epsilon)
        normed[at, :] = (values * inverse * gain[0:1, :]).astype(jnp.bfloat16)

    begin, forward, end = gather_steps(normed, whole, gather_send, gather_recv, gather_local, 0)
    begin()
    gate_swap.wait()
    block = gates.shape[1]
    for k, target in enumerate((decay_blocks, input_blocks)):
        target[...] = jnp.zeros_like(target)
        for e in range(2):
            for j in range(planes):
                for h in range(2):
                    row, column = (e * planes + j) * block, (h * planes + j) * block
                    target[row : row + block, column : column + block] = gates_all[
                        e, j, :, (2 * k + h) * block : (2 * k + h + 1) * block
                    ]
    forward()
    end()
    for copy in swaps:
        copy.wait()


def opening(small, gates, tokens, mlp_gate, mlp_up, pairs, collective_id):
    planes = lax.axis_size("seq") // 8
    rows, width = tokens.shape
    channels = 2 * planes * gates.shape[1]
    piece = (CHIPS, mlp_gate.shape[0], mlp_gate.shape[1] // CHIPS)
    return pl.pallas_call(
        functools.partial(opening_kernel, planes, pairs),
        out_shape=[
            jax.ShapeDtypeStruct((8, planes) + small.shape, small.dtype),
            jax.ShapeDtypeStruct((channels, channels), gates.dtype),
            jax.ShapeDtypeStruct((channels, channels), gates.dtype),
            jax.ShapeDtypeStruct(piece, mlp_gate.dtype),
            jax.ShapeDtypeStruct((CHIPS, rows, width), jnp.bfloat16),
            jax.ShapeDtypeStruct(piece, mlp_gate.dtype),
        ],
        in_specs=[VMEM] * 5,
        out_specs=[VMEM] * 4 + [ANY, ANY],
        scratch_shapes=[
            pltpu.VMEM(piece, mlp_gate.dtype),
            pltpu.VMEM((2,) + gates.shape, gates.dtype),
            pltpu.VMEM((8, width), jnp.float32),
            pltpu.VMEM((rows, width), jnp.bfloat16),
            pltpu.SemaphoreType.DMA((planes + 7,)),
            pltpu.SemaphoreType.DMA((planes + 7,)),
            pltpu.SemaphoreType.DMA,
            pltpu.SemaphoreType.DMA,
            pltpu.SemaphoreType.DMA((3,)),
            pltpu.SemaphoreType.DMA((3,)),
            pltpu.SemaphoreType.DMA,
            pltpu.SemaphoreType.DMA((4,)),
            pltpu.SemaphoreType.DMA((4,)),
            pltpu.SemaphoreType.DMA,
        ],
        compiler_params=comm_params(collective_id, 60),
        cost_estimate=lasting(65),
        name="opening",
    )(small, gates, tokens, mlp_gate, mlp_up)


def column_peers(planes, z, p, c):
    count = 2 * planes
    q = 2 * z + c
    peers = []
    for d in range(1, count):
        other = lax.rem(q + d, count)
        peers.append(8 * lax.div(other, 2) + 2 * p + lax.rem(other, 2))
    return q, peers


def carry_in(planes, reverse, z, c, q, peers, everyone, before, entering, send, recv):
    own = everyone.at[q]
    copies = [remote(own, own, send.at[d], recv.at[d], device) for d, device in enumerate(peers)]
    for copy in copies:
        copy.start()
    for copy in copies:
        copy.wait()
    carried = jnp.zeros((1, everyone.shape[2]), jnp.float32)
    order = [(k, j, e) for k in range(planes) for j in range(CHIPS) for e in range(2)]
    for k, j, e in reversed(order) if reverse else order:
        before[8 * k + 2 * j + e : 8 * k + 2 * j + e + 1, :] = carried
        part = everyone.at[2 * k + e]
        carried = part[j : j + 1, :] * carried + part[CHIPS + j : CHIPS + j + 1, :]
    for j in range(CHIPS):
        entering[j : j + 1, :] = before[pl.ds(8 * z + 2 * j + c, 1), :]


def shift_down(earlier, values, step, row):
    return jnp.where(row >= step, pltpu.roll(values, step, 0), pltpu.roll(earlier, step, 0))


def shift_up(values, later, step, row):
    return jnp.where(row < 8 - step, pltpu.roll(values, 8 - step, 0), pltpu.roll(later, 8 - step, 0))


def tile_scan(a, b, row, reverse):
    for step in (1, 2, 4):
        if reverse:
            keep = row < 8 - step
            shifted_a, shifted_b = pltpu.roll(a, 8 - step, 0), pltpu.roll(b, 8 - step, 0)
        else:
            keep = row >= step
            shifted_a, shifted_b = pltpu.roll(a, step, 0), pltpu.roll(b, step, 0)
        b = a * jnp.where(keep, shifted_b, 0.0) + b
        a = a * jnp.where(keep, shifted_a, 1.0)
    return a, b


def sigmoid(values):
    return 1.0 / (1.0 + jnp.exp(-values))


def gate_terms(decay_pre, rate, flag):
    opened = sigmoid(decay_pre)
    log_decay = rate * opened
    decay = jnp.exp(log_decay)
    keep = 1.0 - flag
    squared = decay * decay
    return opened, decay * keep, keep, squared, jnp.tanh(-log_decay) * (1.0 + squared)


GELU_A, GELU_B = 0.7978845608028654, 0.044715


def eight(i):
    return pl.ds(pl.multiple_of(i * 8, 8), 8)


def recurrence_kernel(
    planes,
    gate_pre,
    conv_input,
    masks,
    vectors,
    decay_blocks,
    input_blocks,
    cot,
    piece,
    normed,
    conv_out,
    conv_low,
    decay_pre,
    input_pre,
    states,
    mixed,
    mixed_zero,
    mixed_one,
    entering,
    halo,
    cot_all,
    swapped,
    normed_other,
    cumulative,
    sibling_tails,
    below_tail,
    everyone,
    before,
    send,
    recv,
    local,
    swap_send,
    swap_recv,
    other_send,
    other_recv,
):
    me, z, p, c, x, y = place()
    rows, channels = conv_input.shape[1:]
    q, peers = column_peers(planes, z, p, c)
    greet(peers + [*plane_neighbours()[0]])
    cot_begin, cot_forward, cot_end = gather_steps(cot, cot_all, send, recv, local.at[0], 9)
    cot_begin()
    half = normed.shape[1] // 2
    other = remote(
        normed.at[:, pl.ds(pl.multiple_of((1 - c) * half, 128), half)],
        normed_other,
        other_send,
        other_recv,
        me + 1 - 2 * c,
    )
    other.start()
    swaps = swap_copies(piece, swapped, swap_send, swap_recv, local.at[1])
    f32 = jnp.float32
    tail = pl.ds(rows - 16, 16)
    to_sibling = remote(conv_input.at[:, tail], sibling_tails, send.at[7], recv.at[7], me + 1 - 2 * c)
    to_above = remote(conv_input.at[CHIPS - 1, tail], below_tail, send.at[8], recv.at[8], me + 7)
    from_below = remote(conv_input.at[CHIPS - 1, tail], below_tail, send.at[8], recv.at[8], me - 7)
    to_sibling.start()

    @pl.when((c == 1) & (z < planes - 1))
    def send_above():
        to_above.start()

    to_sibling.wait()

    @pl.when((c == 1) & (z < planes - 1))
    def sent_above():
        to_above.wait_send()

    @pl.when((c == 0) & (z > 0))
    def had_below():
        from_below.wait_recv()

    @pl.when(c == 1)
    def halo_one():
        for j in range(CHIPS):
            halo[j] = sibling_tails[j].astype(f32)[8:]

    @pl.when(c == 0)
    def halo_zero():
        for j in range(1, CHIPS):
            halo[j] = sibling_tails[j - 1].astype(f32)[8:]

        @pl.when(z > 0)
        def halo_below():
            halo[0] = below_tail[...].astype(f32)[8:]

        @pl.when(z == 0)
        def halo_none():
            halo[0] = jnp.zeros((8, channels), f32)

    row = lax.broadcasted_iota(jnp.int32, (8, channels), 0)

    @pl.loop(0, CHIPS)
    def block(j):
        def conv_tile(i, earlier):
            both = conv_input[j, sixteen(i), :].astype(f32)
            outs = []
            for h in range(2):
                now = both[8 * h : 8 * h + 8]
                keep = masks[j, eight(2 * i + h), :]
                out = vectors[CW : CW + 1, :] + vectors[0:1, :] * now
                for k in range(1, CW):
                    out = out + vectors[k : k + 1, :] * (
                        shift_down(earlier, now, k, row) * keep[:, k : k + 1]
                    )
                conv_out[j, eight(2 * i + h), :] = out
                outs.append(out)
                earlier = now
            conv_low[j, sixteen(i), :] = jnp.concatenate(outs, axis=0).astype(jnp.bfloat16)
            return earlier

        lax.fori_loop(0, rows // 16, conv_tile, halo[j], unroll=2)
        low = conv_low[j]
        decay_pre[j] = jnp.dot(low, decay_blocks[...], preferred_element_type=f32) + vectors[CW + 1 : CW + 2, :]
        input_pre[j] = jnp.dot(low, input_blocks[...], preferred_element_type=f32) + vectors[CW + 2 : CW + 3, :]

        def scan_tile(i, carry):
            at = eight(i)
            flag = masks[j, at, :][:, 0:1]
            opened, coef, keep, squared, gap = gate_terms(decay_pre[j, at, :], vectors[CW + 3 : CW + 4, :], flag)
            drive = (flag + keep * jnp.sqrt(gap)) * sigmoid(input_pre[j, at, :]) * conv_out[j, at, :]
            a, b = tile_scan(coef, drive, row, False)
            before_a, before_b = carry
            b = a * before_b + b
            a = a * before_a
            cumulative[j, at, :] = a
            states[j, at, :] = b
            return a[7:8], b[7:8]

        last_a, last_b = lax.fori_loop(
            0,
            rows // 8,
            scan_tile,
            (jnp.ones((1, channels), f32), jnp.zeros((1, channels), f32)),
            unroll=4,
        )
        everyone[q, pl.ds(j, 1), :] = last_a
        everyone[q, pl.ds(CHIPS + j, 1), :] = last_b

    cot_forward()
    for copy in swaps:
        copy.start()
    carry_in(planes, False, z, c, q, peers, everyone, before, entering, send, recv)

    @pl.loop(0, CHIPS)
    def finish(j):
        start = entering[pl.ds(j, 1), :]

        def state_tile(i, unused):
            at = sixteen(i)
            state = states[j, at, :] + cumulative[j, at, :] * start
            states[j, at, :] = state
            v = gate_pre[j, at, :]
            act = 0.5 * v * (1.0 + jnp.tanh(GELU_A * (v + GELU_B * (v * v * v))))
            product = (state * act).astype(jnp.bfloat16)
            mixed[j, at, :] = product
            mixed_zero[j, at, :] = product[:, : channels // 2]
            mixed_one[j, at, :] = product[:, channels // 2 :]
            return unused

        lax.fori_loop(0, rows // 16, state_tile, 0, unroll=2)

    cot_end()
    other.wait()
    for copy in swaps:
        copy.wait()


def recurrence(gate_pre, conv_input, masks, vectors, decay_blocks, input_blocks, cot, piece, normed, collective_id):
    planes = lax.axis_size("seq") // 8
    blocks, rows, channels = conv_input.shape
    f32, bf16 = jnp.float32, jnp.bfloat16
    cube = conv_input.shape

    def out(dtype, shape=cube):
        return jax.ShapeDtypeStruct(shape, dtype)

    return pl.pallas_call(
        functools.partial(recurrence_kernel, planes),
        out_shape=[
            out(f32),
            out(bf16),
            out(f32),
            out(f32),
            out(f32),
            out(bf16),
            *[out(bf16, (CHIPS, rows, channels // 2))] * 2,
            out(f32, (CHIPS, channels)),
            out(f32, (CHIPS, 8, channels)),
            out(cot.dtype, (CHIPS,) + cot.shape),
            out(piece.dtype, piece.shape),
            out(normed.dtype, (normed.shape[0], normed.shape[1] // 2)),
        ],
        in_specs=[VMEM] * 6 + [ANY] * 3,
        out_specs=[VMEM] * 10 + [ANY] * 3,
        scratch_shapes=[
            pltpu.VMEM(cube, f32),
            pltpu.VMEM((CHIPS, 16, channels), bf16),
            pltpu.VMEM((16, channels), bf16),
            pltpu.VMEM((2 * planes, 2 * CHIPS, channels), f32),
            pltpu.VMEM((8 * planes, channels), f32),
            pltpu.SemaphoreType.DMA((13,)),
            pltpu.SemaphoreType.DMA((13,)),
            pltpu.SemaphoreType.DMA((2,)),
            pltpu.SemaphoreType.DMA((3,)),
            pltpu.SemaphoreType.DMA((3,)),
            pltpu.SemaphoreType.DMA,
            pltpu.SemaphoreType.DMA,
        ],
        compiler_params=comm_params(collective_id, 60),
        cost_estimate=lasting(46),
        name="recurrence",
    )(gate_pre, conv_input, masks, vectors, decay_blocks, input_blocks, cot, piece, normed)


def recurrence_back_kernel(
    planes,
    grad_branch,
    rows_all,
    gate_pre,
    conv_input,
    conv_out,
    decay_pre,
    input_pre,
    states,
    entering,
    halo,
    masks,
    after_masks,
    vectors,
    decay_blocks,
    input_blocks,
    middle,
    down_parts,
    piece,
    in_low,
    decay_low,
    input_low,
    sums,
    block_out,
    swapped,
    grad_mixed,
    branch_here,
    out_here,
    cumulative,
    local,
    grad_conv,
    sibling_heads,
    above_head,
    ahead,
    everyone,
    before,
    leaving,
    send,
    recv,
    piece_sem,
    loads,
    *down_scratch,
):
    me, z, p, c, x, y = place()
    rows, channels = conv_input.shape[1:]
    q, peers = column_peers(planes, z, p, c)
    devices, chips = plane_neighbours()
    greet(peers + [*devices])
    down_begin, down_forward, down_end = sum_steps(down_parts, *down_scratch)
    down_begin()
    swaps = swap_copies(piece, swapped, send.at[pl.ds(9, 3)], recv.at[pl.ds(9, 3)], piece_sem.at[0])
    fetched = fetch_rows(rows_all, 0, 0, out_here, loads)
    fetched.append(pltpu.make_async_copy(grad_branch, branch_here, piece_sem.at[1]))
    for copy in fetched:
        copy.start()
    for copy in fetched:
        copy.wait()
    f32, bf16 = jnp.float32, jnp.bfloat16
    row = lax.broadcasted_iota(jnp.int32, (8, channels), 0)
    rate = vectors[CW + 3 : CW + 4, :]
    nothing = jnp.zeros((8, channels), f32)

    @pl.loop(0, CHIPS)
    def scan_block(j):
        grad_mixed[j] = lax.dot_general(
            branch_here[j], out_here[...], (((1,), (1,)), ((), ())), preferred_element_type=f32
        )

        def scan_tile(i, carry):
            i = rows // 16 - 1 - i
            at = sixteen(i)
            v = gate_pre[j, at, :]
            grad = grad_mixed[j, at, :]
            t = jnp.tanh(GELU_A * (v + GELU_B * (v * v * v)))
            act = 0.5 * v * (1.0 + t)
            slope = 0.5 * (1.0 + t) + 0.5 * v * (1.0 - t * t) * (GELU_A * (1.0 + 3.0 * GELU_B * (v * v)))
            in_low[j, at, 0:channels] = (grad * states[j, at, :] * slope).astype(bf16)
            drive = grad * act
            later_a, later_b, later_coef = carry
            for h in (1, 0):
                here = eight(2 * i + h)
                flag = masks[j, here, :][:, 0:1]
                coef = gate_terms(decay_pre[j, here, :], rate, flag)[1]
                shifted = jnp.where(row < 7, pltpu.roll(coef, 7, 0), later_coef)
                a, b = tile_scan(shifted, drive[8 * h : 8 * h + 8], row, True)
                b = a * later_b + b
                a = a * later_a
                cumulative[j, here, :] = a
                local[j, here, :] = b
                later_a, later_b, later_coef = a[0:1], b[0:1], coef[0:1]
            return later_a, later_b, later_coef

        ones = jnp.ones((1, channels), f32)
        first_a, first_b, first_coef = lax.fori_loop(
            0, rows // 16, scan_tile, (ones, jnp.zeros((1, channels), f32), ones), unroll=2
        )
        everyone[q, pl.ds(j, 1), :] = first_coef * first_a
        everyone[q, pl.ds(CHIPS + j, 1), :] = first_coef * first_b

    carry_in(planes, True, z, c, q, peers, everyone, before, leaving, send, recv)
    down_forward()
    for copy in swaps:
        copy.start()

    def terms_block(j, totals):
        behind_all = leaving[pl.ds(j, 1), :]

        def terms_tile(i, carry):
            previous, decay_sum, input_sum, param_sum = carry
            lows = []
            for h in range(2):
                at = eight(2 * i + h)
                adjoint = local[j, at, :] + cumulative[j, at, :] * behind_all
                state = states[j, at, :]
                earlier = jnp.where(row >= 1, pltpu.roll(state, 1, 0), previous)
                previous = state[7:8]
                flag = masks[j, at, :][:, 0:1]
                opened, coef, keep, squared, gap = gate_terms(decay_pre[j, at, :], rate, flag)
                passed = sigmoid(input_pre[j, at, :])
                conv = conv_out[j, at, :]
                inverse = lax.rsqrt(gap)
                scale = flag + keep * (gap * inverse)
                grad_log = adjoint * (earlier * coef - keep * passed * conv * squared * inverse)
                log_open = grad_log * opened
                decay_full = log_open * rate * (1.0 - opened)
                direct = adjoint * scale * passed
                input_full = direct * (1.0 - passed) * conv
                grad_conv[j, at, :] = direct
                lows.append((decay_full, input_full))
                decay_sum = decay_sum + decay_full
                input_sum = input_sum + input_full
                param_sum = param_sum + log_open
            decay_low[j, sixteen(i), :] = jnp.concatenate([low[0] for low in lows], axis=0).astype(bf16)
            input_low[j, sixteen(i), :] = jnp.concatenate([low[1] for low in lows], axis=0).astype(bf16)
            return previous, decay_sum, input_sum, param_sum

        totals = lax.fori_loop(
            0, rows // 16, terms_tile, (entering[pl.ds(j, 1), :], *totals), unroll=2
        )[1:]

        def dot_t(left, right):
            return lax.dot_general(left, right, (((1,), (1,)), ((), ())), preferred_element_type=f32)

        grad_conv[j] = (
            grad_conv[j] + dot_t(decay_low[j], decay_blocks[...]) + dot_t(input_low[j], input_blocks[...])
        )
        return totals

    decay_sum, input_sum, param_sum = lax.fori_loop(0, CHIPS, terms_block, (nothing,) * 3)

    to_sibling = remote(grad_conv.at[:, pl.ds(0, 8)], sibling_heads, send.at[7], recv.at[7], me + 1 - 2 * c)
    to_below = remote(grad_conv.at[0, pl.ds(0, 8)], above_head, send.at[8], recv.at[8], me - 7)
    from_above = remote(grad_conv.at[0, pl.ds(0, 8)], above_head, send.at[8], recv.at[8], me + 7)
    to_sibling.start()

    @pl.when((c == 0) & (z > 0))
    def send_below():
        to_below.start()

    to_sibling.wait()

    @pl.when((c == 0) & (z > 0))
    def sent_below():
        to_below.wait_send()

    @pl.when((c == 1) & (z < planes - 1))
    def had_above():
        from_above.wait_recv()

    @pl.when(c == 0)
    def ahead_zero():
        for j in range(CHIPS):
            ahead[j] = sibling_heads[j]

    @pl.when(c == 1)
    def ahead_one():
        for j in range(CHIPS - 1):
            ahead[j] = sibling_heads[j + 1]

        @pl.when(z < planes - 1)
        def ahead_above():
            ahead[CHIPS - 1] = above_head[...]

        @pl.when(z == planes - 1)
        def ahead_none():
            ahead[CHIPS - 1] = nothing

    def conv_block(j, totals):
        def conv_pair(i, now, later, keep, later_keep, outs, earlier, given, totals):
            out = vectors[0:1, :] * now
            new_totals = [totals[0] + now * given]
            for k in range(1, CW):
                masked = now * keep[:, k : k + 1]
                out = out + vectors[k : k + 1, :] * shift_up(
                    masked, later * later_keep[:, k : k + 1], k, row
                )
                new_totals.append(totals[k] + masked * shift_down(earlier, given, k, row))
            new_totals.append(totals[CW] + now)
            outs.append(out)
            return tuple(new_totals)

        def conv_tile(i, carry, last):
            earlier, totals = carry
            inputs = conv_input[j, sixteen(i), :].astype(f32)
            first, second = grad_conv[j, eight(2 * i), :], grad_conv[j, eight(2 * i + 1), :]
            first_keep, second_keep = masks[j, eight(2 * i), :], masks[j, eight(2 * i + 1), :]
            if last:
                third, third_keep = ahead[j], after_masks[j]
            else:
                third, third_keep = grad_conv[j, eight(2 * i + 2), :], masks[j, eight(2 * i + 2), :]
            outs = []
            totals = conv_pair(i, first, second, first_keep, second_keep, outs, earlier, inputs[:8], totals)
            totals = conv_pair(i, second, third, second_keep, third_keep, outs, inputs[:8], inputs[8:], totals)
            in_low[j, sixteen(i), channels : 2 * channels] = jnp.concatenate(outs, axis=0).astype(bf16)
            return inputs[8:], totals

        carry = lax.fori_loop(
            0, rows // 16 - 1, lambda i, carry: conv_tile(i, carry, False), (halo[j], totals)
        )
        return conv_tile(rows // 16 - 1, carry, True)[1]

    totals = lax.fori_loop(0, CHIPS, conv_block, (nothing,) * (CW + 1))
    for k, total in enumerate((*totals, decay_sum, input_sum, param_sum)):
        sums[k : k + 1, :] = jnp.sum(total, axis=0, keepdims=True)
    down_end()
    own, from_x, from_y = down_scratch[:3]

    @pl.loop(0, own.shape[0] // 16)
    def sum_rows(i):
        at = sixteen(i)
        block_out[at, :] = middle[at, :] + (
            own[at, :].astype(f32) + from_x[at, :].astype(f32) + from_y[at, :].astype(f32)
        )

    for copy in swaps:
        copy.wait()


def recurrence_back(
    grad_branch,
    rows_all,
    gate_pre,
    conv_input,
    conv_out,
    decay_pre,
    input_pre,
    states,
    entering,
    halo,
    masks,
    after_masks,
    vectors,
    decay_blocks,
    input_blocks,
    middle,
    down_parts,
    piece,
    collective_id,
):
    planes = lax.axis_size("seq") // 8
    cube = conv_input.shape
    blocks, rows, channels = cube
    f32, bf16 = jnp.float32, jnp.bfloat16
    return pl.pallas_call(
        functools.partial(recurrence_back_kernel, planes),
        out_shape=[
            jax.ShapeDtypeStruct((CHIPS, rows, 2 * channels), bf16),
            jax.ShapeDtypeStruct(cube, bf16),
            jax.ShapeDtypeStruct(cube, bf16),
            jax.ShapeDtypeStruct((CW + 4, channels), f32),
            jax.ShapeDtypeStruct(down_parts.shape[1:], f32),
            jax.ShapeDtypeStruct(piece.shape, bf16),
        ],
        in_specs=[ANY] * 2 + [VMEM] * 14 + [ANY] * 2,
        out_specs=[VMEM] * 5 + [ANY],
        scratch_shapes=[
            pltpu.VMEM(cube, f32),
            pltpu.VMEM(grad_branch.shape, bf16),
            pltpu.VMEM((channels, grad_branch.shape[2]), bf16),
            pltpu.VMEM(cube, f32),
            pltpu.VMEM(cube, f32),
            pltpu.VMEM(cube, f32),
            pltpu.VMEM((CHIPS, 8, channels), f32),
            pltpu.VMEM((8, channels), f32),
            pltpu.VMEM((CHIPS, 8, channels), f32),
            pltpu.VMEM((2 * planes, 2 * CHIPS, channels), f32),
            pltpu.VMEM((8 * planes, channels), f32),
            pltpu.VMEM((CHIPS, channels), f32),
            pltpu.SemaphoreType.DMA((12,)),
            pltpu.SemaphoreType.DMA((12,)),
            pltpu.SemaphoreType.DMA((2,)),
            pltpu.SemaphoreType.DMA((rows_all.shape[0],)),
            *sum_scratch(*down_parts.shape[1:], bf16),
        ],
        compiler_params=comm_params(collective_id, 60),
        cost_estimate=lasting(58),
        name="recurrence_back",
    )(
        grad_branch,
        rows_all,
        gate_pre,
        conv_input,
        conv_out,
        decay_pre,
        input_pre,
        states,
        entering,
        halo,
        masks,
        after_masks,
        vectors,
        decay_blocks,
        input_blocks,
        middle,
        down_parts,
        piece,
    )


def input_grads_kernel(
    normed, normed_other, low, grad, here, there, low_here, low_there, kept, send, recv, loads
):
    me, z, p, c, x, y = place()
    sibling = me + 1 - 2 * c
    greet((sibling,))
    swap = remote(low, low_there, send, recv, sibling)
    swap.start()
    half, columns = grad.shape
    fetched = [
        pltpu.make_async_copy(source, target, loads.at[k])
        for k, (source, target) in enumerate(
            (
                (normed.at[:, pl.ds(pl.multiple_of(c * half, 128), half)], here),
                (low, low_here),
                (normed_other, there),
            )
        )
    ]
    for copy in fetched:
        copy.start()
    for copy in fetched[:2]:
        copy.wait()
    block, tile = 512, 256

    def products(left, right, keep):
        @pl.loop(0, half // block)
        def product_block(m):
            at = pl.ds(pl.multiple_of(m * block, block), block)

            @pl.loop(0, columns // tile)
            def product_tile(k):
                across = pl.ds(pl.multiple_of(k * tile, tile), tile)
                keep(
                    at,
                    across,
                    lax.dot_general(
                        left[:, at], right[:, across], (((0,), (0,)), ((), ())), preferred_element_type=jnp.float32
                    ),
                )

    def keep_first(at, across, values):
        kept[at, across] = values

    def keep_sum(at, across, values):
        grad[at, across] = (kept[at, across] + values).astype(grad.dtype)

    products(here, low_here, keep_first)
    fetched[2].wait()
    swap.wait()
    products(there, low_there, keep_sum)


def input_grads(normed, normed_other, low, collective_id):
    tokens, width = normed.shape
    columns = low.shape[1]
    bf16 = low.dtype
    return pl.pallas_call(
        input_grads_kernel,
        out_shape=jax.ShapeDtypeStruct((width // 2, columns), bf16),
        in_specs=[ANY] * 3,
        out_specs=VMEM,
        scratch_shapes=[
            pltpu.VMEM((tokens, width // 2), bf16),
            pltpu.VMEM((tokens, width // 2), bf16),
            pltpu.VMEM((tokens, columns), bf16),
            pltpu.VMEM((tokens, columns), bf16),
            pltpu.VMEM((width // 2, columns), jnp.float32),
            pltpu.SemaphoreType.DMA,
            pltpu.SemaphoreType.DMA,
            pltpu.SemaphoreType.DMA((3,)),
        ],
        compiler_params=comm_params(collective_id, 60),
        name="input_grads",
    )(normed, normed_other, low)


def regrouped_kernel(back, devices, places, *refs):
    count = 1 + max(place[0] for place in places)
    for source, first, rows, target, row in places:
        source, target = refs[source], refs[count + target]
        step = source.shape[1] // devices
        for k in range(devices // 2):
            for e in range(2):
                split, joined = (2 * k + e) * step, (devices // 2 * e + k) * step
                start, end = (joined, split) if back else (split, joined)
                target[row : row + rows, end : end + step] = source[
                    first : first + rows, start : start + step
                ].astype(target.dtype)


def regrouped_columns(arrays, places, dtypes, back, vmem_mib):
    devices = lax.axis_size("seq")
    sizes = [max(row + rows for unused, unused, rows, m, row in places if m == k) for k in range(len(dtypes))]
    return pl.pallas_call(
        functools.partial(regrouped_kernel, back, devices, places),
        out_shape=[jax.ShapeDtypeStruct((r, arrays[0].shape[1]), dtype) for r, dtype in zip(sizes, dtypes)],
        in_specs=[VMEM] * len(arrays),
        out_specs=[VMEM] * len(dtypes),
        compiler_params=pltpu.CompilerParams(vmem_limit_bytes=vmem_mib * 2**20),
        name="regrouped_columns",
    )(*arrays)


def to_chips_kernel(planes, pairs, *refs):
    ins, outs = refs[: len(pairs)], refs[len(pairs) :]
    for source, targets in zip(ins, pairs):
        width = source.shape[1] // (planes * 8)
        for z in range(planes):
            for p in range(CHIPS):
                for c in range(2):
                    k, at = targets[c]
                    start = ((z * CHIPS + p) * 2 + c) * width
                    outs[k][p, :, at + z * width : at + (z + 1) * width] = source[:, start : start + width]


def from_chips_kernel(planes, pairs, *refs):
    outs, ins = refs[-len(pairs) :], refs[: -len(pairs)]
    for target, sources in zip(outs, pairs):
        width = target.shape[1] // (planes * 8)
        for z in range(planes):
            for p in range(CHIPS):
                for c in range(2):
                    k, at = sources[c]
                    start = ((z * CHIPS + p) * 2 + c) * width
                    target[:, start : start + width] = ins[k][
                        p, :, at + z * width : at + (z + 1) * width
                    ].astype(jnp.float32)


def from_chips(parts, pairs, widths):
    planes = lax.axis_size("seq") // 8
    return pl.pallas_call(
        functools.partial(from_chips_kernel, planes, pairs),
        out_shape=[jax.ShapeDtypeStruct((parts[0].shape[1], width), jnp.float32) for width in widths],
        in_specs=[VMEM] * len(parts),
        out_specs=[VMEM] * len(widths),
        compiler_params=pltpu.CompilerParams(vmem_limit_bytes=32 * 2**20),
        name="from_chips",
    )(*parts)


def regrouped(values, axis, n):
    shape = values.shape
    split = shape[:axis] + (n // 2, 2, shape[axis] // n) + shape[axis + 1 :]
    return jnp.moveaxis(values.reshape(split), axis + 1, axis).reshape(shape)


def behind(value, *earlier):
    return lax.optimization_barrier((value, *earlier))[0]


def plane_body(
    tokens,
    starts,
    cotangent,
    norm_gain,
    gate_branch,
    input_branch,
    conv_weight,
    conv_bias,
    decay_gate,
    decay_bias,
    input_gate,
    input_bias,
    decay_param,
    out_proj,
    mlp_gain,
    mlp_gate,
    mlp_up,
    mlp_down,
):
    f32, bf16 = jnp.float32, jnp.bfloat16
    n = lax.axis_size("seq")
    planes = n // 8
    me, z, p, c, x, y = place()
    groups = column_groups(n)
    rows, width = tokens.shape
    rows_d, lru_width = gate_branch.shape
    head = decay_gate.shape[1]
    rows_r, rows_f = out_proj.shape[0], mlp_down.shape[0]
    channels = lru_width // CHIPS
    units = mlp_gate.shape[1] // CHIPS
    half_units = units // 2

    def column_gather(block):
        return lax.all_gather(block, "seq", axis=0, tiled=True, axis_index_groups=groups)

    def line_sum(parts):
        return lax.psum_scatter(
            parts, "seq", scatter_dimension=0, tiled=True, axis_index_groups=line_groups(n)
        )

    def product(left, right):
        return jnp.dot(left, right, preferred_element_type=f32)

    def product_t(left, right):
        return jnp.einsum("tk,nk->tn", left, right, preferred_element_type=f32)

    def weight_grad(left, right):
        return jnp.einsum("ta,tb->ab", left, right, preferred_element_type=f32)

    lanes = 128

    def row(values):
        return jnp.pad(values.astype(f32), (0, lanes - values.shape[0]))[None]

    small = jnp.concatenate(
        [
            row(norm_gain),
            row(mlp_gain),
            starts.astype(f32).reshape(rows // lanes, lanes),
            *[row(conv_weight[k]) for k in range(CW)],
            row(conv_bias),
            row(decay_bias),
            row(input_bias),
            row(decay_param),
            jnp.zeros((4, lanes), f32),
        ],
        axis=0,
    )
    half = channels // 2
    in_pairs = (((0, 0), (0, half)), ((0, channels), (0, channels + half)))
    swapped_in, gates = first_swap(
        [gate_branch, input_branch], in_pairs, 2 * channels, [decay_gate, input_gate], 2
    )
    whole_in = column_gather(swapped_in.reshape(CHIPS * rows_d, 2 * channels))
    tokens, cot, row_shards = regrouped_columns(
        [tokens, cotangent, out_proj, mlp_down],
        [(0, 0, rows, 0, 0), (1, 0, rows, 1, 0), (2, 0, rows_r, 2, 0), (3, 0, rows_f, 2, rows_r)],
        [bf16] * 3,
        False,
        60,
    )
    mlp_pairs = (((0, 0), (1, 0)), ((0, half_units), (1, half_units)))
    small, decay_blocks, input_blocks, second_part, normed_all, first_piece = opening(
        behind(small, swapped_in), gates, tokens, mlp_gate, mlp_up, mlp_pairs, 1
    )
    normed_all = normed_all.reshape(CHIPS * rows, width)
    small = small.transpose(1, 0, 2, 3)
    flags = 2 + rows // lanes
    gain_one = regrouped(small[:, :, 0, :rows_d].reshape(width), 0, n)
    gain_two = regrouped(small[:, :, 1, :rows_d].reshape(width), 0, n)
    all_flags = small[:, :, 2:flags].reshape(n * rows)
    vectors = lax.dynamic_slice_in_dim(
        small.reshape(planes, CHIPS, 2, 16, lanes), p, 1, axis=1
    )[:, 0, :, flags : flags + CW + 4, :rows_r]
    vectors = vectors.transpose(2, 1, 0, 3).reshape(CW + 4, channels)
    param = vectors[CW + 3]
    vectors = vectors.at[CW + 3].set(-rate_scale * jax.nn.softplus(param))

    running = jnp.ones((n * rows,), f32)
    masks_all = [running]
    for offset in range(1, CW):
        earlier = jnp.concatenate([jnp.zeros((offset - 1,), f32), all_flags[: n * rows - (offset - 1)]])
        running = running * (1.0 - earlier)
        masks_all.append(running)
    masks_all = jnp.stack(masks_all).reshape(CW, planes, CHIPS, 2, rows)

    def own_blocks(values):
        return lax.dynamic_slice(
            values,
            (0, z, 0, c, 0),
            (values.shape[0], 1, CHIPS, 1, values.shape[4]),
        )[:, 0, :, 0]

    after_masks = masks_all[..., :8].reshape(CW, n, 8)
    after_masks = jnp.concatenate([after_masks[:, 1:], jnp.zeros((CW, 1, 8), f32)], axis=1)
    after_masks = own_blocks(after_masks.reshape(CW, planes, CHIPS, 2, 8)).transpose(1, 2, 0)
    masks_all = jnp.concatenate([all_flags.reshape(1, planes, CHIPS, 2, rows), masks_all[1:]], axis=0)
    masks = own_blocks(masks_all).transpose(1, 2, 0)

    rows_all = column_gather(behind(row_shards, swapped_in)).reshape(2 * planes, rows_r + rows_f, width)

    gate_pre = product(normed_all, whole_in[:, :channels])
    cube = (CHIPS, rows, channels)
    gate_pre = gate_pre.reshape(cube)
    conv_input = product(normed_all, whole_in[:, channels:]).astype(bf16).reshape(cube)
    conv_out, conv_low, decay_pre, input_pre, states, mixed, *mixeds, entering, halo, cot_all, second_piece, normed_other = recurrence(
        gate_pre,
        conv_input,
        masks,
        vectors,
        decay_blocks,
        input_blocks,
        cot,
        second_part,
        normed_all,
        6,
    )
    whole_mlp = [
        column_gather(part.reshape(CHIPS * rows_d, 2 * half_units)) for part in (first_piece, second_piece)
    ]
    cot_all = cot_all.reshape(CHIPS * rows, width)
    middle, two_all, cot_other = middle_of(mixed, rows_all, tokens, gain_two, cot_all, 7)
    mixeds = [part.reshape(CHIPS * rows, channels // 2) for part in mixeds]
    two_all = two_all.reshape(CHIPS * rows, width)

    hidden_zero, first_grad, first_parts = feed_forward(0, two_all, cot_all, whole_mlp[0], rows_all, (), 8)
    hidden_one, second_grad, two_parts = feed_forward(
        1, two_all, cot_all, whole_mlp[1], rows_all, (first_parts,), 14
    )
    piece_grads = [line_sum(first_grad), line_sum(second_grad)]
    grad_middle, grad_mlp_gain, grad_branch, row_grads, down_parts = grads_of_middle(
        two_parts.reshape(CHIPS, rows, width),
        middle,
        cot,
        gain_two,
        (hidden_zero, hidden_one),
        rows_all,
        (cot_all, cot_other),
        mixeds,
        9,
    )
    grad_rows = line_sum(row_grads.reshape(planes * (rows_r + rows_f), width))

    in_low, grad_decay_low, grad_input_low, sums, block_out, first_swapped = recurrence_back(
        grad_branch,
        rows_all,
        gate_pre,
        conv_input,
        conv_out,
        decay_pre,
        input_pre,
        states,
        entering,
        halo,
        masks,
        after_masks,
        vectors,
        decay_blocks,
        input_blocks,
        middle,
        down_parts,
        piece_grads[0].reshape(CHIPS, rows_d, 2 * half_units),
        12,
    )
    sums = sums.at[CW + 3].multiply(-rate_scale * jax.nn.sigmoid(param))
    low_cube = in_low
    in_low = low_cube.reshape(CHIPS * rows, 2 * channels)
    flat = (CHIPS * rows, channels)
    conv_low, grad_decay_low, grad_input_low = (
        a.reshape(flat) for a in (conv_low, grad_decay_low, grad_input_low)
    )

    in_total = input_grads(normed_all, normed_other, in_low, 15)
    in_grads = line_sum(in_total)
    low_cube = behind(low_cube, in_total)
    vector_parts = sums.reshape(CW + 4, 2, planes, rows_r).transpose(2, 1, 0, 3)
    vector_parts = jnp.pad(vector_parts, ((0, 0), (0, 0), (0, 0), (0, lanes - rows_r)))
    grad_tokens, small_grads, gate_grads, second_swapped = closing(
        low_cube,
        whole_in,
        tokens,
        gain_one,
        grad_middle,
        vector_parts,
        grad_mlp_gain,
        (conv_low, grad_decay_low, grad_input_low),
        piece_grads[1].reshape(CHIPS, rows_d, 2 * half_units),
        head,
        13,
    )
    grad_mlp_gate, grad_mlp_up = from_chips(
        [first_swapped, second_swapped], mlp_pairs, [mlp_gate.shape[1]] * 2
    )
    block_out, grad_out_proj, grad_mlp_down = regrouped_columns(
        [block_out, behind(grad_rows, grad_tokens)],
        [(0, 0, rows, 0, 0), (1, 0, rows_r, 1, 0), (1, rows_r, rows_f, 2, 0)],
        [bf16, f32, f32],
        True,
        24,
    )
    in_grads = behind(in_grads, grad_out_proj)
    in_out = plane_swap([in_grads.reshape(CHIPS, rows_d, 2 * channels)], 16)
    grad_gate_branch, grad_input_branch = from_chips(in_out, in_pairs, [lru_width] * 2)
    vector_grads = small_grads[: CW + 4, :rows_r]
    return (
        block_out,
        grad_tokens,
        small_grads[CW + 4, :rows_d],
        grad_gate_branch,
        grad_input_branch,
        vector_grads[:CW],
        vector_grads[CW],
        gate_grads[:, :head],
        vector_grads[CW + 1],
        gate_grads[:, head:],
        vector_grads[CW + 2],
        vector_grads[CW + 3],
        grad_out_proj,
        small_grads[CW + 4, rows_d : 2 * rows_d],
        grad_mlp_gate,
        grad_mlp_up,
        grad_mlp_down,
    )


def solution(mesh):
    in_specs = (
        P("seq", None),
        P("seq"),
        P("seq", None),
        P("seq"),
        P("seq", None),
        P("seq", None),
        P(None, "seq"),
        P("seq"),
        P("seq", None),
        P("seq"),
        P("seq", None),
        P("seq"),
        P("seq"),
        P("seq", None),
        P("seq"),
        P("seq", None),
        P("seq", None),
        P("seq", None),
    )
    out_specs = (
        P("seq", None),
        P("seq", None),
        P("seq"),
        P("seq", None),
        P("seq", None),
        P(None, "seq"),
        P("seq"),
        P("seq", None),
        P("seq"),
        P("seq", None),
        P("seq"),
        P("seq"),
        P("seq", None),
        P("seq"),
        P("seq", None),
        P("seq", None),
        P("seq", None),
    )
    body = plane_body if mesh.shape["seq"] == 2 * H else token_split_body
    return jax.shard_map(body, mesh=mesh, in_specs=in_specs, out_specs=out_specs, check_vma=False)
```

```python
import functools

import jax
import jax.numpy as jnp
from jax import lax
from jax.experimental import pallas as pl
from jax.experimental.pallas import tpu as pltpu
from jax.sharding import PartitionSpec as P

H = 16
CW = 4


epsilon = 1e-06
rate_scale = 8.0


def passed_along(block, axis, distance):
    devices = range(lax.axis_size(axis))
    route = [(i - distance, i) for i in devices if i - distance in devices]
    return lax.ppermute(block, axis, route)


def prefix(value, axis, combine, identity, reverse):
    peers, place = (lax.axis_size(axis), lax.axis_index(axis))
    everything = jax.tree.map(lambda part: lax.all_gather(part, axis), value)
    start = jax.tree.map(
        lambda part, zero: jnp.broadcast_to(jnp.asarray(zero, part.dtype), part.shape),
        value,
        identity,
    )

    def hop(k, before):
        at = peers - 1 - k if reverse else k
        reached = at > place if reverse else at < place
        new = combine(before, jax.tree.map(lambda part: part[at], everything))
        return jax.tree.map(lambda a, b: jnp.where(reached, a, b), new, before)

    return lax.fori_loop(0, peers, hop, start)


def gelu_tanh(values):
    return jax.nn.gelu(values, approximate=True)


def rms_norm(values, scales):
    return values * lax.rsqrt(jnp.mean(values * values, axis=-1, keepdims=True) + epsilon) * scales


def combine(earlier_part, later_part):
    return (earlier_part[0] * later_part[0], later_part[0] * earlier_part[1] + later_part[1])


def heads_product(values, weight):
    row_count, lru_width = values.shape
    shaped = values.reshape(row_count, H, lru_width // H)
    blocks = weight.reshape(H, lru_width // H, lru_width // H)
    return jnp.einsum("thi,hij->thj", shaped, blocks, preferred_element_type=jnp.float32).reshape(
        row_count, lru_width
    )


def heads_back(grads_low, weight):
    row_count, lru_width = grads_low.shape
    shaped = grads_low.reshape(row_count, H, lru_width // H)
    blocks = weight.reshape(H, lru_width // H, lru_width // H)
    return jnp.einsum("thj,hij->thi", shaped, blocks, preferred_element_type=jnp.float32).reshape(
        row_count, lru_width
    )


def heads_grad(values, grads_low):
    row_count, lru_width = values.shape
    left_side = values.reshape(row_count, H, lru_width // H)
    right_side = grads_low.reshape(row_count, H, lru_width // H)
    return jnp.einsum(
        "thi,thj->hij", left_side, right_side, preferred_element_type=jnp.float32
    ).reshape(lru_width, lru_width // H)


def lru_terms(decay_pre, input_pre, conv_out, decay_param, flag_rows):
    log_decay = -rate_scale * jax.nn.sigmoid(decay_pre) * jax.nn.softplus(decay_param)
    keep_rows = 1.0 - flag_rows[:, None]
    coefficient = jnp.exp(log_decay) * keep_rows
    scale_in = flag_rows[:, None] + keep_rows * jnp.sqrt(-jnp.expm1(2.0 * log_decay))
    drive_term = scale_in * jax.nn.sigmoid(input_pre) * conv_out
    return (coefficient, drive_term)


def build_masks(flag_rows):
    row_count = flag_rows.shape[0]
    running = jnp.ones((row_count,), jnp.float32)
    masks = [running]
    for offset in range(1, CW):
        earlier_flags = jnp.concatenate(
            [jnp.zeros((offset - 1,), jnp.float32), flag_rows[: row_count - (offset - 1)]]
        )
        running = running * (1.0 - earlier_flags)
        masks.append(running)
    return masks


def send_mask(flag_rows):
    tail_keep = 1.0 - flag_rows[flag_rows.shape[0] - (CW - 1) :]
    after_rows = jnp.cumprod(tail_keep[::-1])[::-1]
    return jnp.concatenate([after_rows[1:], jnp.ones((1,), jnp.float32)])


def conv_local(padded, weight, bias, masks):
    row_count = masks[0].shape[0]
    conv_total = bias + jnp.zeros((row_count, padded.shape[1]), jnp.float32)
    for offset in range(CW):
        lead = CW - 1 - offset
        conv_total = conv_total + weight[offset] * (
            padded[lead : lead + row_count] * masks[offset][:, None]
        )
    return conv_total


def mlp_act(gate_values, up_values):
    return gelu_tanh(gate_values) * up_values


def token_split_body(
    tokens,
    starts,
    cotangent,
    norm_gain,
    gate_branch,
    input_branch,
    conv_weight,
    conv_bias,
    decay_gate,
    decay_bias,
    input_gate,
    input_bias,
    decay_param,
    out_proj,
    mlp_gain,
    mlp_gate,
    mlp_up,
    mlp_down,
):
    (
        whole_norm_gain,
        whole_gate_branch,
        whole_input_branch,
        whole_conv_weight,
        whole_conv_bias,
        whole_decay_gate,
        whole_decay_bias,
        whole_input_gate,
        whole_input_bias,
        whole_decay_param,
        whole_out_proj,
    ) = (
        lax.all_gather(norm_gain, "seq", axis=0, tiled=True),
        lax.all_gather(gate_branch, "seq", axis=0, tiled=True),
        lax.all_gather(input_branch, "seq", axis=0, tiled=True),
        lax.all_gather(conv_weight, "seq", axis=1, tiled=True),
        lax.all_gather(conv_bias, "seq", axis=0, tiled=True),
        lax.all_gather(decay_gate, "seq", axis=0, tiled=True),
        lax.all_gather(decay_bias, "seq", axis=0, tiled=True),
        lax.all_gather(input_gate, "seq", axis=0, tiled=True),
        lax.all_gather(input_bias, "seq", axis=0, tiled=True),
        lax.all_gather(decay_param, "seq", axis=0, tiled=True),
        lax.all_gather(out_proj, "seq", axis=0, tiled=True),
    )
    flag_rows = starts.astype(jnp.float32)
    row_count = tokens.shape[0]
    values = tokens.astype(jnp.float32)
    normed = rms_norm(values, whole_norm_gain.astype(jnp.float32)).astype(jnp.bfloat16)
    gate_pre = jnp.dot(normed, whole_gate_branch, preferred_element_type=jnp.float32)
    gate_act = gelu_tanh(gate_pre)
    conv_input = jnp.dot(normed, whole_input_branch, preferred_element_type=jnp.float32).astype(
        jnp.bfloat16
    )
    lru_width = conv_input.shape[1]
    alive_rows = send_mask(flag_rows)
    masks = build_masks(flag_rows)
    outgoing = conv_input[row_count - (CW - 1) :] * alive_rows[:, None].astype(jnp.bfloat16)
    incoming = passed_along(outgoing, "seq", 1)
    padded = jnp.concatenate([incoming, conv_input], axis=0).astype(jnp.float32)
    conv_out = conv_local(
        padded, whole_conv_weight.astype(jnp.float32), whole_conv_bias.astype(jnp.float32), masks
    )
    conv_low = conv_out.astype(jnp.bfloat16)
    decay_pre = heads_product(conv_low, whole_decay_gate) + whole_decay_bias.astype(jnp.float32)
    input_pre = heads_product(conv_low, whole_input_gate) + whole_input_bias.astype(jnp.float32)
    param_full = whole_decay_param.astype(jnp.float32)
    coefficient, drive_term = lru_terms(decay_pre, input_pre, conv_out, param_full, flag_rows)
    cumulative, local_state = lax.associative_scan(combine, (coefficient, drive_term), axis=0)
    entering = prefix(
        (cumulative[-1], local_state[-1]),
        "seq",
        combine,
        (jnp.ones_like(cumulative[-1]), jnp.zeros_like(local_state[-1])),
        False,
    )
    incoming_state = entering[1]
    states = local_state + cumulative * incoming_state[None, :]
    mixed_rows = (states * gate_act).astype(jnp.bfloat16)
    middle = values + jnp.dot(mixed_rows, whole_out_proj, preferred_element_type=jnp.float32)
    whole_mlp_gain, whole_mlp_gate, whole_mlp_up, whole_mlp_down = (
        lax.all_gather(mlp_gain, "seq", axis=0, tiled=True),
        lax.all_gather(mlp_gate, "seq", axis=0, tiled=True),
        lax.all_gather(mlp_up, "seq", axis=0, tiled=True),
        lax.all_gather(mlp_down, "seq", axis=0, tiled=True),
    )
    gain_two = whole_mlp_gain.astype(jnp.float32)
    normed_two = rms_norm(middle, gain_two).astype(jnp.bfloat16)
    gate_mlp = jnp.dot(normed_two, whole_mlp_gate, preferred_element_type=jnp.float32)
    up_mlp = jnp.dot(normed_two, whole_mlp_up, preferred_element_type=jnp.float32)
    hidden = mlp_act(gate_mlp, up_mlp).astype(jnp.bfloat16)
    result = middle + jnp.dot(hidden, whole_mlp_down, preferred_element_type=jnp.float32)
    block_out = result.astype(jnp.bfloat16)
    back_mlp_gain, back_mlp_gate, back_mlp_up, back_mlp_down = (
        lax.all_gather(mlp_gain, "seq", axis=0, tiled=True),
        lax.all_gather(mlp_gate, "seq", axis=0, tiled=True),
        lax.all_gather(mlp_up, "seq", axis=0, tiled=True),
        lax.all_gather(mlp_down, "seq", axis=0, tiled=True),
    )
    grad_mlp_down = jnp.einsum("tf,td->fd", hidden, cotangent, preferred_element_type=jnp.float32)
    grad_hidden = jnp.einsum(
        "td,fd->tf", cotangent, back_mlp_down, preferred_element_type=jnp.float32
    )
    unused_act, pull_act = jax.vjp(mlp_act, gate_mlp, up_mlp)
    grad_gate_full, grad_up_full = pull_act(grad_hidden)
    grad_gate_low = grad_gate_full.astype(jnp.bfloat16)
    grad_up_low = grad_up_full.astype(jnp.bfloat16)
    grad_mlp_gate = jnp.einsum(
        "td,tf->df", normed_two, grad_gate_low, preferred_element_type=jnp.float32
    )
    grad_mlp_up = jnp.einsum(
        "td,tf->df", normed_two, grad_up_low, preferred_element_type=jnp.float32
    )
    grad_normed_two = jnp.einsum(
        "tf,df->td", grad_gate_low, back_mlp_gate, preferred_element_type=jnp.float32
    ) + jnp.einsum("tf,df->td", grad_up_low, back_mlp_up, preferred_element_type=jnp.float32)
    unused_norm, pull_norm = jax.vjp(rms_norm, middle, back_mlp_gain.astype(jnp.float32))
    grad_middle_norm, grad_mlp_gain = pull_norm(grad_normed_two)
    mlp_sums = (
        lax.psum_scatter(grad_mlp_gain, "seq", scatter_dimension=0, tiled=True),
        lax.psum_scatter(grad_mlp_gate, "seq", scatter_dimension=0, tiled=True),
        lax.psum_scatter(grad_mlp_up, "seq", scatter_dimension=0, tiled=True),
        lax.psum_scatter(grad_mlp_down, "seq", scatter_dimension=0, tiled=True),
    )
    grad_middle = cotangent.astype(jnp.float32) + grad_middle_norm
    grad_branch = grad_middle.astype(jnp.bfloat16)
    (
        back_norm_gain,
        back_gate_branch,
        back_input_branch,
        back_conv_weight,
        back_conv_bias,
        back_decay_gate,
        back_decay_bias,
        back_input_gate,
        back_input_bias,
        back_decay_param,
        back_out_proj,
    ) = (
        lax.all_gather(norm_gain, "seq", axis=0, tiled=True),
        lax.all_gather(gate_branch, "seq", axis=0, tiled=True),
        lax.all_gather(input_branch, "seq", axis=0, tiled=True),
        lax.all_gather(conv_weight, "seq", axis=1, tiled=True),
        lax.all_gather(conv_bias, "seq", axis=0, tiled=True),
        lax.all_gather(decay_gate, "seq", axis=0, tiled=True),
        lax.all_gather(decay_bias, "seq", axis=0, tiled=True),
        lax.all_gather(input_gate, "seq", axis=0, tiled=True),
        lax.all_gather(input_bias, "seq", axis=0, tiled=True),
        lax.all_gather(decay_param, "seq", axis=0, tiled=True),
        lax.all_gather(out_proj, "seq", axis=0, tiled=True),
    )
    grad_out_proj = jnp.einsum(
        "tr,td->rd", mixed_rows, grad_branch, preferred_element_type=jnp.float32
    )
    grad_mixed = jnp.einsum(
        "td,rd->tr", grad_branch, back_out_proj, preferred_element_type=jnp.float32
    )
    grad_states = grad_mixed * gate_act
    unused_gelu, pull_gelu = jax.vjp(gelu_tanh, gate_pre)
    grad_gate_pre = pull_gelu(grad_mixed * states)[0].astype(jnp.bfloat16)
    shifted_coef = jnp.concatenate([coefficient[1:], jnp.ones((1, lru_width), jnp.float32)], axis=0)
    back_cumulative, back_local = lax.associative_scan(
        combine, (shifted_coef[::-1], grad_states[::-1]), axis=0
    )
    back_cumulative = back_cumulative[::-1]
    back_local = back_local[::-1]
    leaving = prefix(
        (coefficient[0] * back_cumulative[0], coefficient[0] * back_local[0]),
        "seq",
        combine,
        (jnp.ones_like(back_local[0]), jnp.zeros_like(back_local[0])),
        True,
    )
    incoming_adjoint = leaving[1]
    adjoint = back_local + back_cumulative * incoming_adjoint[None, :]
    previous = jnp.concatenate([incoming_state[None, :], states[:-1]], axis=0)

    def terms_only(decay_values, input_values, conv_values, param_values):
        return lru_terms(decay_values, input_values, conv_values, param_values, flag_rows)

    unused_terms, pull_terms = jax.vjp(
        terms_only, decay_pre, input_pre, conv_out, back_decay_param.astype(jnp.float32)
    )
    grad_decay_full, grad_input_full, grad_conv_direct, grad_decay_param = pull_terms(
        (adjoint * previous, adjoint)
    )
    grad_decay_bias = jnp.sum(grad_decay_full, axis=0)
    grad_input_bias = jnp.sum(grad_input_full, axis=0)
    grad_decay_low = grad_decay_full.astype(jnp.bfloat16)
    grad_input_low = grad_input_full.astype(jnp.bfloat16)
    grad_decay_gate = heads_grad(conv_low, grad_decay_low)
    grad_input_gate = heads_grad(conv_low, grad_input_low)
    grad_conv_out = (
        grad_conv_direct
        + heads_back(grad_decay_low, back_decay_gate)
        + heads_back(grad_input_low, back_input_gate)
    )

    def conv_only(padded_values, weight_values, bias_values):
        return conv_local(padded_values, weight_values, bias_values, masks)

    unused_conv, pull_conv = jax.vjp(
        conv_only, padded, back_conv_weight.astype(jnp.float32), back_conv_bias.astype(jnp.float32)
    )
    grad_padded, grad_conv_weight, grad_conv_bias = pull_conv(grad_conv_out)
    returned_rows = passed_along(grad_padded[: CW - 1], "seq", -1)
    addition = jnp.concatenate(
        [
            jnp.zeros((row_count - (CW - 1), lru_width), jnp.float32),
            returned_rows * alive_rows[:, None],
        ],
        axis=0,
    )
    grad_conv_input = (grad_padded[CW - 1 :] + addition).astype(jnp.bfloat16)
    grad_input_branch = jnp.einsum(
        "td,tr->dr", normed, grad_conv_input, preferred_element_type=jnp.float32
    )
    grad_gate_branch = jnp.einsum(
        "td,tr->dr", normed, grad_gate_pre, preferred_element_type=jnp.float32
    )
    grad_normed = jnp.einsum(
        "tr,dr->td", grad_conv_input, back_input_branch, preferred_element_type=jnp.float32
    ) + jnp.einsum("tr,dr->td", grad_gate_pre, back_gate_branch, preferred_element_type=jnp.float32)
    unused_first, pull_first = jax.vjp(rms_norm, values, back_norm_gain.astype(jnp.float32))
    grad_values_norm, grad_norm_gain = pull_first(grad_normed)
    grad_tokens = grad_middle + grad_values_norm
    rec_sums = (
        lax.psum_scatter(grad_norm_gain, "seq", scatter_dimension=0, tiled=True),
        lax.psum_scatter(grad_gate_branch, "seq", scatter_dimension=0, tiled=True),
        lax.psum_scatter(grad_input_branch, "seq", scatter_dimension=0, tiled=True),
        lax.psum_scatter(grad_conv_weight, "seq", scatter_dimension=1, tiled=True),
        lax.psum_scatter(grad_conv_bias, "seq", scatter_dimension=0, tiled=True),
        lax.psum_scatter(grad_decay_gate, "seq", scatter_dimension=0, tiled=True),
        lax.psum_scatter(grad_decay_bias, "seq", scatter_dimension=0, tiled=True),
        lax.psum_scatter(grad_input_gate, "seq", scatter_dimension=0, tiled=True),
        lax.psum_scatter(grad_input_bias, "seq", scatter_dimension=0, tiled=True),
        lax.psum_scatter(grad_decay_param, "seq", scatter_dimension=0, tiled=True),
        lax.psum_scatter(grad_out_proj, "seq", scatter_dimension=0, tiled=True),
    )
    return (
        block_out,
        grad_tokens,
        rec_sums[0],
        rec_sums[1],
        rec_sums[2],
        rec_sums[3],
        rec_sums[4],
        rec_sums[5],
        rec_sums[6],
        rec_sums[7],
        rec_sums[8],
        rec_sums[9],
        rec_sums[10],
        mlp_sums[0],
        mlp_sums[1],
        mlp_sums[2],
        mlp_sums[3],
    )


CHIPS = 4
MESH = pl.DeviceIdType.MESH


def place():
    me = lax.axis_index("seq")
    core = lax.rem(me, 2)
    x = lax.rem(lax.div(me, 2), 2)
    y = lax.rem(lax.div(me, 4), 2)
    return me, lax.div(me, 8), 2 * y + x, core, x, y


def column_groups(n):
    return [[8 * z + 2 * p + c for c in range(2) for z in range(n // 8)] for p in range(CHIPS)]


def line_groups(n):
    return [[8 * z + r for z in range(n // 8)] for r in range(8)]


def greet(devices):
    barrier = pltpu.get_barrier_semaphore()
    for device in devices:
        pl.semaphore_signal(barrier, inc=1, device_id=(device,), device_id_type=MESH)
    pl.semaphore_wait(barrier, len(devices))


def remote(source, target, send_sem, recv_sem, device):
    return pltpu.make_async_remote_copy(
        src_ref=source,
        dst_ref=target,
        send_sem=send_sem,
        recv_sem=recv_sem,
        device_id=(device,),
        device_id_type=MESH,
    )


def comm_params(collective_id, vmem_mib=None):
    return pltpu.CompilerParams(
        collective_id=collective_id,
        has_side_effects=True,
        vmem_limit_bytes=None if vmem_mib is None else vmem_mib * 2**20,
    )


def lasting(microseconds):
    return pl.CostEstimate(
        flops=int(microseconds * 1e9), bytes_accessed=int(microseconds * 3e6), transcendentals=0
    )


ANY = pl.BlockSpec(memory_space=pl.ANY)
VMEM = pl.BlockSpec(memory_space=pltpu.VMEM)


def plane_neighbours():
    me, z, p, c, x, y = place()
    x_dev, y_dev = me + 2 - 4 * x, me + 4 - 8 * y
    return (x_dev, y_dev, y_dev + 2 - 4 * x), (p + 1 - 2 * x, p + 2 - 4 * y, 3 - p)


def gather_steps(source, whole, send, recv, local, first):
    me, z, p, c, x, y = place()
    (x_dev, y_dev, d_dev), (p_x, p_y, p_d) = plane_neighbours()
    half = source.shape[0] // 2

    def copy(k, source, target, device):
        return remote(source, target, send.at[first + k], recv.at[first + k], device)

    to_x, to_y = copy(0, source, whole.at[p], x_dev), copy(1, source, whole.at[p], y_dev)
    low, high = whole.at[p_x, pl.ds(0, half)], whole.at[p_y, pl.ds(half, half)]
    on_y, on_x = copy(2, low, low, y_dev), copy(3, high, high, x_dev)
    own = pltpu.make_async_copy(source, whole.at[p], local)

    def begin():
        to_x.start()
        to_y.start()
        own.start()

    def forward():
        to_x.wait_recv()
        on_y.start()
        to_y.wait_recv()
        on_x.start()

    def end():
        to_x.wait_send()
        to_y.wait_send()
        on_y.wait()
        on_x.wait()
        own.wait()

    return begin, forward, end


def sum_scratch(rows, columns, dtype):
    whole, part = pltpu.VMEM((rows, columns), dtype), pltpu.VMEM((rows // 2, columns), dtype)
    return [whole] * 3 + [part] * 4 + [pltpu.SemaphoreType.DMA((6,)), pltpu.SemaphoreType.DMA((6,)), pltpu.SemaphoreType.DMA((3,))]


def sum_steps(part, own, from_x, from_y, diag_x, diag_y, on_x, on_y, send, recv, local):
    me, z, p, c, x, y = place()
    (x_dev, y_dev, d_dev), (p_x, p_y, p_d) = plane_neighbours()
    half = part.shape[1] // 2
    low, high = pl.ds(0, half), pl.ds(half, half)
    copies = [
        remote(part.at[p_d, low], diag_x, send.at[0], recv.at[0], x_dev),
        remote(part.at[p_d, high], diag_y, send.at[1], recv.at[1], y_dev),
        remote(part.at[p_x, low], from_x.at[low], send.at[2], recv.at[2], x_dev),
        remote(part.at[p_y, high], from_y.at[high], send.at[3], recv.at[3], y_dev),
    ]
    locals_ = [
        pltpu.make_async_copy(part.at[p_y, low], on_y, local.at[0]),
        pltpu.make_async_copy(part.at[p_x, high], on_x, local.at[1]),
        pltpu.make_async_copy(part.at[p], own, local.at[2]),
    ]
    to_y = remote(on_y, from_y.at[low], send.at[4], recv.at[4], y_dev)
    to_x = remote(on_x, from_x.at[high], send.at[5], recv.at[5], x_dev)

    def add_into(target, addend):
        @pl.loop(0, half // 16)
        def add_rows(i):
            at = pl.ds(pl.multiple_of(i * 16, 16), 16)
            target[at, :] = (
                target[at, :].astype(jnp.float32) + addend[at, :].astype(jnp.float32)
            ).astype(target.dtype)

    def begin():
        for copy in copies + locals_:
            copy.start()

    def forward():
        locals_[0].wait()
        copies[0].wait_recv()
        add_into(on_y, diag_x)
        to_y.start()
        locals_[1].wait()
        copies[1].wait_recv()
        add_into(on_x, diag_y)
        to_x.start()

    def end():
        locals_[2].wait()
        copies[2].wait_recv()
        copies[3].wait_recv()
        to_y.wait()
        to_x.wait()
        for copy in copies:
            copy.wait_send()

    return begin, forward, end


def sixteen(i):
    return pl.ds(pl.multiple_of(i * 16, 16), 16)


def fetch_rows(rows_all, first, start, target, sems):
    count = sems.shape[0]
    rows = target.shape[0] // count
    return [
        pltpu.make_async_copy(
            rows_all.at[first + k, pl.ds(start, rows)], target.at[pl.ds(k * rows, rows)], sems.at[k]
        )
        for k in range(count)
    ]


def computed_scratch(rows, columns, dtype):
    f32, bf16 = jnp.float32, jnp.bfloat16
    whole, half = (rows, columns), (rows // 2, columns)
    shapes = [(whole, bf16), (whole, f32)] + [(half, f32)] * 2 + [(half, bf16)] * 6 + [(half, dtype)] * 4
    return [pltpu.VMEM(*shape) for shape in shapes] + [pltpu.SemaphoreType.DMA((6,))] * 2


def computed_sum(product, sent_d, own, kept_x, kept_y, *refs):
    sent_x, sent_y, from_x, from_y, diag_x, diag_y, joint_x, joint_y, also_x, also_y, send, recv = refs
    (x_dev, y_dev, d_dev), (p_x, p_y, p_d) = plane_neighbours()
    p = place()[2]
    rows, width = own.shape
    half = rows // 2
    low, high = pl.ds(0, half), pl.ds(half, half)
    tile = 512

    def into(chip, at, target):
        @pl.loop(0, width // tile)
        def product_tile(k):
            columns = pl.ds(pl.multiple_of(k * tile, tile), tile)
            target[:, columns] = product(chip, at, columns).astype(target.dtype)

    def copy(k, source, target, device):
        return remote(source, target, send.at[k], recv.at[k], device)

    first = [copy(0, sent_d.at[low], diag_x, x_dev), copy(1, sent_d.at[high], diag_y, y_dev)]
    second = [copy(2, sent_x, from_x, x_dev), copy(3, sent_y, from_y, y_dev)]
    third = [copy(4, joint_y, also_y, y_dev), copy(5, joint_x, also_x, x_dev)]

    def begin():
        into(p_d, slice(None), sent_d)
        for sent in first:
            sent.start()
        into(p_x, low, sent_x)
        into(p_y, high, sent_y)
        for sent in second:
            sent.start()
        into(p_y, low, kept_y)
        into(p_x, high, kept_x)
        into(p, slice(None), own)

    def add(target, kept, addend):
        @pl.loop(0, half // 16)
        def add_rows(i):
            at = sixteen(i)
            target[at, :] = (kept[at, :] + addend[at, :].astype(jnp.float32)).astype(target.dtype)

    def forward():
        first[0].wait_recv()
        add(joint_y, kept_y, diag_x)
        third[0].start()
        first[1].wait_recv()
        add(joint_x, kept_x, diag_y)
        third[1].start()

    def end():
        for sent in first:
            sent.wait_send()
        for sent in second + third:
            sent.wait()

    def total(i, j):
        at = sixteen(j)
        parts = (from_x, also_y) if i == 0 else (also_x, from_y)
        here = pl.ds(pl.multiple_of(i * half + j * 16, 16), 16)
        return here, own[here, :] + parts[0][at, :].astype(jnp.float32) + parts[1][at, :].astype(jnp.float32)

    return begin, forward, end, total


def middle_kernel(
    mixed, rows_all, tokens, gain, cot, middle, whole, cot_other, normed, out_here, send, recv, local, loads, *sums
):
    me, z, p, c, x, y = place()
    sibling = me + 1 - 2 * c
    greet((*plane_neighbours()[0][:2], sibling))
    to_sibling = remote(cot, cot_other, send.at[4], recv.at[4], sibling)
    to_sibling.start()
    f32, bf16 = jnp.float32, jnp.bfloat16
    fetched = fetch_rows(rows_all, 0, 0, out_here, loads)
    for copy in fetched:
        copy.start()
    for copy in fetched:
        copy.wait()

    def product(chip, at, columns):
        return jnp.dot(mixed[chip, at, :], out_here[:, columns], preferred_element_type=f32)

    *steps, total = computed_sum(product, *sums)
    for step in steps:
        step()
    for i in range(2):

        @pl.loop(0, tokens.shape[0] // 32)
        def norm_rows(j):
            at, values = total(i, j)
            values = tokens[at, :].astype(f32) + values
            middle[at, :] = values
            inverse = lax.rsqrt(jnp.mean(values * values, axis=-1, keepdims=True) + epsilon)
            normed[at, :] = (values * inverse * gain[...]).astype(bf16)

    for step in gather_steps(normed, whole, send, recv, local, 0):
        step()
    to_sibling.wait()


def middle_of(mixed, rows_all, tokens, gain, cot, collective_id):
    rows, width = tokens.shape
    channels = mixed.shape[2]
    f32, bf16 = jnp.float32, jnp.bfloat16
    return pl.pallas_call(
        middle_kernel,
        out_shape=[
            jax.ShapeDtypeStruct((rows, width), f32),
            jax.ShapeDtypeStruct((CHIPS, rows, width), bf16),
            jax.ShapeDtypeStruct(cot.shape, cot.dtype),
        ],
        in_specs=[VMEM, ANY, VMEM, VMEM, ANY],
        out_specs=[VMEM, ANY, ANY],
        scratch_shapes=[
            pltpu.VMEM((rows, width), bf16),
            pltpu.VMEM((channels, width), bf16),
            pltpu.SemaphoreType.DMA((5,)),
            pltpu.SemaphoreType.DMA((5,)),
            pltpu.SemaphoreType.DMA,
            pltpu.SemaphoreType.DMA((rows_all.shape[0],)),
            *computed_scratch(rows, width, f32),
        ],
        compiler_params=comm_params(collective_id, 60),
        cost_estimate=lasting(75),
        name="middle",
    )(mixed, rows_all, tokens, gain[None], cot)


def feed_forward_kernel(
    piece,
    two,
    cot,
    weights,
    down,
    *refs,
):
    last = piece == 1
    if last:
        earlier, hidden, grad, parts, earlier_here, *refs = refs
    else:
        hidden, grad, parts, *refs = refs
    low, two_here, two_there, cot_here, weights_here, down_here, low_there, send, recv, loads, down_loads = refs
    me, z, p, c, x, y = place()
    sibling = me + 1 - 2 * c
    greet((sibling,))
    f32, bf16 = jnp.float32, jnp.bfloat16
    tokens, width = two.shape
    units = hidden.shape[1]
    half = width // 2
    pairs = [
        (two, two_here),
        (weights, weights_here),
        (cot, cot_here),
    ]
    if last:
        pairs.append((earlier, earlier_here))
    fetched = [pltpu.make_async_copy(a, b, loads.at[k]) for k, (a, b) in enumerate(pairs)]
    count = down_loads.shape[0]
    fetched[3:3] = fetch_rows(down, count * piece, down.shape[1] - units // count, down_here, down_loads)
    for copy in fetched:
        copy.start()
    other_half = two.at[:, pl.ds(pl.multiple_of((1 - c) * half, 128), half)]
    two_swap = remote(other_half, two_there, send.at[0], recv.at[0], sibling)
    two_swap.start()
    for copy in fetched[: 3 + count]:
        copy.wait()
    tile, block = 256, 512

    def dot_t(left, right):
        return lax.dot_general(left, right, (((1,), (1,)), ((), ())), preferred_element_type=f32)

    def dot_first(left, right):
        return lax.dot_general(left, right, (((0,), (0,)), ((), ())), preferred_element_type=f32)

    low_swaps = []
    for t in range(units // tile):
        gate_at, up_at = pl.ds(t * tile, tile), pl.ds(units + t * tile, tile)

        @pl.loop(0, tokens // block)
        def rows_block(j):
            at = pl.ds(pl.multiple_of(j * block, block), block)
            v = jnp.dot(two_here[at, :], weights_here[:, gate_at], preferred_element_type=f32)
            up = jnp.dot(two_here[at, :], weights_here[:, up_at], preferred_element_type=f32)
            grad_hidden = dot_t(cot_here[at, :], down_here[gate_at, :])
            square = v * v
            bent = jnp.tanh(v * (GELU_A + GELU_A * GELU_B * square))
            rising = 0.5 + 0.5 * bent
            act = v * rising
            slope = rising + 0.5 * v * (1.0 - bent * bent) * (GELU_A + 3.0 * GELU_A * GELU_B * square)
            hidden[at, gate_at] = (act * up).astype(bf16)
            low[at, gate_at] = (grad_hidden * up * slope).astype(bf16)
            low[at, up_at] = (grad_hidden * act).astype(bf16)

        for k, columns in enumerate((gate_at, up_at)):
            sems = 1 + 2 * t + k
            low_swaps.append(
                remote(low.at[:, columns], low_there.at[:, columns], send.at[sems], recv.at[sems], sibling)
            )
            low_swaps[-1].start()
    for copy in fetched[3 + count :]:
        copy.wait()

    @pl.loop(0, tokens // block)
    def parts_block(j):
        at = pl.ds(pl.multiple_of(j * block, block), block)

        @pl.loop(0, width // block)
        def parts_tile(k):
            columns = pl.ds(pl.multiple_of(k * block, block), block)
            values = dot_t(low[at, :], weights_here[columns, :])
            if last:
                values = values + earlier_here[at, columns]
            parts[at, columns] = values.astype(parts.dtype)

    two_swap.wait()
    for copy in low_swaps:
        copy.wait()

    @pl.loop(0, half // block)
    def grad_block(m):
        here = pl.ds(pl.multiple_of(c * half + m * block, 128), block)
        there = pl.ds(pl.multiple_of(m * block, block), block)

        @pl.loop(0, 2 * units // block)
        def grad_tile(k):
            columns = pl.ds(pl.multiple_of(k * block, block), block)
            grad[there, columns] = (
                dot_first(two_here[:, here], low[:, columns]) + dot_first(two_there[:, there], low_there[:, columns])
            ).astype(bf16)


def feed_forward(piece, two, cot, weights, down, earlier, collective_id):
    tokens, width = two.shape
    units = weights.shape[1] // 2
    bf16 = jnp.bfloat16
    out_shape = [
        jax.ShapeDtypeStruct((tokens, units), bf16),
        jax.ShapeDtypeStruct((width // 2, 2 * units), bf16),
    ]
    low = pltpu.VMEM((tokens, 2 * units), bf16)
    scratch = []
    if earlier:
        out_shape.append(jax.ShapeDtypeStruct((tokens, width), bf16))
        scratch = [pltpu.VMEM((tokens, width), jnp.float32)]
    else:
        out_shape.append(jax.ShapeDtypeStruct((tokens, width), jnp.float32))
    swaps = 1 + 2 * (units // 256)
    return pl.pallas_call(
        functools.partial(feed_forward_kernel, piece),
        out_shape=out_shape,
        in_specs=[ANY] * (4 + len(earlier)),
        out_specs=[VMEM] * 3,
        scratch_shapes=[
            *scratch,
            low,
            pltpu.VMEM((tokens, width), bf16),
            pltpu.VMEM((tokens, width // 2), bf16),
            pltpu.VMEM((tokens, width), bf16),
            pltpu.VMEM(weights.shape, bf16),
            pltpu.VMEM((units, width), bf16),
            low,
            pltpu.SemaphoreType.DMA((swaps,)),
            pltpu.SemaphoreType.DMA((swaps,)),
            pltpu.SemaphoreType.DMA((3 + len(earlier),)),
            pltpu.SemaphoreType.DMA((down.shape[0] // 2,)),
        ],
        compiler_params=comm_params(collective_id, 60),
        cost_estimate=lasting(35),
        name="feed_forward",
    )(two, cot, weights, down, *earlier)


def norm_back_rows(values, gain, grad, rest):
    inverse = lax.rsqrt(jnp.mean(values * values, axis=-1, keepdims=True) + epsilon)
    scaled = gain * grad
    pull = jnp.mean(scaled * values, axis=-1, keepdims=True) * (inverse * inverse * inverse)
    return rest + inverse * scaled - values * pull, grad * values * inverse


def grads_of_middle_kernel(
    parts,
    middle,
    cot,
    gain,
    hidden_zero,
    hidden_one,
    down,
    cot_all,
    cot_other,
    mixed_zero,
    mixed_one,
    grad_middle,
    grad_gain,
    whole,
    row_grads,
    down_parts,
    branch,
    branch_all,
    branch_other,
    mixed_here,
    mixed_there,
    out_sum,
    hidden_here,
    hidden_other,
    down_here,
    cot_here,
    cot_there,
    *scratch,
):
    sums, (send, recv, local, loads, down_loads) = scratch[:10], scratch[10:]
    me, z, p, c, x, y = place()
    f32, bf16 = jnp.float32, jnp.bfloat16
    sibling = me + 1 - 2 * c
    greet((*plane_neighbours()[0][:2], sibling))
    own, from_x, from_y = sums[:3]
    begin, forward, end = sum_steps(parts, *sums)
    begin()
    half = hidden_zero.shape[1]
    swaps = [remote(hidden, hidden_other, send.at[4], recv.at[4], sibling) for hidden in (hidden_one, hidden_zero)]
    mixed_swaps = [remote(mixed, mixed_there, send.at[9], recv.at[9], sibling) for mixed in (mixed_one, mixed_zero)]
    mixed_loads = [pltpu.make_async_copy(mixed, mixed_here, loads.at[4]) for mixed in (mixed_zero, mixed_one)]

    @pl.when(c == 0)
    def send_one():
        swaps[0].start()
        mixed_swaps[0].start()
        mixed_loads[0].start()

    @pl.when(c == 1)
    def send_zero():
        swaps[1].start()
        mixed_swaps[1].start()
        mixed_loads[1].start()

    fetched = [
        pltpu.make_async_copy(source, target, loads.at[k])
        for k, (source, target) in enumerate(
            (
                (hidden_zero, hidden_here.at[:, pl.ds(0, half)]),
                (hidden_one, hidden_here.at[:, pl.ds(half, half)]),
                (cot_all, cot_here),
                (cot_other, cot_there),
            )
        )
    ]
    count = down_loads.shape[0]
    down_fetched = fetch_rows(down, 0, down.shape[1] - down_here.shape[0] // count, down_here, down_loads)
    for copy in fetched + down_fetched:
        copy.start()
    for copy in fetched[:4]:
        copy.wait()
    swaps[0].wait()
    tile = 256

    planes = row_grads.shape[0]
    units = half // planes
    above = row_grads.shape[1] - units

    def grad_tiles(m):
        rows_here = pl.ds(pl.multiple_of(c * half + m * tile, 128), tile)

        @pl.loop(0, cot_all.shape[1] // (2 * tile))
        def grad_tile(k):
            columns = pl.ds(pl.multiple_of(k * 2 * tile, 128), 2 * tile)

            def dot_t(left, right):
                return lax.dot_general(left, right, (((0,), (0,)), ((), ())), preferred_element_type=f32)

            values = (
                dot_t(hidden_here[:, rows_here], cot_here[:, columns])
                + dot_t(hidden_other[:, m * tile : (m + 1) * tile], cot_there[:, columns])
            ).astype(bf16)
            for j in range(planes):
                start, stop = max(j * units, m * tile), min((j + 1) * units, (m + 1) * tile)
                if start < stop:
                    row_grads[j, above + start - j * units : above + stop - j * units, columns] = values[
                        start - m * tile : stop - m * tile
                    ]

    grad_tiles(0)
    forward()
    for m in range(1, half // tile):
        grad_tiles(m)
    end()
    rows, width = middle.shape

    def norm_rows(i, total):
        at = sixteen(i)
        grad = own[at, :].astype(f32) + from_x[at, :].astype(f32) + from_y[at, :].astype(f32)
        given, terms = norm_back_rows(middle[at, :], gain[...], grad, cot[at, :].astype(f32))
        grad_middle[at, :] = given
        branch[at, :] = given.astype(bf16)
        return total + terms[:8] + terms[8:]

    total = lax.fori_loop(0, rows // 16, norm_rows, jnp.zeros((8, width), f32))
    grad_gain[...] = jnp.sum(total, axis=0, keepdims=True)
    begin, forward, end = gather_steps(branch, branch_all, send, recv, local, 0)
    (p_x, p_y, p_d) = plane_neighbours()[1]

    def to_sibling(k, chip, source):
        return remote(source, branch_other.at[chip], send.at[5 + k], recv.at[5 + k], sibling)

    shares = [to_sibling(0, p, branch)] + [
        to_sibling(1 + k, chip, branch_all.at[chip]) for k, chip in enumerate((p_x, p_y, p_d))
    ]
    begin()
    shares[0].start()
    for copy in down_fetched + [mixed_loads[0], mixed_swaps[0]]:
        copy.wait()

    def down_tiles(j):
        @pl.loop(0, width // (2 * tile))
        def down_tile(k):
            columns = pl.ds(pl.multiple_of(k * 2 * tile, 128), 2 * tile)
            down_parts[j, :, columns] = jnp.dot(
                hidden_here[pl.ds(pl.multiple_of(j * rows, 16), rows), :],
                down_here[:, columns],
                preferred_element_type=f32,
            ).astype(bf16)

    pl.loop(0, CHIPS)(down_tiles)

    def out_tiles(mixed, branches, chips, finish):
        @pl.loop(0, width // (2 * tile))
        def out_tile(k):
            columns = pl.ds(pl.multiple_of(k * 2 * tile, 128), 2 * tile)
            values = out_sum[:, columns]
            for chip in chips:
                values = values + lax.dot_general(
                    mixed[pl.ds(pl.multiple_of(chip * rows, 16), rows), :],
                    branches[chip, :, columns],
                    (((0,), (0,)), ((), ())),
                    preferred_element_type=f32,
                )
            if finish:
                for j in range(planes):
                    row_grads[j, 0:above, columns] = values[j * above : (j + 1) * above].astype(bf16)
            else:
                out_sum[:, columns] = values

    forward()
    shares[1].start()
    shares[2].start()
    out_sum[...] = jnp.zeros_like(out_sum)
    out_tiles(mixed_here, branch_all, (p_x, p_y), False)
    end()
    shares[3].start()
    to_whole = pltpu.make_async_copy(branch_all, whole, local)
    to_whole.start()
    out_tiles(mixed_here, branch_all, (p, p_d), False)
    for copy in shares:
        copy.wait()
    out_tiles(mixed_there, branch_other, range(CHIPS), True)
    to_whole.wait()


def grads_of_middle(parts, middle, cot, gain, hiddens, down, cots, mixeds, collective_id):
    rows, width = middle.shape
    tokens, units = hiddens[0].shape[0], 2 * hiddens[0].shape[1]
    f32, bf16 = jnp.float32, jnp.bfloat16
    return pl.pallas_call(
        grads_of_middle_kernel,
        out_shape=[
            jax.ShapeDtypeStruct((rows, width), f32),
            jax.ShapeDtypeStruct((1, width), f32),
            jax.ShapeDtypeStruct((CHIPS, rows, width), bf16),
            jax.ShapeDtypeStruct(
                (down.shape[0] // 2, down.shape[1], width), bf16
            ),
            jax.ShapeDtypeStruct((CHIPS, rows, width), bf16),
        ],
        in_specs=[ANY, VMEM, VMEM, VMEM] + [ANY] * 7,
        out_specs=[VMEM, VMEM, ANY, VMEM, VMEM],
        scratch_shapes=[
            pltpu.VMEM((rows, width), bf16),
            pltpu.VMEM((CHIPS, rows, width), bf16),
            pltpu.VMEM((CHIPS, rows, width), bf16),
            pltpu.VMEM(mixeds[0].shape, bf16),
            pltpu.VMEM(mixeds[0].shape, bf16),
            pltpu.VMEM((mixeds[0].shape[1], width), f32),
            pltpu.VMEM((tokens, units), bf16),
            pltpu.VMEM((tokens, units // 2), bf16),
            pltpu.VMEM((units, width), bf16),
            pltpu.VMEM((tokens, width), bf16),
            pltpu.VMEM((tokens, width), bf16),
            *sum_scratch(rows, width, parts.dtype),
            pltpu.SemaphoreType.DMA((10,)),
            pltpu.SemaphoreType.DMA((10,)),
            pltpu.SemaphoreType.DMA,
            pltpu.SemaphoreType.DMA((5,)),
            pltpu.SemaphoreType.DMA((down.shape[0],)),
        ],
        compiler_params=comm_params(collective_id, 60),
        cost_estimate=lasting(80),
        name="grads_of_middle",
    )(parts, middle, cot, gain[None], *hiddens, down, *cots, *mixeds)


def closing_kernel(
    planes,
    in_low,
    whole_in,
    tokens,
    gain,
    rest,
    small,
    mlp_gain,
    conv_low,
    decay_low,
    input_low,
    piece,
    grad_tokens,
    small_out,
    gates_out,
    swapped,
    conv_a,
    conv_b,
    decay_a,
    decay_b,
    input_a,
    input_b,
    full,
    gates,
    gate_lines,
    lines,
    line,
    near_part,
    gains,
    gain_lines,
    gain_line,
    gain_near,
    gain_sum,
    send,
    recv,
    loads,
    swap_send,
    swap_recv,
    *sums,
):
    me, z, p, c, x, y = place()
    f32 = jnp.float32
    r = lax.rem(me, 8)
    near = [(lax.rem(r + d, 8), me - r + lax.rem(r + d, 8)) for d in range(1, 8)]
    far = [(lax.rem(z + d, planes), 8 * lax.rem(z + d, planes) + r) for d in range(1, planes)]
    greet([device for unused, device in near + far])

    def copy(k, source, target, device):
        return remote(source, target, send.at[k], recv.at[k], device)

    lows = ((conv_low, conv_a, conv_b), (decay_low, decay_a, decay_b), (input_low, input_a, input_b))
    fetched = [pltpu.make_async_copy(source, here, loads.at[k]) for k, (source, here, there) in enumerate(lows)]
    exchanges = [copy(k, source, there, me + 1 - 2 * c) for k, (source, here, there) in enumerate(lows)]
    at = 3
    small_far = [copy(at + d, small.at[there], lines.at[d], device) for d, (there, device) in enumerate(far)]
    at += len(far)
    for started in small_far + fetched + exchanges:
        started.start()

    def product(chip, rows_at, columns):
        return lax.dot_general(
            in_low[chip, rows_at, :], whole_in[columns, :], (((1,), (1,)), ((), ())), preferred_element_type=f32
        )

    begin, forward, end, part_of = computed_sum(product, *sums)
    begin()
    for ended in fetched + exchanges:
        ended.wait()
    swaps = swap_copies(piece, swapped, swap_send, swap_recv, loads.at[3])

    def dot_first(left, right):
        return lax.dot_general(left, right, (((0,), (0,)), ((), ())), preferred_element_type=f32)

    block = gates.shape[1]
    count = planes * block
    for k, (first, second) in enumerate(((decay_a, decay_b), (input_a, input_b))):
        full[...] = dot_first(conv_a[...], first[...]) + dot_first(conv_b[...], second[...])
        for j in range(planes):
            rows_at = pl.ds(pl.multiple_of(c * count + j * block, 8), block)
            for e in range(2):
                gates[j, :, (2 * k + e) * block : (2 * k + e + 1) * block] = full[
                    rows_at, e * count + j * block : e * count + (j + 1) * block
                ].astype(gates.dtype)
    gate_far = [copy(at + d, gates.at[there], gate_lines.at[d], device) for d, (there, device) in enumerate(far)]
    at += len(far)
    for sent in gate_far:
        sent.start()
    forward()
    for sent in swaps:
        sent.start()
    for sent in small_far:
        sent.wait()
    line[...] = small[z] + sum(lines[d] for d in range(planes - 1))
    small_near = copy(at, line.at[1 - c], near_part, me + 1 - 2 * c)
    small_near.start()
    at += 1
    end()
    rows, width = tokens.shape
    step = width // (8 * planes)

    def norm_rows(i, j, total):
        here, grad = part_of(i, j)
        given, terms = norm_back_rows(tokens[here, :].astype(f32), gain[...], grad, rest[here, :])
        for k in range(4 * planes):
            for e in range(2):
                grad_tokens[here, (2 * k + e) * step : (2 * k + e + 1) * step] = given[
                    :, (4 * planes * e + k) * step : (4 * planes * e + k + 1) * step
                ]
        return total + terms[:8] + terms[8:]

    total = jnp.zeros((8, width), f32)
    for i in range(2):
        total = lax.fori_loop(0, rows // 32, functools.partial(norm_rows, i), total)
    total = jnp.sum(total, axis=0, keepdims=True)
    for j in range(planes):
        for q in range(CHIPS):
            for e in range(2):
                start = ((e * planes + j) * CHIPS + q) * step
                gains[j, 2 * q + e : 2 * q + e + 1, 0:step] = total[:, start : start + step]
                gains[j, 2 * q + e : 2 * q + e + 1, step : 2 * step] = mlp_gain[:, start : start + step]
    gain_far = [copy(at + d, gains.at[there], gain_lines.at[d], device) for d, (there, device) in enumerate(far)]
    at += len(far)
    for sent in gain_far:
        sent.start()
    for sent in gain_far:
        sent.wait()
    gain_line[...] = gains[z] + sum(gain_lines[d] for d in range(planes - 1))
    last = [copy(at + d, gain_line, gain_near.at[d], device) for d, (there, device) in enumerate(near)]
    for sent in last:
        sent.start()
    for sent in gate_far + swaps + [small_near]:
        sent.wait()
    gates_out[...] = gates[z].astype(f32) + sum(gate_lines[d].astype(f32) for d in range(planes - 1))
    for sent in last:
        sent.wait()
    rows_small = line.shape[1]
    small_out[0:rows_small, :] = line[c] + near_part[...]
    gain_sum[...] = gain_line[...] + sum(gain_near[d] for d in range(7))
    small_out[rows_small : rows_small + 1, :] = gain_sum[pl.ds(r, 1), :]


def closing(in_low, whole_in, tokens, gain, rest, small, mlp_gain, lows, piece, head, collective_id):
    planes = lax.axis_size("seq") // 8
    rows, width = tokens.shape
    f32, bf16 = jnp.float32, jnp.bfloat16
    rows_small, lanes = small.shape[2:]
    channels = lows[0].shape[1]
    block = channels // (2 * planes)
    count = 3 + 3 * (planes - 1) + 8
    return pl.pallas_call(
        functools.partial(closing_kernel, planes),
        out_shape=[
            jax.ShapeDtypeStruct((rows, width), f32),
            jax.ShapeDtypeStruct((rows_small + 1, lanes), f32),
            jax.ShapeDtypeStruct((block, 2 * head), f32),
            jax.ShapeDtypeStruct(piece.shape, bf16),
        ],
        in_specs=[VMEM] * 7 + [ANY] * 4,
        out_specs=[VMEM] * 3 + [ANY],
        scratch_shapes=[
            *[pltpu.VMEM(lows[0].shape, bf16)] * 6,
            pltpu.VMEM((channels, channels), f32),
            pltpu.VMEM((planes, block, 2 * head), bf16),
            pltpu.VMEM((planes - 1, block, 2 * head), bf16),
            pltpu.VMEM((planes - 1, 2, rows_small, lanes), f32),
            pltpu.VMEM((2, rows_small, lanes), f32),
            pltpu.VMEM((rows_small, lanes), f32),
            pltpu.VMEM((planes, 8, lanes), f32),
            pltpu.VMEM((planes - 1, 8, lanes), f32),
            pltpu.VMEM((8, lanes), f32),
            pltpu.VMEM((7, 8, lanes), f32),
            pltpu.VMEM((8, lanes), f32),
            pltpu.SemaphoreType.DMA((count,)),
            pltpu.SemaphoreType.DMA((count,)),
            pltpu.SemaphoreType.DMA((4,)),
            pltpu.SemaphoreType.DMA((3,)),
            pltpu.SemaphoreType.DMA((3,)),
            *computed_scratch(rows, width, bf16),
        ],
        compiler_params=comm_params(collective_id, 60),
        cost_estimate=lasting(50),
        name="closing",
    )(in_low, whole_in, tokens, gain[None], rest, small, mlp_gain, *lows, piece)


def first_swap_kernel(planes, pairs, *refs):
    count = len(pairs)
    ins, refs = refs[:count], refs[count:]
    decay_gate, input_gate, out, line, gates, parts, send, recv, local, line_send, line_recv = refs
    me, z, p, c, x, y = place()
    far = [8 * lax.rem(z + d, planes) + lax.rem(me, 8) for d in range(1, planes)]
    head = decay_gate.shape[1]
    gates[:, :head] = decay_gate[...]
    gates[:, head:] = input_gate[...]
    to_chips_kernel(planes, pairs, *ins, parts)
    greet([*plane_neighbours()[0], *far])
    copies = swap_copies(parts, out, send, recv, local) + [
        remote(gates, line.at[z], line_send.at[d], line_recv.at[d], device) for d, device in enumerate(far)
    ]
    for copy in copies:
        copy.start()
    line[z] = gates[...]
    for copy in copies:
        copy.wait()


def first_swap(weights, pairs, width, gates, collective_id):
    planes = lax.axis_size("seq") // 8
    rows, head = gates[0].shape
    shape = (CHIPS, weights[0].shape[0], width)
    return pl.pallas_call(
        functools.partial(first_swap_kernel, planes, pairs),
        out_shape=[
            jax.ShapeDtypeStruct(shape, weights[0].dtype),
            jax.ShapeDtypeStruct((planes, rows, 2 * head), gates[0].dtype),
        ],
        in_specs=[VMEM] * (len(weights) + 2),
        out_specs=[ANY, VMEM],
        scratch_shapes=[
            pltpu.VMEM((rows, 2 * head), gates[0].dtype),
            pltpu.VMEM(shape, weights[0].dtype),
            pltpu.SemaphoreType.DMA((3,)),
            pltpu.SemaphoreType.DMA((3,)),
            pltpu.SemaphoreType.DMA,
            pltpu.SemaphoreType.DMA((planes - 1,)),
            pltpu.SemaphoreType.DMA((planes - 1,)),
        ],
        compiler_params=comm_params(collective_id, 60),
        name="first_swap",
    )(*weights, *gates)


def plane_swap_kernel(count, *refs):
    ins, outs = refs[:count], refs[count : 2 * count]
    send, recv, local = refs[2 * count :]
    me, z, p, c, x, y = place()
    x_dev, y_dev = me + 2 - 4 * x, me + 4 - 8 * y
    d_dev = y_dev + 2 - 4 * x
    p_x, p_y, p_d = p + 1 - 2 * x, p + 2 - 4 * y, 3 - p
    peers = ((x_dev, p_x), (y_dev, p_y), (d_dev, p_d))
    greet([device for device, unused in peers])
    copies = []
    for k in range(count):
        for j, (device, chip) in enumerate(peers):
            copies.append(remote(ins[k].at[chip], outs[k].at[p], send.at[k, j], recv.at[k, j], device))
        copies.append(pltpu.make_async_copy(ins[k].at[p], outs[k].at[p], local.at[k]))
    for copy in copies:
        copy.start()
    for copy in copies:
        copy.wait()


def plane_swap(arrays, collective_id):
    count = len(arrays)
    return pl.pallas_call(
        functools.partial(plane_swap_kernel, count),
        out_shape=[jax.ShapeDtypeStruct(a.shape, a.dtype) for a in arrays],
        in_specs=[ANY] * count,
        out_specs=[ANY] * count,
        scratch_shapes=[
            pltpu.SemaphoreType.DMA((count, 3)),
            pltpu.SemaphoreType.DMA((count, 3)),
            pltpu.SemaphoreType.DMA((count,)),
        ],
        compiler_params=comm_params(collective_id, 60),
        cost_estimate=lasting(10),
        name="plane_swap",
    )(*arrays)


def swap_copies(source, target, send, recv, local):
    devices, chips = plane_neighbours()
    p = place()[2]
    return [
        *[remote(source.at[chips[j]], target.at[p], send.at[j], recv.at[j], devices[j]) for j in range(3)],
        pltpu.make_async_copy(source.at[p], target.at[p], local),
    ]


def opening_kernel(
    planes,
    pairs,
    small,
    gates,
    tokens,
    mlp_gate,
    mlp_up,
    gathered,
    decay_blocks,
    input_blocks,
    second_piece,
    whole,
    swapped,
    piece,
    gates_all,
    gain,
    normed,
    *sems,
):
    send, recv, gate_send, gate_recv, swap_send, swap_recv, swap_local, gather_send, gather_recv, gather_local = sems
    me, z, p, c, x, y = place()
    r = lax.rem(me, 8)
    near = [me - r + lax.rem(r + d, 8) for d in range(1, 8)]
    far = [8 * lax.rem(z + d, planes) + r for d in range(1, planes)]
    greet(near + far)
    lines = [
        remote(small, gathered.at[r, z], send.at[d], recv.at[d], device) for d, device in enumerate(far)
    ]
    gate_swap = remote(gates, gates_all.at[c], gate_send, gate_recv, me + 1 - 2 * c)
    for copy in lines + [gate_swap]:
        copy.start()
    gathered[r, z] = small[...]
    gates_all[c] = gates[...]
    to_chips_kernel(planes, pairs, mlp_gate, mlp_up, piece, second_piece)
    swaps = swap_copies(piece, swapped, swap_send, swap_recv, swap_local)
    for copy in swaps:
        copy.start()
    for copy in lines:
        copy.wait()
    spreads = [
        remote(gathered.at[r], gathered.at[r], send.at[planes + d], recv.at[planes + d], device)
        for d, device in enumerate(near)
    ]
    for copy in spreads:
        copy.start()
    for copy in spreads:
        copy.wait()
    rows, width = tokens.shape
    step = width // (8 * planes)
    for j in range(planes):
        for q in range(CHIPS):
            for e in range(2):
                start = ((e * planes + j) * CHIPS + q) * step
                gain[0:1, start : start + step] = gathered[2 * q + e, j, 0:1, 0:step]

    @pl.loop(0, rows // 16)
    def norm_rows(i):
        at = sixteen(i)
        values = tokens[at, :].astype(jnp.float32)
        inverse = lax.rsqrt(jnp.mean(values * values, axis=-1, keepdims=True) + epsilon)
        normed[at, :] = (values * inverse * gain[0:1, :]).astype(jnp.bfloat16)

    begin, forward, end = gather_steps(normed, whole, gather_send, gather_recv, gather_local, 0)
    begin()
    gate_swap.wait()
    block = gates.shape[1]
    for k, target in enumerate((decay_blocks, input_blocks)):
        target[...] = jnp.zeros_like(target)
        for e in range(2):
            for j in range(planes):
                for h in range(2):
                    row, column = (e * planes + j) * block, (h * planes + j) * block
                    target[row : row + block, column : column + block] = gates_all[
                        e, j, :, (2 * k + h) * block : (2 * k + h + 1) * block
                    ]
    forward()
    end()
    for copy in swaps:
        copy.wait()


def opening(small, gates, tokens, mlp_gate, mlp_up, pairs, collective_id):
    planes = lax.axis_size("seq") // 8
    rows, width = tokens.shape
    channels = 2 * planes * gates.shape[1]
    piece = (CHIPS, mlp_gate.shape[0], mlp_gate.shape[1] // CHIPS)
    return pl.pallas_call(
        functools.partial(opening_kernel, planes, pairs),
        out_shape=[
            jax.ShapeDtypeStruct((8, planes) + small.shape, small.dtype),
            jax.ShapeDtypeStruct((channels, channels), gates.dtype),
            jax.ShapeDtypeStruct((channels, channels), gates.dtype),
            jax.ShapeDtypeStruct(piece, mlp_gate.dtype),
            jax.ShapeDtypeStruct((CHIPS, rows, width), jnp.bfloat16),
            jax.ShapeDtypeStruct(piece, mlp_gate.dtype),
        ],
        in_specs=[VMEM] * 5,
        out_specs=[VMEM] * 4 + [ANY, ANY],
        scratch_shapes=[
            pltpu.VMEM(piece, mlp_gate.dtype),
            pltpu.VMEM((2,) + gates.shape, gates.dtype),
            pltpu.VMEM((8, width), jnp.float32),
            pltpu.VMEM((rows, width), jnp.bfloat16),
            pltpu.SemaphoreType.DMA((planes + 7,)),
            pltpu.SemaphoreType.DMA((planes + 7,)),
            pltpu.SemaphoreType.DMA,
            pltpu.SemaphoreType.DMA,
            pltpu.SemaphoreType.DMA((3,)),
            pltpu.SemaphoreType.DMA((3,)),
            pltpu.SemaphoreType.DMA,
            pltpu.SemaphoreType.DMA((4,)),
            pltpu.SemaphoreType.DMA((4,)),
            pltpu.SemaphoreType.DMA,
        ],
        compiler_params=comm_params(collective_id, 60),
        cost_estimate=lasting(65),
        name="opening",
    )(small, gates, tokens, mlp_gate, mlp_up)


def column_peers(planes, z, p, c):
    count = 2 * planes
    q = 2 * z + c
    peers = []
    for d in range(1, count):
        other = lax.rem(q + d, count)
        peers.append(8 * lax.div(other, 2) + 2 * p + lax.rem(other, 2))
    return q, peers


def carry_in(planes, reverse, z, c, me, everyone, before, entering, send, recv):
    own = everyone.at[c, z]
    r = lax.rem(me, 8)
    lines = [
        remote(own, own, send.at[d], recv.at[d], 8 * lax.rem(z + d, planes) + r) for d in range(1, planes)
    ]
    for copy in lines:
        copy.start()
    for copy in lines:
        copy.wait()
    share = remote(everyone.at[c], everyone.at[c], send.at[0], recv.at[0], me + 1 - 2 * c)
    share.start()
    share.wait()
    carried = jnp.zeros((1, everyone.shape[3]), jnp.float32)
    order = [(k, j, e) for k in range(planes) for j in range(CHIPS) for e in range(2)]
    for k, j, e in reversed(order) if reverse else order:
        before[8 * k + 2 * j + e : 8 * k + 2 * j + e + 1, :] = carried
        part = everyone.at[e, k]
        carried = part[j : j + 1, :] * carried + part[CHIPS + j : CHIPS + j + 1, :]
    for j in range(CHIPS):
        entering[j : j + 1, :] = before[pl.ds(8 * z + 2 * j + c, 1), :]


def shift_down(earlier, values, step, row):
    return jnp.where(row >= step, pltpu.roll(values, step, 0), pltpu.roll(earlier, step, 0))


def shift_up(values, later, step, row):
    return jnp.where(row < 8 - step, pltpu.roll(values, 8 - step, 0), pltpu.roll(later, 8 - step, 0))


def tile_scan(a, b, row, reverse):
    for step in (1, 2, 4):
        if reverse:
            keep = row < 8 - step
            shifted_a, shifted_b = pltpu.roll(a, 8 - step, 0), pltpu.roll(b, 8 - step, 0)
        else:
            keep = row >= step
            shifted_a, shifted_b = pltpu.roll(a, step, 0), pltpu.roll(b, step, 0)
        b = a * jnp.where(keep, shifted_b, 0.0) + b
        a = a * jnp.where(keep, shifted_a, 1.0)
    return a, b


def sigmoid(values):
    return 1.0 / (1.0 + jnp.exp(-values))


def gate_terms(decay_pre, rate, flag):
    opened = sigmoid(decay_pre)
    log_decay = rate * opened
    decay = jnp.exp(log_decay)
    keep = 1.0 - flag
    squared = decay * decay
    return opened, decay * keep, keep, squared, jnp.tanh(-log_decay) * (1.0 + squared)


GELU_A, GELU_B = 0.7978845608028654, 0.044715


def eight(i):
    return pl.ds(pl.multiple_of(i * 8, 8), 8)


def recurrence_kernel(
    planes,
    gate_pre,
    conv_input,
    masks,
    vectors,
    decay_blocks,
    input_blocks,
    cot,
    piece,
    normed,
    conv_out,
    conv_low,
    decay_pre,
    input_pre,
    states,
    mixed,
    mixed_zero,
    mixed_one,
    entering,
    halo,
    cot_all,
    swapped,
    normed_other,
    cumulative,
    sibling_tails,
    below_tail,
    everyone,
    before,
    send,
    recv,
    local,
    swap_send,
    swap_recv,
    other_send,
    other_recv,
):
    me, z, p, c, x, y = place()
    rows, channels = conv_input.shape[1:]
    q, peers = column_peers(planes, z, p, c)
    greet(peers + [*plane_neighbours()[0]])
    cot_begin, cot_forward, cot_end = gather_steps(cot, cot_all, send, recv, local.at[0], 9)
    cot_begin()
    half = normed.shape[1] // 2
    other = remote(
        normed.at[:, pl.ds(pl.multiple_of((1 - c) * half, 128), half)],
        normed_other,
        other_send,
        other_recv,
        me + 1 - 2 * c,
    )
    other.start()
    swaps = swap_copies(piece, swapped, swap_send, swap_recv, local.at[1])
    f32 = jnp.float32
    tail = pl.ds(rows - 16, 16)
    to_sibling = remote(conv_input.at[:, tail], sibling_tails, send.at[7], recv.at[7], me + 1 - 2 * c)
    to_above = remote(conv_input.at[CHIPS - 1, tail], below_tail, send.at[8], recv.at[8], me + 7)
    from_below = remote(conv_input.at[CHIPS - 1, tail], below_tail, send.at[8], recv.at[8], me - 7)
    to_sibling.start()

    @pl.when((c == 1) & (z < planes - 1))
    def send_above():
        to_above.start()

    to_sibling.wait()

    @pl.when((c == 1) & (z < planes - 1))
    def sent_above():
        to_above.wait_send()

    @pl.when((c == 0) & (z > 0))
    def had_below():
        from_below.wait_recv()

    @pl.when(c == 1)
    def halo_one():
        for j in range(CHIPS):
            halo[j] = sibling_tails[j].astype(f32)[8:]

    @pl.when(c == 0)
    def halo_zero():
        for j in range(1, CHIPS):
            halo[j] = sibling_tails[j - 1].astype(f32)[8:]

        @pl.when(z > 0)
        def halo_below():
            halo[0] = below_tail[...].astype(f32)[8:]

        @pl.when(z == 0)
        def halo_none():
            halo[0] = jnp.zeros((8, channels), f32)

    row = lax.broadcasted_iota(jnp.int32, (8, channels), 0)

    @pl.loop(0, CHIPS)
    def block(j):
        def conv_tile(i, earlier):
            both = conv_input[j, sixteen(i), :].astype(f32)
            outs = []
            for h in range(2):
                now = both[8 * h : 8 * h + 8]
                keep = masks[j, eight(2 * i + h), :]
                out = vectors[CW : CW + 1, :] + vectors[0:1, :] * now
                for k in range(1, CW):
                    out = out + vectors[k : k + 1, :] * (
                        shift_down(earlier, now, k, row) * keep[:, k : k + 1]
                    )
                conv_out[j, eight(2 * i + h), :] = out
                outs.append(out)
                earlier = now
            conv_low[j, sixteen(i), :] = jnp.concatenate(outs, axis=0).astype(jnp.bfloat16)
            return earlier

        lax.fori_loop(0, rows // 16, conv_tile, halo[j], unroll=2)
        low = conv_low[j]
        decay_pre[j] = jnp.dot(low, decay_blocks[...], preferred_element_type=f32) + vectors[CW + 1 : CW + 2, :]
        input_pre[j] = jnp.dot(low, input_blocks[...], preferred_element_type=f32) + vectors[CW + 2 : CW + 3, :]

        def scan_tile(i, carry):
            at = eight(i)
            flag = masks[j, at, :][:, 0:1]
            opened, coef, keep, squared, gap = gate_terms(decay_pre[j, at, :], vectors[CW + 3 : CW + 4, :], flag)
            drive = (flag + keep * jnp.sqrt(gap)) * sigmoid(input_pre[j, at, :]) * conv_out[j, at, :]
            a, b = tile_scan(coef, drive, row, False)
            before_a, before_b = carry
            b = a * before_b + b
            a = a * before_a
            cumulative[j, at, :] = a
            states[j, at, :] = b
            return a[7:8], b[7:8]

        last_a, last_b = lax.fori_loop(
            0,
            rows // 8,
            scan_tile,
            (jnp.ones((1, channels), f32), jnp.zeros((1, channels), f32)),
            unroll=4,
        )
        everyone[c, z, pl.ds(j, 1), :] = last_a
        everyone[c, z, pl.ds(CHIPS + j, 1), :] = last_b

    cot_forward()
    for copy in swaps:
        copy.start()
    carry_in(planes, False, z, c, me, everyone, before, entering, send, recv)

    @pl.loop(0, CHIPS)
    def finish(j):
        start = entering[pl.ds(j, 1), :]

        def state_tile(i, unused):
            at = sixteen(i)
            state = states[j, at, :] + cumulative[j, at, :] * start
            states[j, at, :] = state
            v = gate_pre[j, at, :]
            act = 0.5 * v * (1.0 + jnp.tanh(GELU_A * (v + GELU_B * (v * v * v))))
            product = (state * act).astype(jnp.bfloat16)
            mixed[j, at, :] = product
            mixed_zero[j, at, :] = product[:, : channels // 2]
            mixed_one[j, at, :] = product[:, channels // 2 :]
            return unused

        lax.fori_loop(0, rows // 16, state_tile, 0, unroll=2)

    cot_end()
    other.wait()
    for copy in swaps:
        copy.wait()


def recurrence(gate_pre, conv_input, masks, vectors, decay_blocks, input_blocks, cot, piece, normed, collective_id):
    planes = lax.axis_size("seq") // 8
    blocks, rows, channels = conv_input.shape
    f32, bf16 = jnp.float32, jnp.bfloat16
    cube = conv_input.shape

    def out(dtype, shape=cube):
        return jax.ShapeDtypeStruct(shape, dtype)

    return pl.pallas_call(
        functools.partial(recurrence_kernel, planes),
        out_shape=[
            out(f32),
            out(bf16),
            out(f32),
            out(f32),
            out(f32),
            out(bf16),
            *[out(bf16, (CHIPS, rows, channels // 2))] * 2,
            out(f32, (CHIPS, channels)),
            out(f32, (CHIPS, 8, channels)),
            out(cot.dtype, (CHIPS,) + cot.shape),
            out(piece.dtype, piece.shape),
            out(normed.dtype, (normed.shape[0], normed.shape[1] // 2)),
        ],
        in_specs=[VMEM] * 6 + [ANY] * 3,
        out_specs=[VMEM] * 10 + [ANY] * 3,
        scratch_shapes=[
            pltpu.VMEM(cube, f32),
            pltpu.VMEM((CHIPS, 16, channels), bf16),
            pltpu.VMEM((16, channels), bf16),
            pltpu.VMEM((2, planes, 2 * CHIPS, channels), f32),
            pltpu.VMEM((8 * planes, channels), f32),
            pltpu.SemaphoreType.DMA((13,)),
            pltpu.SemaphoreType.DMA((13,)),
            pltpu.SemaphoreType.DMA((2,)),
            pltpu.SemaphoreType.DMA((3,)),
            pltpu.SemaphoreType.DMA((3,)),
            pltpu.SemaphoreType.DMA,
            pltpu.SemaphoreType.DMA,
        ],
        compiler_params=comm_params(collective_id, 60),
        cost_estimate=lasting(46),
        name="recurrence",
    )(gate_pre, conv_input, masks, vectors, decay_blocks, input_blocks, cot, piece, normed)


def recurrence_back_kernel(
    planes,
    grad_branch,
    rows_all,
    gate_pre,
    conv_input,
    conv_out,
    decay_pre,
    input_pre,
    states,
    entering,
    halo,
    masks,
    after_masks,
    vectors,
    decay_blocks,
    input_blocks,
    middle,
    down_parts,
    piece,
    in_low,
    decay_low,
    input_low,
    sums,
    block_out,
    swapped,
    grad_mixed,
    branch_here,
    out_here,
    cumulative,
    local,
    grad_conv,
    sibling_heads,
    above_head,
    ahead,
    everyone,
    before,
    leaving,
    send,
    recv,
    piece_sem,
    loads,
    *down_scratch,
):
    me, z, p, c, x, y = place()
    rows, channels = conv_input.shape[1:]
    q, peers = column_peers(planes, z, p, c)
    devices, chips = plane_neighbours()
    greet(peers + [*devices])
    down_begin, down_forward, down_end = sum_steps(down_parts, *down_scratch)
    down_begin()
    swaps = swap_copies(piece, swapped, send.at[pl.ds(9, 3)], recv.at[pl.ds(9, 3)], piece_sem.at[0])
    fetched = fetch_rows(rows_all, 0, 0, out_here, loads)
    fetched.append(pltpu.make_async_copy(grad_branch, branch_here, piece_sem.at[1]))
    for copy in fetched:
        copy.start()
    for copy in fetched:
        copy.wait()
    f32, bf16 = jnp.float32, jnp.bfloat16
    row = lax.broadcasted_iota(jnp.int32, (8, channels), 0)
    rate = vectors[CW + 3 : CW + 4, :]
    nothing = jnp.zeros((8, channels), f32)

    @pl.loop(0, CHIPS)
    def scan_block(j):
        grad_mixed[j] = lax.dot_general(
            branch_here[j], out_here[...], (((1,), (1,)), ((), ())), preferred_element_type=f32
        )

        def scan_tile(i, carry):
            i = rows // 16 - 1 - i
            at = sixteen(i)
            v = gate_pre[j, at, :]
            grad = grad_mixed[j, at, :]
            t = jnp.tanh(GELU_A * (v + GELU_B * (v * v * v)))
            act = 0.5 * v * (1.0 + t)
            slope = 0.5 * (1.0 + t) + 0.5 * v * (1.0 - t * t) * (GELU_A * (1.0 + 3.0 * GELU_B * (v * v)))
            in_low[j, at, 0:channels] = (grad * states[j, at, :] * slope).astype(bf16)
            drive = grad * act
            later_a, later_b, later_coef = carry
            for h in (1, 0):
                here = eight(2 * i + h)
                flag = masks[j, here, :][:, 0:1]
                coef = gate_terms(decay_pre[j, here, :], rate, flag)[1]
                shifted = jnp.where(row < 7, pltpu.roll(coef, 7, 0), later_coef)
                a, b = tile_scan(shifted, drive[8 * h : 8 * h + 8], row, True)
                b = a * later_b + b
                a = a * later_a
                cumulative[j, here, :] = a
                local[j, here, :] = b
                later_a, later_b, later_coef = a[0:1], b[0:1], coef[0:1]
            return later_a, later_b, later_coef

        ones = jnp.ones((1, channels), f32)
        first_a, first_b, first_coef = lax.fori_loop(
            0, rows // 16, scan_tile, (ones, jnp.zeros((1, channels), f32), ones), unroll=2
        )
        everyone[c, z, pl.ds(j, 1), :] = first_coef * first_a
        everyone[c, z, pl.ds(CHIPS + j, 1), :] = first_coef * first_b

    carry_in(planes, True, z, c, me, everyone, before, leaving, send, recv)
    down_forward()
    for copy in swaps:
        copy.start()

    def terms_block(j, totals):
        behind_all = leaving[pl.ds(j, 1), :]

        def terms_tile(i, carry):
            previous, decay_sum, input_sum, param_sum = carry
            lows = []
            for h in range(2):
                at = eight(2 * i + h)
                adjoint = local[j, at, :] + cumulative[j, at, :] * behind_all
                state = states[j, at, :]
                earlier = jnp.where(row >= 1, pltpu.roll(state, 1, 0), previous)
                previous = state[7:8]
                flag = masks[j, at, :][:, 0:1]
                opened, coef, keep, squared, gap = gate_terms(decay_pre[j, at, :], rate, flag)
                passed = sigmoid(input_pre[j, at, :])
                conv = conv_out[j, at, :]
                inverse = lax.rsqrt(gap)
                scale = flag + keep * (gap * inverse)
                grad_log = adjoint * (earlier * coef - keep * passed * conv * squared * inverse)
                log_open = grad_log * opened
                decay_full = log_open * rate * (1.0 - opened)
                direct = adjoint * scale * passed
                input_full = direct * (1.0 - passed) * conv
                grad_conv[j, at, :] = direct
                lows.append((decay_full, input_full))
                decay_sum = decay_sum + decay_full
                input_sum = input_sum + input_full
                param_sum = param_sum + log_open
            decay_low[j, sixteen(i), :] = jnp.concatenate([low[0] for low in lows], axis=0).astype(bf16)
            input_low[j, sixteen(i), :] = jnp.concatenate([low[1] for low in lows], axis=0).astype(bf16)
            return previous, decay_sum, input_sum, param_sum

        totals = lax.fori_loop(
            0, rows // 16, terms_tile, (entering[pl.ds(j, 1), :], *totals), unroll=2
        )[1:]

        def dot_t(left, right):
            return lax.dot_general(left, right, (((1,), (1,)), ((), ())), preferred_element_type=f32)

        grad_conv[j] = (
            grad_conv[j] + dot_t(decay_low[j], decay_blocks[...]) + dot_t(input_low[j], input_blocks[...])
        )
        return totals

    decay_sum, input_sum, param_sum = lax.fori_loop(0, CHIPS, terms_block, (nothing,) * 3)

    to_sibling = remote(grad_conv.at[:, pl.ds(0, 8)], sibling_heads, send.at[7], recv.at[7], me + 1 - 2 * c)
    to_below = remote(grad_conv.at[0, pl.ds(0, 8)], above_head, send.at[8], recv.at[8], me - 7)
    from_above = remote(grad_conv.at[0, pl.ds(0, 8)], above_head, send.at[8], recv.at[8], me + 7)
    to_sibling.start()

    @pl.when((c == 0) & (z > 0))
    def send_below():
        to_below.start()

    to_sibling.wait()

    @pl.when((c == 0) & (z > 0))
    def sent_below():
        to_below.wait_send()

    @pl.when((c == 1) & (z < planes - 1))
    def had_above():
        from_above.wait_recv()

    @pl.when(c == 0)
    def ahead_zero():
        for j in range(CHIPS):
            ahead[j] = sibling_heads[j]

    @pl.when(c == 1)
    def ahead_one():
        for j in range(CHIPS - 1):
            ahead[j] = sibling_heads[j + 1]

        @pl.when(z < planes - 1)
        def ahead_above():
            ahead[CHIPS - 1] = above_head[...]

        @pl.when(z == planes - 1)
        def ahead_none():
            ahead[CHIPS - 1] = nothing

    def conv_block(j, totals):
        def conv_pair(i, now, later, keep, later_keep, outs, earlier, given, totals):
            out = vectors[0:1, :] * now
            new_totals = [totals[0] + now * given]
            for k in range(1, CW):
                masked = now * keep[:, k : k + 1]
                out = out + vectors[k : k + 1, :] * shift_up(
                    masked, later * later_keep[:, k : k + 1], k, row
                )
                new_totals.append(totals[k] + masked * shift_down(earlier, given, k, row))
            new_totals.append(totals[CW] + now)
            outs.append(out)
            return tuple(new_totals)

        def conv_tile(i, carry, last):
            earlier, totals = carry
            inputs = conv_input[j, sixteen(i), :].astype(f32)
            first, second = grad_conv[j, eight(2 * i), :], grad_conv[j, eight(2 * i + 1), :]
            first_keep, second_keep = masks[j, eight(2 * i), :], masks[j, eight(2 * i + 1), :]
            if last:
                third, third_keep = ahead[j], after_masks[j]
            else:
                third, third_keep = grad_conv[j, eight(2 * i + 2), :], masks[j, eight(2 * i + 2), :]
            outs = []
            totals = conv_pair(i, first, second, first_keep, second_keep, outs, earlier, inputs[:8], totals)
            totals = conv_pair(i, second, third, second_keep, third_keep, outs, inputs[:8], inputs[8:], totals)
            in_low[j, sixteen(i), channels : 2 * channels] = jnp.concatenate(outs, axis=0).astype(bf16)
            return inputs[8:], totals

        carry = lax.fori_loop(
            0, rows // 16 - 1, lambda i, carry: conv_tile(i, carry, False), (halo[j], totals)
        )
        return conv_tile(rows // 16 - 1, carry, True)[1]

    totals = lax.fori_loop(0, CHIPS, conv_block, (nothing,) * (CW + 1))
    for k, total in enumerate((*totals, decay_sum, input_sum, param_sum)):
        sums[k : k + 1, :] = jnp.sum(total, axis=0, keepdims=True)
    down_end()
    own, from_x, from_y = down_scratch[:3]

    @pl.loop(0, own.shape[0] // 16)
    def sum_rows(i):
        at = sixteen(i)
        block_out[at, :] = middle[at, :] + (
            own[at, :].astype(f32) + from_x[at, :].astype(f32) + from_y[at, :].astype(f32)
        )

    for copy in swaps:
        copy.wait()


def recurrence_back(
    grad_branch,
    rows_all,
    gate_pre,
    conv_input,
    conv_out,
    decay_pre,
    input_pre,
    states,
    entering,
    halo,
    masks,
    after_masks,
    vectors,
    decay_blocks,
    input_blocks,
    middle,
    down_parts,
    piece,
    collective_id,
):
    planes = lax.axis_size("seq") // 8
    cube = conv_input.shape
    blocks, rows, channels = cube
    f32, bf16 = jnp.float32, jnp.bfloat16
    return pl.pallas_call(
        functools.partial(recurrence_back_kernel, planes),
        out_shape=[
            jax.ShapeDtypeStruct((CHIPS, rows, 2 * channels), bf16),
            jax.ShapeDtypeStruct(cube, bf16),
            jax.ShapeDtypeStruct(cube, bf16),
            jax.ShapeDtypeStruct((CW + 4, channels), f32),
            jax.ShapeDtypeStruct(down_parts.shape[1:], f32),
            jax.ShapeDtypeStruct(piece.shape, bf16),
        ],
        in_specs=[ANY] * 2 + [VMEM] * 14 + [ANY] * 2,
        out_specs=[VMEM] * 5 + [ANY],
        scratch_shapes=[
            pltpu.VMEM(cube, f32),
            pltpu.VMEM(grad_branch.shape, bf16),
            pltpu.VMEM((channels, grad_branch.shape[2]), bf16),
            pltpu.VMEM(cube, f32),
            pltpu.VMEM(cube, f32),
            pltpu.VMEM(cube, f32),
            pltpu.VMEM((CHIPS, 8, channels), f32),
            pltpu.VMEM((8, channels), f32),
            pltpu.VMEM((CHIPS, 8, channels), f32),
            pltpu.VMEM((2, planes, 2 * CHIPS, channels), f32),
            pltpu.VMEM((8 * planes, channels), f32),
            pltpu.VMEM((CHIPS, channels), f32),
            pltpu.SemaphoreType.DMA((12,)),
            pltpu.SemaphoreType.DMA((12,)),
            pltpu.SemaphoreType.DMA((2,)),
            pltpu.SemaphoreType.DMA((rows_all.shape[0],)),
            *sum_scratch(*down_parts.shape[1:], bf16),
        ],
        compiler_params=comm_params(collective_id, 60),
        cost_estimate=lasting(58),
        name="recurrence_back",
    )(
        grad_branch,
        rows_all,
        gate_pre,
        conv_input,
        conv_out,
        decay_pre,
        input_pre,
        states,
        entering,
        halo,
        masks,
        after_masks,
        vectors,
        decay_blocks,
        input_blocks,
        middle,
        down_parts,
        piece,
    )


def input_grads_kernel(
    normed, normed_other, low, grad, here, there, low_here, low_there, kept, send, recv, loads
):
    me, z, p, c, x, y = place()
    sibling = me + 1 - 2 * c
    greet((sibling,))
    swap = remote(low, low_there, send, recv, sibling)
    swap.start()
    half, columns = grad.shape
    fetched = [
        pltpu.make_async_copy(source, target, loads.at[k])
        for k, (source, target) in enumerate(
            (
                (normed.at[:, pl.ds(pl.multiple_of(c * half, 128), half)], here),
                (low, low_here),
                (normed_other, there),
            )
        )
    ]
    for copy in fetched:
        copy.start()
    for copy in fetched[:2]:
        copy.wait()
    block, tile = 512, 256

    def products(left, right, keep):
        @pl.loop(0, half // block)
        def product_block(m):
            at = pl.ds(pl.multiple_of(m * block, block), block)

            @pl.loop(0, columns // tile)
            def product_tile(k):
                across = pl.ds(pl.multiple_of(k * tile, tile), tile)
                keep(
                    at,
                    across,
                    lax.dot_general(
                        left[:, at], right[:, across], (((0,), (0,)), ((), ())), preferred_element_type=jnp.float32
                    ),
                )

    def keep_first(at, across, values):
        kept[at, across] = values

    def keep_sum(at, across, values):
        grad[at, across] = (kept[at, across] + values).astype(grad.dtype)

    products(here, low_here, keep_first)
    fetched[2].wait()
    swap.wait()
    products(there, low_there, keep_sum)


def input_grads(normed, normed_other, low, collective_id):
    tokens, width = normed.shape
    columns = low.shape[1]
    bf16 = low.dtype
    return pl.pallas_call(
        input_grads_kernel,
        out_shape=jax.ShapeDtypeStruct((width // 2, columns), bf16),
        in_specs=[ANY] * 3,
        out_specs=VMEM,
        scratch_shapes=[
            pltpu.VMEM((tokens, width // 2), bf16),
            pltpu.VMEM((tokens, width // 2), bf16),
            pltpu.VMEM((tokens, columns), bf16),
            pltpu.VMEM((tokens, columns), bf16),
            pltpu.VMEM((width // 2, columns), jnp.float32),
            pltpu.SemaphoreType.DMA,
            pltpu.SemaphoreType.DMA,
            pltpu.SemaphoreType.DMA((3,)),
        ],
        compiler_params=comm_params(collective_id, 60),
        name="input_grads",
    )(normed, normed_other, low)


def regrouped_kernel(back, devices, places, *refs):
    count = 1 + max(place[0] for place in places)
    for source, first, rows, target, row in places:
        source, target = refs[source], refs[count + target]
        step = source.shape[1] // devices
        for k in range(devices // 2):
            for e in range(2):
                split, joined = (2 * k + e) * step, (devices // 2 * e + k) * step
                start, end = (joined, split) if back else (split, joined)
                target[row : row + rows, end : end + step] = source[
                    first : first + rows, start : start + step
                ].astype(target.dtype)


def regrouped_columns(arrays, places, dtypes, back, vmem_mib):
    devices = lax.axis_size("seq")
    sizes = [max(row + rows for unused, unused, rows, m, row in places if m == k) for k in range(len(dtypes))]
    return pl.pallas_call(
        functools.partial(regrouped_kernel, back, devices, places),
        out_shape=[jax.ShapeDtypeStruct((r, arrays[0].shape[1]), dtype) for r, dtype in zip(sizes, dtypes)],
        in_specs=[VMEM] * len(arrays),
        out_specs=[VMEM] * len(dtypes),
        compiler_params=pltpu.CompilerParams(vmem_limit_bytes=vmem_mib * 2**20),
        name="regrouped_columns",
    )(*arrays)


def to_chips_kernel(planes, pairs, *refs):
    ins, outs = refs[: len(pairs)], refs[len(pairs) :]
    for source, targets in zip(ins, pairs):
        width = source.shape[1] // (planes * 8)
        for z in range(planes):
            for p in range(CHIPS):
                for c in range(2):
                    k, at = targets[c]
                    start = ((z * CHIPS + p) * 2 + c) * width
                    outs[k][p, :, at + z * width : at + (z + 1) * width] = source[:, start : start + width]


def from_chips_kernel(planes, pairs, *refs):
    outs, ins = refs[-len(pairs) :], refs[: -len(pairs)]
    for target, sources in zip(outs, pairs):
        width = target.shape[1] // (planes * 8)
        for z in range(planes):
            for p in range(CHIPS):
                for c in range(2):
                    k, at = sources[c]
                    start = ((z * CHIPS + p) * 2 + c) * width
                    target[:, start : start + width] = ins[k][
                        p, :, at + z * width : at + (z + 1) * width
                    ].astype(jnp.float32)


def from_chips(parts, pairs, widths):
    planes = lax.axis_size("seq") // 8
    return pl.pallas_call(
        functools.partial(from_chips_kernel, planes, pairs),
        out_shape=[jax.ShapeDtypeStruct((parts[0].shape[1], width), jnp.float32) for width in widths],
        in_specs=[VMEM] * len(parts),
        out_specs=[VMEM] * len(widths),
        compiler_params=pltpu.CompilerParams(vmem_limit_bytes=32 * 2**20),
        name="from_chips",
    )(*parts)


def regrouped(values, axis, n):
    shape = values.shape
    split = shape[:axis] + (n // 2, 2, shape[axis] // n) + shape[axis + 1 :]
    return jnp.moveaxis(values.reshape(split), axis + 1, axis).reshape(shape)


def behind(value, *earlier):
    return lax.optimization_barrier((value, *earlier))[0]


def plane_body(
    tokens,
    starts,
    cotangent,
    norm_gain,
    gate_branch,
    input_branch,
    conv_weight,
    conv_bias,
    decay_gate,
    decay_bias,
    input_gate,
    input_bias,
    decay_param,
    out_proj,
    mlp_gain,
    mlp_gate,
    mlp_up,
    mlp_down,
):
    f32, bf16 = jnp.float32, jnp.bfloat16
    n = lax.axis_size("seq")
    planes = n // 8
    me, z, p, c, x, y = place()
    groups = column_groups(n)
    rows, width = tokens.shape
    rows_d, lru_width = gate_branch.shape
    head = decay_gate.shape[1]
    rows_r, rows_f = out_proj.shape[0], mlp_down.shape[0]
    channels = lru_width // CHIPS
    units = mlp_gate.shape[1] // CHIPS
    half_units = units // 2

    def column_gather(block):
        return lax.all_gather(block, "seq", axis=0, tiled=True, axis_index_groups=groups)

    def line_sum(parts):
        return lax.psum_scatter(
            parts, "seq", scatter_dimension=0, tiled=True, axis_index_groups=line_groups(n)
        )

    def product(left, right):
        return jnp.dot(left, right, preferred_element_type=f32)

    def product_t(left, right):
        return jnp.einsum("tk,nk->tn", left, right, preferred_element_type=f32)

    def weight_grad(left, right):
        return jnp.einsum("ta,tb->ab", left, right, preferred_element_type=f32)

    lanes = 128

    def row(values):
        return jnp.pad(values.astype(f32), (0, lanes - values.shape[0]))[None]

    small = jnp.concatenate(
        [
            row(norm_gain),
            row(mlp_gain),
            starts.astype(f32).reshape(rows // lanes, lanes),
            *[row(conv_weight[k]) for k in range(CW)],
            row(conv_bias),
            row(decay_bias),
            row(input_bias),
            row(decay_param),
            jnp.zeros((4, lanes), f32),
        ],
        axis=0,
    )
    half = channels // 2
    in_pairs = (((0, 0), (0, half)), ((0, channels), (0, channels + half)))
    swapped_in, gates = first_swap(
        [gate_branch, input_branch], in_pairs, 2 * channels, [decay_gate, input_gate], 2
    )
    whole_in = column_gather(swapped_in.reshape(CHIPS * rows_d, 2 * channels))
    tokens, cot, row_shards = regrouped_columns(
        [tokens, cotangent, out_proj, mlp_down],
        [(0, 0, rows, 0, 0), (1, 0, rows, 1, 0), (2, 0, rows_r, 2, 0), (3, 0, rows_f, 2, rows_r)],
        [bf16] * 3,
        False,
        60,
    )
    mlp_pairs = (((0, 0), (1, 0)), ((0, half_units), (1, half_units)))
    small, decay_blocks, input_blocks, second_part, normed_all, first_piece = opening(
        behind(small, swapped_in), gates, tokens, mlp_gate, mlp_up, mlp_pairs, 1
    )
    normed_all = normed_all.reshape(CHIPS * rows, width)
    small = small.transpose(1, 0, 2, 3)
    flags = 2 + rows // lanes
    gain_one = regrouped(small[:, :, 0, :rows_d].reshape(width), 0, n)
    gain_two = regrouped(small[:, :, 1, :rows_d].reshape(width), 0, n)
    all_flags = small[:, :, 2:flags].reshape(n * rows)
    vectors = lax.dynamic_slice_in_dim(
        small.reshape(planes, CHIPS, 2, 16, lanes), p, 1, axis=1
    )[:, 0, :, flags : flags + CW + 4, :rows_r]
    vectors = vectors.transpose(2, 1, 0, 3).reshape(CW + 4, channels)
    param = vectors[CW + 3]
    vectors = vectors.at[CW + 3].set(-rate_scale * jax.nn.softplus(param))

    running = jnp.ones((n * rows,), f32)
    masks_all = [running]
    for offset in range(1, CW):
        earlier = jnp.concatenate([jnp.zeros((offset - 1,), f32), all_flags[: n * rows - (offset - 1)]])
        running = running * (1.0 - earlier)
        masks_all.append(running)
    masks_all = jnp.stack(masks_all).reshape(CW, planes, CHIPS, 2, rows)

    def own_blocks(values):
        return lax.dynamic_slice(
            values,
            (0, z, 0, c, 0),
            (values.shape[0], 1, CHIPS, 1, values.shape[4]),
        )[:, 0, :, 0]

    after_masks = masks_all[..., :8].reshape(CW, n, 8)
    after_masks = jnp.concatenate([after_masks[:, 1:], jnp.zeros((CW, 1, 8), f32)], axis=1)
    after_masks = own_blocks(after_masks.reshape(CW, planes, CHIPS, 2, 8)).transpose(1, 2, 0)
    masks_all = jnp.concatenate([all_flags.reshape(1, planes, CHIPS, 2, rows), masks_all[1:]], axis=0)
    masks = own_blocks(masks_all).transpose(1, 2, 0)

    rows_all = column_gather(behind(row_shards, swapped_in)).reshape(2 * planes, rows_r + rows_f, width)

    gate_pre = product(normed_all, whole_in[:, :channels])
    cube = (CHIPS, rows, channels)
    gate_pre = gate_pre.reshape(cube)
    conv_input = product(normed_all, whole_in[:, channels:]).astype(bf16).reshape(cube)
    conv_out, conv_low, decay_pre, input_pre, states, mixed, *mixeds, entering, halo, cot_all, second_piece, normed_other = recurrence(
        gate_pre,
        conv_input,
        masks,
        vectors,
        decay_blocks,
        input_blocks,
        cot,
        second_part,
        normed_all,
        6,
    )
    whole_mlp = [
        column_gather(part.reshape(CHIPS * rows_d, 2 * half_units)) for part in (first_piece, second_piece)
    ]
    cot_all = cot_all.reshape(CHIPS * rows, width)
    middle, two_all, cot_other = middle_of(mixed, rows_all, tokens, gain_two, cot_all, 7)
    mixeds = [part.reshape(CHIPS * rows, channels // 2) for part in mixeds]
    two_all = two_all.reshape(CHIPS * rows, width)

    hidden_zero, first_grad, first_parts = feed_forward(0, two_all, cot_all, whole_mlp[0], rows_all, (), 8)
    hidden_one, second_grad, two_parts = feed_forward(
        1, two_all, cot_all, whole_mlp[1], rows_all, (first_parts,), 14
    )
    piece_grads = [line_sum(first_grad), line_sum(second_grad)]
    grad_middle, grad_mlp_gain, grad_branch, row_grads, down_parts = grads_of_middle(
        two_parts.reshape(CHIPS, rows, width),
        middle,
        cot,
        gain_two,
        (hidden_zero, hidden_one),
        rows_all,
        (cot_all, cot_other),
        mixeds,
        9,
    )
    grad_rows = line_sum(row_grads.reshape(planes * (rows_r + rows_f), width))

    in_low, grad_decay_low, grad_input_low, sums, block_out, first_swapped = recurrence_back(
        grad_branch,
        rows_all,
        gate_pre,
        conv_input,
        conv_out,
        decay_pre,
        input_pre,
        states,
        entering,
        halo,
        masks,
        after_masks,
        vectors,
        decay_blocks,
        input_blocks,
        middle,
        down_parts,
        piece_grads[0].reshape(CHIPS, rows_d, 2 * half_units),
        12,
    )
    sums = sums.at[CW + 3].multiply(-rate_scale * jax.nn.sigmoid(param))
    low_cube = in_low
    in_low = low_cube.reshape(CHIPS * rows, 2 * channels)
    flat = (CHIPS * rows, channels)
    conv_low, grad_decay_low, grad_input_low = (
        a.reshape(flat) for a in (conv_low, grad_decay_low, grad_input_low)
    )

    in_total = input_grads(normed_all, normed_other, in_low, 15)
    in_grads = line_sum(in_total)
    low_cube = behind(low_cube, in_total)
    vector_parts = sums.reshape(CW + 4, 2, planes, rows_r).transpose(2, 1, 0, 3)
    vector_parts = jnp.pad(vector_parts, ((0, 0), (0, 0), (0, 0), (0, lanes - rows_r)))
    grad_tokens, small_grads, gate_grads, second_swapped = closing(
        low_cube,
        whole_in,
        tokens,
        gain_one,
        grad_middle,
        vector_parts,
        grad_mlp_gain,
        (conv_low, grad_decay_low, grad_input_low),
        piece_grads[1].reshape(CHIPS, rows_d, 2 * half_units),
        head,
        13,
    )
    grad_mlp_gate, grad_mlp_up = from_chips(
        [first_swapped, second_swapped], mlp_pairs, [mlp_gate.shape[1]] * 2
    )
    block_out, grad_out_proj, grad_mlp_down = regrouped_columns(
        [block_out, behind(grad_rows, grad_tokens)],
        [(0, 0, rows, 0, 0), (1, 0, rows_r, 1, 0), (1, rows_r, rows_f, 2, 0)],
        [bf16, f32, f32],
        True,
        24,
    )
    in_grads = behind(in_grads, grad_out_proj)
    in_out = plane_swap([in_grads.reshape(CHIPS, rows_d, 2 * channels)], 16)
    grad_gate_branch, grad_input_branch = from_chips(in_out, in_pairs, [lru_width] * 2)
    vector_grads = small_grads[: CW + 4, :rows_r]
    return (
        block_out,
        grad_tokens,
        small_grads[CW + 4, :rows_d],
        grad_gate_branch,
        grad_input_branch,
        vector_grads[:CW],
        vector_grads[CW],
        gate_grads[:, :head],
        vector_grads[CW + 1],
        gate_grads[:, head:],
        vector_grads[CW + 2],
        vector_grads[CW + 3],
        grad_out_proj,
        small_grads[CW + 4, rows_d : 2 * rows_d],
        grad_mlp_gate,
        grad_mlp_up,
        grad_mlp_down,
    )


def solution(mesh):
    in_specs = (
        P("seq", None),
        P("seq"),
        P("seq", None),
        P("seq"),
        P("seq", None),
        P("seq", None),
        P(None, "seq"),
        P("seq"),
        P("seq", None),
        P("seq"),
        P("seq", None),
        P("seq"),
        P("seq"),
        P("seq", None),
        P("seq"),
        P("seq", None),
        P("seq", None),
        P("seq", None),
    )
    out_specs = (
        P("seq", None),
        P("seq", None),
        P("seq"),
        P("seq", None),
        P("seq", None),
        P(None, "seq"),
        P("seq"),
        P("seq", None),
        P("seq"),
        P("seq", None),
        P("seq"),
        P("seq"),
        P("seq", None),
        P("seq"),
        P("seq", None),
        P("seq", None),
        P("seq", None),
    )
    body = plane_body if mesh.shape["seq"] == 2 * H else token_split_body
    return jax.shard_map(body, mesh=mesh, in_specs=in_specs, out_specs=out_specs, check_vma=False)
```
